32 devices in a mesh: groups: 2 (over y), wide: 4 (over z), sub: 2 (over x), pair: 2 (over core).
Axes of the slice: x: 2, y: 2, z: 4, core: 2. Of those that a mesh axis runs over, the one named last changes fastest.
Arguments:
- latent_cache: bfloat16 [32, 768, 576], P(('groups', 'sub', 'pair'), 'wide'), parts along dimension 0, may hold values from -4 to 4
- queries: bfloat16 [32, 128, 576], P(('groups', 'sub', 'pair'), 'wide'), parts along dimension 0, may hold values from -192 to 192
- new_latent: bfloat16 [32, 576], P(('groups', 'sub', 'pair')), parts along dimension 0, may hold values from -4.5 to 4.5
- context_len: int32 [32], P(('groups', 'sub', 'pair')), parts along dimension 0, may hold values from 195 to 768, as said below
- block_start: int32 [32, 4], P(('groups', 'sub', 'pair')), parts along dimension 0, may hold values from 0 to 576, as said below
- owner: int32 [32], P('groups'), parts along dimension 0, may hold values from 0 to 3, as said below
- value_up: bfloat16 [128, 512, 128], P(('wide', 'sub'), None, 'pair'), may hold values from -1 to 1
- out_proj: bfloat16 [128, 128, 7168], P(('wide', 'sub'), 'pair'), may hold values from -0.25 to 0.25
- residual_in: bfloat16 [32, 7168], P(('groups', 'sub', 'pair'), 'wide'), parts along dimension 0, may hold values from -8 to 8
- norm_gain: bfloat16 [7168], P('wide'), may hold values from 0.5 to 1.5
- gate_up: bfloat16 [2, 7168, 18432], P(None, None, ('wide', 'sub', 'pair')), may hold values from -0.0625 to 0.0625
- down_weight: bfloat16 [18432, 7168], P(('wide', 'sub', 'pair')), may hold values from -0.0625 to 0.0625
Outputs:
- mixed: bfloat16 [32, 7168], P(('groups', 'sub', 'pair'), 'wide'), parts along dimension 0
The draws below stay inside these ranges and needn't reach their ends.
There are 2 independent parts, one for each index of `groups`. The reference program is written for one: setup_inputs(seed, part) draws one part's arguments, and reference() takes and returns one part's arrays. A program takes and returns all parts, laid end to end along the dimension named above; an argument that names none is the same for every part. Nothing has to cross between parts.
Inputs may be any that keep to these rules, and one draw needn't show every extreme that they name: `context_len`: live rows of one request on one prefill shard number 1 to 192; every request has a full block, and in every draw some request is full on every shard. `block_start`: each row rises from 0; block w + 1 starts at most 192 positions after block w and the request's length is at most 192 past its last start. Within each run of 4 consecutive requests no owner serves more than 1 of them, and some owner serves exactly 1.
All inputs are finite; a program needn't handle non-finite values.
Results may differ from the reference program's by a relative error of at most 0.0075.
Values may be sent and summed in bfloat16 or wider, within the bound.
No kernel may reach another device: no remote copies, remote signals or barrier semaphores. Data moves between devices by JAX's collectives and lax.ppermute only.
A program may use at most 192 MiB of HBM per device.

```python
import jax
import jax.numpy as jnp
from jax import lax

D = 7168
FF = 18432
H = 128
KV_RANK = 512
ROPE = 64
NOPE = 128
VHEAD = 128
REQ_GRP = 4
BLOCK = 192
LATENT = 576
REQUESTS = 16
OWN_MAX = 1
CONTEXT = 768
N_WIDE = 4


def cache_base(key):
    return jnp.clip(jax.random.normal(key, (REQUESTS, CONTEXT, LATENT), jnp.float32), -4.0, 4.0)


def block_lengths(key):
    first, second, third = jax.random.split(key, 3)
    lengths = jax.random.randint(first, (REQUESTS, N_WIDE), 1, BLOCK + 1)
    column = jax.random.randint(second, (REQUESTS, 1), 0, N_WIDE)
    lengths = jnp.where(jnp.arange(N_WIDE)[None, :] == column, BLOCK, lengths)
    chosen = jax.random.randint(third, (), 0, REQUESTS)
    return jnp.where(jnp.arange(REQUESTS)[:, None] == chosen, BLOCK, lengths)


def draw_latent_cache(key, part):
    return cache_base(key).astype(jnp.bfloat16)


def draw_queries(key, part):
    key = jax.random.fold_in(key, 3)
    values = jnp.clip(0.85 * jax.random.normal(key, (REQUESTS, H, LATENT), jnp.float32), -3.4, 3.4)
    return values.astype(jnp.bfloat16)


def draw_new_latent(key, part):
    key = jax.random.fold_in(key, 4)
    first = jax.random.fold_in(key, 0)
    drawn = jnp.clip(jax.random.normal(first, (REQUESTS, LATENT), jnp.float32), -4.0, 4.0)
    return drawn.astype(jnp.bfloat16)


def draw_context_len(key, part):
    lengths = block_lengths(key)
    return jnp.sum(lengths, axis=1).astype(jnp.int32)


def draw_block_start(key, part):
    lengths = block_lengths(key)
    return (jnp.cumsum(lengths, axis=1) - lengths).astype(jnp.int32)


def draw_owner(key, part):
    key = jax.random.fold_in(key, 5)
    keys = jax.random.split(key, REQUESTS // REQ_GRP)

    def one_group(group_key):
        first, second = jax.random.split(group_key)
        wides = jax.random.permutation(first, N_WIDE)
        order = jax.random.permutation(second, REQ_GRP)
        picks = wides[jnp.arange(REQ_GRP) // OWN_MAX % N_WIDE]
        return jnp.zeros((REQ_GRP,), jnp.int32).at[order].set(picks.astype(jnp.int32))
    return jax.vmap(one_group)(keys).reshape(REQUESTS).astype(jnp.int32)


def draw_residual_in(key, part):
    key = jax.random.fold_in(key, 7)
    first = jax.random.fold_in(key, 0)
    columns = jnp.arange(D, dtype=jnp.float32) / D
    values = 0.5 * jnp.clip(jax.random.normal(first, (REQUESTS, D), jnp.float32), -4.0, 4.0) * jnp.exp(1.0986 * columns)[None, :]
    return values.astype(jnp.bfloat16)


def spiked(result, stream_key, source, target, blocks, factor):
    def block_of(dim):
        return (jnp.arange(result.shape[dim]) // (result.shape[dim] // blocks)).reshape((-1,) + (1,) * (result.ndim - 1 - dim))

    one_side = jax.random.permutation(stream_key, blocks)[block_of(target)]
    other_side = (block_of(target) + blocks // 2) % blocks
    return jnp.where((block_of(source) == one_side) | (block_of(source) == other_side), factor * result, result)


def level_of(key, shape, shards, least, top_value):
    gain = 1.0
    for axis_at, shards_of in shards:
        steps = jax.random.uniform(jax.random.fold_in(jax.random.fold_in(key, 6), axis_at), (shards_of,), jnp.float32, least / len(shards), top_value / len(shards))
        gain = gain * jnp.repeat(jnp.exp(steps), shape[axis_at] // shards_of).reshape((-1,) + (1,) * (len(shape) - 1 - axis_at))
    return gain


def noise(rng, dims, width, reach, cuts=(), held_as=jnp.bfloat16):
    loudness = level_of(rng, dims, cuts, -0.22, 0.18) if cuts else 1.0
    result = jax.random.normal(rng, dims, jnp.float32) * width * loudness
    return jnp.minimum(jnp.maximum(result, -reach), reach).astype(held_as)


def heavy_noise(rng, dims, deviation, limit, pieces, heavy, kind=jnp.bfloat16):
    drawn = deviation * jax.random.normal(rng, dims, jnp.float32)
    if pieces:
        drawn = drawn * level_of(rng, dims, pieces, -0.22, 0.18)
    return jnp.clip(spiked(drawn, jax.random.fold_in(rng, 3), *heavy), -limit, limit).astype(kind)


def setup_inputs(seed: int = 0, part: int = 0) -> dict:
    key_list = jax.random.split(jax.random.key(seed), 13)
    own_keys = jax.random.split(jax.random.fold_in(key_list[12], part), 13)
    return {
        "latent_cache": draw_latent_cache(jax.random.fold_in(jax.random.fold_in(key_list[12], part), 71), part),
        "queries": draw_queries(jax.random.fold_in(jax.random.fold_in(key_list[12], part), 71), part),
        "new_latent": draw_new_latent(jax.random.fold_in(jax.random.fold_in(key_list[12], part), 71), part),
        "context_len": draw_context_len(jax.random.fold_in(jax.random.fold_in(key_list[12], part), 71), part),
        "block_start": draw_block_start(jax.random.fold_in(jax.random.fold_in(key_list[12], part), 71), part),
        "owner": draw_owner(jax.random.fold_in(jax.random.fold_in(key_list[12], part), 71), part),
        "value_up": noise(key_list[6], (H, KV_RANK, VHEAD), (KV_RANK // 16) ** -0.5, 1.0, ((0, 8), (2, 2))),
        "out_proj": heavy_noise(key_list[7], (H, VHEAD, D), (H * VHEAD // 16) ** -0.5, 0.25, ((0, 8), (1, 2)), (0, 2, 8, 2.0)),
        "residual_in": draw_residual_in(jax.random.fold_in(jax.random.fold_in(key_list[12], part), 71), part),
        "norm_gain": jnp.clip(1.0 + 0.1 * jax.random.normal(key_list[9], (D,), jnp.float32), 0.5, 1.5).astype(jnp.bfloat16),
        "gate_up": noise(key_list[10], (2, D, FF), D ** -0.5, 0.0625, ((2, 16),)),
        "down_weight": heavy_noise(key_list[11], (FF, D), FF ** -0.5, 0.0625, ((0, 16),), (0, 1, 16, 2.0)),
    }


def attend_one(items):
    cache_rows, query_rows, fresh, live = items
    scale = (NOPE + ROPE) ** (-0.5)
    scores = jnp.dot(query_rows, cache_rows.T, preferred_element_type=jnp.float32) * scale
    scores = jnp.where(live[None, :], scores, jnp.float32(-1e+30))
    own_score = jnp.dot(query_rows, fresh, preferred_element_type=jnp.float32) * scale
    top = jnp.maximum(lax.optimization_barrier(jnp.max(scores, axis=1)), own_score)
    expo = jnp.exp(scores - top[:, None])
    expo_own = jnp.exp(own_score - top)
    den = lax.optimization_barrier(jnp.sum(expo, axis=1)) + expo_own
    num = jnp.dot(expo.astype(jnp.bfloat16), cache_rows[:, :KV_RANK], preferred_element_type=jnp.float32)
    num = num + expo_own.astype(jnp.bfloat16).astype(jnp.float32)[:, None] * fresh[:KV_RANK].astype(jnp.float32)[None, :]
    return (num / den[:, None]).astype(jnp.bfloat16)

def reference(latent_cache, queries, new_latent, context_len, block_start, owner, value_up, out_proj, residual_in, norm_gain, gate_up, down_weight):
    following = jnp.concatenate([block_start[:, 1:], context_len[:, None]], axis=1)
    blen = following - block_start
    inner = jnp.arange(BLOCK, dtype=jnp.int32)
    live = (inner[None, None, :] < blen[:, :, None]).reshape(REQUESTS, CONTEXT)
    attn = lax.map(attend_one, (latent_cache, queries, new_latent, live))
    vals = jnp.einsum('rhc,hck->rhk', attn.astype(jnp.float32), value_up.astype(jnp.float32)).astype(jnp.bfloat16)
    proj = jnp.dot(vals.reshape(REQUESTS, H * VHEAD), out_proj.reshape(H * VHEAD, D), preferred_element_type=jnp.float32)
    stream = residual_in.astype(jnp.float32) + proj
    meansq = lax.optimization_barrier(jnp.mean(stream * stream, axis=1))
    normed = (stream * lax.rsqrt(meansq + 1e-06)[:, None] * norm_gain.astype(jnp.float32)[None, :]).astype(jnp.bfloat16)
    gate = jnp.dot(normed, gate_up[0], preferred_element_type=jnp.float32)
    upper = jnp.dot(normed, gate_up[1], preferred_element_type=jnp.float32)
    hidden = (jax.nn.silu(gate) * upper).astype(jnp.bfloat16)
    out = stream + jnp.dot(hidden, down_weight, preferred_element_type=jnp.float32)
    owners = owner.reshape(REQUESTS // REQ_GRP, REQ_GRP)
    order = jnp.argsort(owners, axis=1, stable=True).astype(jnp.int32)
    rows = (jnp.arange(REQUESTS // REQ_GRP, dtype=jnp.int32)[:, None] * REQ_GRP + order).reshape(REQUESTS)
    return out[rows].astype(jnp.bfloat16)
```

```python
import jax
import jax.numpy as jnp
from jax import lax
from jax.sharding import PartitionSpec as P

D = 7168
KV_RANK = 512
ROPE = 64
NOPE = 128


def hop(x, axis, k):
    n = lax.axis_size(axis)
    return lax.ppermute(x, axis, [(i, i ^ k) for i in range(n)])


def split3(x):
    hi = lax.reduce_precision(x, 8, 7)
    mid = lax.reduce_precision(x - hi, 8, 7)
    lo = lax.reduce_precision(x - hi - mid, 8, 7)
    return jnp.stack([hi, mid, lo], axis=-1).astype(jnp.bfloat16)


def attend_block(q, cache, live, scale):
    scores = jnp.einsum("rhc,rjc->rhj", q, cache, preferred_element_type=jnp.float32) * scale
    scores = jnp.where(live[:, None, :], scores, jnp.float32(-1e30))
    top = jnp.max(scores, axis=2, keepdims=True)
    expo = jnp.exp(scores - top)
    den = jnp.sum(expo, axis=2)
    num = jnp.einsum(
        "rhj,rjc->rhc",
        expo.astype(jnp.bfloat16),
        cache[..., :KV_RANK],
        preferred_element_type=jnp.float32,
    )
    return (num / den[..., None]).astype(jnp.bfloat16), top[..., 0] + jnp.log(den)


def scatter_rows(x, n_sub, n_pair, rows):
    total = x[:, 0]
    for k in range(1, n_pair):
        total = total + hop(x[:, k].astype(jnp.bfloat16), "pair", k).astype(jnp.float32)
    out = total[0]
    for k in range(1, n_sub):
        out = out + hop(total[k].astype(jnp.bfloat16), "sub", k).astype(jnp.float32)
    return out


def body(
    latent_cache,
    queries,
    new_latent,
    context_len,
    block_start,
    owner,
    value_up,
    out_proj,
    residual_in,
    norm_gain,
    gate_up,
    down_weight,
):
    n_wide = lax.axis_size("wide")
    n_sub = lax.axis_size("sub")
    n_pair = lax.axis_size("pair")
    me_wide = lax.axis_index("wide")
    me_sub = lax.axis_index("sub")
    me_pair = lax.axis_index("pair")
    req_grp, block, latent = latent_cache.shape
    n_groups = n_sub * n_pair
    heads_dev = value_up.shape[0]
    heads_loc = queries.shape[1]
    width_dev = residual_in.shape[1]
    units_dev = down_weight.shape[0]
    scale = (NOPE + ROPE) ** (-0.5)
    group = me_sub * n_pair + me_pair

    arrived = [queries] + [hop(queries, "wide", k) for k in range(1, n_wide)]
    following = jnp.concatenate([block_start[:, 1:], context_len[:, None]], axis=1)
    blen = lax.dynamic_index_in_dim(following - block_start, me_wide, 1, keepdims=False)
    live = jnp.arange(block, dtype=jnp.int32)[None, :] < blen[:, None]
    parts, lses = [], []
    for k in range(n_wide):
        part, lse = attend_block(arrived[k], latent_cache, live, scale)
        if k:
            part, lse = hop(part, "wide", k), hop(lse, "wide", k)
        parts.append(part)
        lses.append(lse)
    own_score = (
        jnp.einsum("rhc,rc->rh", queries, new_latent, preferred_element_type=jnp.float32) * scale
    )
    lses.append(own_score)
    lse = jnp.stack(lses)
    top = jnp.max(lse, axis=0)
    weight = jnp.exp(lse - top[None])
    den = jnp.sum(weight, axis=0)
    num = weight[n_wide][..., None] * new_latent[:, None, :KV_RANK].astype(jnp.float32)
    for k in range(n_wide):
        num = num + weight[k][..., None] * parts[k].astype(jnp.float32)
    attn = (num / den[..., None]).astype(jnp.bfloat16)

    by_sub = attn.reshape(req_grp, n_sub, heads_dev, KV_RANK)
    landed = []
    for k in range(n_sub):
        chunk = lax.dynamic_index_in_dim(by_sub, me_sub ^ k, 1, keepdims=False)
        landed.append(hop(chunk, "sub", k) if k else chunk)
    landed = jnp.stack(landed)
    both = jnp.stack([landed] + [hop(landed, "pair", k) for k in range(1, n_pair)], axis=1)
    attn_head = both.reshape(n_groups * req_grp, heads_dev, KV_RANK)
    vals = jnp.einsum(
        "rhc,hck->rhk", attn_head, value_up, preferred_element_type=jnp.float32
    ).astype(jnp.bfloat16)
    head_terms = jnp.einsum("rhk,hkd->rd", vals, out_proj, preferred_element_type=jnp.float32)
    mine = scatter_rows(head_terms.reshape(n_sub, n_pair, req_grp, D), n_sub, n_pair, req_grp)
    mine = mine.astype(jnp.bfloat16).reshape(req_grp, n_wide, width_dev).transpose(1, 0, 2)
    proj = jnp.sum(
        lax.all_to_all(mine, "wide", split_axis=0, concat_axis=0, tiled=True).astype(jnp.float32),
        axis=0,
    )
    stream = residual_in.astype(jnp.float32) + proj
    squares = split3(jnp.sum(stream * stream, axis=1))
    gained = (stream * norm_gain.astype(jnp.float32)[None, :]).astype(jnp.bfloat16)
    sent = jnp.concatenate([gained, jnp.pad(squares, ((0, 0), (0, 125)))], axis=1)
    wide_all = lax.all_gather(sent, "wide", axis=0)
    subs = jnp.stack([wide_all] + [hop(wide_all, "sub", k) for k in range(1, n_sub)])
    pairs = jnp.stack([subs] + [hop(subs, "pair", k) for k in range(1, n_pair)], axis=1)
    rows = pairs.transpose(0, 1, 3, 2, 4).reshape(n_groups * req_grp, n_wide, width_dev + 128)
    square = jnp.sum(rows[:, :, width_dev : width_dev + 3].astype(jnp.float32), axis=(1, 2))
    inv = lax.rsqrt(square / D + 1e-06)
    normed = rows[:, :, :width_dev].reshape(n_groups * req_grp, D)
    gate_parts = (
        jnp.einsum("rd,xdf->xrf", normed, gate_up, preferred_element_type=jnp.float32)
        * inv[None, :, None]
    )
    hidden = (jax.nn.silu(gate_parts[0]) * gate_parts[1]).astype(jnp.bfloat16)
    unit_terms = jnp.dot(hidden, down_weight, preferred_element_type=jnp.float32)
    mine = scatter_rows(unit_terms.reshape(n_sub, n_pair, req_grp, D), n_sub, n_pair, req_grp)
    mine = mine.reshape(req_grp, n_wide, width_dev)
    out = stream
    for k in range(n_wide):
        chunk = lax.dynamic_index_in_dim(mine, me_wide ^ k, 1, keepdims=False)
        if k:
            chunk = hop(chunk.astype(jnp.bfloat16), "wide", k).astype(jnp.float32)
        out = out + chunk

    own_grp = lax.dynamic_index_in_dim(owner.reshape(n_groups, req_grp), group, 0, keepdims=False)
    pos_i = jnp.arange(req_grp, dtype=jnp.int32)
    ahead = (own_grp[None, :] < own_grp[:, None]) | (
        (own_grp[None, :] == own_grp[:, None]) & (pos_i[None, :] < pos_i[:, None])
    )
    placed = jnp.sum(ahead.astype(jnp.int32), axis=1)
    source_row = jnp.sum(jnp.where(placed[None, :] == pos_i[:, None], pos_i[None, :], 0), axis=1)
    return out[source_row].astype(jnp.bfloat16)


def solution(mesh):
    in_specs = (
        P(("groups", "sub", "pair"), "wide", None),
        P(("groups", "sub", "pair"), "wide", None),
        P(("groups", "sub", "pair"), None),
        P(("groups", "sub", "pair")),
        P(("groups", "sub", "pair"), None),
        P("groups"),
        P(("wide", "sub"), None, "pair"),
        P(("wide", "sub"), "pair", None),
        P(("groups", "sub", "pair"), "wide"),
        P("wide"),
        P(None, None, ("wide", "sub", "pair")),
        P(("wide", "sub", "pair"), None),
    )
    out_specs = P(("groups", "sub", "pair"), "wide")
    return jax.shard_map(body, mesh=mesh, in_specs=in_specs, out_specs=out_specs, check_vma=False)
```

```python
import functools

import jax
import jax.numpy as jnp
from jax import lax
from jax.experimental import pallas as pl
from jax.experimental.pallas import tpu as pltpu
from jax.sharding import PartitionSpec as P

D = 7168
KV_RANK = 512
ROPE = 64
NOPE = 128
F32 = jnp.float32
BF16 = jnp.bfloat16
TAIL = 16
GAIN_ROW = 8
VMEM = pl.BlockSpec(memory_space=pltpu.VMEM)
SMEM = pl.BlockSpec(memory_space=pltpu.SMEM)


def hop(x, axis, k):
    n = lax.axis_size(axis)
    return lax.ppermute(x, axis, [(i, i ^ k) for i in range(n)])


def eye(rows, cols):
    row = lax.broadcasted_iota(jnp.int32, (rows, cols), 0)
    col = lax.broadcasted_iota(jnp.int32, (rows, cols), 1)
    return (row == col).astype(BF16)


def attend_kernel(place_ref, length_ref, start_ref, q_ref, cache_ref, gain_ref, out_ref):
    req, heads, latent = q_ref.shape
    block = cache_ref.shape[1]
    n_wide = start_ref.shape[1]
    width = gain_ref.shape[1]
    me = place_ref[0]
    scale = (NOPE + ROPE) ** (-0.5)
    lses = []
    for r in range(req):
        following = jnp.where(
            me == n_wide - 1, length_ref[r], start_ref[r, jnp.minimum(me + 1, n_wide - 1)]
        )
        live = following - start_ref[r, me]
        scores = (
            lax.dot_general(
                q_ref[r], cache_ref[r], (((1,), (1,)), ((), ())), preferred_element_type=F32
            )
            * scale
        )
        position = lax.broadcasted_iota(jnp.int32, scores.shape, 1)
        scores = jnp.where(position < live, scores, F32(-1e30))
        top = jnp.max(scores, axis=1, keepdims=True)
        expo = jnp.exp(scores - top)
        den = jnp.sum(expo, axis=1, keepdims=True)
        num = jnp.dot(expo.astype(BF16), cache_ref[r, :, :KV_RANK], preferred_element_type=F32)
        out_ref[r * heads : (r + 1) * heads, :] = (num / den).astype(BF16)
        lses.append(top + jnp.log(den))
    rows = req * heads
    lse = jnp.concatenate(lses, axis=0)
    hi = lse.astype(BF16).astype(F32)
    mid = (lse - hi).astype(BF16).astype(F32)
    lo = (lse - hi - mid).astype(BF16).astype(F32)
    lane = lax.broadcasted_iota(jnp.int32, (rows, 128), 1)
    spread = jnp.where(lane == 0, hi, jnp.where(lane == 1, mid, jnp.where(lane == 2, lo, 0.0)))
    turned = lax.dot_general(
        spread.astype(BF16), eye(rows, 128), (((0,), (0,)), ((), ())), preferred_element_type=F32
    )
    tail = [jnp.pad(turned[:GAIN_ROW], ((0, 0), (0, KV_RANK - 128)))]
    gain = gain_ref[...].astype(F32)
    used = 0
    for at in range(0, width, KV_RANK):
        piece = gain[:, at : at + KV_RANK]
        if piece.shape[1] < KV_RANK:
            piece = jnp.pad(piece, ((0, 0), (0, KV_RANK - piece.shape[1])))
        tail.append(piece)
        used += 1
    tail.append(jnp.zeros((TAIL - GAIN_ROW - used, KV_RANK), F32))
    out_ref[rows:, :] = jnp.concatenate(tail, axis=0).astype(BF16)


def attend(place, length, start, q, cache, gain):
    req, heads, latent = q.shape
    block = cache.shape[1]
    return pl.pallas_call(
        attend_kernel,
        out_shape=jax.ShapeDtypeStruct((req * heads + TAIL, KV_RANK), BF16),
        in_specs=[SMEM, SMEM, SMEM, VMEM, VMEM, VMEM],
        out_specs=VMEM,
        compiler_params=pltpu.CompilerParams(vmem_limit_bytes=16 * 2**20),
        cost_estimate=pl.CostEstimate(
            flops=2 * req * heads * block * (latent + KV_RANK),
            bytes_accessed=2 * req * (block * latent + heads * (latent + KV_RANK)),
            transcendentals=req * heads * block,
        ),
        name="attend",
    )(place, length, start, q, cache, gain)


def combine_kernel(n_wide, n_sub, width, place_ref, q_ref, fresh_ref, *refs):
    payloads, outs, gain_ref, hold = refs[:n_wide], refs[n_wide : n_wide + n_sub], refs[-2], refs[-1]
    req, heads, latent = q_ref.shape
    rows = req * heads
    heads_dev = heads // n_sub
    scale = (NOPE + ROPE) ** (-0.5)
    me_wide, me_sub = place_ref[0], place_ref[1]
    tails = [p[rows:, :].astype(F32) for p in payloads]
    lses = []
    for tail in tails:
        turned = lax.dot_general(
            eye(rows, 128),
            tail[:, :128].astype(BF16),
            (((1,), (1,)), ((), ())),
            preferred_element_type=F32,
        )
        lses.append(turned[:, 0:1] + turned[:, 1:2] + turned[:, 2:3])
    own = jnp.concatenate(
        [
            jnp.sum(q_ref[r].astype(F32) * fresh_ref[r : r + 1, :].astype(F32), axis=1, keepdims=True)
            for r in range(req)
        ],
        axis=0,
    ) * scale
    top = own
    for lse in lses:
        top = jnp.maximum(top, lse)
    own_weight = jnp.exp(own - top)
    weights = [jnp.exp(lse - top) for lse in lses]
    den = own_weight
    for weight in weights:
        den = den + weight
    for r in range(req):
        at = slice(r * heads, (r + 1) * heads)
        num = own_weight[at] * fresh_ref[r : r + 1, :KV_RANK].astype(F32)
        for weight, payload in zip(weights, payloads):
            num = num + weight[at] * payload[at, :].astype(F32)
        attn = (num / den[at]).astype(BF16)
        for s in range(n_sub):
            hold[s, r] = attn[s * heads_dev : (s + 1) * heads_dev]
    for k in range(n_sub):
        outs[k][...] = hold[me_sub ^ k]
    for w in range(n_wide):
        chosen = jnp.zeros((1, width), F32)
        for k in range(n_wide):
            pieces = [
                tails[k][GAIN_ROW + i : GAIN_ROW + i + 1, : min(KV_RANK, width - i * KV_RANK)]
                for i in range(pl.cdiv(width, KV_RANK))
            ]
            gain = pieces[0] if len(pieces) == 1 else jnp.concatenate(pieces, axis=1)
            chosen = jnp.where((me_wide ^ k) == w, gain, chosen)
        gain_ref[:, w * width : (w + 1) * width] = chosen


def combine(place, q, fresh, payloads, n_sub, width):
    req, heads, latent = q.shape
    n_wide = len(payloads)
    heads_dev = heads // n_sub
    piece = jax.ShapeDtypeStruct((req, heads_dev, KV_RANK), BF16)
    out = pl.pallas_call(
        functools.partial(combine_kernel, n_wide, n_sub, width),
        out_shape=[piece] * n_sub + [jax.ShapeDtypeStruct((1, n_wide * width), F32)],
        in_specs=[SMEM, VMEM, VMEM] + [VMEM] * n_wide,
        out_specs=[VMEM] * (n_sub + 1),
        scratch_shapes=[pltpu.VMEM((n_sub, req, heads_dev, KV_RANK), BF16)],
        compiler_params=pltpu.CompilerParams(vmem_limit_bytes=16 * 2**20),
        name="combine",
    )(place, q, fresh, *payloads)
    return out[:n_sub], out[n_sub]


def project_kernel(count, *refs):
    pieces, (up_ref, weight_ref, keep_ref, send_ref, vals) = refs[:count], refs[count:]
    req, heads, rank = pieces[0].shape
    rows = count * req
    cols = up_ref.shape[2]

    @pl.when(pl.program_id(0) == 0)
    def _():
        stacked = jnp.concatenate([p[...].reshape(req * heads, rank) for p in pieces], axis=0)
        total = rows * heads
        to = lax.broadcasted_iota(jnp.int32, (total, total), 0)
        source = lax.broadcasted_iota(jnp.int32, (total, total), 1)
        turn = (to // rows == source % heads) & (to % rows == source // heads)
        turned = jnp.dot(turn.astype(BF16), stacked, preferred_element_type=F32).astype(BF16)
        for h in range(heads):
            val = jnp.dot(
                turned[h * rows : (h + 1) * rows], up_ref[h], preferred_element_type=F32
            )
            vals[:, h * cols : (h + 1) * cols] = val.astype(BF16)

    out = jnp.dot(vals[...], weight_ref[...], preferred_element_type=F32)
    kept = keep_ref.shape[0]
    keep_ref[...] = out[:kept]
    send_ref[...] = out[kept:].astype(BF16)


def project(pieces, value_up, weight, n_pair, steps):
    count = len(pieces)
    req, heads, rank = pieces[0].shape
    rows = count * req
    kept = rows // n_pair
    depth, wide = weight.shape
    cb = wide // steps
    return pl.pallas_call(
        functools.partial(project_kernel, count),
        grid=(steps,),
        out_shape=[
            jax.ShapeDtypeStruct((kept, wide), F32),
            jax.ShapeDtypeStruct((rows - kept, wide), BF16),
        ],
        in_specs=[pl.BlockSpec(p.shape, lambda i: (0, 0, 0)) for p in pieces]
        + [
            pl.BlockSpec(value_up.shape, lambda i: (0, 0, 0)),
            pl.BlockSpec((depth, cb), lambda i: (0, i)),
        ],
        out_specs=[
            pl.BlockSpec((kept, cb), lambda i: (0, i)),
            pl.BlockSpec((rows - kept, cb), lambda i: (0, i)),
        ],
        scratch_shapes=[pltpu.VMEM((rows, depth), BF16)],
        compiler_params=pltpu.CompilerParams(vmem_limit_bytes=24 * 2**20),
        cost_estimate=pl.CostEstimate(
            flops=2 * rows * depth * wide, bytes_accessed=2 * depth * wide, transcendentals=0
        ),
        name="project",
    )(*pieces, value_up, weight)


def merge_kernel(n_wide, place_ref, mine_ref, residual_ref, *refs):
    arrived, (keep_ref, send_ref) = refs[:-2], refs[-2:]
    width = residual_ref.shape[1]
    residual = residual_ref[...].astype(F32)
    for w in range(n_wide):
        at = slice(w * width, (w + 1) * width)
        total = mine_ref[:, at]
        for a in arrived:
            total = total + a[:, at].astype(F32)
        total = total + jnp.where(place_ref[0] == w, residual, 0.0)
        keep_ref[:, at] = total
        send_ref[:, at] = total.astype(BF16)


def merge(place, mine, residual, arrived):
    n_wide = mine.shape[1] // residual.shape[1]
    return pl.pallas_call(
        functools.partial(merge_kernel, n_wide),
        out_shape=[jax.ShapeDtypeStruct(mine.shape, F32), jax.ShapeDtypeStruct(mine.shape, BF16)],
        in_specs=[SMEM] + [VMEM] * (2 + len(arrived)),
        out_specs=[VMEM] * 2,
        compiler_params=pltpu.CompilerParams(vmem_limit_bytes=16 * 2**20),
        name="merge",
    )(place, mine, residual, *arrived)


def norm_kernel(n_wide, place_ref, mine_ref, gain_ref, *refs):
    arrived, (normed_ref, stream_ref) = refs[:-2], refs[-2:]
    width = stream_ref.shape[1]
    total = mine_ref[...]
    for a in arrived:
        total = total + a[...].astype(F32)
    inv = lax.rsqrt(jnp.sum(total * total, axis=1, keepdims=True) / D + 1e-06)
    normed_ref[...] = (total * inv * gain_ref[...]).astype(BF16)
    chosen = jnp.zeros(stream_ref.shape, F32)
    for w in range(n_wide):
        chosen = jnp.where(place_ref[0] == w, total[:, w * width : (w + 1) * width], chosen)
    stream_ref[...] = chosen


def norm(place, mine, gain, arrived, width):
    rows = mine.shape[0]
    return pl.pallas_call(
        functools.partial(norm_kernel, mine.shape[1] // width),
        out_shape=[
            jax.ShapeDtypeStruct(mine.shape, BF16),
            jax.ShapeDtypeStruct((rows, width), F32),
        ],
        in_specs=[SMEM] + [VMEM] * (2 + len(arrived)),
        out_specs=[VMEM] * 2,
        compiler_params=pltpu.CompilerParams(vmem_limit_bytes=16 * 2**20),
        name="norm",
    )(place, mine, gain, *arrived)


def mlp_kernel(count, deep, *refs):
    pieces = refs[:count]
    both_ref, down_ref, keep_ref, send_ref, rows_f32, blocks, gates, hidden = refs[count:]
    step = pl.program_id(0)
    req = pieces[0].shape[0]
    depth = both_ref.shape[1]

    @pl.when(step == 0)
    def _():
        for j, piece in enumerate(pieces):
            rows_f32[j * req : (j + 1) * req, :] = piece[...].astype(F32)
        for j in range(deep):
            blocks[j] = rows_f32[:, j * depth : (j + 1) * depth].astype(BF16)
        gates[...] = jnp.zeros_like(gates)

    @pl.when(step < deep)
    def _():
        x = blocks[step]
        for g in range(2):
            gates[g] += jnp.dot(x, both_ref[g], preferred_element_type=F32)

    @pl.when(step == deep - 1)
    def _():
        gate = gates[0]
        hidden[...] = (gate / (1.0 + jnp.exp(-gate)) * gates[1]).astype(BF16)

    @pl.when(step >= deep)
    def _():
        out = jnp.dot(hidden[...], down_ref[...], preferred_element_type=F32)
        kept = keep_ref.shape[0]
        keep_ref[...] = out[:kept]
        send_ref[...] = out[kept:].astype(BF16)


def mlp(pieces, gate_up, down, n_pair, deep, steps):
    count = len(pieces)
    req, wide = pieces[0].shape
    rows = count * req
    kept = rows // n_pair
    units = down.shape[0]
    cb = wide // steps
    return pl.pallas_call(
        functools.partial(mlp_kernel, count, deep),
        grid=(deep + steps,),
        out_shape=[
            jax.ShapeDtypeStruct((kept, wide), F32),
            jax.ShapeDtypeStruct((rows - kept, wide), BF16),
        ],
        in_specs=[pl.BlockSpec(p.shape, lambda i: (0, 0)) for p in pieces]
        + [
            pl.BlockSpec((2, wide // deep, units), lambda i: (0, jnp.minimum(i, deep - 1), 0)),
            pl.BlockSpec((units, cb), lambda i: (0, jnp.maximum(i - deep, 0))),
        ],
        out_specs=[
            pl.BlockSpec((kept, cb), lambda i: (0, jnp.maximum(i - deep, 0))),
            pl.BlockSpec((rows - kept, cb), lambda i: (0, jnp.maximum(i - deep, 0))),
        ],
        scratch_shapes=[
            pltpu.VMEM((rows, wide), F32),
            pltpu.VMEM((deep, rows, wide // deep), BF16),
            pltpu.VMEM((2, rows, units), F32),
            pltpu.VMEM((rows, units), BF16),
        ],
        compiler_params=pltpu.CompilerParams(vmem_limit_bytes=32 * 2**20),
        cost_estimate=pl.CostEstimate(
            flops=6 * rows * wide * units,
            bytes_accessed=6 * wide * units,
            transcendentals=rows * units,
        ),
        name="mlp",
    )(*pieces, gate_up, down)


def sum_pair(keep, send, n_pair):
    for k in range(1, n_pair):
        rows = keep.shape[0]
        keep = keep + hop(send[(k - 1) * rows : k * rows], "pair", k).astype(F32)
    return keep


def body(
    latent_cache,
    queries,
    new_latent,
    context_len,
    block_start,
    owner,
    value_up,
    out_proj,
    residual_in,
    norm_gain,
    gate_up,
    down_weight,
):
    n_wide = lax.axis_size("wide")
    n_sub = lax.axis_size("sub")
    n_pair = lax.axis_size("pair")
    me_wide = lax.axis_index("wide")
    me_sub = lax.axis_index("sub")
    me_pair = lax.axis_index("pair")
    req_grp, block, latent = latent_cache.shape
    n_groups = n_sub * n_pair
    width_dev = residual_in.shape[1]
    group = me_sub * n_pair + me_pair
    place = jnp.stack([me_wide, me_sub]).astype(jnp.int32)

    arrived = [queries] + [hop(queries, "wide", k) for k in range(1, n_wide)]
    gain_row = norm_gain.reshape(1, width_dev)
    payloads = []
    for k in range(n_wide):
        payload = attend(place, context_len, block_start, arrived[k], latent_cache, gain_row)
        payloads.append(hop(payload, "wide", k) if k else payload)
    chunks, gain = combine(place, queries, new_latent, payloads, n_sub, width_dev)

    landed = [chunks[0]] + [hop(chunks[k], "sub", k) for k in range(1, n_sub)]
    pieces = landed + [hop(p, "pair", k) for k in range(1, n_pair) for p in landed]
    weight = out_proj.reshape(out_proj.shape[0] * out_proj.shape[1], D)
    keep, send = project(pieces, value_up, weight, n_pair, 8)
    total = sum_pair(keep, send, n_pair)
    sent = total.astype(BF16)
    back = [
        hop(sent[k * req_grp : (k + 1) * req_grp], "sub", k) for k in range(1, n_sub)
    ]
    mine, share = merge(place, total[:req_grp], residual_in, back)
    shares = [hop(share, "wide", k) for k in range(1, n_wide)]
    normed, stream = norm(place, mine, gain, shares, width_dev)

    landed = [normed] + [hop(normed, "sub", k) for k in range(1, n_sub)]
    pieces = landed + [hop(p, "pair", k) for k in range(1, n_pair) for p in landed]
    keep, send = mlp(pieces, gate_up, down_weight, n_pair, 8, 8)
    total = sum_pair(keep, send, n_pair)
    sent = total.astype(BF16)
    mine = total[:req_grp]
    for k in range(1, n_sub):
        mine = mine + hop(sent[k * req_grp : (k + 1) * req_grp], "sub", k).astype(F32)
    out = stream
    for k in range(n_wide):
        chunk = lax.dynamic_slice_in_dim(mine, (me_wide ^ k) * width_dev, width_dev, 1)
        if k:
            chunk = hop(chunk.astype(BF16), "wide", k).astype(F32)
        out = out + chunk

    own_grp = lax.dynamic_index_in_dim(owner.reshape(n_groups, req_grp), group, 0, keepdims=False)
    pos_i = jnp.arange(req_grp, dtype=jnp.int32)
    ahead = (own_grp[None, :] < own_grp[:, None]) | (
        (own_grp[None, :] == own_grp[:, None]) & (pos_i[None, :] < pos_i[:, None])
    )
    placed = jnp.sum(ahead.astype(jnp.int32), axis=1)
    source_row = jnp.sum(jnp.where(placed[None, :] == pos_i[:, None], pos_i[None, :], 0), axis=1)
    return out[source_row].astype(BF16)


def solution(mesh):
    in_specs = (
        P(("groups", "sub", "pair"), "wide", None),
        P(("groups", "sub", "pair"), "wide", None),
        P(("groups", "sub", "pair"), None),
        P(("groups", "sub", "pair")),
        P(("groups", "sub", "pair"), None),
        P("groups"),
        P(("wide", "sub"), None, "pair"),
        P(("wide", "sub"), "pair", None),
        P(("groups", "sub", "pair"), "wide"),
        P("wide"),
        P(None, None, ("wide", "sub", "pair")),
        P(("wide", "sub", "pair"), None),
    )
    out_specs = P(("groups", "sub", "pair"), "wide")
    return jax.shard_map(body, mesh=mesh, in_specs=in_specs, out_specs=out_specs, check_vma=False)
```

```python
import functools

import jax
import jax.numpy as jnp
from jax import lax
from jax.experimental import pallas as pl
from jax.experimental.pallas import tpu as pltpu
from jax.sharding import PartitionSpec as P

D = 7168
KV_RANK = 512
ROPE = 64
NOPE = 128
F32 = jnp.float32
BF16 = jnp.bfloat16
TAIL = 8
GAIN_ROW = 3
VMEM = pl.BlockSpec(memory_space=pltpu.VMEM)
SMEM = pl.BlockSpec(memory_space=pltpu.SMEM)
ANY = pl.BlockSpec(memory_space=pl.ANY)


def hop(x, axis, k):
    n = lax.axis_size(axis)
    return lax.ppermute(x, axis, [(i, i ^ k) for i in range(n)])


def eye(rows, cols):
    row = lax.broadcasted_iota(jnp.int32, (rows, cols), 0)
    col = lax.broadcasted_iota(jnp.int32, (rows, cols), 1)
    return (row == col).astype(BF16)


def partial_scores(q_ref, cache_ref, bias):
    req, heads, latent = q_ref.shape
    scores = [
        lax.dot_general(
            q_ref[r], cache_ref[r], (((1,), (1,)), ((), ())), preferred_element_type=F32
        )
        * (NOPE + ROPE) ** (-0.5)
        + bias[r : r + 1, :]
        for r in range(req)
    ]
    return jnp.concatenate(scores, axis=0)


def partial_sums(expo, cache_ref, heads):
    expo = expo.astype(BF16)
    sums = [
        jnp.dot(
            expo[r * heads : (r + 1) * heads],
            cache_ref[r, :, :KV_RANK],
            preferred_element_type=F32,
        )
        for r in range(cache_ref.shape[0])
    ]
    return jnp.concatenate(sums, axis=0)


def payload_tail(lse, tail):
    rows = lse.shape[0]
    hi = lse.astype(BF16).astype(F32)
    mid = (lse - hi).astype(BF16).astype(F32)
    lo = (lse - hi - mid).astype(BF16).astype(F32)
    lane = lax.broadcasted_iota(jnp.int32, (rows, 128), 1)
    spread = jnp.where(lane == 0, hi, jnp.where(lane == 1, mid, jnp.where(lane == 2, lo, 0.0)))
    turned = lax.dot_general(
        spread.astype(BF16), eye(rows, 128), (((0,), (0,)), ((), ())), preferred_element_type=F32
    )
    return tail + jnp.pad(turned[:TAIL], ((0, 0), (0, KV_RANK - 128)))


def prepare_kernel(
    n_wide,
    place_ref,
    length_ref,
    start_ref,
    owner_ref,
    q_ref,
    cache_ref,
    fresh_ref,
    gain_ref,
    residual_ref,
    out_ref,
    bias_ref,
    tail_ref,
    full_ref,
    order_ref,
):
    req, heads, latent = q_ref.shape
    block = cache_ref.shape[1]
    width = gain_ref.shape[1]
    me, group = place_ref[0], place_ref[2]

    owners = [owner_ref[group * req + r] for r in range(req)]
    placed = []
    for r in range(req):
        at = jnp.int32(0)
        for j in range(req):
            if j != r:
                ahead = owners[j] <= owners[r] if j < r else owners[j] < owners[r]
                at = at + jnp.where(ahead, 1, 0)
        placed.append(at)
        order_ref[2 + r] = at
    order_ref[0] = place_ref[1]
    order_ref[1] = me

    rows = []
    for i in range(req):
        row = jnp.zeros((1, width), F32)
        for r in range(req):
            row = jnp.where(placed[r] == i, residual_ref[r : r + 1, :].astype(F32), row)
        rows.append(row)
    mine = jnp.concatenate(rows, axis=0)
    for w in range(n_wide):
        full_ref[:, w * width : (w + 1) * width] = jnp.where(me == w, mine, 0.0)

    gain = gain_ref[...].astype(F32)
    tail = [jnp.zeros((GAIN_ROW, KV_RANK), F32)]
    for at in range(0, width, KV_RANK):
        piece = gain[:, at : at + KV_RANK]
        if piece.shape[1] < KV_RANK:
            piece = jnp.pad(piece, ((0, 0), (0, KV_RANK - piece.shape[1])))
        tail.append(piece)
    tail.append(jnp.zeros((TAIL - GAIN_ROW - len(tail) + 1, KV_RANK), F32))
    tail = jnp.concatenate(tail, axis=0)
    tail_ref[...] = tail

    biases = []
    for r in range(req):
        following = jnp.where(
            me == n_wide - 1, length_ref[r], start_ref[r, jnp.minimum(me + 1, n_wide - 1)]
        )
        position = lax.broadcasted_iota(jnp.int32, (1, block), 1)
        biases.append(jnp.where(position < following - start_ref[r, me], 0.0, F32(-1e30)))
    bias = jnp.concatenate(biases, axis=0)
    bias_ref[...] = bias

    scores = partial_scores(q_ref, cache_ref, bias)
    fresh = [fresh_ref[r : r + 1, :].astype(F32) for r in range(req)]
    own = jnp.concatenate(
        [
            jnp.sum(q_ref[r].astype(F32) * fresh[r], axis=1, keepdims=True)
            * (NOPE + ROPE) ** (-0.5)
            for r in range(req)
        ],
        axis=0,
    )
    top = jnp.maximum(jnp.max(scores, axis=1, keepdims=True), own)
    expo = jnp.exp(scores - top)
    expo_own = jnp.exp(own - top)
    den = jnp.sum(expo, axis=1, keepdims=True) + expo_own
    weight_own = expo_own.astype(BF16).astype(F32)
    num = partial_sums(expo, cache_ref, heads) + jnp.concatenate(
        [weight_own[r * heads : (r + 1) * heads] * fresh[r][:, :KV_RANK] for r in range(req)],
        axis=0,
    )
    count = req * heads
    out_ref[:count, :] = (num / den).astype(BF16)
    out_ref[count:, :] = payload_tail(top + jnp.log(den), tail).astype(BF16)


def attend_cost(req, heads, block, latent):
    return pl.CostEstimate(
        flops=2 * req * heads * block * (latent + KV_RANK),
        bytes_accessed=2 * req * (block * latent + heads * (latent + KV_RANK)),
        transcendentals=req * heads * block,
    )


def prepare(place, length, start, owner, q, cache, fresh, gain, residual):
    req, heads, latent = q.shape
    block, width = cache.shape[1], residual.shape[1]
    n_wide = start.shape[1]
    return pl.pallas_call(
        functools.partial(prepare_kernel, n_wide),
        out_shape=[
            jax.ShapeDtypeStruct((req * heads + TAIL, KV_RANK), BF16),
            jax.ShapeDtypeStruct((req, block), F32),
            jax.ShapeDtypeStruct((TAIL, KV_RANK), F32),
            jax.ShapeDtypeStruct((req, n_wide * width), F32),
            jax.ShapeDtypeStruct((2 + req,), jnp.int32),
        ],
        in_specs=[SMEM] * 4 + [VMEM] * 5,
        out_specs=[VMEM] * 4 + [SMEM],
        compiler_params=pltpu.CompilerParams(vmem_limit_bytes=16 * 2**20),
        cost_estimate=attend_cost(req, heads, block, latent),
        name="prepare",
    )(place, length, start, owner, q, cache, fresh, gain, residual)


def attend_kernel(q_ref, cache_ref, bias_ref, tail_ref, after_ref, out_ref):
    req, heads, latent = q_ref.shape
    scores = partial_scores(q_ref, cache_ref, bias_ref[...])
    top = jnp.max(scores, axis=1, keepdims=True)
    expo = jnp.exp(scores - top)
    den = jnp.sum(expo, axis=1, keepdims=True)
    num = partial_sums(expo, cache_ref, heads)
    count = req * heads
    out_ref[:count, :] = (num / den).astype(BF16)
    out_ref[count:, :] = payload_tail(top + jnp.log(den), tail_ref[...]).astype(BF16)


def attend(q, cache, bias, tail, after):
    req, heads, latent = q.shape
    return pl.pallas_call(
        attend_kernel,
        out_shape=jax.ShapeDtypeStruct((req * heads + TAIL, KV_RANK), BF16),
        in_specs=[VMEM] * 4 + [ANY],
        out_specs=VMEM,
        compiler_params=pltpu.CompilerParams(vmem_limit_bytes=16 * 2**20),
        cost_estimate=attend_cost(req, heads, cache.shape[1], latent),
        name="attend",
    )(q, cache, bias, tail, after)


def combine_kernel(n_wide, n_sub, width, req, order_ref, *refs):
    payloads, outs, gain_ref, hold = refs[:n_wide], refs[n_wide : n_wide + n_sub], refs[-2], refs[-1]
    rows = payloads[0].shape[0] - TAIL
    heads = rows // req
    heads_dev = heads // n_sub
    me_sub, me_wide = order_ref[0], order_ref[1]
    tails = [p[rows:, :].astype(F32) for p in payloads]
    lses = []
    for tail in tails:
        turned = lax.dot_general(
            eye(rows, 128),
            tail[:, :128].astype(BF16),
            (((1,), (1,)), ((), ())),
            preferred_element_type=F32,
        )
        lses.append(turned[:, 0:1] + turned[:, 1:2] + turned[:, 2:3])
    top = functools.reduce(jnp.maximum, lses)
    weights = [jnp.exp(lse - top) for lse in lses]
    inv = 1.0 / functools.reduce(jnp.add, weights)
    weights = [weight * inv for weight in weights]
    for r in range(req):
        at = slice(r * heads, (r + 1) * heads)
        attn = functools.reduce(
            jnp.add, [w[at] * p[at, :].astype(F32) for w, p in zip(weights, payloads)]
        ).astype(BF16)
        for s in range(n_sub):
            hold[s, order_ref[2 + r]] = attn[s * heads_dev : (s + 1) * heads_dev]
    for k in range(n_sub):
        outs[k][...] = hold[me_sub ^ k]
    for w in range(n_wide):
        chosen = jnp.zeros((1, width), F32)
        for k in range(n_wide):
            pieces = [
                tails[k][GAIN_ROW + i : GAIN_ROW + i + 1, : min(KV_RANK, width - i * KV_RANK)]
                for i in range(pl.cdiv(width, KV_RANK))
            ]
            gain = pieces[0] if len(pieces) == 1 else jnp.concatenate(pieces, axis=1)
            chosen = jnp.where((me_wide ^ k) == w, gain, chosen)
        gain_ref[:, w * width : (w + 1) * width] = chosen


def combine(order, payloads, req, n_sub, width):
    n_wide = len(payloads)
    heads_dev = (payloads[0].shape[0] - TAIL) // req // n_sub
    piece = jax.ShapeDtypeStruct((req, heads_dev, KV_RANK), BF16)
    out = pl.pallas_call(
        functools.partial(combine_kernel, n_wide, n_sub, width, req),
        out_shape=[piece] * n_sub + [jax.ShapeDtypeStruct((1, n_wide * width), F32)],
        in_specs=[SMEM] + [VMEM] * n_wide,
        out_specs=[VMEM] * (n_sub + 1),
        scratch_shapes=[pltpu.VMEM((n_sub, req, heads_dev, KV_RANK), BF16)],
        compiler_params=pltpu.CompilerParams(vmem_limit_bytes=16 * 2**20),
        name="combine",
    )(order, *payloads)
    return out[:n_sub], out[n_sub]


def project_kernel(count, *refs):
    pieces, (up_ref, weight_ref, keep_ref, send_ref, vals) = refs[:count], refs[count:]
    req, heads, rank = pieces[0].shape
    rows = count * req
    cols = up_ref.shape[1]

    @pl.when(pl.program_id(0) == 0)
    def _():
        stacked = jnp.concatenate([p[...].reshape(req * heads, rank) for p in pieces], axis=0)
        total = rows * heads
        to = lax.broadcasted_iota(jnp.int32, (total, total), 0)
        source = lax.broadcasted_iota(jnp.int32, (total, total), 1)
        turn = (to // rows == source % heads) & (to % rows == source // heads)
        turned = jnp.dot(turn.astype(BF16), stacked, preferred_element_type=F32).astype(BF16)
        for h in range(heads):
            val = lax.dot_general(
                turned[h * rows : (h + 1) * rows],
                up_ref[h],
                (((1,), (1,)), ((), ())),
                preferred_element_type=F32,
            )
            vals[:, h * cols : (h + 1) * cols] = val.astype(BF16)

    out = jnp.dot(vals[...], weight_ref[...], preferred_element_type=F32)
    kept = keep_ref.shape[0]
    keep_ref[...] = out[:kept]
    send_ref[...] = out[kept:].astype(BF16)


def project(pieces, value_up, weight, n_pair, steps):
    count = len(pieces)
    req, heads, rank = pieces[0].shape
    rows = count * req
    kept = rows // n_pair
    depth, wide = weight.shape
    cb = wide // steps
    return pl.pallas_call(
        functools.partial(project_kernel, count),
        grid=(steps,),
        out_shape=[
            jax.ShapeDtypeStruct((kept, wide), F32),
            jax.ShapeDtypeStruct((rows - kept, wide), BF16),
        ],
        in_specs=[pl.BlockSpec(p.shape, lambda i: (0, 0, 0)) for p in pieces]
        + [
            pl.BlockSpec(value_up.shape, lambda i: (0, 0, 0)),
            pl.BlockSpec((depth, cb), lambda i: (0, i)),
        ],
        out_specs=[
            pl.BlockSpec((kept, cb), lambda i: (0, i)),
            pl.BlockSpec((rows - kept, cb), lambda i: (0, i)),
        ],
        scratch_shapes=[pltpu.VMEM((rows, depth), BF16)],
        compiler_params=pltpu.CompilerParams(vmem_limit_bytes=56 * 2**20),
        cost_estimate=pl.CostEstimate(
            flops=2 * rows * depth * wide, bytes_accessed=2 * depth * wide, transcendentals=0
        ),
        name="project",
    )(*pieces, value_up, weight)


def norm_kernel(mine_ref, arrived_ref, gain_ref, normed_ref, stream_ref):
    total = mine_ref[...] + arrived_ref[...].astype(F32)
    inv = lax.rsqrt(jnp.sum(total * total, axis=1, keepdims=True) / D + 1e-06)
    normed_ref[...] = (total * inv * gain_ref[...]).astype(BF16)
    stream_ref[...] = total


def norm(mine, arrived, gain):
    return pl.pallas_call(
        norm_kernel,
        out_shape=[
            jax.ShapeDtypeStruct(mine.shape, BF16),
            jax.ShapeDtypeStruct(mine.shape, F32),
        ],
        in_specs=[VMEM] * 3,
        out_specs=[VMEM] * 2,
        compiler_params=pltpu.CompilerParams(vmem_limit_bytes=16 * 2**20),
        name="norm",
    )(mine, arrived, gain)


def mlp_kernel(count, deep, *refs):
    pieces = refs[:count]
    both_ref, down_ref, keep_ref, send_ref, rows_f32, blocks, gates, hidden = refs[count:]
    step = pl.program_id(0)
    req = pieces[0].shape[0]
    depth = both_ref.shape[1]

    @pl.when(step == 0)
    def _():
        for j, piece in enumerate(pieces):
            rows_f32[j * req : (j + 1) * req, :] = piece[...].astype(F32)
        for j in range(deep):
            blocks[j] = rows_f32[:, j * depth : (j + 1) * depth].astype(BF16)
        gates[...] = jnp.zeros_like(gates)

    @pl.when(step < deep)
    def _():
        x = blocks[step]
        units = both_ref.shape[2]
        full = units - 128 if units % 256 == 128 else units
        for g in range(2):
            gates[g, :, :full] += jnp.dot(x, both_ref[g, :, :full], preferred_element_type=F32)
        if full < units:
            rest = jnp.concatenate([both_ref[0, :, full:], both_ref[1, :, full:]], axis=1)
            product = jnp.dot(x, rest, preferred_element_type=F32)
            for g in range(2):
                gates[g, :, full:] += product[:, g * 128 : (g + 1) * 128]

    @pl.when(step == deep - 1)
    def _():
        gate = gates[0]
        hidden[...] = (gate / (1.0 + jnp.exp(-gate)) * gates[1]).astype(BF16)

    @pl.when(step >= deep)
    def _():
        out = jnp.dot(hidden[...], down_ref[...], preferred_element_type=F32)
        kept = keep_ref.shape[0]
        keep_ref[...] = out[:kept]
        send_ref[...] = out[kept:].astype(BF16)


def mlp(pieces, gate_up, down, n_pair, deep, steps):
    count = len(pieces)
    req, wide = pieces[0].shape
    rows = count * req
    kept = rows // n_pair
    units = down.shape[0]
    cb = wide // steps
    return pl.pallas_call(
        functools.partial(mlp_kernel, count, deep),
        grid=(deep + steps,),
        out_shape=[
            jax.ShapeDtypeStruct((kept, wide), F32),
            jax.ShapeDtypeStruct((rows - kept, wide), BF16),
        ],
        in_specs=[pl.BlockSpec(p.shape, lambda i: (0, 0)) for p in pieces]
        + [
            pl.BlockSpec((2, wide // deep, units), lambda i: (0, jnp.minimum(i, deep - 1), 0)),
            pl.BlockSpec((units, cb), lambda i: (0, jnp.maximum(i - deep, 0))),
        ],
        out_specs=[
            pl.BlockSpec((kept, cb), lambda i: (0, jnp.maximum(i - deep, 0))),
            pl.BlockSpec((rows - kept, cb), lambda i: (0, jnp.maximum(i - deep, 0))),
        ],
        scratch_shapes=[
            pltpu.VMEM((rows, wide), F32),
            pltpu.VMEM((deep, rows, wide // deep), BF16),
            pltpu.VMEM((2, rows, units), F32),
            pltpu.VMEM((rows, units), BF16),
        ],
        compiler_params=pltpu.CompilerParams(vmem_limit_bytes=56 * 2**20),
        cost_estimate=pl.CostEstimate(
            flops=6 * rows * wide * units,
            bytes_accessed=6 * wide * units,
            transcendentals=rows * units,
        ),
        name="mlp",
    )(*pieces, gate_up, down)


def sum_pair(keep, send, n_pair):
    for k in range(1, n_pair):
        rows = keep.shape[0]
        keep = keep + hop(send[(k - 1) * rows : k * rows], "pair", k).astype(F32)
    return keep


def sum_sub(total, rows, n_sub):
    sent = total.astype(BF16)
    mine = total[:rows]
    for k in range(1, n_sub):
        mine = mine + hop(sent[k * rows : (k + 1) * rows], "sub", k).astype(F32)
    return mine


def body(
    latent_cache,
    queries,
    new_latent,
    context_len,
    block_start,
    owner,
    value_up,
    out_proj,
    residual_in,
    norm_gain,
    gate_up,
    down_weight,
):
    n_wide = lax.axis_size("wide")
    n_sub = lax.axis_size("sub")
    n_pair = lax.axis_size("pair")
    me_wide = lax.axis_index("wide")
    me_sub = lax.axis_index("sub")
    me_pair = lax.axis_index("pair")
    req_grp, block, latent = latent_cache.shape
    n_groups = n_sub * n_pair
    width_dev = residual_in.shape[1]
    group = me_sub * n_pair + me_pair
    place = jnp.stack([me_wide, me_sub, group]).astype(jnp.int32)

    arrived = [queries]
    for k in range(1, n_wide):
        low = k & -k
        arrived.append(hop(arrived[k - low] if k > low else queries, "wide", low))
    payload, bias, tail, residual, order = prepare(
        place,
        context_len,
        block_start,
        owner,
        queries,
        latent_cache,
        new_latent,
        norm_gain.reshape(1, width_dev),
        residual_in,
    )
    payloads = [payload]
    for k in range(1, n_wide):
        payload = attend(arrived[k], latent_cache, bias, tail, payload)
        payloads.append(hop(payload, "wide", k))
    chunks, gain = combine(order, payloads, req_grp, n_sub, width_dev)

    landed = [chunks[0]] + [hop(chunks[k], "sub", k) for k in range(1, n_sub)]
    pieces = landed + [hop(p, "pair", k) for k in range(1, n_pair) for p in landed]
    weight = out_proj.reshape(out_proj.shape[0] * out_proj.shape[1], D)
    keep, send = project(pieces, jnp.swapaxes(value_up, 1, 2), weight, n_pair, 7)
    mine = sum_sub(sum_pair(keep, send, n_pair), req_grp, n_sub) + residual
    k = 1
    while 2 * k < n_wide:
        mine = mine + hop(mine.astype(BF16), "wide", k).astype(F32)
        k = 2 * k
    normed, stream = norm(mine, hop(mine.astype(BF16), "wide", k), gain)

    landed = [normed] + [hop(normed, "sub", k) for k in range(1, n_sub)]
    pieces = landed + [hop(p, "pair", k) for k in range(1, n_pair) for p in landed]
    keep, send = mlp(pieces, gate_up, down_weight, n_pair, 7, 7)
    mine = sum_sub(sum_pair(keep, send, n_pair), req_grp, n_sub)
    out = lax.dynamic_slice_in_dim(mine + stream, me_wide * width_dev, width_dev, 1)
    for k in range(1, n_wide):
        chunk = lax.dynamic_slice_in_dim(mine, (me_wide ^ k) * width_dev, width_dev, 1)
        out = out + hop(chunk.astype(BF16), "wide", k).astype(F32)
    return out.astype(BF16)


def solution(mesh):
    in_specs = (
        P(("groups", "sub", "pair"), "wide", None),
        P(("groups", "sub", "pair"), "wide", None),
        P(("groups", "sub", "pair"), None),
        P(("groups", "sub", "pair")),
        P(("groups", "sub", "pair"), None),
        P("groups"),
        P(("wide", "sub"), None, "pair"),
        P(("wide", "sub"), "pair", None),
        P(("groups", "sub", "pair"), "wide"),
        P("wide"),
        P(None, None, ("wide", "sub", "pair")),
        P(("wide", "sub", "pair"), None),
    )
    out_specs = P(("groups", "sub", "pair"), "wide")
    return jax.shard_map(body, mesh=mesh, in_specs=in_specs, out_specs=out_specs, check_vma=False)
```

```python
import functools

import jax
import jax.numpy as jnp
from jax import lax
from jax.experimental import pallas as pl
from jax.experimental.pallas import tpu as pltpu
from jax.sharding import PartitionSpec as P

D = 7168
KV_RANK = 512
ROPE = 64
NOPE = 128
F32 = jnp.float32
BF16 = jnp.bfloat16
TAIL = 8
GAIN_ROW = 3
VMEM = pl.BlockSpec(memory_space=pltpu.VMEM)
SMEM = pl.BlockSpec(memory_space=pltpu.SMEM)
ANY = pl.BlockSpec(memory_space=pl.ANY)
HBM = pl.BlockSpec(memory_space=pltpu.HBM)
SMALL = pltpu.CompilerParams(vmem_limit_bytes=4 * 2**20)


def hop(x, axis, k):
    n = lax.axis_size(axis)
    return lax.ppermute(x, axis, [(i, i ^ k) for i in range(n)])


def in_hbm(x):
    return pltpu.with_memory_space_constraint(x, pltpu.HBM)


def eye(rows, cols):
    row = lax.broadcasted_iota(jnp.int32, (rows, cols), 0)
    col = lax.broadcasted_iota(jnp.int32, (rows, cols), 1)
    return (row == col).astype(BF16)


def partial_scores(q_ref, cache_ref, bias):
    req, heads, latent = q_ref.shape
    scores = [
        lax.dot_general(
            q_ref[r], cache_ref[r], (((1,), (1,)), ((), ())), preferred_element_type=F32
        )
        * (NOPE + ROPE) ** (-0.5)
        + bias[r : r + 1, :]
        for r in range(req)
    ]
    return jnp.concatenate(scores, axis=0)


def partial_sums(expo, cache_ref, heads):
    expo = expo.astype(BF16)
    sums = [
        jnp.dot(
            expo[r * heads : (r + 1) * heads],
            cache_ref[r, :, :KV_RANK],
            preferred_element_type=F32,
        )
        for r in range(cache_ref.shape[0])
    ]
    return jnp.concatenate(sums, axis=0)


def payload_tail(lse, tail):
    rows = lse.shape[0]
    hi = lse.astype(BF16).astype(F32)
    mid = (lse - hi).astype(BF16).astype(F32)
    lo = (lse - hi - mid).astype(BF16).astype(F32)
    lane = lax.broadcasted_iota(jnp.int32, (rows, 128), 1)
    spread = jnp.where(lane == 0, hi, jnp.where(lane == 1, mid, jnp.where(lane == 2, lo, 0.0)))
    turned = lax.dot_general(
        spread.astype(BF16), eye(rows, 128), (((0,), (0,)), ((), ())), preferred_element_type=F32
    )
    return tail + jnp.pad(turned[:TAIL], ((0, 0), (0, KV_RANK - 128)))


def prepare_kernel(
    n_wide,
    length_hbm,
    start_hbm,
    owner_hbm,
    gain_hbm,
    q_hbm,
    cache_hbm,
    fresh_hbm,
    residual_hbm,
    weight_hbm,
    out_ref,
    bias_ref,
    tail_ref,
    full_ref,
    order_ref,
    cache_ref,
    weight_ref,
    length_ref,
    start_ref,
    owner_ref,
    gain_ref,
    q_ref,
    fresh_ref,
    residual_ref,
    sems,
):
    copies = [
        pltpu.make_async_copy(source, target, sems.at[i])
        for i, (source, target) in enumerate(
            [
                (length_hbm, length_ref),
                (start_hbm, start_ref),
                (owner_hbm, owner_ref),
                (gain_hbm, gain_ref),
                (q_hbm, q_ref),
                (cache_hbm, cache_ref),
                (fresh_hbm, fresh_ref),
                (residual_hbm, residual_ref),
                (weight_hbm, weight_ref),
            ]
        )
    ]
    for copy in copies:
        copy.start()
    for copy in copies[:4]:
        copy.wait()
    req, heads, latent = q_ref.shape
    block = cache_ref.shape[1]
    width = gain_ref.shape[0]
    me, me_sub = lax.axis_index("wide"), lax.axis_index("sub")
    group = me_sub * lax.axis_size("pair") + lax.axis_index("pair")

    owners = [owner_ref[group * req + r] for r in range(req)]
    placed = []
    for r in range(req):
        at = jnp.int32(0)
        for j in range(req):
            if j != r:
                ahead = owners[j] <= owners[r] if j < r else owners[j] < owners[r]
                at = at + jnp.where(ahead, 1, 0)
        placed.append(at)
        order_ref[2 + r] = at
    order_ref[0] = me_sub
    order_ref[1] = me

    gain = gain_ref[...].reshape(1, width).astype(F32)
    tail = [jnp.zeros((GAIN_ROW, KV_RANK), F32)]
    for at in range(0, width, KV_RANK):
        piece = gain[:, at : at + KV_RANK]
        if piece.shape[1] < KV_RANK:
            piece = jnp.pad(piece, ((0, 0), (0, KV_RANK - piece.shape[1])))
        tail.append(piece)
    tail.append(jnp.zeros((TAIL - GAIN_ROW - len(tail) + 1, KV_RANK), F32))
    tail = jnp.concatenate(tail, axis=0)
    tail_ref[...] = tail

    biases = []
    for r in range(req):
        following = jnp.where(
            me == n_wide - 1, length_ref[r], start_ref[r, jnp.minimum(me + 1, n_wide - 1)]
        )
        position = lax.broadcasted_iota(jnp.int32, (1, block), 1)
        biases.append(jnp.where(position < following - start_ref[r, me], 0.0, F32(-1e30)))
    bias = jnp.concatenate(biases, axis=0)
    bias_ref[...] = bias

    for copy in copies[4:-1]:
        copy.wait()
    rows = []
    for i in range(req):
        row = jnp.zeros((1, width), F32)
        for r in range(req):
            row = jnp.where(placed[r] == i, residual_ref[r : r + 1, :].astype(F32), row)
        rows.append(row)
    mine = jnp.concatenate(rows, axis=0)
    for w in range(n_wide):
        full_ref[:, w * width : (w + 1) * width] = jnp.where(me == w, mine, 0.0)

    scores = partial_scores(q_ref, cache_ref, bias)
    fresh = [fresh_ref[r : r + 1, :].astype(F32) for r in range(req)]
    own = jnp.concatenate(
        [
            jnp.sum(q_ref[r].astype(F32) * fresh[r], axis=1, keepdims=True)
            * (NOPE + ROPE) ** (-0.5)
            for r in range(req)
        ],
        axis=0,
    )
    top = jnp.maximum(jnp.max(scores, axis=1, keepdims=True), own)
    expo = jnp.exp(scores - top)
    expo_own = jnp.exp(own - top)
    den = jnp.sum(expo, axis=1, keepdims=True) + expo_own
    weight_own = expo_own.astype(BF16).astype(F32)
    num = partial_sums(expo, cache_ref, heads) + jnp.concatenate(
        [weight_own[r * heads : (r + 1) * heads] * fresh[r][:, :KV_RANK] for r in range(req)],
        axis=0,
    )
    count = req * heads
    out_ref[:count, :] = (num / den).astype(BF16)
    out_ref[count:, :] = payload_tail(top + jnp.log(den), tail).astype(BF16)
    copies[-1].wait()


def attend_cost(req, heads, block, latent):
    return pl.CostEstimate(
        flops=2 * req * heads * block * (latent + KV_RANK),
        bytes_accessed=2 * req * (block * latent + heads * (latent + KV_RANK)),
        transcendentals=req * heads * block,
    )


def prepare(length, start, owner, gain, q, cache, fresh, residual, weight):
    req, heads, latent = q.shape
    block, width = cache.shape[1], residual.shape[1]
    n_wide = start.shape[1]
    operands = (length, start, owner, gain, q, cache, fresh, residual, weight)
    return pl.pallas_call(
        functools.partial(prepare_kernel, n_wide),
        out_shape=[
            jax.ShapeDtypeStruct((req * heads + TAIL, KV_RANK), BF16),
            jax.ShapeDtypeStruct((req, block), F32),
            jax.ShapeDtypeStruct((TAIL, KV_RANK), F32),
            jax.ShapeDtypeStruct((req, n_wide * width), F32),
            jax.ShapeDtypeStruct((2 + req,), jnp.int32),
            pltpu.VMEM(cache.shape, BF16),
            pltpu.VMEM(weight.shape, BF16),
        ],
        in_specs=[HBM] * len(operands),
        out_specs=[VMEM] * 4 + [SMEM, VMEM, VMEM],
        scratch_shapes=[
            pltpu.SMEM(length.shape, jnp.int32),
            pltpu.SMEM(start.shape, jnp.int32),
            pltpu.SMEM(owner.shape, jnp.int32),
            pltpu.VMEM(gain.shape, BF16),
            pltpu.VMEM(q.shape, BF16),
            pltpu.VMEM(fresh.shape, BF16),
            pltpu.VMEM(residual.shape, BF16),
            pltpu.SemaphoreType.DMA((len(operands),)),
        ],
        compiler_params=SMALL,
        cost_estimate=pl.CostEstimate(
            flops=2 * req * heads * block * (latent + KV_RANK),
            bytes_accessed=2 * (weight.size + cache.size + q.size),
            transcendentals=req * heads * block,
        ),
        name="prepare",
    )(*[in_hbm(x) for x in operands])


def attend_kernel(q_ref, cache_ref, bias_ref, tail_ref, after_ref, out_ref):
    req, heads, latent = q_ref.shape
    scores = partial_scores(q_ref, cache_ref, bias_ref[...])
    top = jnp.max(scores, axis=1, keepdims=True)
    expo = jnp.exp(scores - top)
    den = jnp.sum(expo, axis=1, keepdims=True)
    num = partial_sums(expo, cache_ref, heads)
    count = req * heads
    out_ref[:count, :] = (num / den).astype(BF16)
    out_ref[count:, :] = payload_tail(top + jnp.log(den), tail_ref[...]).astype(BF16)


def attend(q, cache, bias, tail, after):
    req, heads, latent = q.shape
    return pl.pallas_call(
        attend_kernel,
        out_shape=jax.ShapeDtypeStruct((req * heads + TAIL, KV_RANK), BF16),
        in_specs=[VMEM] * 4 + [ANY],
        out_specs=VMEM,
        compiler_params=SMALL,
        cost_estimate=attend_cost(req, heads, cache.shape[1], latent),
        name="attend",
    )(q, cache, bias, tail, after)


def fetch_kernel(both_hbm, down_hbm, after_ref, first_ref, down_ref, sems):
    count, _, depth, _ = first_ref.shape
    copies = [
        pltpu.make_async_copy(
            both_hbm.at[:, pl.ds(i * depth, depth), :], first_ref.at[i], sems.at[i]
        )
        for i in range(count)
    ]
    copies.append(pltpu.make_async_copy(down_hbm, down_ref, sems.at[count]))
    for copy in copies:
        copy.start()
    for copy in copies:
        copy.wait()


def fetch(both, down, after, count, depth):
    units = both.shape[2]
    return pl.pallas_call(
        fetch_kernel,
        out_shape=[
            pltpu.VMEM((count, 2, depth, units), BF16),
            pltpu.VMEM(down.shape, BF16),
        ],
        in_specs=[HBM, HBM, ANY],
        out_specs=[VMEM] * 2,
        scratch_shapes=[pltpu.SemaphoreType.DMA((count + 1,))],
        compiler_params=SMALL,
        cost_estimate=pl.CostEstimate(
            flops=0,
            bytes_accessed=2 * (down.size + 2 * count * depth * units),
            transcendentals=0,
        ),
        name="fetch",
    )(in_hbm(both), in_hbm(down), after)


def combine_kernel(n_wide, n_sub, width, req, order_ref, after_ref, *refs):
    payloads, outs, gain_ref, hold = refs[:n_wide], refs[n_wide : n_wide + n_sub], refs[-2], refs[-1]
    rows = payloads[0].shape[0] - TAIL
    heads = rows // req
    heads_dev = heads // n_sub
    me_sub, me_wide = order_ref[0], order_ref[1]
    tails = [p[rows:, :].astype(F32) for p in payloads]
    lses = []
    for tail in tails:
        turned = lax.dot_general(
            eye(rows, 128),
            tail[:, :128].astype(BF16),
            (((1,), (1,)), ((), ())),
            preferred_element_type=F32,
        )
        lses.append(turned[:, 0:1] + turned[:, 1:2] + turned[:, 2:3])
    top = functools.reduce(jnp.maximum, lses)
    weights = [jnp.exp(lse - top) for lse in lses]
    inv = 1.0 / functools.reduce(jnp.add, weights)
    weights = [weight * inv for weight in weights]
    for r in range(req):
        at = slice(r * heads, (r + 1) * heads)
        attn = functools.reduce(
            jnp.add, [w[at] * p[at, :].astype(F32) for w, p in zip(weights, payloads)]
        ).astype(BF16)
        for s in range(n_sub):
            hold[s, order_ref[2 + r]] = attn[s * heads_dev : (s + 1) * heads_dev]
    for k in range(n_sub):
        outs[k][...] = hold[me_sub ^ k]
    for w in range(n_wide):
        chosen = jnp.zeros((1, width), F32)
        for k in range(n_wide):
            pieces = [
                tails[k][GAIN_ROW + i : GAIN_ROW + i + 1, : min(KV_RANK, width - i * KV_RANK)]
                for i in range(pl.cdiv(width, KV_RANK))
            ]
            gain = pieces[0] if len(pieces) == 1 else jnp.concatenate(pieces, axis=1)
            chosen = jnp.where((me_wide ^ k) == w, gain, chosen)
        gain_ref[:, w * width : (w + 1) * width] = chosen


def combine(order, after, payloads, req, n_sub, width):
    n_wide = len(payloads)
    heads_dev = (payloads[0].shape[0] - TAIL) // req // n_sub
    piece = jax.ShapeDtypeStruct((req, heads_dev, KV_RANK), BF16)
    out = pl.pallas_call(
        functools.partial(combine_kernel, n_wide, n_sub, width, req),
        out_shape=[piece] * n_sub + [jax.ShapeDtypeStruct((1, n_wide * width), F32)],
        in_specs=[SMEM, ANY] + [VMEM] * n_wide,
        out_specs=[VMEM] * (n_sub + 1),
        scratch_shapes=[pltpu.VMEM((n_sub, req, heads_dev, KV_RANK), BF16)],
        compiler_params=SMALL,
        name="combine",
    )(order, after, *payloads)
    return out[:n_sub], out[n_sub]


def project_kernel(count, *refs):
    pieces, (up_ref, weight_ref, keep_ref, send_ref, vals) = refs[:count], refs[count:]
    req, heads, rank = pieces[0].shape
    rows = count * req
    cols = up_ref.shape[1]

    stacked = jnp.concatenate([p[...].reshape(req * heads, rank) for p in pieces], axis=0)
    total = rows * heads
    to = lax.broadcasted_iota(jnp.int32, (total, total), 0)
    source = lax.broadcasted_iota(jnp.int32, (total, total), 1)
    turn = (to // rows == source % heads) & (to % rows == source // heads)
    turned = jnp.dot(turn.astype(BF16), stacked, preferred_element_type=F32).astype(BF16)
    for h in range(heads):
        val = lax.dot_general(
            turned[h * rows : (h + 1) * rows],
            up_ref[h],
            (((1,), (1,)), ((), ())),
            preferred_element_type=F32,
        )
        vals[:, h * cols : (h + 1) * cols] = val.astype(BF16)

    cb = 1024

    @pl.loop(0, weight_ref.shape[1] // cb)
    def _(i):
        at = pl.ds(pl.multiple_of(i * cb, cb), cb)
        out = jnp.dot(vals[...], weight_ref[:, at], preferred_element_type=F32)
        kept = keep_ref.shape[0]
        keep_ref[:, at] = out[:kept]
        send_ref[:, at] = out[kept:].astype(BF16)


def project(pieces, value_up, weight, n_pair):
    count = len(pieces)
    req, heads, rank = pieces[0].shape
    rows = count * req
    kept = rows // n_pair
    depth, wide = weight.shape
    return pl.pallas_call(
        functools.partial(project_kernel, count),
        out_shape=[
            jax.ShapeDtypeStruct((kept, wide), F32),
            jax.ShapeDtypeStruct((rows - kept, wide), BF16),
        ],
        in_specs=[VMEM] * (count + 2),
        out_specs=[VMEM] * 2,
        scratch_shapes=[pltpu.VMEM((rows, depth), BF16)],
        compiler_params=SMALL,
        cost_estimate=pl.CostEstimate(
            flops=2 * rows * depth * wide, bytes_accessed=2 * depth * wide, transcendentals=0
        ),
        name="project",
    )(*pieces, value_up, weight)


def norm_kernel(mine_ref, arrived_ref, gain_ref, normed_ref, stream_ref):
    total = mine_ref[...] + arrived_ref[...].astype(F32)
    inv = lax.rsqrt(jnp.sum(total * total, axis=1, keepdims=True) / D + 1e-06)
    normed_ref[...] = (total * inv * gain_ref[...]).astype(BF16)
    stream_ref[...] = total


def norm(mine, arrived, gain):
    return pl.pallas_call(
        norm_kernel,
        out_shape=[
            jax.ShapeDtypeStruct(mine.shape, BF16),
            jax.ShapeDtypeStruct(mine.shape, F32),
        ],
        in_specs=[VMEM] * 3,
        out_specs=[VMEM] * 2,
        compiler_params=SMALL,
        name="norm",
    )(mine, arrived, gain)


def mlp_kernel(count, *refs):
    pieces = refs[:count]
    both_hbm, first_ref, down_ref, keep_ref, send_ref, rows_f32, blocks, gates, both, sems = refs[
        count:
    ]
    req = pieces[0].shape[0]
    deep, rows, depth = blocks.shape
    slots, units = both.shape[0], both.shape[3]
    early = first_ref.shape[0]
    full = units - 128 if units % 256 == 128 else units

    def load(i):
        at = pl.ds(pl.multiple_of(i * depth, depth), depth)
        slot = lax.rem(i - early, slots)
        return pltpu.make_async_copy(both_hbm.at[:, at, :], both.at[slot], sems.at[slot])

    @pl.loop(early, early + slots)
    def _(i):
        load(i).start()

    for j, piece in enumerate(pieces):
        rows_f32[j * req : (j + 1) * req, :] = piece[...].astype(F32)
    for j in range(deep):
        blocks[j] = rows_f32[:, j * depth : (j + 1) * depth].astype(BF16)
    gates[...] = jnp.zeros_like(gates)

    def add(x, weight):
        for g in range(2):
            gates[g, :, :full] += jnp.dot(x, weight[g, :, :full], preferred_element_type=F32)
        if full < units:
            rest = jnp.concatenate([weight[0, :, full:], weight[1, :, full:]], axis=1)
            product = jnp.dot(x, rest, preferred_element_type=F32)
            for g in range(2):
                gates[g, :, full:] += product[:, g * 128 : (g + 1) * 128]

    @pl.loop(0, early)
    def _(i):
        add(blocks[i], first_ref.at[i])

    @pl.loop(early, deep)
    def _(i):
        load(i).wait()
        add(blocks[i], both.at[lax.rem(i - early, slots)])

        @pl.when(i + slots < deep)
        def _():
            load(i + slots).start()

    gate = gates[0]
    hidden = (gate / (1.0 + jnp.exp(-gate)) * gates[1]).astype(BF16)
    cb = 1024
    kept = keep_ref.shape[0]

    @pl.loop(0, down_ref.shape[1] // cb)
    def _(i):
        at = pl.ds(pl.multiple_of(i * cb, cb), cb)
        out = jnp.dot(hidden, down_ref[:, at], preferred_element_type=F32)
        keep_ref[:, at] = out[:kept]
        send_ref[:, at] = out[kept:].astype(BF16)


def mlp(pieces, gate_up, first, down, n_pair):
    count = len(pieces)
    req, wide = pieces[0].shape
    rows = count * req
    kept = rows // n_pair
    units = down.shape[0]
    depth, slots = first.shape[2], 6
    deep = wide // depth
    return pl.pallas_call(
        functools.partial(mlp_kernel, count),
        out_shape=[
            jax.ShapeDtypeStruct((kept, wide), F32),
            jax.ShapeDtypeStruct((rows - kept, wide), BF16),
        ],
        in_specs=[VMEM] * count + [HBM, VMEM, VMEM],
        out_specs=[VMEM] * 2,
        scratch_shapes=[
            pltpu.VMEM((rows, wide), F32),
            pltpu.VMEM((deep, rows, depth), BF16),
            pltpu.VMEM((2, rows, units), F32),
            pltpu.VMEM((slots, 2, depth, units), BF16),
            pltpu.SemaphoreType.DMA((slots,)),
        ],
        compiler_params=pltpu.CompilerParams(vmem_limit_bytes=20 * 2**20),
        cost_estimate=pl.CostEstimate(
            flops=6 * rows * wide * units,
            bytes_accessed=4 * wide * units,
            transcendentals=rows * units,
        ),
        name="mlp",
    )(*pieces, in_hbm(gate_up), first, down)


def split_kernel(n_wide, order_ref, mine_ref, stream_ref, *refs):
    n_sub = len(refs) - n_wide
    arrived, own_ref, sends = refs[:n_sub], refs[n_sub], refs[n_sub + 1 :]
    width = own_ref.shape[1]
    me = order_ref[1]
    total = mine_ref[...]
    for a in arrived:
        total = total + a[...].astype(F32)
    cuts = [total[:, w * width : (w + 1) * width] for w in range(n_wide)]
    own = jnp.zeros(own_ref.shape, F32)
    for w in range(n_wide):
        own = jnp.where(me == w, cuts[w] + stream_ref[:, w * width : (w + 1) * width], own)
    own_ref[...] = own
    for k in range(1, n_wide):
        send = jnp.zeros(own_ref.shape, F32)
        for w in range(n_wide):
            send = jnp.where((me ^ k) == w, cuts[w], send)
        sends[k - 1][...] = send.astype(BF16)


def split(order, mine, stream, arrived, n_wide):
    rows, wide = mine.shape
    width = wide // n_wide
    return pl.pallas_call(
        functools.partial(split_kernel, n_wide),
        out_shape=[jax.ShapeDtypeStruct((rows, width), F32)]
        + [jax.ShapeDtypeStruct((rows, width), BF16)] * (n_wide - 1),
        in_specs=[SMEM] + [VMEM] * (2 + len(arrived)),
        out_specs=[VMEM] * n_wide,
        compiler_params=SMALL,
        name="split",
    )(order, mine, stream, *arrived)


def sum_pair(keep, send, n_pair):
    for k in range(1, n_pair):
        rows = keep.shape[0]
        keep = keep + hop(send[(k - 1) * rows : k * rows], "pair", k).astype(F32)
    return keep


def send_sub(total, rows, n_sub):
    sent = total.astype(BF16)
    return [hop(sent[k * rows : (k + 1) * rows], "sub", k) for k in range(1, n_sub)]


def body(
    latent_cache,
    queries,
    new_latent,
    context_len,
    block_start,
    owner,
    value_up,
    out_proj,
    residual_in,
    norm_gain,
    gate_up,
    down_weight,
):
    n_wide = lax.axis_size("wide")
    n_sub = lax.axis_size("sub")
    n_pair = lax.axis_size("pair")
    req_grp = latent_cache.shape[0]
    width_dev = residual_in.shape[1]

    arrived = {k: hop(queries, "wide", k) for k in range(1, n_wide) if k & (k - 1) == 0}
    payload, bias, tail, residual, order, cache, weight = prepare(
        context_len,
        block_start,
        owner,
        norm_gain,
        queries,
        latent_cache,
        new_latent,
        residual_in,
        out_proj.reshape(out_proj.shape[0] * out_proj.shape[1], D),
    )
    payloads = [payload]
    for k in range(1, n_wide):
        if k not in arrived:
            low = k & -k
            arrived[k] = hop(arrived[k - low], "wide", low)
        elif k > 1:
            arrived[k], payload = lax.optimization_barrier((arrived[k], payload))
        payload = attend(arrived[k], cache, bias, tail, payload)
        payloads.append(hop(payload, "wide", k))
    first, down = fetch(gate_up, down_weight, payload, 2, 512)
    chunks, gain = combine(order, first, payloads, req_grp, n_sub, width_dev)

    landed = [chunks[0]] + [hop(chunks[k], "sub", k) for k in range(1, n_sub)]
    pieces = landed + [hop(p, "pair", k) for k in range(1, n_pair) for p in landed]
    keep, send = project(pieces, jnp.swapaxes(value_up, 1, 2), weight, n_pair)
    total = sum_pair(keep, send, n_pair)
    mine = total[:req_grp] + residual
    for a in send_sub(total, req_grp, n_sub):
        mine = mine + a.astype(F32)
    k = 1
    while 2 * k < n_wide:
        mine = mine + hop(mine.astype(BF16), "wide", k).astype(F32)
        k = 2 * k
    normed, stream = norm(mine, hop(mine.astype(BF16), "wide", k), gain)

    landed = [normed] + [hop(normed, "sub", k) for k in range(1, n_sub)]
    pieces = landed + [hop(p, "pair", k) for k in range(1, n_pair) for p in landed]
    keep, send = mlp(pieces, gate_up, first, down, n_pair)
    total = sum_pair(keep, send, n_pair)
    back = send_sub(total, req_grp, n_sub)
    out, *sends = split(order, total[:req_grp], stream, back, n_wide)
    for k in range(1, n_wide):
        out = out + hop(sends[k - 1], "wide", k).astype(F32)
    return out.astype(BF16)


def solution(mesh):
    in_specs = (
        P(("groups", "sub", "pair"), "wide", None),
        P(("groups", "sub", "pair"), "wide", None),
        P(("groups", "sub", "pair"), None),
        P(("groups", "sub", "pair")),
        P(("groups", "sub", "pair"), None),
        P("groups"),
        P(("wide", "sub"), None, "pair"),
        P(("wide", "sub"), "pair", None),
        P(("groups", "sub", "pair"), "wide"),
        P("wide"),
        P(None, None, ("wide", "sub", "pair")),
        P(("wide", "sub", "pair"), None),
    )
    out_specs = P(("groups", "sub", "pair"), "wide")
    return jax.shard_map(body, mesh=mesh, in_specs=in_specs, out_specs=out_specs, check_vma=False)
```

```python
import functools

import jax
import jax.numpy as jnp
from jax import lax
from jax.experimental import pallas as pl
from jax.experimental.pallas import tpu as pltpu
from jax.sharding import PartitionSpec as P

D = 7168
KV_RANK = 512
ROPE = 64
NOPE = 128
F32 = jnp.float32
BF16 = jnp.bfloat16
TAIL = 8
GAIN_ROW = 3
VMEM = pl.BlockSpec(memory_space=pltpu.VMEM)
SMEM = pl.BlockSpec(memory_space=pltpu.SMEM)
ANY = pl.BlockSpec(memory_space=pl.ANY)
HBM = pl.BlockSpec(memory_space=pltpu.HBM)
SMALL = pltpu.CompilerParams(vmem_limit_bytes=4 * 2**20)


def hop(x, axis, k):
    n = lax.axis_size(axis)
    return lax.ppermute(x, axis, [(i, i ^ k) for i in range(n)])


def hop_group(x, k):
    n = lax.axis_size("sub") * lax.axis_size("pair")
    return lax.ppermute(x, ("sub", "pair"), [(i, i ^ k) for i in range(n)])


def in_hbm(x):
    return pltpu.with_memory_space_constraint(x, pltpu.HBM)


def eye(rows, cols):
    row = lax.broadcasted_iota(jnp.int32, (rows, cols), 0)
    col = lax.broadcasted_iota(jnp.int32, (rows, cols), 1)
    return (row == col).astype(BF16)


def partial_scores(q_ref, cache_ref, bias):
    req, heads, latent = q_ref.shape
    scores = [
        lax.dot_general(
            q_ref[r], cache_ref[r], (((1,), (1,)), ((), ())), preferred_element_type=F32
        )
        * (NOPE + ROPE) ** (-0.5)
        + bias[r : r + 1, :]
        for r in range(req)
    ]
    return jnp.concatenate(scores, axis=0)


def partial_sums(expo, cache_ref, heads):
    expo = expo.astype(BF16)
    sums = [
        jnp.dot(
            expo[r * heads : (r + 1) * heads],
            cache_ref[r, :, :KV_RANK],
            preferred_element_type=F32,
        )
        for r in range(cache_ref.shape[0])
    ]
    return jnp.concatenate(sums, axis=0)


def payload_tail(lse, tail):
    rows = lse.shape[0]
    hi = lse.astype(BF16).astype(F32)
    mid = (lse - hi).astype(BF16).astype(F32)
    lo = (lse - hi - mid).astype(BF16).astype(F32)
    lane = lax.broadcasted_iota(jnp.int32, (rows, 128), 1)
    spread = jnp.where(lane == 0, hi, jnp.where(lane == 1, mid, jnp.where(lane == 2, lo, 0.0)))
    turned = lax.dot_general(
        spread.astype(BF16), eye(rows, 128), (((0,), (0,)), ((), ())), preferred_element_type=F32
    )
    return tail + jnp.pad(turned[:TAIL], ((0, 0), (0, KV_RANK - 128)))


def prepare_kernel(
    n_wide,
    length_hbm,
    start_hbm,
    owner_hbm,
    gain_hbm,
    q_hbm,
    cache_hbm,
    fresh_hbm,
    residual_hbm,
    weight_hbm,
    out_ref,
    bias_ref,
    tail_ref,
    full_ref,
    order_ref,
    cache_ref,
    weight_ref,
    length_ref,
    start_ref,
    owner_ref,
    gain_ref,
    q_ref,
    fresh_ref,
    residual_ref,
    sems,
):
    copies = [
        pltpu.make_async_copy(source, target, sems.at[i])
        for i, (source, target) in enumerate(
            [
                (length_hbm, length_ref),
                (start_hbm, start_ref),
                (owner_hbm, owner_ref),
                (gain_hbm, gain_ref),
                (q_hbm, q_ref),
                (cache_hbm, cache_ref),
                (fresh_hbm, fresh_ref),
                (residual_hbm, residual_ref),
                (weight_hbm, weight_ref),
            ]
        )
    ]
    for copy in copies:
        copy.start()
    for copy in copies[:4]:
        copy.wait()
    req, heads, latent = q_ref.shape
    block = cache_ref.shape[1]
    width = gain_ref.shape[0]
    me, me_sub = lax.axis_index("wide"), lax.axis_index("sub")
    group = me_sub * lax.axis_size("pair") + lax.axis_index("pair")

    owners = [owner_ref[group * req + r] for r in range(req)]
    placed = []
    for r in range(req):
        at = jnp.int32(0)
        for j in range(req):
            if j != r:
                ahead = owners[j] <= owners[r] if j < r else owners[j] < owners[r]
                at = at + jnp.where(ahead, 1, 0)
        placed.append(at)
        order_ref[2 + r] = at
    order_ref[0] = me_sub
    order_ref[1] = me

    gain = gain_ref[...].reshape(1, width).astype(F32)
    tail = [jnp.zeros((GAIN_ROW, KV_RANK), F32)]
    for at in range(0, width, KV_RANK):
        piece = gain[:, at : at + KV_RANK]
        if piece.shape[1] < KV_RANK:
            piece = jnp.pad(piece, ((0, 0), (0, KV_RANK - piece.shape[1])))
        tail.append(piece)
    tail.append(jnp.zeros((TAIL - GAIN_ROW - len(tail) + 1, KV_RANK), F32))
    tail = jnp.concatenate(tail, axis=0)
    tail_ref[...] = tail

    biases = []
    for r in range(req):
        following = jnp.where(
            me == n_wide - 1, length_ref[r], start_ref[r, jnp.minimum(me + 1, n_wide - 1)]
        )
        position = lax.broadcasted_iota(jnp.int32, (1, block), 1)
        biases.append(jnp.where(position < following - start_ref[r, me], 0.0, F32(-1e30)))
    bias = jnp.concatenate(biases, axis=0)
    bias_ref[...] = bias

    for copy in copies[4:-1]:
        copy.wait()
    rows = []
    for i in range(req):
        row = jnp.zeros((1, width), F32)
        for r in range(req):
            row = jnp.where(placed[r] == i, residual_ref[r : r + 1, :].astype(F32), row)
        rows.append(row)
    mine = jnp.concatenate(rows, axis=0)
    for w in range(n_wide):
        full_ref[:, w * width : (w + 1) * width] = jnp.where(me == w, mine, 0.0)

    scores = partial_scores(q_ref, cache_ref, bias)
    fresh = [fresh_ref[r : r + 1, :].astype(F32) for r in range(req)]
    own = jnp.concatenate(
        [
            jnp.sum(q_ref[r].astype(F32) * fresh[r], axis=1, keepdims=True)
            * (NOPE + ROPE) ** (-0.5)
            for r in range(req)
        ],
        axis=0,
    )
    top = jnp.maximum(jnp.max(scores, axis=1, keepdims=True), own)
    expo = jnp.exp(scores - top)
    expo_own = jnp.exp(own - top)
    den = jnp.sum(expo, axis=1, keepdims=True) + expo_own
    weight_own = expo_own.astype(BF16).astype(F32)
    num = partial_sums(expo, cache_ref, heads) + jnp.concatenate(
        [weight_own[r * heads : (r + 1) * heads] * fresh[r][:, :KV_RANK] for r in range(req)],
        axis=0,
    )
    count = req * heads
    out_ref[:count, :] = (num / den).astype(BF16)
    out_ref[count:, :] = payload_tail(top + jnp.log(den), tail).astype(BF16)
    copies[-1].wait()


def attend_cost(req, heads, block, latent):
    return pl.CostEstimate(
        flops=2 * req * heads * block * (latent + KV_RANK),
        bytes_accessed=2 * req * (block * latent + heads * (latent + KV_RANK)),
        transcendentals=req * heads * block,
    )


def prepare(length, start, owner, gain, q, cache, fresh, residual, weight):
    req, heads, latent = q.shape
    block, width = cache.shape[1], residual.shape[1]
    n_wide = start.shape[1]
    operands = (length, start, owner, gain, q, cache, fresh, residual, weight)
    return pl.pallas_call(
        functools.partial(prepare_kernel, n_wide),
        out_shape=[
            jax.ShapeDtypeStruct((req * heads + TAIL, KV_RANK), BF16),
            jax.ShapeDtypeStruct((req, block), F32),
            jax.ShapeDtypeStruct((TAIL, KV_RANK), F32),
            jax.ShapeDtypeStruct((req, n_wide * width), F32),
            jax.ShapeDtypeStruct((2 + req,), jnp.int32),
            pltpu.VMEM(cache.shape, BF16),
            pltpu.VMEM(weight.shape, BF16),
        ],
        in_specs=[HBM] * len(operands),
        out_specs=[VMEM] * 4 + [SMEM, VMEM, VMEM],
        scratch_shapes=[
            pltpu.SMEM(length.shape, jnp.int32),
            pltpu.SMEM(start.shape, jnp.int32),
            pltpu.SMEM(owner.shape, jnp.int32),
            pltpu.VMEM(gain.shape, BF16),
            pltpu.VMEM(q.shape, BF16),
            pltpu.VMEM(fresh.shape, BF16),
            pltpu.VMEM(residual.shape, BF16),
            pltpu.SemaphoreType.DMA((len(operands),)),
        ],
        compiler_params=SMALL,
        cost_estimate=pl.CostEstimate(
            flops=2 * req * heads * block * (latent + KV_RANK),
            bytes_accessed=2 * (weight.size + cache.size + q.size),
            transcendentals=req * heads * block,
        ),
        name="prepare",
    )(*[in_hbm(x) for x in operands])


def attend_kernel(q_ref, cache_ref, bias_ref, tail_ref, after_ref, out_ref):
    req, heads, latent = q_ref.shape
    scores = partial_scores(q_ref, cache_ref, bias_ref[...])
    top = jnp.max(scores, axis=1, keepdims=True)
    expo = jnp.exp(scores - top)
    den = jnp.sum(expo, axis=1, keepdims=True)
    num = partial_sums(expo, cache_ref, heads)
    count = req * heads
    out_ref[:count, :] = (num / den).astype(BF16)
    out_ref[count:, :] = payload_tail(top + jnp.log(den), tail_ref[...]).astype(BF16)


def attend(q, cache, bias, tail, after):
    req, heads, latent = q.shape
    return pl.pallas_call(
        attend_kernel,
        out_shape=jax.ShapeDtypeStruct((req * heads + TAIL, KV_RANK), BF16),
        in_specs=[VMEM] * 4 + [ANY],
        out_specs=VMEM,
        compiler_params=SMALL,
        cost_estimate=attend_cost(req, heads, cache.shape[1], latent),
        name="attend",
    )(q, cache, bias, tail, after)


def fetch_kernel(both_hbm, down_hbm, after_ref, first_ref, down_ref, sems):
    count, _, depth, _ = first_ref.shape
    copies = [
        pltpu.make_async_copy(
            both_hbm.at[:, pl.ds(i * depth, depth), :], first_ref.at[i], sems.at[i]
        )
        for i in range(count)
    ]
    copies.append(pltpu.make_async_copy(down_hbm, down_ref, sems.at[count]))
    for copy in copies:
        copy.start()
    for copy in copies:
        copy.wait()


def fetch(both, down, after, count, depth):
    units = both.shape[2]
    return pl.pallas_call(
        fetch_kernel,
        out_shape=[
            pltpu.VMEM((count, 2, depth, units), BF16),
            pltpu.VMEM(down.shape, BF16),
        ],
        in_specs=[HBM, HBM, ANY],
        out_specs=[VMEM] * 2,
        scratch_shapes=[pltpu.SemaphoreType.DMA((count + 1,))],
        compiler_params=SMALL,
        cost_estimate=pl.CostEstimate(
            flops=0,
            bytes_accessed=2 * (down.size + 2 * count * depth * units),
            transcendentals=0,
        ),
        name="fetch",
    )(in_hbm(both), in_hbm(down), after)


def combine_kernel(n_wide, n_sub, width, req, order_ref, after_ref, *refs):
    payloads, outs, gain_ref, hold = refs[:n_wide], refs[n_wide : n_wide + n_sub], refs[-2], refs[-1]
    rows = payloads[0].shape[0] - TAIL
    heads = rows // req
    heads_dev = heads // n_sub
    me_sub, me_wide = order_ref[0], order_ref[1]
    tails = [p[rows:, :].astype(F32) for p in payloads]
    lses = []
    for tail in tails:
        turned = lax.dot_general(
            eye(rows, 128),
            tail[:, :128].astype(BF16),
            (((1,), (1,)), ((), ())),
            preferred_element_type=F32,
        )
        lses.append(turned[:, 0:1] + turned[:, 1:2] + turned[:, 2:3])
    top = functools.reduce(jnp.maximum, lses)
    weights = [jnp.exp(lse - top) for lse in lses]
    inv = 1.0 / functools.reduce(jnp.add, weights)
    weights = [weight * inv for weight in weights]
    for r in range(req):
        at = slice(r * heads, (r + 1) * heads)
        attn = functools.reduce(
            jnp.add, [w[at] * p[at, :].astype(F32) for w, p in zip(weights, payloads)]
        ).astype(BF16)
        for s in range(n_sub):
            hold[s, order_ref[2 + r]] = attn[s * heads_dev : (s + 1) * heads_dev]
    for k in range(n_sub):
        outs[k][...] = hold[me_sub ^ k]
    for w in range(n_wide):
        chosen = jnp.zeros((1, width), F32)
        for k in range(n_wide):
            pieces = [
                tails[k][GAIN_ROW + i : GAIN_ROW + i + 1, : min(KV_RANK, width - i * KV_RANK)]
                for i in range(pl.cdiv(width, KV_RANK))
            ]
            gain = pieces[0] if len(pieces) == 1 else jnp.concatenate(pieces, axis=1)
            chosen = jnp.where((me_wide ^ k) == w, gain, chosen)
        gain_ref[:, w * width : (w + 1) * width] = chosen


def combine(order, after, payloads, req, n_sub, width):
    n_wide = len(payloads)
    heads_dev = (payloads[0].shape[0] - TAIL) // req // n_sub
    piece = jax.ShapeDtypeStruct((req, heads_dev, KV_RANK), BF16)
    out = pl.pallas_call(
        functools.partial(combine_kernel, n_wide, n_sub, width, req),
        out_shape=[piece] * n_sub + [jax.ShapeDtypeStruct((1, n_wide * width), F32)],
        in_specs=[SMEM, ANY] + [VMEM] * n_wide,
        out_specs=[VMEM] * (n_sub + 1),
        scratch_shapes=[pltpu.VMEM((n_sub, req, heads_dev, KV_RANK), BF16)],
        compiler_params=SMALL,
        name="combine",
    )(order, after, *payloads)
    return out[:n_sub], out[n_sub]


def project_kernel(count, early, *refs):
    pieces = refs[:count]
    up_ref, weight_ref, both_hbm, keep_ref, send_ref, next_ref, vals, sems = refs[count:]
    chunks, _, chunk, _ = next_ref.shape
    copies = [
        pltpu.make_async_copy(
            both_hbm.at[:, pl.ds((early + i) * chunk, chunk), :], next_ref.at[i], sems.at[i]
        )
        for i in range(chunks)
    ]
    for copy in copies:
        copy.start()
    req, heads, rank = pieces[0].shape
    rows = count * req
    cols = up_ref.shape[1]

    stacked = jnp.concatenate([p[...].reshape(req * heads, rank) for p in pieces], axis=0)
    total = rows * heads
    to = lax.broadcasted_iota(jnp.int32, (total, total), 0)
    source = lax.broadcasted_iota(jnp.int32, (total, total), 1)
    turn = (to // rows == source % heads) & (to % rows == source // heads)
    turned = jnp.dot(turn.astype(BF16), stacked, preferred_element_type=F32).astype(BF16)
    for h in range(heads):
        val = lax.dot_general(
            turned[h * rows : (h + 1) * rows],
            up_ref[h],
            (((1,), (1,)), ((), ())),
            preferred_element_type=F32,
        )
        vals[:, h * cols : (h + 1) * cols] = val.astype(BF16)

    cb = 1024

    @pl.loop(0, weight_ref.shape[1] // cb)
    def _(i):
        at = pl.ds(pl.multiple_of(i * cb, cb), cb)
        out = jnp.dot(vals[...], weight_ref[:, at], preferred_element_type=F32)
        kept = keep_ref.shape[0]
        keep_ref[:, at] = out[:kept]
        send_ref[:, at] = out[kept:].astype(BF16)

    for copy in copies:
        copy.wait()


def project(pieces, value_up, weight, gate_up, n_pair, early, chunks, chunk):
    count = len(pieces)
    req, heads, rank = pieces[0].shape
    rows = count * req
    kept = rows // n_pair
    depth, wide = weight.shape
    return pl.pallas_call(
        functools.partial(project_kernel, count, early),
        out_shape=[
            jax.ShapeDtypeStruct((kept, wide), F32),
            jax.ShapeDtypeStruct((rows - kept, wide), BF16),
            pltpu.VMEM((chunks, 2, chunk, gate_up.shape[2]), BF16),
        ],
        in_specs=[VMEM] * (count + 2) + [HBM],
        out_specs=[VMEM] * 3,
        scratch_shapes=[pltpu.VMEM((rows, depth), BF16), pltpu.SemaphoreType.DMA((chunks,))],
        compiler_params=SMALL,
        cost_estimate=pl.CostEstimate(
            flops=2 * rows * depth * wide, bytes_accessed=2 * depth * wide, transcendentals=0
        ),
        name="project",
    )(*pieces, value_up, weight, in_hbm(gate_up))


def norm_kernel(mine_ref, gain_ref, *refs):
    arrived, (normed_ref, stream_ref) = refs[:-2], refs[-2:]
    total = mine_ref[...]
    for a in arrived:
        total = total + a[...].astype(F32)
    inv = lax.rsqrt(jnp.sum(total * total, axis=1, keepdims=True) / D + 1e-06)
    normed_ref[...] = (total * inv * gain_ref[...]).astype(BF16)
    stream_ref[...] = total


def norm(mine, gain, arrived):
    return pl.pallas_call(
        norm_kernel,
        out_shape=[
            jax.ShapeDtypeStruct(mine.shape, BF16),
            jax.ShapeDtypeStruct(mine.shape, F32),
        ],
        in_specs=[VMEM] * (2 + len(arrived)),
        out_specs=[VMEM] * 2,
        compiler_params=SMALL,
        name="norm",
    )(mine, gain, *arrived)


def mlp_kernel(count, *refs):
    pieces = refs[:count]
    both_hbm, first_ref, next_ref, down_ref, keep_ref, send_ref = refs[count : count + 6]
    rows_f32, blocks, gates, both, sems = refs[count + 6 :]
    req = pieces[0].shape[0]
    deep, rows, depth = blocks.shape
    slots, units = both.shape[0], both.shape[3]
    ready = first_ref.shape[0]
    early = ready + next_ref.shape[0]
    full = units - 128 if units % 256 == 128 else units

    def load(i):
        at = pl.ds(pl.multiple_of(i * depth, depth), depth)
        slot = lax.rem(i - early, slots)
        return pltpu.make_async_copy(both_hbm.at[:, at, :], both.at[slot], sems.at[slot])

    @pl.loop(early, early + slots)
    def _(i):
        load(i).start()

    for j, piece in enumerate(pieces):
        rows_f32[j * req : (j + 1) * req, :] = piece[...].astype(F32)
    for j in range(deep):
        blocks[j] = rows_f32[:, j * depth : (j + 1) * depth].astype(BF16)
    gates[...] = jnp.zeros_like(gates)

    def add(x, weight):
        for g in range(2):
            gates[g, :, :full] += jnp.dot(x, weight[g, :, :full], preferred_element_type=F32)
        if full < units:
            rest = jnp.concatenate([weight[0, :, full:], weight[1, :, full:]], axis=1)
            product = jnp.dot(x, rest, preferred_element_type=F32)
            for g in range(2):
                gates[g, :, full:] += product[:, g * 128 : (g + 1) * 128]

    @pl.loop(0, ready)
    def _(i):
        add(blocks[i], first_ref.at[i])

    @pl.loop(ready, early)
    def _(i):
        add(blocks[i], next_ref.at[i - ready])

    @pl.loop(early, deep)
    def _(i):
        load(i).wait()
        add(blocks[i], both.at[lax.rem(i - early, slots)])

        @pl.when(i + slots < deep)
        def _():
            load(i + slots).start()

    gate = gates[0]
    hidden = (gate / (1.0 + jnp.exp(-gate)) * gates[1]).astype(BF16)
    cb = 1024
    kept = keep_ref.shape[0]

    @pl.loop(0, down_ref.shape[1] // cb)
    def _(i):
        at = pl.ds(pl.multiple_of(i * cb, cb), cb)
        out = jnp.dot(hidden, down_ref[:, at], preferred_element_type=F32)
        keep_ref[:, at] = out[:kept]
        send_ref[:, at] = out[kept:].astype(BF16)


def mlp(pieces, gate_up, first, after, down, n_pair):
    count = len(pieces)
    req, wide = pieces[0].shape
    rows = count * req
    kept = rows // n_pair
    units = down.shape[0]
    depth, slots = first.shape[2], 6
    deep = wide // depth
    return pl.pallas_call(
        functools.partial(mlp_kernel, count),
        out_shape=[
            jax.ShapeDtypeStruct((kept, wide), F32),
            jax.ShapeDtypeStruct((rows - kept, wide), BF16),
        ],
        in_specs=[VMEM] * count + [HBM, VMEM, VMEM, VMEM],
        out_specs=[VMEM] * 2,
        scratch_shapes=[
            pltpu.VMEM((rows, wide), F32),
            pltpu.VMEM((deep, rows, depth), BF16),
            pltpu.VMEM((2, rows, units), F32),
            pltpu.VMEM((slots, 2, depth, units), BF16),
            pltpu.SemaphoreType.DMA((slots,)),
        ],
        compiler_params=pltpu.CompilerParams(vmem_limit_bytes=17 * 2**20),
        cost_estimate=pl.CostEstimate(
            flops=6 * rows * wide * units,
            bytes_accessed=4 * wide * units,
            transcendentals=rows * units,
        ),
        name="mlp",
    )(*pieces, in_hbm(gate_up), first, after, down)


def split_kernel(n_wide, order_ref, mine_ref, stream_ref, *refs):
    n_sub = len(refs) - n_wide
    arrived, own_ref, sends = refs[:n_sub], refs[n_sub], refs[n_sub + 1 :]
    width = own_ref.shape[1]
    me = order_ref[1]
    total = mine_ref[...]
    for a in arrived:
        total = total + a[...].astype(F32)
    cuts = [total[:, w * width : (w + 1) * width] for w in range(n_wide)]
    own = jnp.zeros(own_ref.shape, F32)
    for w in range(n_wide):
        own = jnp.where(me == w, cuts[w] + stream_ref[:, w * width : (w + 1) * width], own)
    own_ref[...] = own
    for k in range(1, n_wide):
        send = jnp.zeros(own_ref.shape, F32)
        for w in range(n_wide):
            send = jnp.where((me ^ k) == w, cuts[w], send)
        sends[k - 1][...] = send.astype(BF16)


def split(order, mine, stream, arrived, n_wide):
    rows, wide = mine.shape
    width = wide // n_wide
    return pl.pallas_call(
        functools.partial(split_kernel, n_wide),
        out_shape=[jax.ShapeDtypeStruct((rows, width), F32)]
        + [jax.ShapeDtypeStruct((rows, width), BF16)] * (n_wide - 1),
        in_specs=[SMEM] + [VMEM] * (2 + len(arrived)),
        out_specs=[VMEM] * n_wide,
        compiler_params=SMALL,
        name="split",
    )(order, mine, stream, *arrived)


def sum_pair(keep, send, n_pair):
    for k in range(1, n_pair):
        rows = keep.shape[0]
        keep = keep + hop(send[(k - 1) * rows : k * rows], "pair", k).astype(F32)
    return keep


def send_sub(total, rows, n_sub):
    sent = total.astype(BF16)
    return [hop(sent[k * rows : (k + 1) * rows], "sub", k) for k in range(1, n_sub)]


def body(
    latent_cache,
    queries,
    new_latent,
    context_len,
    block_start,
    owner,
    value_up,
    out_proj,
    residual_in,
    norm_gain,
    gate_up,
    down_weight,
):
    n_wide = lax.axis_size("wide")
    n_sub = lax.axis_size("sub")
    n_pair = lax.axis_size("pair")
    req_grp = latent_cache.shape[0]
    width_dev = residual_in.shape[1]

    powers = [k for k in range(1, n_wide) if k & (k - 1) == 0]
    arrived = {k: hop(queries, "wide", k) for k in reversed(powers)}
    payload, bias, tail, residual, order, cache, weight = prepare(
        context_len,
        block_start,
        owner,
        norm_gain,
        queries,
        latent_cache,
        new_latent,
        residual_in,
        out_proj.reshape(out_proj.shape[0] * out_proj.shape[1], D),
    )
    payloads = [payload]
    for k in range(1, n_wide):
        if k not in arrived:
            low = k & -k
            arrived[k] = hop(arrived[k - low], "wide", low)
        elif k > 1:
            arrived[k], payload = lax.optimization_barrier((arrived[k], payload))
        payload = attend(arrived[k], cache, bias, tail, payload)
        payloads.append(payload)
    if n_wide > 2:
        payloads[1], payloads[2] = lax.optimization_barrier((payloads[1], payloads[2]))
    chunk, early, more = 512, 1, 4
    first, down = fetch(gate_up, down_weight, payload, early, chunk)
    payloads = [payloads[0]] + [hop(payloads[k], "wide", k) for k in range(1, n_wide)]
    chunks, gain = combine(order, first, payloads, req_grp, n_sub, width_dev)

    peers = [(ks, kp) for kp in range(n_pair) for ks in range(n_sub)]
    pieces = [hop_group(chunks[ks], ks * n_pair + kp) if ks or kp else chunks[0] for ks, kp in peers]
    keep, send, after = project(
        pieces, jnp.swapaxes(value_up, 1, 2), weight, gate_up, n_pair, early, more, chunk
    )
    total = sum_pair(keep, send, n_pair)
    mine = total[:req_grp] + residual
    for a in send_sub(total, req_grp, n_sub):
        mine = mine + a.astype(F32)
    share = mine.astype(BF16)
    normed, stream = norm(mine, gain, [hop(share, "wide", k) for k in range(1, n_wide)])

    pieces = [hop_group(normed, ks * n_pair + kp) if ks or kp else normed for ks, kp in peers]
    keep, send = mlp(pieces, gate_up, first, after, down, n_pair)
    total = sum_pair(keep, send, n_pair)
    back = send_sub(total, req_grp, n_sub)
    out, *sends = split(order, total[:req_grp], stream, back, n_wide)
    for k in range(1, n_wide):
        out = out + hop(sends[k - 1], "wide", k).astype(F32)
    return out.astype(BF16)


def solution(mesh):
    in_specs = (
        P(("groups", "sub", "pair"), "wide", None),
        P(("groups", "sub", "pair"), "wide", None),
        P(("groups", "sub", "pair"), None),
        P(("groups", "sub", "pair")),
        P(("groups", "sub", "pair"), None),
        P("groups"),
        P(("wide", "sub"), None, "pair"),
        P(("wide", "sub"), "pair", None),
        P(("groups", "sub", "pair"), "wide"),
        P("wide"),
        P(None, None, ("wide", "sub", "pair")),
        P(("wide", "sub", "pair"), None),
    )
    out_specs = P(("groups", "sub", "pair"), "wide")
    return jax.shard_map(body, mesh=mesh, in_specs=in_specs, out_specs=out_specs, check_vma=False)
```

```python
import functools

import jax
import jax.numpy as jnp
from jax import lax
from jax.experimental import pallas as pl
from jax.experimental.pallas import tpu as pltpu
from jax.sharding import PartitionSpec as P

D = 7168
KV_RANK = 512
ROPE = 64
NOPE = 128
F32 = jnp.float32
BF16 = jnp.bfloat16
TAIL = 8
GAIN_ROW = 3
VMEM = pl.BlockSpec(memory_space=pltpu.VMEM)
SMEM = pl.BlockSpec(memory_space=pltpu.SMEM)
ANY = pl.BlockSpec(memory_space=pl.ANY)
HBM = pl.BlockSpec(memory_space=pltpu.HBM)
SMALL = pltpu.CompilerParams(vmem_limit_bytes=4 * 2**20)


def hop(x, axis, k):
    n = lax.axis_size(axis)
    return lax.ppermute(x, axis, [(i, i ^ k) for i in range(n)])


def hop_group(x, k):
    n = lax.axis_size("sub") * lax.axis_size("pair")
    return lax.ppermute(x, ("sub", "pair"), [(i, i ^ k) for i in range(n)])


def in_hbm(x):
    return pltpu.with_memory_space_constraint(x, pltpu.HBM)


def eye(rows, cols):
    row = lax.broadcasted_iota(jnp.int32, (rows, cols), 0)
    col = lax.broadcasted_iota(jnp.int32, (rows, cols), 1)
    return (row == col).astype(BF16)


def partial_scores(q_ref, cache_ref, bias):
    req, heads, latent = q_ref.shape
    scores = [
        lax.dot_general(
            q_ref[r], cache_ref[r], (((1,), (1,)), ((), ())), preferred_element_type=F32
        )
        * (NOPE + ROPE) ** (-0.5)
        + bias[r : r + 1, :]
        for r in range(req)
    ]
    return jnp.concatenate(scores, axis=0)


def partial_sums(expo, cache_ref, heads):
    expo = expo.astype(BF16)
    sums = [
        jnp.dot(
            expo[r * heads : (r + 1) * heads],
            cache_ref[r, :, :KV_RANK],
            preferred_element_type=F32,
        )
        for r in range(cache_ref.shape[0])
    ]
    return jnp.concatenate(sums, axis=0)


def payload_tail(lse, tail):
    rows = lse.shape[0]
    hi = lse.astype(BF16).astype(F32)
    mid = (lse - hi).astype(BF16).astype(F32)
    lo = (lse - hi - mid).astype(BF16).astype(F32)
    lane = lax.broadcasted_iota(jnp.int32, (rows, 128), 1)
    spread = jnp.where(lane == 0, hi, jnp.where(lane == 1, mid, jnp.where(lane == 2, lo, 0.0)))
    turned = lax.dot_general(
        spread.astype(BF16), eye(rows, 128), (((0,), (0,)), ((), ())), preferred_element_type=F32
    )
    return tail + jnp.pad(turned[:TAIL], ((0, 0), (0, KV_RANK - 128)))


def prepare_kernel(
    n_wide,
    length_hbm,
    start_hbm,
    owner_hbm,
    gain_hbm,
    q_hbm,
    cache_hbm,
    fresh_hbm,
    residual_hbm,
    weight_hbm,
    out_ref,
    bias_ref,
    tail_ref,
    full_ref,
    order_ref,
    cache_ref,
    weight_ref,
    length_ref,
    start_ref,
    owner_ref,
    gain_ref,
    q_ref,
    fresh_ref,
    residual_ref,
    sems,
):
    copies = [
        pltpu.make_async_copy(source, target, sems.at[i])
        for i, (source, target) in enumerate(
            [
                (length_hbm, length_ref),
                (start_hbm, start_ref),
                (owner_hbm, owner_ref),
                (gain_hbm, gain_ref),
                (q_hbm, q_ref),
                (cache_hbm, cache_ref),
                (fresh_hbm, fresh_ref),
                (residual_hbm, residual_ref),
                (weight_hbm, weight_ref),
            ]
        )
    ]
    for copy in copies:
        copy.start()
    for copy in copies[:4]:
        copy.wait()
    req, heads, latent = q_ref.shape
    block = cache_ref.shape[1]
    width = gain_ref.shape[0]
    me, me_sub = lax.axis_index("wide"), lax.axis_index("sub")
    group = me_sub * lax.axis_size("pair") + lax.axis_index("pair")

    owners = [owner_ref[group * req + r] for r in range(req)]
    placed = []
    for r in range(req):
        at = jnp.int32(0)
        for j in range(req):
            if j != r:
                ahead = owners[j] <= owners[r] if j < r else owners[j] < owners[r]
                at = at + jnp.where(ahead, 1, 0)
        placed.append(at)
        order_ref[r] = at

    gain = gain_ref[...].reshape(1, width).astype(F32)
    tail = [jnp.zeros((GAIN_ROW, KV_RANK), F32)]
    for at in range(0, width, KV_RANK):
        piece = gain[:, at : at + KV_RANK]
        if piece.shape[1] < KV_RANK:
            piece = jnp.pad(piece, ((0, 0), (0, KV_RANK - piece.shape[1])))
        tail.append(piece)
    tail.append(jnp.zeros((TAIL - GAIN_ROW - len(tail) + 1, KV_RANK), F32))
    tail = jnp.concatenate(tail, axis=0)
    tail_ref[...] = tail

    biases = []
    for r in range(req):
        following = jnp.where(
            me == n_wide - 1, length_ref[r], start_ref[r, jnp.minimum(me + 1, n_wide - 1)]
        )
        position = lax.broadcasted_iota(jnp.int32, (1, block), 1)
        biases.append(jnp.where(position < following - start_ref[r, me], 0.0, F32(-1e30)))
    bias = jnp.concatenate(biases, axis=0)
    bias_ref[...] = bias

    for copy in copies[4:-1]:
        copy.wait()
    rows = []
    for i in range(req):
        row = jnp.zeros((1, width), F32)
        for r in range(req):
            row = jnp.where(placed[r] == i, residual_ref[r : r + 1, :].astype(F32), row)
        rows.append(row)
    mine = jnp.concatenate(rows, axis=0)
    for w in range(n_wide):
        full_ref[:, w * width : (w + 1) * width] = jnp.where(me == w, mine, 0.0)

    scores = partial_scores(q_ref, cache_ref, bias)
    fresh = [fresh_ref[r : r + 1, :].astype(F32) for r in range(req)]
    own = jnp.concatenate(
        [
            jnp.sum(q_ref[r].astype(F32) * fresh[r], axis=1, keepdims=True)
            * (NOPE + ROPE) ** (-0.5)
            for r in range(req)
        ],
        axis=0,
    )
    top = jnp.maximum(jnp.max(scores, axis=1, keepdims=True), own)
    expo = jnp.exp(scores - top)
    expo_own = jnp.exp(own - top)
    den = jnp.sum(expo, axis=1, keepdims=True) + expo_own
    weight_own = expo_own.astype(BF16).astype(F32)
    num = partial_sums(expo, cache_ref, heads) + jnp.concatenate(
        [weight_own[r * heads : (r + 1) * heads] * fresh[r][:, :KV_RANK] for r in range(req)],
        axis=0,
    )
    count = req * heads
    out_ref[:count, :] = (num / den).astype(BF16)
    out_ref[count:, :] = payload_tail(top + jnp.log(den), tail).astype(BF16)
    copies[-1].wait()


def attend_cost(req, heads, block, latent):
    return pl.CostEstimate(
        flops=2 * req * heads * block * (latent + KV_RANK),
        bytes_accessed=2 * req * (block * latent + heads * (latent + KV_RANK)),
        transcendentals=req * heads * block,
    )


def prepare(length, start, owner, gain, q, cache, fresh, residual, weight):
    req, heads, latent = q.shape
    block, width = cache.shape[1], residual.shape[1]
    n_wide = start.shape[1]
    operands = (length, start, owner, gain, q, cache, fresh, residual, weight)
    return pl.pallas_call(
        functools.partial(prepare_kernel, n_wide),
        out_shape=[
            jax.ShapeDtypeStruct((req * heads + TAIL, KV_RANK), BF16),
            jax.ShapeDtypeStruct((req, block), F32),
            jax.ShapeDtypeStruct((TAIL, KV_RANK), F32),
            jax.ShapeDtypeStruct((req, n_wide * width), F32),
            jax.ShapeDtypeStruct((req,), jnp.int32),
            pltpu.VMEM(cache.shape, BF16),
            pltpu.VMEM(weight.shape, BF16),
        ],
        in_specs=[HBM] * len(operands),
        out_specs=[VMEM] * 4 + [SMEM, VMEM, VMEM],
        scratch_shapes=[
            pltpu.SMEM(length.shape, jnp.int32),
            pltpu.SMEM(start.shape, jnp.int32),
            pltpu.SMEM(owner.shape, jnp.int32),
            pltpu.VMEM(gain.shape, BF16),
            pltpu.VMEM(q.shape, BF16),
            pltpu.VMEM(fresh.shape, BF16),
            pltpu.VMEM(residual.shape, BF16),
            pltpu.SemaphoreType.DMA((len(operands),)),
        ],
        compiler_params=SMALL,
        cost_estimate=pl.CostEstimate(
            flops=2 * req * heads * block * (latent + KV_RANK),
            bytes_accessed=2 * (weight.size + cache.size + q.size),
            transcendentals=req * heads * block,
        ),
        name="prepare",
    )(*[in_hbm(x) for x in operands])


def attend_kernel(q_ref, cache_ref, bias_ref, tail_ref, after_ref, out_ref):
    req, heads, latent = q_ref.shape
    scores = partial_scores(q_ref, cache_ref, bias_ref[...])
    top = jnp.max(scores, axis=1, keepdims=True)
    expo = jnp.exp(scores - top)
    den = jnp.sum(expo, axis=1, keepdims=True)
    num = partial_sums(expo, cache_ref, heads)
    count = req * heads
    out_ref[:count, :] = (num / den).astype(BF16)
    out_ref[count:, :] = payload_tail(top + jnp.log(den), tail_ref[...]).astype(BF16)


def attend(q, cache, bias, tail, after):
    req, heads, latent = q.shape
    return pl.pallas_call(
        attend_kernel,
        out_shape=jax.ShapeDtypeStruct((req * heads + TAIL, KV_RANK), BF16),
        in_specs=[VMEM] * 4 + [ANY],
        out_specs=VMEM,
        compiler_params=SMALL,
        cost_estimate=attend_cost(req, heads, cache.shape[1], latent),
        name="attend",
    )(q, cache, bias, tail, after)


def fetch_kernel(both_hbm, down_hbm, after_ref, first_ref, down_ref, sems):
    count, _, depth, _ = first_ref.shape
    copies = [
        pltpu.make_async_copy(
            both_hbm.at[:, pl.ds(i * depth, depth), :], first_ref.at[i], sems.at[i]
        )
        for i in range(count)
    ]
    held = down_ref.shape[1]
    copies.append(pltpu.make_async_copy(down_hbm.at[:, pl.ds(0, held)], down_ref, sems.at[count]))
    for copy in copies:
        copy.start()
    for copy in copies:
        copy.wait()


def fetch(both, down, after, count, depth, held):
    units = both.shape[2]
    return pl.pallas_call(
        fetch_kernel,
        out_shape=[
            pltpu.VMEM((count, 2, depth, units), BF16),
            pltpu.VMEM((units, held), BF16),
        ],
        in_specs=[HBM, HBM, ANY],
        out_specs=[VMEM] * 2,
        scratch_shapes=[pltpu.SemaphoreType.DMA((count + 1,))],
        compiler_params=SMALL,
        cost_estimate=pl.CostEstimate(
            flops=0,
            bytes_accessed=2 * units * (held + 2 * count * depth),
            transcendentals=0,
        ),
        name="fetch",
    )(in_hbm(both), in_hbm(down), after)


def combine_kernel(n_wide, n_sub, width, req, order_any, after_ref, *refs):
    payloads, outs = refs[:n_wide], refs[n_wide : n_wide + n_sub]
    gain_ref, hold, order_ref, sem = refs[n_wide + n_sub :]
    copy = pltpu.make_async_copy(order_any, order_ref, sem)
    copy.start()
    rows = payloads[0].shape[0] - TAIL
    heads = rows // req
    heads_dev = heads // n_sub
    me_sub, me_wide = lax.axis_index("sub"), lax.axis_index("wide")
    tails = [p[rows:, :].astype(F32) for p in payloads]
    lses = []
    for tail in tails:
        turned = lax.dot_general(
            eye(rows, 128),
            tail[:, :128].astype(BF16),
            (((1,), (1,)), ((), ())),
            preferred_element_type=F32,
        )
        lses.append(turned[:, 0:1] + turned[:, 1:2] + turned[:, 2:3])
    top = functools.reduce(jnp.maximum, lses)
    weights = [jnp.exp(lse - top) for lse in lses]
    inv = 1.0 / functools.reduce(jnp.add, weights)
    weights = [weight * inv for weight in weights]
    copy.wait()
    for r in range(req):
        at = slice(r * heads, (r + 1) * heads)
        attn = functools.reduce(
            jnp.add, [w[at] * p[at, :].astype(F32) for w, p in zip(weights, payloads)]
        ).astype(BF16)
        for s in range(n_sub):
            hold[s, order_ref[r]] = attn[s * heads_dev : (s + 1) * heads_dev]
    for k in range(n_sub):
        outs[k][...] = hold[me_sub ^ k]
    for w in range(n_wide):
        chosen = jnp.zeros((1, width), F32)
        for k in range(n_wide):
            pieces = [
                tails[k][GAIN_ROW + i : GAIN_ROW + i + 1, : min(KV_RANK, width - i * KV_RANK)]
                for i in range(pl.cdiv(width, KV_RANK))
            ]
            gain = pieces[0] if len(pieces) == 1 else jnp.concatenate(pieces, axis=1)
            chosen = jnp.where((me_wide ^ k) == w, gain, chosen)
        gain_ref[:, w * width : (w + 1) * width] = chosen


def combine(order, after, payloads, req, n_sub, width):
    n_wide = len(payloads)
    heads_dev = (payloads[0].shape[0] - TAIL) // req // n_sub
    piece = jax.ShapeDtypeStruct((req, heads_dev, KV_RANK), BF16)
    out = pl.pallas_call(
        functools.partial(combine_kernel, n_wide, n_sub, width, req),
        out_shape=[piece] * n_sub + [jax.ShapeDtypeStruct((1, n_wide * width), F32)],
        in_specs=[ANY, ANY] + [VMEM] * n_wide,
        out_specs=[VMEM] * (n_sub + 1),
        scratch_shapes=[
            pltpu.VMEM((n_sub, req, heads_dev, KV_RANK), BF16),
            pltpu.SMEM(order.shape, jnp.int32),
            pltpu.SemaphoreType.DMA(()),
        ],
        compiler_params=SMALL,
        name="combine",
    )(order, after, *payloads)
    return out[:n_sub], out[n_sub]


def project_kernel(count, early, *refs):
    pieces = refs[:count]
    up_ref, weight_ref, both_hbm, keep_ref, *sends, next_ref, vals, sems = refs[count:]
    chunks, _, chunk, _ = next_ref.shape
    copies = [
        pltpu.make_async_copy(
            both_hbm.at[:, pl.ds((early + i) * chunk, chunk), :], next_ref.at[i], sems.at[i]
        )
        for i in range(chunks)
    ]
    for copy in copies:
        copy.start()
    req, heads, rank = pieces[0].shape
    rows = count * req
    cols = up_ref.shape[1]

    stacked = jnp.concatenate([p[...].reshape(req * heads, rank) for p in pieces], axis=0)
    total = rows * heads
    to = lax.broadcasted_iota(jnp.int32, (total, total), 0)
    source = lax.broadcasted_iota(jnp.int32, (total, total), 1)
    turn = (to // rows == source % heads) & (to % rows == source // heads)
    turned = jnp.dot(turn.astype(BF16), stacked, preferred_element_type=F32).astype(BF16)
    for h in range(heads):
        val = lax.dot_general(
            turned[h * rows : (h + 1) * rows],
            up_ref[h],
            (((1,), (1,)), ((), ())),
            preferred_element_type=F32,
        )
        vals[:, h * cols : (h + 1) * cols] = val.astype(BF16)

    cb = 1024

    @pl.loop(0, weight_ref.shape[1] // cb)
    def _(i):
        at = pl.ds(pl.multiple_of(i * cb, cb), cb)
        out = jnp.dot(vals[...], weight_ref[:, at], preferred_element_type=F32)
        keep_ref[:, at] = out[:req]
        for j, send in enumerate(sends):
            send[:, at] = out[(j + 1) * req : (j + 2) * req].astype(BF16)

    for copy in copies:
        copy.wait()


def project(pieces, value_up, weight, gate_up, early, chunks, chunk):
    count = len(pieces)
    req, heads, rank = pieces[0].shape
    rows = count * req
    depth, wide = weight.shape
    return pl.pallas_call(
        functools.partial(project_kernel, count, early),
        out_shape=[jax.ShapeDtypeStruct((req, wide), F32)]
        + [jax.ShapeDtypeStruct((req, wide), BF16)] * (count - 1)
        + [pltpu.VMEM((chunks, 2, chunk, gate_up.shape[2]), BF16)],
        in_specs=[VMEM] * (count + 2) + [HBM],
        out_specs=[VMEM] * (count + 1),
        scratch_shapes=[pltpu.VMEM((rows, depth), BF16), pltpu.SemaphoreType.DMA((chunks,))],
        compiler_params=SMALL,
        cost_estimate=pl.CostEstimate(
            flops=2 * rows * depth * wide, bytes_accessed=2 * depth * wide, transcendentals=0
        ),
        name="project",
    )(*pieces, value_up, weight, in_hbm(gate_up))


def norm_kernel(mine_ref, gain_ref, *refs):
    arrived, (normed_ref, stream_ref) = refs[:-2], refs[-2:]
    total = mine_ref[...]
    for a in arrived:
        total = total + a[...].astype(F32)
    inv = lax.rsqrt(jnp.sum(total * total, axis=1, keepdims=True) / D + 1e-06)
    normed_ref[...] = (total * inv * gain_ref[...]).astype(BF16)
    stream_ref[...] = total


def norm(mine, gain, arrived):
    return pl.pallas_call(
        norm_kernel,
        out_shape=[
            jax.ShapeDtypeStruct(mine.shape, BF16),
            jax.ShapeDtypeStruct(mine.shape, F32),
        ],
        in_specs=[VMEM] * (2 + len(arrived)),
        out_specs=[VMEM] * 2,
        compiler_params=SMALL,
        name="norm",
    )(mine, gain, *arrived)


def mlp_kernel(count, *refs):
    pieces = refs[:count]
    both_hbm, first_ref, next_ref, down_hbm, down_ref, keep_ref, *sends = refs[count:-7]
    rows_f32, blocks, gates, both, down, sems, down_sems = refs[-7:]
    req = pieces[0].shape[0]
    deep, rows, depth = blocks.shape
    slots, units = both.shape[0], both.shape[3]
    ready = first_ref.shape[0]
    early = ready + next_ref.shape[0]
    full = units - 128 if units % 256 == 128 else units

    def load(i):
        at = pl.ds(pl.multiple_of(i * depth, depth), depth)
        slot = lax.rem(i - early, slots)
        return pltpu.make_async_copy(both_hbm.at[:, at, :], both.at[slot], sems.at[slot])

    late, _, cb = down.shape
    held = down_ref.shape[1]
    down_copies = [
        pltpu.make_async_copy(
            down_hbm.at[:, pl.ds(held + i * cb, cb)], down.at[i], down_sems.at[i]
        )
        for i in range(late)
    ]

    @pl.loop(early, early + slots)
    def _(i):
        load(i).start()

    for j, piece in enumerate(pieces):
        rows_f32[j * req : (j + 1) * req, :] = piece[...].astype(F32)
    for j in range(deep):
        blocks[j] = rows_f32[:, j * depth : (j + 1) * depth].astype(BF16)
    gates[...] = jnp.zeros_like(gates)

    def add(x, weight):
        for g in range(2):
            gates[g, :, :full] += jnp.dot(x, weight[g, :, :full], preferred_element_type=F32)
        if full < units:
            rest = jnp.concatenate([weight[0, :, full:], weight[1, :, full:]], axis=1)
            product = jnp.dot(x, rest, preferred_element_type=F32)
            for g in range(2):
                gates[g, :, full:] += product[:, g * 128 : (g + 1) * 128]

    @pl.loop(0, ready)
    def _(i):
        add(blocks[i], first_ref.at[i])

    @pl.loop(ready, early)
    def _(i):
        add(blocks[i], next_ref.at[i - ready])

    @pl.loop(early, deep)
    def _(i):
        load(i).wait()
        add(blocks[i], both.at[lax.rem(i - early, slots)])

        @pl.when(i + slots < deep)
        def _():
            load(i + slots).start()

        @pl.when(i + slots == deep)
        def _():
            for copy in down_copies:
                copy.start()

    gate = gates[0]
    hidden = (gate / (1.0 + jnp.exp(-gate)) * gates[1]).astype(BF16)

    def write(at, weight):
        out = jnp.dot(hidden, weight, preferred_element_type=F32)
        keep_ref[:, at] = out[:req]
        for j, send in enumerate(sends):
            send[:, at] = out[(j + 1) * req : (j + 2) * req].astype(BF16)

    @pl.loop(0, held // cb)
    def _(i):
        at = pl.ds(pl.multiple_of(i * cb, cb), cb)
        write(at, down_ref[:, at])

    for i, copy in enumerate(down_copies):
        copy.wait()
        write(pl.ds(held + i * cb, cb), down[i])


def mlp(pieces, gate_up, first, after, down_weight, down):
    count = len(pieces)
    req, wide = pieces[0].shape
    rows = count * req
    units, held = down.shape
    depth, slots, cb = first.shape[2], 6, 1024
    late = (wide - held) // cb
    deep = wide // depth
    return pl.pallas_call(
        functools.partial(mlp_kernel, count),
        out_shape=[jax.ShapeDtypeStruct((req, wide), F32)]
        + [jax.ShapeDtypeStruct((req, wide), BF16)] * (count - 1),
        in_specs=[VMEM] * count + [HBM, VMEM, VMEM, HBM, VMEM],
        out_specs=[VMEM] * count,
        scratch_shapes=[
            pltpu.VMEM((rows, wide), F32),
            pltpu.VMEM((deep, rows, depth), BF16),
            pltpu.VMEM((2, rows, units), F32),
            pltpu.VMEM((slots, 2, depth, units), BF16),
            pltpu.VMEM((late, units, cb), BF16),
            pltpu.SemaphoreType.DMA((slots,)),
            pltpu.SemaphoreType.DMA((late,)),
        ],
        compiler_params=pltpu.CompilerParams(vmem_limit_bytes=24 * 2**20),
        cost_estimate=pl.CostEstimate(
            flops=6 * rows * wide * units,
            bytes_accessed=4 * wide * units,
            transcendentals=rows * units,
        ),
        name="mlp",
    )(*pieces, in_hbm(gate_up), first, after, in_hbm(down_weight), down)


def split_kernel(n_wide, mine_ref, stream_ref, *refs):
    count = len(refs) - n_wide
    arrived, own_ref, sends = refs[:count], refs[count], refs[count + 1 :]
    width = own_ref.shape[1]
    me = lax.axis_index("wide")
    total = mine_ref[...]
    for a in arrived:
        total = total + a[...].astype(F32)
    cuts = [total[:, w * width : (w + 1) * width] for w in range(n_wide)]
    own = jnp.zeros(own_ref.shape, F32)
    for w in range(n_wide):
        own = jnp.where(me == w, cuts[w] + stream_ref[:, w * width : (w + 1) * width], own)
    own_ref[...] = own
    for k in range(1, n_wide):
        send = jnp.zeros(own_ref.shape, F32)
        for w in range(n_wide):
            send = jnp.where((me ^ k) == w, cuts[w], send)
        sends[k - 1][...] = send.astype(BF16)


def split(mine, stream, arrived, n_wide):
    rows, wide = mine.shape
    width = wide // n_wide
    return pl.pallas_call(
        functools.partial(split_kernel, n_wide),
        out_shape=[jax.ShapeDtypeStruct((rows, width), F32)]
        + [jax.ShapeDtypeStruct((rows, width), BF16)] * (n_wide - 1),
        in_specs=[VMEM] * (2 + len(arrived)),
        out_specs=[VMEM] * n_wide,
        compiler_params=SMALL,
        name="split",
    )(mine, stream, *arrived)


def body(
    latent_cache,
    queries,
    new_latent,
    context_len,
    block_start,
    owner,
    value_up,
    out_proj,
    residual_in,
    norm_gain,
    gate_up,
    down_weight,
):
    n_wide = lax.axis_size("wide")
    n_sub = lax.axis_size("sub")
    n_pair = lax.axis_size("pair")
    req_grp = latent_cache.shape[0]
    width_dev = residual_in.shape[1]

    powers = [k for k in range(1, n_wide) if k & (k - 1) == 0]
    arrived = {k: hop(queries, "wide", k) for k in reversed(powers)}
    payload, bias, tail, residual, order, cache, weight = prepare(
        context_len,
        block_start,
        owner,
        norm_gain,
        queries,
        latent_cache,
        new_latent,
        residual_in,
        out_proj.reshape(out_proj.shape[0] * out_proj.shape[1], D),
    )
    payloads = [payload]
    for k in range(1, n_wide):
        if k not in arrived:
            low = k & -k
            arrived[k] = hop(arrived[k - low], "wide", low)
        elif k > 1:
            arrived[k], payload = lax.optimization_barrier((arrived[k], payload))
        payload = attend(arrived[k], cache, bias, tail, payload)
        payloads.append(payload)
    payloads[1], payloads[-1] = lax.optimization_barrier((payloads[1], payloads[-1]))
    chunk, early, more, held = 512, 1, 4, 4096
    first, down = fetch(gate_up, down_weight, payload, early, chunk, held)
    payloads = [payloads[0]] + [hop(payloads[k], "wide", k) for k in range(1, n_wide)]
    chunks, gain = combine(order, first, payloads, req_grp, n_sub, width_dev)

    peers = [(ks, kp) for kp in range(n_pair) for ks in range(n_sub)]
    masks = [ks * n_pair + kp for ks, kp in peers]
    pieces = [chunks[0]] + [hop_group(chunks[ks], ks * n_pair + kp) for ks, kp in peers[1:]]
    keep, *sends, after = project(
        pieces, jnp.swapaxes(value_up, 1, 2), weight, gate_up, early, more, chunk
    )
    mine = keep + residual
    for k, send in zip(masks[1:], sends):
        mine = mine + hop_group(send, k).astype(F32)
    share = mine.astype(BF16)
    normed, stream = norm(mine, gain, [hop(share, "wide", k) for k in range(1, n_wide)])

    pieces = [normed] + [hop_group(normed, k) for k in masks[1:]]
    keep, *sends = mlp(pieces, gate_up, first, after, down_weight, down)
    back = [hop_group(send, k) for k, send in zip(masks[1:], sends)]
    out, *sends = split(keep, stream, back, n_wide)
    for k in range(1, n_wide):
        out = out + hop(sends[k - 1], "wide", k).astype(F32)
    return out.astype(BF16)


def solution(mesh):
    in_specs = (
        P(("groups", "sub", "pair"), "wide", None),
        P(("groups", "sub", "pair"), "wide", None),
        P(("groups", "sub", "pair"), None),
        P(("groups", "sub", "pair")),
        P(("groups", "sub", "pair"), None),
        P("groups"),
        P(("wide", "sub"), None, "pair"),
        P(("wide", "sub"), "pair", None),
        P(("groups", "sub", "pair"), "wide"),
        P("wide"),
        P(None, None, ("wide", "sub", "pair")),
        P(("wide", "sub", "pair"), None),
    )
    out_specs = P(("groups", "sub", "pair"), "wide")
    return jax.shard_map(body, mesh=mesh, in_specs=in_specs, out_specs=out_specs, check_vma=False)
```

```python
import functools
import math

import jax
import jax.numpy as jnp
from jax import lax
from jax.experimental import pallas as pl
from jax.experimental.pallas import tpu as pltpu
from jax.sharding import PartitionSpec as P

D = 7168
KV_RANK = 512
ROPE = 64
NOPE = 128
F32 = jnp.float32
BF16 = jnp.bfloat16
TAIL = 8
GAIN_ROW = 3
VMEM = pl.BlockSpec(memory_space=pltpu.VMEM)
SMEM = pl.BlockSpec(memory_space=pltpu.SMEM)
ANY = pl.BlockSpec(memory_space=pl.ANY)
HBM = pl.BlockSpec(memory_space=pltpu.HBM)
SMALL = pltpu.CompilerParams(vmem_limit_bytes=4 * 2**20)


def hop(x, axis, k):
    n = lax.axis_size(axis)
    return lax.ppermute(x, axis, [(i, i ^ k) for i in range(n)])


def hop_two(x, axes, k):
    n = lax.axis_size(axes[0]) * lax.axis_size(axes[1])
    return lax.ppermute(x, axes, [(i, i ^ k) for i in range(n)])


def hop_group(x, k):
    return hop_two(x, ("sub", "pair"), k)


def in_hbm(x):
    return pltpu.with_memory_space_constraint(x, pltpu.HBM)


def eye(rows, cols):
    row = lax.broadcasted_iota(jnp.int32, (rows, cols), 0)
    col = lax.broadcasted_iota(jnp.int32, (rows, cols), 1)
    return (row == col).astype(BF16)


def partial_scores(q_ref, cache_ref, bias):
    req, heads, latent = q_ref.shape
    scores = [
        lax.dot_general(
            q_ref[r], cache_ref[r], (((1,), (1,)), ((), ())), preferred_element_type=F32
        )
        * (NOPE + ROPE) ** (-0.5)
        + bias[r : r + 1, :]
        for r in range(req)
    ]
    return jnp.concatenate(scores, axis=0)


def partial_sums(expo, cache_ref, heads):
    expo = expo.astype(BF16)
    sums = [
        jnp.dot(
            expo[r * heads : (r + 1) * heads],
            cache_ref[r, :, :KV_RANK],
            preferred_element_type=F32,
        )
        for r in range(cache_ref.shape[0])
    ]
    return jnp.concatenate(sums, axis=0)


def payload_tail(lse, tail):
    rows = lse.shape[0]
    hi = lse.astype(BF16).astype(F32)
    mid = (lse - hi).astype(BF16).astype(F32)
    lo = (lse - hi - mid).astype(BF16).astype(F32)
    lane = lax.broadcasted_iota(jnp.int32, (rows, 128), 1)
    spread = jnp.where(lane == 0, hi, jnp.where(lane == 1, mid, jnp.where(lane == 2, lo, 0.0)))
    turned = lax.dot_general(
        spread.astype(BF16), eye(rows, 128), (((0,), (0,)), ((), ())), preferred_element_type=F32
    )
    return tail + jnp.pad(turned[:TAIL], ((0, 0), (0, KV_RANK - 128)))


def prepare_kernel(
    n_wide,
    length_hbm,
    start_hbm,
    owner_hbm,
    gain_hbm,
    q_hbm,
    cache_hbm,
    fresh_hbm,
    residual_hbm,
    weight_hbm,
    out_ref,
    bias_ref,
    tail_ref,
    full_ref,
    order_ref,
    cache_ref,
    weight_ref,
    length_ref,
    start_ref,
    owner_ref,
    gain_ref,
    q_ref,
    fresh_ref,
    residual_ref,
    sems,
):
    copies = [
        pltpu.make_async_copy(source, target, sems.at[i])
        for i, (source, target) in enumerate(
            [
                (length_hbm, length_ref),
                (start_hbm, start_ref),
                (owner_hbm, owner_ref),
                (gain_hbm, gain_ref),
                (q_hbm, q_ref),
                (cache_hbm, cache_ref),
                (fresh_hbm, fresh_ref),
                (residual_hbm, residual_ref),
                (weight_hbm, weight_ref),
            ]
        )
    ]
    for copy in copies:
        copy.start()
    for copy in copies[:4]:
        copy.wait()
    req, heads, latent = q_ref.shape
    block = cache_ref.shape[1]
    width = gain_ref.shape[0]
    me, me_sub = lax.axis_index("wide"), lax.axis_index("sub")
    group = me_sub * lax.axis_size("pair") + lax.axis_index("pair")

    owners = [owner_ref[group * req + r] for r in range(req)]
    placed = []
    for r in range(req):
        at = jnp.int32(0)
        for j in range(req):
            if j != r:
                ahead = owners[j] <= owners[r] if j < r else owners[j] < owners[r]
                at = at + jnp.where(ahead, 1, 0)
        placed.append(at)
        order_ref[r] = at

    gain = gain_ref[...].reshape(1, width).astype(F32)
    tail = [jnp.zeros((GAIN_ROW, KV_RANK), F32)]
    for at in range(0, width, KV_RANK):
        piece = gain[:, at : at + KV_RANK]
        if piece.shape[1] < KV_RANK:
            piece = jnp.pad(piece, ((0, 0), (0, KV_RANK - piece.shape[1])))
        tail.append(piece)
    tail.append(jnp.zeros((TAIL - GAIN_ROW - len(tail) + 1, KV_RANK), F32))
    tail = jnp.concatenate(tail, axis=0)
    tail_ref[...] = tail

    biases = []
    for r in range(req):
        following = jnp.where(
            me == n_wide - 1, length_ref[r], start_ref[r, jnp.minimum(me + 1, n_wide - 1)]
        )
        position = lax.broadcasted_iota(jnp.int32, (1, block), 1)
        biases.append(jnp.where(position < following - start_ref[r, me], 0.0, F32(-1e30)))
    bias = jnp.concatenate(biases, axis=0)
    bias_ref[...] = bias

    for copy in copies[4:-1]:
        copy.wait()
    rows = []
    for i in range(req):
        row = jnp.zeros((1, width), F32)
        for r in range(req):
            row = jnp.where(placed[r] == i, residual_ref[r : r + 1, :].astype(F32), row)
        rows.append(row)
    mine = jnp.concatenate(rows, axis=0)
    for w in range(n_wide):
        full_ref[:, w * width : (w + 1) * width] = jnp.where(me == w, mine, 0.0)

    scores = partial_scores(q_ref, cache_ref, bias)
    fresh = [fresh_ref[r : r + 1, :].astype(F32) for r in range(req)]
    own = jnp.concatenate(
        [
            jnp.sum(q_ref[r].astype(F32) * fresh[r], axis=1, keepdims=True)
            * (NOPE + ROPE) ** (-0.5)
            for r in range(req)
        ],
        axis=0,
    )
    top = jnp.maximum(jnp.max(scores, axis=1, keepdims=True), own)
    expo = jnp.exp(scores - top)
    expo_own = jnp.exp(own - top)
    den = jnp.sum(expo, axis=1, keepdims=True) + expo_own
    weight_own = expo_own.astype(BF16).astype(F32)
    num = partial_sums(expo, cache_ref, heads) + jnp.concatenate(
        [weight_own[r * heads : (r + 1) * heads] * fresh[r][:, :KV_RANK] for r in range(req)],
        axis=0,
    )
    count = req * heads
    out_ref[:count, :] = (num / den).astype(BF16)
    out_ref[count:, :] = payload_tail(top + jnp.log(den), tail).astype(BF16)
    copies[-1].wait()


def attend_cost(req, heads, block, latent):
    return pl.CostEstimate(
        flops=2 * req * heads * block * (latent + KV_RANK),
        bytes_accessed=2 * req * (block * latent + heads * (latent + KV_RANK)),
        transcendentals=req * heads * block,
    )


def prepare(length, start, owner, gain, q, cache, fresh, residual, weight):
    req, heads, latent = q.shape
    block, width = cache.shape[1], residual.shape[1]
    n_wide = start.shape[1]
    operands = (length, start, owner, gain, q, cache, fresh, residual, weight)
    return pl.pallas_call(
        functools.partial(prepare_kernel, n_wide),
        out_shape=[
            jax.ShapeDtypeStruct((req * heads + TAIL, KV_RANK), BF16),
            jax.ShapeDtypeStruct((req, block), F32),
            jax.ShapeDtypeStruct((TAIL, KV_RANK), F32),
            jax.ShapeDtypeStruct((req, n_wide * width), F32),
            jax.ShapeDtypeStruct((req,), jnp.int32),
            pltpu.VMEM(cache.shape, BF16),
            pltpu.VMEM(weight.shape, BF16),
        ],
        in_specs=[HBM] * len(operands),
        out_specs=[VMEM] * 4 + [SMEM, VMEM, VMEM],
        scratch_shapes=[
            pltpu.SMEM(length.shape, jnp.int32),
            pltpu.SMEM(start.shape, jnp.int32),
            pltpu.SMEM(owner.shape, jnp.int32),
            pltpu.VMEM(gain.shape, BF16),
            pltpu.VMEM(q.shape, BF16),
            pltpu.VMEM(fresh.shape, BF16),
            pltpu.VMEM(residual.shape, BF16),
            pltpu.SemaphoreType.DMA((len(operands),)),
        ],
        compiler_params=SMALL,
        cost_estimate=pl.CostEstimate(
            flops=2 * req * heads * block * (latent + KV_RANK),
            bytes_accessed=2 * (weight.size + cache.size + q.size),
            transcendentals=req * heads * block,
        ),
        name="prepare",
    )(*[in_hbm(x) for x in operands])


def attend_kernel(q_ref, cache_ref, bias_ref, tail_ref, after_ref, out_ref):
    req, heads, latent = q_ref.shape
    scores = partial_scores(q_ref, cache_ref, bias_ref[...])
    top = jnp.max(scores, axis=1, keepdims=True)
    expo = jnp.exp(scores - top)
    den = jnp.sum(expo, axis=1, keepdims=True)
    num = partial_sums(expo, cache_ref, heads)
    count = req * heads
    out_ref[:count, :] = (num / den).astype(BF16)
    out_ref[count:, :] = payload_tail(top + jnp.log(den), tail_ref[...]).astype(BF16)


def attend(q, cache, bias, tail, after):
    req, heads, latent = q.shape
    return pl.pallas_call(
        attend_kernel,
        out_shape=jax.ShapeDtypeStruct((req * heads + TAIL, KV_RANK), BF16),
        in_specs=[VMEM] * 4 + [ANY],
        out_specs=VMEM,
        compiler_params=SMALL,
        cost_estimate=attend_cost(req, heads, cache.shape[1], latent),
        name="attend",
    )(q, cache, bias, tail, after)


def fetch_gate(both_hbm, after_ref, out_ref, sems):
    count, _, depth, _ = out_ref.shape
    copies = [
        pltpu.make_async_copy(both_hbm.at[:, pl.ds(i * depth, depth), :], out_ref.at[i], sems.at[i])
        for i in range(count)
    ]
    for copy in copies:
        copy.start()
    for copy in copies:
        copy.wait()


def fetch_down(down_hbm, after_ref, out_ref, sems):
    units, held = out_ref.shape
    count = sems.shape[0]
    cb = held // count
    copies = [
        pltpu.make_async_copy(
            down_hbm.at[:, pl.ds(i * cb, cb)], out_ref.at[:, pl.ds(i * cb, cb)], sems.at[i]
        )
        for i in range(count)
    ]
    for copy in copies:
        copy.start()
    for copy in copies:
        copy.wait()


def fetch(kernel, source, after, shape, count):
    return pl.pallas_call(
        kernel,
        out_shape=pltpu.VMEM(shape, BF16),
        in_specs=[HBM, ANY],
        out_specs=VMEM,
        scratch_shapes=[pltpu.SemaphoreType.DMA((count,))],
        compiler_params=SMALL,
        cost_estimate=pl.CostEstimate(
            flops=0, bytes_accessed=2 * math.prod(shape), transcendentals=0
        ),
        name="fetch",
    )(in_hbm(source), after)


def combine_kernel(n_wide, n_sub, width, req, order_any, after_ref, *refs):
    payloads, outs = refs[:n_wide], refs[n_wide : n_wide + n_sub]
    gain_ref, hold, order_ref, sem = refs[n_wide + n_sub :]
    copy = pltpu.make_async_copy(order_any, order_ref, sem)
    copy.start()
    rows = payloads[0].shape[0] - TAIL
    heads = rows // req
    heads_dev = heads // n_sub
    me_sub, me_wide = lax.axis_index("sub"), lax.axis_index("wide")
    tails = [p[rows:, :].astype(F32) for p in payloads]
    lses = []
    for tail in tails:
        turned = lax.dot_general(
            eye(rows, 128),
            tail[:, :128].astype(BF16),
            (((1,), (1,)), ((), ())),
            preferred_element_type=F32,
        )
        lses.append(turned[:, 0:1] + turned[:, 1:2] + turned[:, 2:3])
    top = functools.reduce(jnp.maximum, lses)
    weights = [jnp.exp(lse - top) for lse in lses]
    inv = 1.0 / functools.reduce(jnp.add, weights)
    weights = [weight * inv for weight in weights]
    copy.wait()
    for r in range(req):
        at = slice(r * heads, (r + 1) * heads)
        attn = functools.reduce(
            jnp.add, [w[at] * p[at, :].astype(F32) for w, p in zip(weights, payloads)]
        ).astype(BF16)
        for s in range(n_sub):
            hold[s, order_ref[r]] = attn[s * heads_dev : (s + 1) * heads_dev]
    for k in range(n_sub):
        outs[k][...] = hold[me_sub ^ k]
    for w in range(n_wide):
        chosen = jnp.zeros((1, width), F32)
        for k in range(n_wide):
            pieces = [
                tails[k][GAIN_ROW + i : GAIN_ROW + i + 1, : min(KV_RANK, width - i * KV_RANK)]
                for i in range(pl.cdiv(width, KV_RANK))
            ]
            gain = pieces[0] if len(pieces) == 1 else jnp.concatenate(pieces, axis=1)
            chosen = jnp.where((me_wide ^ k) == w, gain, chosen)
        gain_ref[:, w * width : (w + 1) * width] = chosen


def combine(order, after, payloads, req, n_sub, width):
    n_wide = len(payloads)
    heads_dev = (payloads[0].shape[0] - TAIL) // req // n_sub
    piece = jax.ShapeDtypeStruct((req, heads_dev, KV_RANK), BF16)
    out = pl.pallas_call(
        functools.partial(combine_kernel, n_wide, n_sub, width, req),
        out_shape=[piece] * n_sub + [jax.ShapeDtypeStruct((1, n_wide * width), F32)],
        in_specs=[ANY, ANY] + [VMEM] * n_wide,
        out_specs=[VMEM] * (n_sub + 1),
        scratch_shapes=[
            pltpu.VMEM((n_sub, req, heads_dev, KV_RANK), BF16),
            pltpu.SMEM(order.shape, jnp.int32),
            pltpu.SemaphoreType.DMA(()),
        ],
        compiler_params=SMALL,
        name="combine",
    )(order, after, *payloads)
    return out[:n_sub], out[n_sub]


def project_kernel(count, early, *refs):
    pieces = refs[:count]
    up_ref, weight_ref, both_hbm, keep_ref, *sends, next_ref, vals, sems = refs[count:]
    chunks, _, chunk, _ = next_ref.shape
    copies = [
        pltpu.make_async_copy(
            both_hbm.at[:, pl.ds((early + i) * chunk, chunk), :], next_ref.at[i], sems.at[i]
        )
        for i in range(chunks)
    ]
    for copy in copies:
        copy.start()
    req, heads, rank = pieces[0].shape
    rows = count * req
    cols = up_ref.shape[1]

    stacked = jnp.concatenate([p[...].reshape(req * heads, rank) for p in pieces], axis=0)
    total = rows * heads
    to = lax.broadcasted_iota(jnp.int32, (total, total), 0)
    source = lax.broadcasted_iota(jnp.int32, (total, total), 1)
    turn = (to // rows == source % heads) & (to % rows == source // heads)
    turned = jnp.dot(turn.astype(BF16), stacked, preferred_element_type=F32).astype(BF16)
    for h in range(heads):
        val = lax.dot_general(
            turned[h * rows : (h + 1) * rows],
            up_ref[h],
            (((1,), (1,)), ((), ())),
            preferred_element_type=F32,
        )
        vals[:, h * cols : (h + 1) * cols] = val.astype(BF16)

    cb = 1024

    @pl.loop(0, weight_ref.shape[1] // cb)
    def _(i):
        at = pl.ds(pl.multiple_of(i * cb, cb), cb)
        out = jnp.dot(vals[...], weight_ref[:, at], preferred_element_type=F32)
        keep_ref[:, at] = out[:req]
        for j, send in enumerate(sends):
            send[:, at] = out[(j + 1) * req : (j + 2) * req].astype(BF16)

    for copy in copies:
        copy.wait()


def project(pieces, value_up, weight, gate_up, early, chunks, chunk):
    count = len(pieces)
    req, heads, rank = pieces[0].shape
    rows = count * req
    depth, wide = weight.shape
    return pl.pallas_call(
        functools.partial(project_kernel, count, early),
        out_shape=[jax.ShapeDtypeStruct((req, wide), F32)]
        + [jax.ShapeDtypeStruct((req, wide), BF16)] * (count - 1)
        + [pltpu.VMEM((chunks, 2, chunk, gate_up.shape[2]), BF16)],
        in_specs=[VMEM] * (count + 2) + [HBM],
        out_specs=[VMEM] * (count + 1),
        scratch_shapes=[pltpu.VMEM((rows, depth), BF16), pltpu.SemaphoreType.DMA((chunks,))],
        compiler_params=SMALL,
        cost_estimate=pl.CostEstimate(
            flops=2 * rows * depth * wide, bytes_accessed=2 * depth * wide, transcendentals=0
        ),
        name="project",
    )(*pieces, value_up, weight, in_hbm(gate_up))


def norm_kernel(mine_ref, gain_ref, *refs):
    arrived, (normed_ref, stream_ref) = refs[:-2], refs[-2:]
    total = mine_ref[...]
    for a in arrived:
        total = total + a[...].astype(F32)
    inv = lax.rsqrt(jnp.sum(total * total, axis=1, keepdims=True) / D + 1e-06)
    normed_ref[...] = (total * inv * gain_ref[...]).astype(BF16)
    stream_ref[...] = total


def norm(mine, gain, arrived):
    return pl.pallas_call(
        norm_kernel,
        out_shape=[
            jax.ShapeDtypeStruct(mine.shape, BF16),
            jax.ShapeDtypeStruct(mine.shape, F32),
        ],
        in_specs=[VMEM] * (2 + len(arrived)),
        out_specs=[VMEM] * 2,
        compiler_params=SMALL,
        name="norm",
    )(mine, gain, *arrived)


def mlp_kernel(count, *refs):
    pieces = refs[:count]
    both_hbm, first_ref, next_ref, down_hbm, down_ref, keep_ref, send_ref = refs[count:-7]
    rows_f32, blocks, gates, both, down, sems, down_sems = refs[-7:]
    req = pieces[0].shape[0]
    deep, rows, depth = blocks.shape
    slots, units = both.shape[0], both.shape[3]
    ready = first_ref.shape[0]
    early = ready + next_ref.shape[0]
    full = units - 128 if units % 256 == 128 else units

    def load(i):
        at = pl.ds(pl.multiple_of(i * depth, depth), depth)
        slot = lax.rem(i - early, slots)
        return pltpu.make_async_copy(both_hbm.at[:, at, :], both.at[slot], sems.at[slot])

    late, _, cb = down.shape
    held = down_ref.shape[1]
    down_copies = [
        pltpu.make_async_copy(
            down_hbm.at[:, pl.ds(held + i * cb, cb)], down.at[i], down_sems.at[i]
        )
        for i in range(late)
    ]

    @pl.loop(early, early + slots)
    def _(i):
        load(i).start()

    for j, piece in enumerate(pieces):
        rows_f32[j * req : (j + 1) * req, :] = piece[...].astype(F32)
    for j in range(deep):
        blocks[j] = rows_f32[:, j * depth : (j + 1) * depth].astype(BF16)
    gates[...] = jnp.zeros_like(gates)

    def add(x, weight):
        for g in range(2):
            gates[g, :, :full] += jnp.dot(x, weight[g, :, :full], preferred_element_type=F32)
        if full < units:
            rest = jnp.concatenate([weight[0, :, full:], weight[1, :, full:]], axis=1)
            product = jnp.dot(x, rest, preferred_element_type=F32)
            for g in range(2):
                gates[g, :, full:] += product[:, g * 128 : (g + 1) * 128]

    @pl.loop(0, ready)
    def _(i):
        add(blocks[i], first_ref.at[i])

    @pl.loop(ready, early)
    def _(i):
        add(blocks[i], next_ref.at[i - ready])

    @pl.loop(early, deep)
    def _(i):
        load(i).wait()
        add(blocks[i], both.at[lax.rem(i - early, slots)])

        @pl.when(i + slots < deep)
        def _():
            load(i + slots).start()

        @pl.when(i + slots == deep)
        def _():
            for copy in down_copies:
                copy.start()

    gate = gates[0]
    hidden = (gate / (1.0 + jnp.exp(-gate)) * gates[1]).astype(BF16)

    kept = keep_ref.shape[0]

    def write(at, weight):
        out = jnp.dot(hidden, weight, preferred_element_type=F32)
        keep_ref[:, at] = out[:kept]
        send_ref[:, at] = out[kept:].astype(BF16)

    @pl.loop(0, held // cb)
    def _(i):
        at = pl.ds(pl.multiple_of(i * cb, cb), cb)
        write(at, down_ref[:, at])

    for i, copy in enumerate(down_copies):
        copy.wait()
        write(pl.ds(held + i * cb, cb), down[i])


def mlp(pieces, gate_up, first, after, down_weight, down, n_pair):
    count = len(pieces)
    req, wide = pieces[0].shape
    rows = count * req
    kept = rows // n_pair
    units, held = down.shape
    depth, slots, cb = first.shape[2], 6, 1024
    late = (wide - held) // cb
    deep = wide // depth
    return pl.pallas_call(
        functools.partial(mlp_kernel, count),
        out_shape=[
            jax.ShapeDtypeStruct((kept, wide), F32),
            jax.ShapeDtypeStruct((rows - kept, wide), BF16),
        ],
        in_specs=[VMEM] * count + [HBM, VMEM, VMEM, HBM, VMEM],
        out_specs=[VMEM] * 2,
        scratch_shapes=[
            pltpu.VMEM((rows, wide), F32),
            pltpu.VMEM((deep, rows, depth), BF16),
            pltpu.VMEM((2, rows, units), F32),
            pltpu.VMEM((slots, 2, depth, units), BF16),
            pltpu.VMEM((late, units, cb), BF16),
            pltpu.SemaphoreType.DMA((slots,)),
            pltpu.SemaphoreType.DMA((late,)),
        ],
        compiler_params=pltpu.CompilerParams(vmem_limit_bytes=24 * 2**20),
        cost_estimate=pl.CostEstimate(
            flops=6 * rows * wide * units,
            bytes_accessed=4 * wide * units,
            transcendentals=rows * units,
        ),
        name="mlp",
    )(*pieces, in_hbm(gate_up), first, after, in_hbm(down_weight), down)


def split_kernel(n_wide, n_pair, mine_ref, stream_ref, *refs):
    arrived, own_ref, sends = refs[: n_pair - 1], refs[n_pair - 1], refs[n_pair:]
    req, width = own_ref.shape
    me = lax.axis_index("wide")
    total = mine_ref[...]
    for a in arrived:
        total = total + a[...].astype(F32)
    for ks in range(total.shape[0] // req):
        rows = total[ks * req : (ks + 1) * req]
        cuts = [rows[:, w * width : (w + 1) * width] for w in range(n_wide)]
        for kw in range(n_wide):
            chosen = jnp.zeros((req, width), F32)
            for w in range(n_wide):
                cut = cuts[w]
                if not ks and not kw:
                    cut = cut + stream_ref[:, w * width : (w + 1) * width]
                chosen = jnp.where((me ^ kw) == w, cut, chosen)
            if ks or kw:
                sends[ks * n_wide + kw - 1][...] = chosen.astype(BF16)
            else:
                own_ref[...] = chosen


def split(mine, stream, arrived, n_wide, n_sub):
    req, wide = stream.shape
    width = wide // n_wide
    count = n_wide * n_sub
    return pl.pallas_call(
        functools.partial(split_kernel, n_wide, len(arrived) + 1),
        out_shape=[jax.ShapeDtypeStruct((req, width), F32)]
        + [jax.ShapeDtypeStruct((req, width), BF16)] * (count - 1),
        in_specs=[VMEM] * (2 + len(arrived)),
        out_specs=[VMEM] * count,
        compiler_params=SMALL,
        name="split",
    )(mine, stream, *arrived)


def body(
    latent_cache,
    queries,
    new_latent,
    context_len,
    block_start,
    owner,
    value_up,
    out_proj,
    residual_in,
    norm_gain,
    gate_up,
    down_weight,
):
    n_wide = lax.axis_size("wide")
    n_sub = lax.axis_size("sub")
    n_pair = lax.axis_size("pair")
    req_grp = latent_cache.shape[0]
    width_dev = residual_in.shape[1]

    powers = [k for k in range(1, n_wide) if k & (k - 1) == 0]
    arrived = {k: hop(queries, "wide", k) for k in reversed(powers)}
    payload, bias, tail, residual, order, cache, weight = prepare(
        context_len,
        block_start,
        owner,
        norm_gain,
        queries,
        latent_cache,
        new_latent,
        residual_in,
        out_proj.reshape(out_proj.shape[0] * out_proj.shape[1], D),
    )
    payloads = [payload]
    for k in range(1, n_wide):
        if k not in arrived:
            low = k & -k
            arrived[k] = hop(arrived[k - low], "wide", low)
            arrived[k], payloads[k - 1] = lax.optimization_barrier((arrived[k], payload))
            payload = payloads[k - 1]
        elif k > 1:
            arrived[k], payload = lax.optimization_barrier((arrived[k], payload))
        payload = attend(arrived[k], cache, bias, tail, payload)
        payloads.append(payload)
    chunk, early, more, held = 512, 1, 4, 4096
    units_dev = down_weight.shape[0]
    first = fetch(fetch_gate, gate_up, payload, (early, 2, chunk, units_dev), early)
    payloads[1], first = lax.optimization_barrier((payloads[1], first))
    down = fetch(fetch_down, down_weight, first, (units_dev, held), 4)
    payloads = [payloads[0]] + [hop(payloads[k], "wide", k) for k in range(1, n_wide)]
    chunks, gain = combine(order, down, payloads, req_grp, n_sub, width_dev)

    peers = [(ks, kp) for kp in range(n_pair) for ks in range(n_sub)]
    masks = [ks * n_pair + kp for ks, kp in peers]
    pieces = [chunks[0]] + [hop_group(chunks[ks], ks * n_pair + kp) for ks, kp in peers[1:]]
    keep, *sends, after = project(
        pieces, jnp.swapaxes(value_up, 1, 2), weight, gate_up, early, more, chunk
    )
    mine = keep + residual
    for k, send in zip(masks[1:], sends):
        mine = mine + hop_group(send, k).astype(F32)
    share = mine.astype(BF16)
    normed, stream = norm(mine, gain, [hop(share, "wide", k) for k in range(1, n_wide)])

    pieces = [normed] + [hop_group(normed, k) for k in masks[1:]]
    keep, send = mlp(pieces, gate_up, first, after, down_weight, down, n_pair)
    rows = n_sub * req_grp
    back = [hop(send[(k - 1) * rows : k * rows], "pair", k) for k in range(1, n_pair)]
    out, *sends = split(keep, stream, back, n_wide, n_sub)
    for ks in range(n_sub):
        for kw in range(n_wide):
            if ks or kw:
                arrived = hop_two(sends[ks * n_wide + kw - 1], ("wide", "sub"), kw * n_sub + ks)
                out = out + arrived.astype(F32)
    return out.astype(BF16)


def solution(mesh):
    in_specs = (
        P(("groups", "sub", "pair"), "wide", None),
        P(("groups", "sub", "pair"), "wide", None),
        P(("groups", "sub", "pair"), None),
        P(("groups", "sub", "pair")),
        P(("groups", "sub", "pair"), None),
        P("groups"),
        P(("wide", "sub"), None, "pair"),
        P(("wide", "sub"), "pair", None),
        P(("groups", "sub", "pair"), "wide"),
        P("wide"),
        P(None, None, ("wide", "sub", "pair")),
        P(("wide", "sub", "pair"), None),
    )
    out_specs = P(("groups", "sub", "pair"), "wide")
    return jax.shard_map(body, mesh=mesh, in_specs=in_specs, out_specs=out_specs, check_vma=False)
```

```python
import functools
import math

import jax
import jax.numpy as jnp
from jax import lax
from jax.experimental import pallas as pl
from jax.experimental.pallas import tpu as pltpu
from jax.sharding import PartitionSpec as P

D = 7168
KV_RANK = 512
ROPE = 64
NOPE = 128
F32 = jnp.float32
BF16 = jnp.bfloat16
TAIL = 8
VMEM = pl.BlockSpec(memory_space=pltpu.VMEM)
SMEM = pl.BlockSpec(memory_space=pltpu.SMEM)
ANY = pl.BlockSpec(memory_space=pl.ANY)
HBM = pl.BlockSpec(memory_space=pltpu.HBM)
SMALL = pltpu.CompilerParams(vmem_limit_bytes=4 * 2**20)


def hop(x, axis, k):
    n = lax.axis_size(axis)
    return lax.ppermute(x, axis, [(i, i ^ k) for i in range(n)])


def hop_group(x, k):
    n = lax.axis_size("sub") * lax.axis_size("pair")
    return lax.ppermute(x, ("sub", "pair"), [(i, i ^ k) for i in range(n)])


def in_hbm(x):
    return pltpu.with_memory_space_constraint(x, pltpu.HBM)


def eye(rows, cols):
    row = lax.broadcasted_iota(jnp.int32, (rows, cols), 0)
    col = lax.broadcasted_iota(jnp.int32, (rows, cols), 1)
    return (row == col).astype(BF16)


def partial_scores(q_ref, cache_ref, bias):
    req, heads, latent = q_ref.shape
    scores = [
        lax.dot_general(
            q_ref[r], cache_ref[r], (((1,), (1,)), ((), ())), preferred_element_type=F32
        )
        * (NOPE + ROPE) ** (-0.5)
        + bias[r : r + 1, :]
        for r in range(req)
    ]
    return jnp.concatenate(scores, axis=0)


def partial_sums(expo, cache_ref, heads):
    expo = expo.astype(BF16)
    sums = [
        jnp.dot(
            expo[r * heads : (r + 1) * heads],
            cache_ref[r, :, :KV_RANK],
            preferred_element_type=F32,
        )
        for r in range(cache_ref.shape[0])
    ]
    return jnp.concatenate(sums, axis=0)


def payload_tail(lse):
    rows = lse.shape[0]
    hi = lse.astype(BF16).astype(F32)
    mid = (lse - hi).astype(BF16).astype(F32)
    lo = (lse - hi - mid).astype(BF16).astype(F32)
    lane = lax.broadcasted_iota(jnp.int32, (rows, 128), 1)
    spread = jnp.where(lane == 0, hi, jnp.where(lane == 1, mid, jnp.where(lane == 2, lo, 0.0)))
    turned = lax.dot_general(
        spread.astype(BF16), eye(rows, 128), (((0,), (0,)), ((), ())), preferred_element_type=F32
    )
    return jnp.pad(turned[:TAIL], ((0, 0), (0, KV_RANK - 128)))


def prepare_kernel(
    n_wide,
    length_hbm,
    start_hbm,
    owner_hbm,
    gain_hbm,
    q_hbm,
    cache_hbm,
    fresh_hbm,
    residual_hbm,
    weight_hbm,
    out_ref,
    bias_ref,
    gain_out_ref,
    residual_out_ref,
    order_ref,
    cache_ref,
    weight_ref,
    length_ref,
    start_ref,
    owner_ref,
    gain_ref,
    q_ref,
    fresh_ref,
    residual_ref,
    sems,
):
    copies = [
        pltpu.make_async_copy(source, target, sems.at[i])
        for i, (source, target) in enumerate(
            [
                (length_hbm, length_ref),
                (start_hbm, start_ref),
                (owner_hbm, owner_ref),
                (gain_hbm, gain_ref),
                (q_hbm, q_ref),
                (cache_hbm, cache_ref),
                (fresh_hbm, fresh_ref),
                (residual_hbm, residual_ref),
                (weight_hbm, weight_ref),
            ]
        )
    ]
    for copy in copies:
        copy.start()
    for copy in copies[:4]:
        copy.wait()
    req, heads, latent = q_ref.shape
    block = cache_ref.shape[1]
    width = gain_ref.shape[0]
    me, me_sub = lax.axis_index("wide"), lax.axis_index("sub")
    group = me_sub * lax.axis_size("pair") + lax.axis_index("pair")

    owners = [owner_ref[group * req + r] for r in range(req)]
    placed = []
    for r in range(req):
        at = jnp.int32(0)
        for j in range(req):
            if j != r:
                ahead = owners[j] <= owners[r] if j < r else owners[j] < owners[r]
                at = at + jnp.where(ahead, 1, 0)
        placed.append(at)
        order_ref[r] = at

    gain_out_ref[...] = gain_ref[...].reshape(1, width).astype(F32)

    biases = []
    for r in range(req):
        following = jnp.where(
            me == n_wide - 1, length_ref[r], start_ref[r, jnp.minimum(me + 1, n_wide - 1)]
        )
        position = lax.broadcasted_iota(jnp.int32, (1, block), 1)
        biases.append(jnp.where(position < following - start_ref[r, me], 0.0, F32(-1e30)))
    bias = jnp.concatenate(biases, axis=0)
    bias_ref[...] = bias

    for copy in copies[4:-1]:
        copy.wait()
    rows = []
    for i in range(req):
        row = jnp.zeros((1, width), F32)
        for r in range(req):
            row = jnp.where(placed[r] == i, residual_ref[r : r + 1, :].astype(F32), row)
        rows.append(row)
    residual_out_ref[...] = jnp.concatenate(rows, axis=0)

    scores = partial_scores(q_ref, cache_ref, bias)
    fresh = [fresh_ref[r : r + 1, :].astype(F32) for r in range(req)]
    own = jnp.concatenate(
        [
            jnp.sum(q_ref[r].astype(F32) * fresh[r], axis=1, keepdims=True)
            * (NOPE + ROPE) ** (-0.5)
            for r in range(req)
        ],
        axis=0,
    )
    top = jnp.maximum(jnp.max(scores, axis=1, keepdims=True), own)
    expo = jnp.exp(scores - top)
    expo_own = jnp.exp(own - top)
    den = jnp.sum(expo, axis=1, keepdims=True) + expo_own
    weight_own = expo_own.astype(BF16).astype(F32)
    num = partial_sums(expo, cache_ref, heads) + jnp.concatenate(
        [weight_own[r * heads : (r + 1) * heads] * fresh[r][:, :KV_RANK] for r in range(req)],
        axis=0,
    )
    count = req * heads
    out_ref[:count, :] = (num / den).astype(BF16)
    out_ref[count:, :] = payload_tail(top + jnp.log(den)).astype(BF16)
    copies[-1].wait()


def attend_cost(req, heads, block, latent):
    return pl.CostEstimate(
        flops=2 * req * heads * block * (latent + KV_RANK),
        bytes_accessed=2 * req * (block * latent + heads * (latent + KV_RANK)),
        transcendentals=req * heads * block,
    )


def prepare(length, start, owner, gain, q, cache, fresh, residual, weight):
    req, heads, latent = q.shape
    block, width = cache.shape[1], residual.shape[1]
    n_wide = start.shape[1]
    operands = (length, start, owner, gain, q, cache, fresh, residual, weight)
    return pl.pallas_call(
        functools.partial(prepare_kernel, n_wide),
        out_shape=[
            jax.ShapeDtypeStruct((req * heads + TAIL, KV_RANK), BF16),
            jax.ShapeDtypeStruct((req, block), F32),
            jax.ShapeDtypeStruct((1, width), F32),
            jax.ShapeDtypeStruct((req, width), F32),
            jax.ShapeDtypeStruct((req,), jnp.int32),
            pltpu.VMEM(cache.shape, BF16),
            pltpu.VMEM(weight.shape, BF16),
        ],
        in_specs=[HBM] * len(operands),
        out_specs=[VMEM] * 4 + [SMEM, VMEM, VMEM],
        scratch_shapes=[
            pltpu.SMEM(length.shape, jnp.int32),
            pltpu.SMEM(start.shape, jnp.int32),
            pltpu.SMEM(owner.shape, jnp.int32),
            pltpu.VMEM(gain.shape, BF16),
            pltpu.VMEM(q.shape, BF16),
            pltpu.VMEM(fresh.shape, BF16),
            pltpu.VMEM(residual.shape, BF16),
            pltpu.SemaphoreType.DMA((len(operands),)),
        ],
        compiler_params=SMALL,
        cost_estimate=pl.CostEstimate(
            flops=2 * req * heads * block * (latent + KV_RANK),
            bytes_accessed=2 * (weight.size + cache.size + q.size),
            transcendentals=req * heads * block,
        ),
        name="prepare",
    )(*[in_hbm(x) for x in operands])


def attend_kernel(q_ref, cache_ref, bias_ref, after_ref, out_ref):
    req, heads, latent = q_ref.shape
    scores = partial_scores(q_ref, cache_ref, bias_ref[...])
    top = jnp.max(scores, axis=1, keepdims=True)
    expo = jnp.exp(scores - top)
    den = jnp.sum(expo, axis=1, keepdims=True)
    num = partial_sums(expo, cache_ref, heads)
    count = req * heads
    out_ref[:count, :] = (num / den).astype(BF16)
    out_ref[count:, :] = payload_tail(top + jnp.log(den)).astype(BF16)


def attend(q, cache, bias, after):
    req, heads, latent = q.shape
    return pl.pallas_call(
        attend_kernel,
        out_shape=jax.ShapeDtypeStruct((req * heads + TAIL, KV_RANK), BF16),
        in_specs=[VMEM] * 3 + [ANY],
        out_specs=VMEM,
        compiler_params=SMALL,
        cost_estimate=attend_cost(req, heads, cache.shape[1], latent),
        name="attend",
    )(q, cache, bias, after)


def copy_pieces(both_hbm, outs, sems, pieces, width):
    me = lax.axis_index("wide")
    copies = []
    for i, (k, start, size) in enumerate(pieces):
        at = pl.ds(pl.multiple_of((me ^ k) * width + start, 64), size)
        copies.append(pltpu.make_async_copy(both_hbm.at[:, at, :], outs[i], sems.at[i]))
    for copy in copies:
        copy.start()
    return copies


def piece_shapes(both, pieces):
    return [pltpu.VMEM((2, size, both.shape[2]), BF16) for _, _, size in pieces]


def fetch_kernel(pieces, width, both_hbm, after_ref, *refs):
    for copy in copy_pieces(both_hbm, refs[:-1], refs[-1], pieces, width):
        copy.wait()


def fetch(both, after, pieces, width):
    shapes = piece_shapes(both, pieces)
    return pl.pallas_call(
        functools.partial(fetch_kernel, pieces, width),
        out_shape=shapes,
        in_specs=[HBM, ANY],
        out_specs=[VMEM] * len(pieces),
        scratch_shapes=[pltpu.SemaphoreType.DMA((len(pieces),))],
        compiler_params=SMALL,
        cost_estimate=pl.CostEstimate(
            flops=0,
            bytes_accessed=2 * sum(math.prod(shape.shape) for shape in shapes),
            transcendentals=0,
        ),
        name="fetch",
    )(in_hbm(both), after)


def combine_kernel(n_wide, n_sub, req, order_any, after_ref, *refs):
    payloads, outs = refs[:n_wide], refs[n_wide : n_wide + n_sub]
    hold, order_ref, sem = refs[n_wide + n_sub :]
    copy = pltpu.make_async_copy(order_any, order_ref, sem)
    copy.start()
    rows = payloads[0].shape[0] - TAIL
    heads = rows // req
    heads_dev = heads // n_sub
    me_sub = lax.axis_index("sub")
    tails = [p[rows:, :].astype(F32) for p in payloads]
    lses = []
    for tail in tails:
        turned = lax.dot_general(
            eye(rows, 128),
            tail[:, :128].astype(BF16),
            (((1,), (1,)), ((), ())),
            preferred_element_type=F32,
        )
        lses.append(turned[:, 0:1] + turned[:, 1:2] + turned[:, 2:3])
    top = functools.reduce(jnp.maximum, lses)
    weights = [jnp.exp(lse - top) for lse in lses]
    inv = 1.0 / functools.reduce(jnp.add, weights)
    weights = [weight * inv for weight in weights]
    copy.wait()
    for r in range(req):
        at = slice(r * heads, (r + 1) * heads)
        attn = functools.reduce(
            jnp.add, [w[at] * p[at, :].astype(F32) for w, p in zip(weights, payloads)]
        ).astype(BF16)
        for s in range(n_sub):
            hold[s, order_ref[r]] = attn[s * heads_dev : (s + 1) * heads_dev]
    for k in range(n_sub):
        outs[k][...] = hold[me_sub ^ k]


def combine(order, after, payloads, req, n_sub):
    n_wide = len(payloads)
    heads_dev = (payloads[0].shape[0] - TAIL) // req // n_sub
    piece = jax.ShapeDtypeStruct((req, heads_dev, KV_RANK), BF16)
    return pl.pallas_call(
        functools.partial(combine_kernel, n_wide, n_sub, req),
        out_shape=[piece] * n_sub,
        in_specs=[ANY, ANY] + [VMEM] * n_wide,
        out_specs=[VMEM] * n_sub,
        scratch_shapes=[
            pltpu.VMEM((n_sub, req, heads_dev, KV_RANK), BF16),
            pltpu.SMEM(order.shape, jnp.int32),
            pltpu.SemaphoreType.DMA(()),
        ],
        compiler_params=SMALL,
        name="combine",
    )(order, after, *payloads)


def project_kernel(count, more, width, *refs):
    pieces = refs[:count]
    up_ref, weight_ref, both_hbm = refs[count : count + 3]
    vals, hold, sems = refs[-3:]
    outs, fetched = refs[count + 3 : -3 - len(more)], refs[-3 - len(more) : -3]
    copies = copy_pieces(both_hbm, fetched, sems, more, width)
    req, heads, rank = pieces[0].shape
    rows = count * req
    cols = up_ref.shape[1]
    stacked = jnp.concatenate([p[...].reshape(req * heads, rank) for p in pieces], axis=0)
    total = rows * heads
    to = lax.broadcasted_iota(jnp.int32, (total, total), 0)
    source = lax.broadcasted_iota(jnp.int32, (total, total), 1)
    turn = (to // rows == source % heads) & (to % rows == source // heads)
    turned = jnp.dot(turn.astype(BF16), stacked, preferred_element_type=F32).astype(BF16)
    for h in range(heads):
        val = lax.dot_general(
            turned[h * rows : (h + 1) * rows],
            up_ref[h],
            (((1,), (1,)), ((), ())),
            preferred_element_type=F32,
        )
        vals[:, h * cols : (h + 1) * cols] = val.astype(BF16)
    n_wide = hold.shape[0]
    for w in range(n_wide):
        hold[w] = jnp.dot(
            vals[...], weight_ref[:, w * width : (w + 1) * width], preferred_element_type=F32
        )
    me = lax.axis_index("wide")
    for k in range(n_wide):
        outs[k][...] = hold[me ^ k].astype(outs[k].dtype)
    for copy in copies:
        copy.wait()


def project(pieces, value_up, weight, gate_up, more, width):
    count = len(pieces)
    req, heads, rank = pieces[0].shape
    rows = count * req
    depth, wide = weight.shape
    n_wide = wide // width
    return pl.pallas_call(
        functools.partial(project_kernel, count, more, width),
        out_shape=[jax.ShapeDtypeStruct((rows, width), F32)]
        + [jax.ShapeDtypeStruct((rows, width), BF16)] * (n_wide - 1)
        + piece_shapes(gate_up, more),
        in_specs=[VMEM] * (count + 2) + [HBM],
        out_specs=[VMEM] * (n_wide + len(more)),
        scratch_shapes=[
            pltpu.VMEM((rows, depth), BF16),
            pltpu.VMEM((n_wide, rows, width), F32),
            pltpu.SemaphoreType.DMA((len(more),)),
        ],
        compiler_params=SMALL,
        cost_estimate=pl.CostEstimate(
            flops=2 * rows * depth * wide, bytes_accessed=2 * depth * wide, transcendentals=0
        ),
        name="project",
    )(*pieces, value_up, weight, in_hbm(gate_up))


def merge_kernel(mine_ref, residual_ref, after_ref, *refs):
    arrived, (total_ref, send_ref) = refs[:-2], refs[-2:]
    req = residual_ref.shape[0]
    total = mine_ref[...]
    for a in arrived:
        total = total + a[...].astype(F32)
    total_ref[...] = total
    total_ref[:req, :] = total[:req] + residual_ref[...]
    send_ref[...] = total_ref[...].astype(BF16)


def merge(mine, residual, after, arrived):
    return pl.pallas_call(
        merge_kernel,
        out_shape=[jax.ShapeDtypeStruct(mine.shape, F32), jax.ShapeDtypeStruct(mine.shape, BF16)],
        in_specs=[VMEM, VMEM, ANY] + [VMEM] * len(arrived),
        out_specs=[VMEM] * 2,
        compiler_params=SMALL,
        name="merge",
    )(mine, residual, after, *arrived)


def norm_kernel(req, mine_ref, gain_ref, after_ref, *refs):
    arrived, (gained_ref, stream_ref) = refs[:-2], refs[-2:]
    width = mine_ref.shape[1]
    blocks = [mine_ref[i * req : (i + 1) * req, :] for i in range(len(arrived) + 1)]
    for j, a in enumerate(arrived):
        others = a[...].astype(F32)
        for i in range(len(blocks)):
            at = (i ^ (j + 1)) * req
            blocks[i] = blocks[i] + others[at : at + req]
    stream_ref[...] = blocks[0]
    total = jnp.concatenate(blocks, axis=0)
    gained_ref[:, :width] = (total * gain_ref[...]).astype(BF16)
    square = jnp.sum(total * total, axis=1, keepdims=True)
    hi = square.astype(BF16).astype(F32)
    mid = (square - hi).astype(BF16).astype(F32)
    lo = (square - hi - mid).astype(BF16).astype(F32)
    lane = lax.broadcasted_iota(jnp.int32, (total.shape[0], 128), 1)
    spread = jnp.where(lane == 0, hi, jnp.where(lane == 1, mid, jnp.where(lane == 2, lo, 0.0)))
    gained_ref[:, width:] = spread.astype(BF16)


def norm(mine, gain, after, arrived, req):
    rows, width = mine.shape
    return pl.pallas_call(
        functools.partial(norm_kernel, req),
        out_shape=[
            jax.ShapeDtypeStruct((rows, width + 128), BF16),
            jax.ShapeDtypeStruct((req, width), F32),
        ],
        in_specs=[VMEM, VMEM, ANY] + [VMEM] * len(arrived),
        out_specs=[VMEM] * 2,
        compiler_params=SMALL,
        name="norm",
    )(mine, gain, after, *arrived)


def aligned(width):
    return width % 128 == 0


def gate_kernel(k_down, spans, width, first, x_ref, down_hbm, *refs):
    weights, refs = refs[: len(spans)], refs[len(spans) :]
    if not first:
        gates_in, square_in, refs = refs[0], refs[1], refs[2:]
    gates_ref, square_ref, down_ref, sem = refs
    me = lax.axis_index("wide")
    source = down_hbm
    if aligned(width):
        at = pl.ds(pl.multiple_of((me ^ k_down) * width, 128), width)
        source = down_hbm.at[:, at]
    copy = pltpu.make_async_copy(source, down_ref, sem)
    copy.start()
    units = weights[0].shape[2]
    full = units - 128 if units % 256 == 128 else units
    square = x_ref[:, width:].astype(F32)
    square_ref[...] = square if first else square + square_in[...]
    for i, (start, size) in enumerate(spans):
        x = x_ref[:, start : start + size]
        base = gates_ref if i or first else gates_in
        if i == 0 and first:
            gates_ref[...] = jnp.zeros_like(gates_ref)
        for g in range(2):
            gates_ref[g, :, :full] = base[g, :, :full] + jnp.dot(
                x, weights[i][g, :, :full], preferred_element_type=F32
            )
        if full < units:
            rest = jnp.concatenate([weights[i][0, :, full:], weights[i][1, :, full:]], axis=1)
            product = jnp.dot(x, rest, preferred_element_type=F32)
            for g in range(2):
                gates_ref[g, :, full:] = base[g, :, full:] + product[:, g * 128 : (g + 1) * 128]
    copy.wait()


def gate(x, weights, carry, down, k_down, spans):
    rows = x.shape[0]
    width = x.shape[1] - 128
    units, wide = down.shape
    return pl.pallas_call(
        functools.partial(gate_kernel, k_down, spans, width, not carry),
        out_shape=[
            jax.ShapeDtypeStruct((2, rows, units), F32),
            jax.ShapeDtypeStruct((rows, 128), F32),
            pltpu.VMEM((units, width if aligned(width) else wide), BF16),
        ],
        in_specs=[VMEM, HBM] + [VMEM] * (len(spans) + len(carry)),
        out_specs=[VMEM] * 3,
        scratch_shapes=[pltpu.SemaphoreType.DMA(())],
        compiler_params=SMALL,
        cost_estimate=pl.CostEstimate(
            flops=4 * rows * width * units, bytes_accessed=4 * width * units, transcendentals=0
        ),
        name="gate",
    )(x, in_hbm(down), *weights, *carry)


def down_kernel(ks, width, first, *refs):
    weights, refs = refs[: len(ks)], refs[len(ks) :]
    if first:
        gates_ref, square_ref, hidden_ref, *outs = refs
        square = square_ref[:, 0:1] + square_ref[:, 1:2] + square_ref[:, 2:3]
        inv = lax.rsqrt(square / D + 1e-06)
        g = gates_ref[0] * inv
        hidden = (g / (1.0 + jnp.exp(-g)) * (gates_ref[1] * inv)).astype(BF16)
        hidden_ref[...] = hidden
    else:
        hidden_ref, after_ref, *outs = refs
        hidden = hidden_ref[...]
    me = lax.axis_index("wide")
    for k, weight_ref, out in zip(ks, weights, outs):
        if aligned(width):
            weight = weight_ref[...]
        else:
            weight = jnp.zeros((weight_ref.shape[0], width), BF16)
            for w in range(weight_ref.shape[1] // width):
                block = weight_ref[:, w * width : (w + 1) * width]
                weight = jnp.where((me ^ k) == w, block, weight)
        out[...] = jnp.dot(hidden, weight, preferred_element_type=F32).astype(out.dtype)


def down(weights, operands, ks, width, first):
    if first:
        rows, units = operands[0].shape[1:]
    else:
        rows, units = operands[0].shape
    shapes = [jax.ShapeDtypeStruct((rows, width), BF16 if k else F32) for k in ks]
    if first:
        shapes = [jax.ShapeDtypeStruct((rows, units), BF16)] + shapes
    return pl.pallas_call(
        functools.partial(down_kernel, ks, width, first),
        out_shape=shapes,
        in_specs=[VMEM] * (len(ks) + 1) + [VMEM if first else ANY],
        out_specs=[VMEM] * len(shapes),
        compiler_params=SMALL,
        cost_estimate=pl.CostEstimate(
            flops=2 * rows * units * width * len(ks),
            bytes_accessed=2 * units * width * len(ks),
            transcendentals=0,
        ),
        name="down",
    )(*weights, *operands)


def split_kernel(mine_ref, stream_ref, *refs):
    req = stream_ref.shape[0]
    count = mine_ref.shape[0] // req
    arrived, outs = refs[:-count], refs[-count:]
    total = mine_ref[...]
    for a in arrived:
        total = total + a[...].astype(F32)
    outs[0][...] = total[:req] + stream_ref[...]
    for j in range(1, count):
        outs[j][...] = total[j * req : (j + 1) * req].astype(BF16)


def split(mine, stream, arrived):
    req, width = stream.shape
    count = mine.shape[0] // req
    return pl.pallas_call(
        split_kernel,
        out_shape=[jax.ShapeDtypeStruct((req, width), F32)]
        + [jax.ShapeDtypeStruct((req, width), BF16)] * (count - 1),
        in_specs=[VMEM] * (2 + len(arrived)),
        out_specs=[VMEM] * count,
        compiler_params=SMALL,
        name="split",
    )(mine, stream, *arrived)


def body(
    latent_cache,
    queries,
    new_latent,
    context_len,
    block_start,
    owner,
    value_up,
    out_proj,
    residual_in,
    norm_gain,
    gate_up,
    down_weight,
):
    n_wide = lax.axis_size("wide")
    n_sub = lax.axis_size("sub")
    n_pair = lax.axis_size("pair")
    req_grp = latent_cache.shape[0]
    width_dev = residual_in.shape[1]

    powers = [k for k in range(1, n_wide) if k & (k - 1) == 0]
    arrived = {k: hop(queries, "wide", k) for k in reversed(powers)}
    payload, bias, gain, residual, order, cache, weight = prepare(
        context_len,
        block_start,
        owner,
        norm_gain,
        queries,
        latent_cache,
        new_latent,
        residual_in,
        out_proj.reshape(out_proj.shape[0] * out_proj.shape[1], D),
    )
    payloads = [payload]
    for k in range(1, n_wide):
        if k not in arrived:
            low = k & -k
            arrived[k] = hop(arrived[k - low], "wide", low)
        elif k > 1:
            arrived[k], payload = lax.optimization_barrier((arrived[k], payload))
        payload = attend(arrived[k], cache, bias, payload)
        payloads.append(payload)
    spans = [(at, min(1024, width_dev - at)) for at in range(0, width_dev, 1024)]
    queue = [(k, start, size) for k in range(n_wide) for start, size in spans]
    held = list(fetch(gate_up, payload, queue[:1], width_dev))
    payloads[1], held[0] = lax.optimization_barrier((payloads[1], held[0]))
    held += fetch(gate_up, held[0], queue[1:3], width_dev)
    payloads = [payloads[0]] + [hop(payloads[k], "wide", k) for k in range(1, n_wide)]
    chunks = combine(order, held[-1], payloads, req_grp, n_sub)

    peers = [(ks, kp) for kp in range(n_pair) for ks in range(n_sub)]
    masks = [ks * n_pair + kp for ks, kp in peers]
    pieces = [chunks[0]] + [hop_group(chunks[ks], ks * n_pair + kp) for ks, kp in peers[1:]]
    out = project(pieces, jnp.swapaxes(value_up, 1, 2), weight, gate_up, queue[3:5], width_dev)
    mine, sends = out[0], out[1:n_wide]
    held += out[n_wide:]

    back = [hop(send, "wide", k + 1) for k, send in enumerate(sends)]
    held += fetch(gate_up, mine, queue[5:7], width_dev)
    total, send = merge(mine, residual, held[-1], back)
    back = [hop_group(send, k) for k in masks[1:]]
    if queue[7:]:
        held += fetch(gate_up, send, queue[7:], width_dev)
    gained, stream = norm(total, gain, held[-1], back, req_grp)

    carry, blocks = (), {}
    far = list(range(n_wide - 1, -1, -1))
    for k in range(n_wide):
        x = hop(gained, "wide", k) if k else gained
        weights = held[k * len(spans) : (k + 1) * len(spans)]
        *carry, blocks[far[k]] = gate(x, weights, carry, down_weight, far[k], spans)
    away = far[:-1]
    hidden, *sends = down([blocks[k] for k in away], carry, away, width_dev, True)
    back = [hop(send, "wide", k) for k, send in zip(away, sends)]
    (mine,) = down([blocks[0]], (hidden, sends[-1]), [0], width_dev, False)
    out, *sends = split(mine, stream, back)
    for k, send in zip(masks[1:], sends):
        out = out + hop_group(send, k).astype(F32)
    return out.astype(BF16)


def solution(mesh):
    in_specs = (
        P(("groups", "sub", "pair"), "wide", None),
        P(("groups", "sub", "pair"), "wide", None),
        P(("groups", "sub", "pair"), None),
        P(("groups", "sub", "pair")),
        P(("groups", "sub", "pair"), None),
        P("groups"),
        P(("wide", "sub"), None, "pair"),
        P(("wide", "sub"), "pair", None),
        P(("groups", "sub", "pair"), "wide"),
        P("wide"),
        P(None, None, ("wide", "sub", "pair")),
        P(("wide", "sub", "pair"), None),
    )
    out_specs = P(("groups", "sub", "pair"), "wide")
    return jax.shard_map(body, mesh=mesh, in_specs=in_specs, out_specs=out_specs, check_vma=False)
```

```python
import collections
import functools
import math

import jax
import jax.numpy as jnp
from jax import lax
from jax.experimental import pallas as pl
from jax.experimental.pallas import tpu as pltpu
from jax.sharding import PartitionSpec as P

D = 7168
KV_RANK = 512
ROPE = 64
NOPE = 128
F32 = jnp.float32
BF16 = jnp.bfloat16
TAIL = 8
VMEM = pl.BlockSpec(memory_space=pltpu.VMEM)
SMEM = pl.BlockSpec(memory_space=pltpu.SMEM)
ANY = pl.BlockSpec(memory_space=pl.ANY)
HBM = pl.BlockSpec(memory_space=pltpu.HBM)
SMALL = pltpu.CompilerParams(vmem_limit_bytes=4 * 2**20)


def hop(x, axis, k):
    n = lax.axis_size(axis)
    return lax.ppermute(x, axis, [(i, i ^ k) for i in range(n)])


def hop_group(x, k):
    n = lax.axis_size("sub") * lax.axis_size("pair")
    return lax.ppermute(x, ("sub", "pair"), [(i, i ^ k) for i in range(n)])


def in_hbm(x):
    return pltpu.with_memory_space_constraint(x, pltpu.HBM)


Plan = collections.namedtuple("Plan", ["width", "units", "full", "depth", "wide"])


def aligned(plan):
    return plan.width % 128 == 0


def item_shape(item, plan):
    kind, k = item
    cols = plan.width if aligned(plan) else plan.wide
    if kind == "out":
        return (plan.depth, cols)
    if kind == "down":
        return (plan.units, cols)
    if kind == "rest":
        return (plan.width, 2 * (plan.units - plan.full))
    return (plan.width, plan.full)


def item_copies(item, plan, source, out):
    kind, k = item
    start = (lax.axis_index("wide") ^ k) * plan.width
    if kind in ("out", "down"):
        if not aligned(plan):
            return [(source, out)]
        return [(source.at[:, pl.ds(pl.multiple_of(start, 128), plan.width)], out)]
    rows = pl.ds(pl.multiple_of(start, 64), plan.width)
    if kind == "rest":
        half = plan.units - plan.full
        return [
            (source.at[g, rows, plan.full :], out.at[:, g * half : (g + 1) * half])
            for g in range(2)
        ]
    return [(source.at[int(kind == "up"), rows, : plan.full], out)]


def start_items(items, plan, both, down, outs, sems):
    pairs = []
    for item, out in zip(items, outs):
        pairs += item_copies(item, plan, down if item[0] == "down" else both, out)
    copies = [
        pltpu.make_async_copy(source, out, sems.at[i]) for i, (source, out) in enumerate(pairs)
    ]

    @pl.when(lax.axis_index("wide") >= 0)
    def _():
        for copy in copies:
            copy.start()

    return copies


def item_shapes(items, plan):
    return [pltpu.VMEM(item_shape(item, plan), BF16) for item in items]


def item_sems(items):
    return pltpu.SemaphoreType.DMA((max(1, sum(2 if i[0] == "rest" else 1 for i in items)),))


def column_block(ref, k, plan):
    if aligned(plan):
        return ref[...]
    me = lax.axis_index("wide")
    block = ref[:, : plan.width]
    for w in range(1, plan.wide // plan.width):
        block = jnp.where((me ^ k) == w, ref[:, w * plan.width : (w + 1) * plan.width], block)
    return block


def eye(rows, cols):
    row = lax.broadcasted_iota(jnp.int32, (rows, cols), 0)
    col = lax.broadcasted_iota(jnp.int32, (rows, cols), 1)
    return (row == col).astype(BF16)


def partial_scores(q_ref, cache_ref, bias):
    req, heads, latent = q_ref.shape
    scores = [
        lax.dot_general(
            q_ref[r], cache_ref[r], (((1,), (1,)), ((), ())), preferred_element_type=F32
        )
        * (NOPE + ROPE) ** (-0.5)
        + bias[r : r + 1, :]
        for r in range(req)
    ]
    return jnp.concatenate(scores, axis=0)


def partial_sums(expo, cache_ref, heads):
    expo = expo.astype(BF16)
    sums = [
        jnp.dot(
            expo[r * heads : (r + 1) * heads],
            cache_ref[r, :, :KV_RANK],
            preferred_element_type=F32,
        )
        for r in range(cache_ref.shape[0])
    ]
    return jnp.concatenate(sums, axis=0)


def payload_tail(lse):
    rows = lse.shape[0]
    hi = lse.astype(BF16).astype(F32)
    mid = (lse - hi).astype(BF16).astype(F32)
    lo = (lse - hi - mid).astype(BF16).astype(F32)
    lane = lax.broadcasted_iota(jnp.int32, (rows, 128), 1)
    spread = jnp.where(lane == 0, hi, jnp.where(lane == 1, mid, jnp.where(lane == 2, lo, 0.0)))
    turned = lax.dot_general(
        spread.astype(BF16), eye(rows, 128), (((0,), (0,)), ((), ())), preferred_element_type=F32
    )
    return jnp.pad(turned[:TAIL], ((0, 0), (0, KV_RANK - 128)))


def prepare_kernel(
    n_wide,
    plan,
    length_hbm,
    start_hbm,
    owner_hbm,
    gain_hbm,
    q_hbm,
    cache_hbm,
    fresh_hbm,
    residual_hbm,
    weight_hbm,
    out_ref,
    bias_ref,
    gain_out_ref,
    residual_out_ref,
    order_ref,
    cache_ref,
    *refs,
):
    weight_refs = refs[:n_wide]
    length_ref, start_ref, owner_ref, gain_ref, q_ref, fresh_ref, residual_ref, sems = refs[n_wide:]
    copies = [
        pltpu.make_async_copy(source, target, sems.at[i])
        for i, (source, target) in enumerate(
            [
                (length_hbm, length_ref),
                (start_hbm, start_ref),
                (owner_hbm, owner_ref),
                (gain_hbm, gain_ref),
                (q_hbm, q_ref),
                (cache_hbm, cache_ref),
                (fresh_hbm, fresh_ref),
                (residual_hbm, residual_ref),
            ]
            + sum(
                [
                    item_copies(("out", k), plan, weight_hbm, weight_refs[k])
                    for k in range(n_wide)
                ],
                [],
            )
        )
    ]
    for copy in copies:
        copy.start()
    for copy in copies[:4]:
        copy.wait()
    req, heads, latent = q_ref.shape
    block = cache_ref.shape[1]
    width = gain_ref.shape[0]
    me, me_sub = lax.axis_index("wide"), lax.axis_index("sub")
    group = me_sub * lax.axis_size("pair") + lax.axis_index("pair")

    owners = [owner_ref[group * req + r] for r in range(req)]
    placed = []
    for r in range(req):
        at = jnp.int32(0)
        for j in range(req):
            if j != r:
                ahead = owners[j] <= owners[r] if j < r else owners[j] < owners[r]
                at = at + jnp.where(ahead, 1, 0)
        placed.append(at)
        order_ref[r] = at

    gain_out_ref[...] = gain_ref[...].reshape(1, width).astype(F32)

    biases = []
    for r in range(req):
        following = jnp.where(
            me == n_wide - 1, length_ref[r], start_ref[r, jnp.minimum(me + 1, n_wide - 1)]
        )
        position = lax.broadcasted_iota(jnp.int32, (1, block), 1)
        biases.append(jnp.where(position < following - start_ref[r, me], 0.0, F32(-1e30)))
    bias = jnp.concatenate(biases, axis=0)
    bias_ref[...] = bias

    for copy in copies[4:8]:
        copy.wait()
    rows = []
    for i in range(req):
        row = jnp.zeros((1, width), F32)
        for r in range(req):
            row = jnp.where(placed[r] == i, residual_ref[r : r + 1, :].astype(F32), row)
        rows.append(row)
    residual_out_ref[...] = jnp.concatenate(rows, axis=0)

    scores = partial_scores(q_ref, cache_ref, bias)
    fresh = [fresh_ref[r : r + 1, :].astype(F32) for r in range(req)]
    own = jnp.concatenate(
        [
            jnp.sum(q_ref[r].astype(F32) * fresh[r], axis=1, keepdims=True)
            * (NOPE + ROPE) ** (-0.5)
            for r in range(req)
        ],
        axis=0,
    )
    top = jnp.maximum(jnp.max(scores, axis=1, keepdims=True), own)
    expo = jnp.exp(scores - top)
    expo_own = jnp.exp(own - top)
    den = jnp.sum(expo, axis=1, keepdims=True) + expo_own
    weight_own = expo_own.astype(BF16).astype(F32)
    num = partial_sums(expo, cache_ref, heads) + jnp.concatenate(
        [weight_own[r * heads : (r + 1) * heads] * fresh[r][:, :KV_RANK] for r in range(req)],
        axis=0,
    )
    count = req * heads
    out_ref[:count, :] = (num / den).astype(BF16)
    out_ref[count:, :] = payload_tail(top + jnp.log(den)).astype(BF16)
    for copy in copies[8:]:
        copy.wait()


def attend_cost(req, heads, block, latent):
    return pl.CostEstimate(
        flops=2 * req * heads * block * (latent + KV_RANK),
        bytes_accessed=2 * req * (block * latent + heads * (latent + KV_RANK)),
        transcendentals=req * heads * block,
    )


def prepare(length, start, owner, gain, q, cache, fresh, residual, weight, plan):
    req, heads, latent = q.shape
    block, width = cache.shape[1], residual.shape[1]
    n_wide = start.shape[1]
    operands = (length, start, owner, gain, q, cache, fresh, residual, weight)
    return pl.pallas_call(
        functools.partial(prepare_kernel, n_wide, plan),
        out_shape=[
            jax.ShapeDtypeStruct((req * heads + TAIL, KV_RANK), BF16),
            jax.ShapeDtypeStruct((req, block), F32),
            jax.ShapeDtypeStruct((1, width), F32),
            jax.ShapeDtypeStruct((req, width), F32),
            jax.ShapeDtypeStruct((req,), jnp.int32),
            pltpu.VMEM(cache.shape, BF16),
        ]
        + item_shapes([("out", k) for k in range(n_wide)], plan),
        in_specs=[HBM] * len(operands),
        out_specs=[VMEM] * 4 + [SMEM, VMEM] + [VMEM] * n_wide,
        scratch_shapes=[
            pltpu.SMEM(length.shape, jnp.int32),
            pltpu.SMEM(start.shape, jnp.int32),
            pltpu.SMEM(owner.shape, jnp.int32),
            pltpu.VMEM(gain.shape, BF16),
            pltpu.VMEM(q.shape, BF16),
            pltpu.VMEM(fresh.shape, BF16),
            pltpu.VMEM(residual.shape, BF16),
            pltpu.SemaphoreType.DMA((len(operands) - 1 + n_wide,)),
        ],
        compiler_params=SMALL,
        cost_estimate=pl.CostEstimate(
            flops=2 * req * heads * block * (latent + KV_RANK),
            bytes_accessed=2 * (weight.size + cache.size + q.size),
            transcendentals=req * heads * block,
        ),
        name="prepare",
    )(*[in_hbm(x) for x in operands])


def attend_kernel(q_ref, cache_ref, bias_ref, after_ref, out_ref):
    req, heads, latent = q_ref.shape
    scores = partial_scores(q_ref, cache_ref, bias_ref[...])
    top = jnp.max(scores, axis=1, keepdims=True)
    expo = jnp.exp(scores - top)
    den = jnp.sum(expo, axis=1, keepdims=True)
    num = partial_sums(expo, cache_ref, heads)
    count = req * heads
    out_ref[:count, :] = (num / den).astype(BF16)
    out_ref[count:, :] = payload_tail(top + jnp.log(den)).astype(BF16)


def attend(q, cache, bias, after):
    req, heads, latent = q.shape
    return pl.pallas_call(
        attend_kernel,
        out_shape=jax.ShapeDtypeStruct((req * heads + TAIL, KV_RANK), BF16),
        in_specs=[VMEM] * 3 + [ANY],
        out_specs=VMEM,
        compiler_params=SMALL,
        cost_estimate=attend_cost(req, heads, cache.shape[1], latent),
        name="attend",
    )(q, cache, bias, after)


def fetch_kernel(items, plan, both_hbm, down_hbm, after_ref, *refs):
    for copy in start_items(items, plan, both_hbm, down_hbm, refs[:-1], refs[-1]):
        copy.wait()


def fetch(items, plan, both, down, after):
    shapes = item_shapes(items, plan)
    out = pl.pallas_call(
        functools.partial(fetch_kernel, items, plan),
        out_shape=shapes,
        in_specs=[HBM, HBM, ANY],
        out_specs=[VMEM] * len(items),
        scratch_shapes=[item_sems(items)],
        compiler_params=SMALL,
        cost_estimate=pl.CostEstimate(
            flops=0,
            bytes_accessed=2 * sum(math.prod(shape.shape) for shape in shapes),
            transcendentals=0,
        ),
        name="fetch",
    )(in_hbm(both), in_hbm(down), after)
    return dict(zip(items, out))


def combine_kernel(n_wide, n_sub, req, order_any, after_ref, *refs):
    payloads, outs = refs[:n_wide], refs[n_wide : n_wide + n_sub]
    hold, order_ref, sem = refs[n_wide + n_sub :]
    copy = pltpu.make_async_copy(order_any, order_ref, sem)
    copy.start()
    rows = payloads[0].shape[0] - TAIL
    heads = rows // req
    heads_dev = heads // n_sub
    me_sub = lax.axis_index("sub")
    tails = [p[rows:, :].astype(F32) for p in payloads]
    lses = []
    for tail in tails:
        turned = lax.dot_general(
            eye(rows, 128),
            tail[:, :128].astype(BF16),
            (((1,), (1,)), ((), ())),
            preferred_element_type=F32,
        )
        lses.append(turned[:, 0:1] + turned[:, 1:2] + turned[:, 2:3])
    top = functools.reduce(jnp.maximum, lses)
    weights = [jnp.exp(lse - top) for lse in lses]
    inv = 1.0 / functools.reduce(jnp.add, weights)
    weights = [weight * inv for weight in weights]
    copy.wait()
    for r in range(req):
        at = slice(r * heads, (r + 1) * heads)
        attn = functools.reduce(
            jnp.add, [w[at] * p[at, :].astype(F32) for w, p in zip(weights, payloads)]
        ).astype(BF16)
        for s in range(n_sub):
            hold[s, order_ref[r]] = attn[s * heads_dev : (s + 1) * heads_dev]
    for k in range(n_sub):
        outs[k][...] = hold[me_sub ^ k]


def combine(order, after, payloads, req, n_sub):
    n_wide = len(payloads)
    heads_dev = (payloads[0].shape[0] - TAIL) // req // n_sub
    piece = jax.ShapeDtypeStruct((req, heads_dev, KV_RANK), BF16)
    return pl.pallas_call(
        functools.partial(combine_kernel, n_wide, n_sub, req),
        out_shape=[piece] * n_sub,
        in_specs=[ANY, ANY] + [VMEM] * n_wide,
        out_specs=[VMEM] * n_sub,
        scratch_shapes=[
            pltpu.VMEM((n_sub, req, heads_dev, KV_RANK), BF16),
            pltpu.SMEM(order.shape, jnp.int32),
            pltpu.SemaphoreType.DMA(()),
        ],
        compiler_params=SMALL,
        name="combine",
    )(order, after, *payloads)


def project_kernel(count, items, plan, up_ref, both_hbm, down_hbm, after_ref, *refs):
    n_wide = plan.wide // plan.width
    pieces, weights, refs = refs[:count], refs[count : count + n_wide], refs[count + n_wide :]
    outs, fetched, (vals, sems) = refs[:n_wide], refs[n_wide:-2], refs[-2:]
    copies = start_items(items, plan, both_hbm, down_hbm, fetched, sems)
    req, heads, rank = pieces[0].shape
    rows = count * req
    cols = up_ref.shape[1]
    stacked = jnp.concatenate([p[...].reshape(req * heads, rank) for p in pieces], axis=0)
    total = rows * heads
    to = lax.broadcasted_iota(jnp.int32, (total, total), 0)
    source = lax.broadcasted_iota(jnp.int32, (total, total), 1)
    turn = (to // rows == source % heads) & (to % rows == source // heads)
    turned = jnp.dot(turn.astype(BF16), stacked, preferred_element_type=F32).astype(BF16)
    for h in range(heads):
        val = lax.dot_general(
            turned[h * rows : (h + 1) * rows],
            up_ref[h],
            (((1,), (1,)), ((), ())),
            preferred_element_type=F32,
        )
        vals[:, h * cols : (h + 1) * cols] = val.astype(BF16)
    for k in range(n_wide):
        out = jnp.dot(
            vals[...], column_block(weights[k], k, plan), preferred_element_type=F32
        )
        outs[k][...] = out.astype(outs[k].dtype)
    for copy in copies:
        copy.wait()


def project(pieces, value_up, weights, items, plan, both, down, after):
    count = len(pieces)
    req, heads, rank = pieces[0].shape
    rows = count * req
    n_wide = len(weights)
    out = pl.pallas_call(
        functools.partial(project_kernel, count, items, plan),
        out_shape=[jax.ShapeDtypeStruct((rows, plan.width), F32)]
        + [jax.ShapeDtypeStruct((rows, plan.width), BF16)] * (n_wide - 1)
        + item_shapes(items, plan),
        in_specs=[VMEM, HBM, HBM, ANY] + [VMEM] * (count + n_wide),
        out_specs=[VMEM] * (n_wide + len(items)),
        scratch_shapes=[pltpu.VMEM((rows, plan.depth), BF16), item_sems(items)],
        compiler_params=SMALL,
        cost_estimate=pl.CostEstimate(
            flops=2 * rows * plan.depth * plan.wide,
            bytes_accessed=2 * plan.depth * plan.wide,
            transcendentals=0,
        ),
        name="project",
    )(value_up, in_hbm(both), in_hbm(down), after, *pieces, *weights)
    return out[0], out[1:n_wide], dict(zip(items, out[n_wide:]))


def merge_kernel(mine_ref, residual_ref, after_ref, *refs):
    arrived, (total_ref, send_ref) = refs[:-2], refs[-2:]
    req = residual_ref.shape[0]
    total = mine_ref[...]
    for a in arrived:
        total = total + a[...].astype(F32)
    total_ref[...] = total
    total_ref[:req, :] = total[:req] + residual_ref[...]
    send_ref[...] = total_ref[...].astype(BF16)


def merge(mine, residual, after, arrived):
    return pl.pallas_call(
        merge_kernel,
        out_shape=[jax.ShapeDtypeStruct(mine.shape, F32), jax.ShapeDtypeStruct(mine.shape, BF16)],
        in_specs=[VMEM, VMEM, ANY] + [VMEM] * len(arrived),
        out_specs=[VMEM] * 2,
        compiler_params=SMALL,
        name="merge",
    )(mine, residual, after, *arrived)


def norm_kernel(req, mine_ref, gain_ref, after_ref, *refs):
    arrived, (gained_ref, stream_ref) = refs[:-2], refs[-2:]
    width = mine_ref.shape[1]
    blocks = [mine_ref[i * req : (i + 1) * req, :] for i in range(len(arrived) + 1)]
    for j, a in enumerate(arrived):
        others = a[...].astype(F32)
        for i in range(len(blocks)):
            at = (i ^ (j + 1)) * req
            blocks[i] = blocks[i] + others[at : at + req]
    stream_ref[...] = blocks[0]
    total = jnp.concatenate(blocks, axis=0)
    gained_ref[:, :width] = (total * gain_ref[...]).astype(BF16)
    square = jnp.sum(total * total, axis=1, keepdims=True)
    hi = square.astype(BF16).astype(F32)
    mid = (square - hi).astype(BF16).astype(F32)
    lo = (square - hi - mid).astype(BF16).astype(F32)
    lane = lax.broadcasted_iota(jnp.int32, (total.shape[0], 128), 1)
    spread = jnp.where(lane == 0, hi, jnp.where(lane == 1, mid, jnp.where(lane == 2, lo, 0.0)))
    gained_ref[:, width:] = spread.astype(BF16)


def norm(mine, gain, after, arrived, req):
    rows, width = mine.shape
    return pl.pallas_call(
        functools.partial(norm_kernel, req),
        out_shape=[
            jax.ShapeDtypeStruct((rows, width + 128), BF16),
            jax.ShapeDtypeStruct((req, width), F32),
        ],
        in_specs=[VMEM, VMEM, ANY] + [VMEM] * len(arrived),
        out_specs=[VMEM] * 2,
        compiler_params=SMALL,
        name="norm",
    )(mine, gain, after, *arrived)


def gate_kernel(count, first, items, plan, x_ref, both_hbm, down_hbm, *refs):
    weights, refs = refs[:count], refs[count:]
    carry, refs = (None, refs) if first else (refs[: count + 1], refs[count + 1 :])
    outs, fetched, sems = refs[: count + 1], refs[count + 1 : -1], refs[-1]
    copies = start_items(items, plan, both_hbm, down_hbm, fetched, sems)
    square = x_ref[:, plan.width :].astype(F32)
    outs[count][...] = square if first else square + carry[count][...]
    x = x_ref[:, : plan.width]
    for i in range(count):
        product = jnp.dot(x, weights[i][...], preferred_element_type=F32)
        outs[i][...] = product if first else product + carry[i][...]
    for copy in copies:
        copy.wait()


def gate(x, weights, carry, items, plan, both, down):
    rows = x.shape[0]
    count = len(weights)
    shapes = [jax.ShapeDtypeStruct((rows, w.shape[1]), F32) for w in weights]
    shapes += [jax.ShapeDtypeStruct((rows, 128), F32)]
    out = pl.pallas_call(
        functools.partial(gate_kernel, count, not carry, items, plan),
        out_shape=shapes + item_shapes(items, plan),
        in_specs=[VMEM, HBM, HBM] + [VMEM] * (count + len(carry)),
        out_specs=[VMEM] * (count + 1 + len(items)),
        scratch_shapes=[item_sems(items)],
        compiler_params=SMALL,
        cost_estimate=pl.CostEstimate(
            flops=4 * rows * plan.width * plan.units,
            bytes_accessed=4 * plan.width * plan.units,
            transcendentals=0,
        ),
        name="gate",
    )(x, in_hbm(both), in_hbm(down), *weights, *carry)
    return out[: count + 1], dict(zip(items, out[count + 1 :]))


def down_kernel(ks, items, plan, count, both_hbm, down_hbm, *refs):
    weights, operands, refs = refs[: len(ks)], refs[len(ks) : count], refs[count:]
    sems = refs[-1]
    outs, fetched = refs[: -1 - len(items)], refs[-1 - len(items) : -1]
    copies = start_items(items, plan, both_hbm, down_hbm, fetched, sems)
    if len(operands) > 2:
        *sums, square_ref = operands
        hidden_ref, *outs = outs
        square = square_ref[:, 0:1] + square_ref[:, 1:2] + square_ref[:, 2:3]
        inv = lax.rsqrt(square / D + 1e-06)
        both = [sums[0][...], sums[1][...]]
        if len(sums) > 2:
            half = plan.units - plan.full
            both = [
                jnp.concatenate([part, sums[2][:, g * half : (g + 1) * half]], axis=1)
                for g, part in enumerate(both)
            ]
        g = both[0] * inv
        hidden = (g / (1.0 + jnp.exp(-g)) * (both[1] * inv)).astype(BF16)
        hidden_ref[...] = hidden
    else:
        hidden = operands[0][...]
    for k, weight_ref, out in zip(ks, weights, outs):
        product = jnp.dot(hidden, column_block(weight_ref, k, plan), preferred_element_type=F32)
        out[...] = product.astype(out.dtype)
    for copy in copies:
        copy.wait()


def down(weights, operands, ks, items, plan, both, down_weight):
    rows = operands[0].shape[0]
    first = len(operands) > 2
    shapes = [jax.ShapeDtypeStruct((rows, plan.width), BF16 if k else F32) for k in ks]
    if first:
        shapes = [jax.ShapeDtypeStruct((rows, plan.units), BF16)] + shapes
    count = len(ks) + len(operands)
    out = pl.pallas_call(
        functools.partial(down_kernel, ks, items, plan, count),
        out_shape=shapes + item_shapes(items, plan),
        in_specs=[HBM, HBM] + [VMEM] * len(ks) + ([VMEM] * len(operands) if first else [VMEM, ANY]),
        out_specs=[VMEM] * (len(shapes) + len(items)),
        scratch_shapes=[item_sems(items)],
        compiler_params=SMALL,
        cost_estimate=pl.CostEstimate(
            flops=2 * rows * plan.units * plan.width * len(ks),
            bytes_accessed=2 * plan.units * plan.width * len(ks),
            transcendentals=0,
        ),
        name="down",
    )(in_hbm(both), in_hbm(down_weight), *weights, *operands)
    return out[: len(shapes)], dict(zip(items, out[len(shapes) :]))


def split_kernel(mine_ref, stream_ref, *refs):
    req = stream_ref.shape[0]
    count = mine_ref.shape[0] // req
    arrived, outs = refs[:-count], refs[-count:]
    total = mine_ref[...]
    for a in arrived:
        total = total + a[...].astype(F32)
    outs[0][...] = total[:req] + stream_ref[...]
    for j in range(1, count):
        outs[j][...] = total[j * req : (j + 1) * req].astype(BF16)


def split(mine, stream, arrived):
    req, width = stream.shape
    count = mine.shape[0] // req
    return pl.pallas_call(
        split_kernel,
        out_shape=[jax.ShapeDtypeStruct((req, width), F32)]
        + [jax.ShapeDtypeStruct((req, width), BF16)] * (count - 1),
        in_specs=[VMEM] * (2 + len(arrived)),
        out_specs=[VMEM] * count,
        compiler_params=SMALL,
        name="split",
    )(mine, stream, *arrived)


def body(
    latent_cache,
    queries,
    new_latent,
    context_len,
    block_start,
    owner,
    value_up,
    out_proj,
    residual_in,
    norm_gain,
    gate_up,
    down_weight,
):
    n_wide = lax.axis_size("wide")
    n_sub = lax.axis_size("sub")
    n_pair = lax.axis_size("pair")
    req_grp = latent_cache.shape[0]
    width_dev = residual_in.shape[1]

    powers = [k for k in range(1, n_wide) if k & (k - 1) == 0]
    arrived = {k: hop(queries, "wide", k) for k in reversed(powers)}
    units = down_weight.shape[0]
    plan = Plan(
        width=width_dev,
        units=units,
        full=units - 128 if units % 256 == 128 else units,
        depth=out_proj.shape[0] * out_proj.shape[1],
        wide=D,
    )
    payload, bias, gain, residual, order, cache, *out_blocks = prepare(
        context_len,
        block_start,
        owner,
        norm_gain,
        queries,
        latent_cache,
        new_latent,
        residual_in,
        out_proj.reshape(plan.depth, D),
        plan,
    )

    kinds = ("gate", "rest", "up") if plan.full < units else ("gate", "up")
    held = {}

    def bring(items, after):
        got = fetch(items, plan, gate_up, down_weight, after)
        held.update(got)
        return got[items[-1]]

    far = list(range(n_wide - 1, -1, -1))
    queue = [(kind, k) for k in range(n_wide) for kind in kinds] + [("down", k) for k in far]

    def take(count):
        items = queue[:count]
        del queue[:count]
        return items

    payloads = [payload]
    waited = False
    for k in range(1, n_wide):
        if k not in arrived:
            low = k & -k
            arrived[k] = hop(arrived[k - low], "wide", low)
            if not waited:
                payload = bring(take(3), payload)
                waited = True
        elif k > 1:
            arrived[k], payload = lax.optimization_barrier((arrived[k], payload))
        payload = attend(arrived[k], cache, bias, payload)
        payloads.append(payload)
    last = bring(take(1), payload)
    payloads[1], last = lax.optimization_barrier((payloads[1], last))
    last = bring(take(3), last)
    payloads = [payloads[0]] + [hop(payloads[k], "wide", k) for k in range(1, n_wide)]
    chunks = combine(order, last, payloads, req_grp, n_sub)

    peers = [(ks, kp) for kp in range(n_pair) for ks in range(n_sub)]
    masks = [ks * n_pair + kp for ks, kp in peers]
    pieces = [chunks[0]] + [hop_group(chunks[ks], ks * n_pair + kp) for ks, kp in peers[1:]]
    last = bring(take(2), chunks[0])
    mine, sends, got = project(
        pieces,
        jnp.swapaxes(value_up, 1, 2),
        out_blocks,
        take(2),
        plan,
        gate_up,
        down_weight,
        last,
    )
    held.update(got)

    back = [hop(send, "wide", k + 1) for k, send in enumerate(sends)]
    last = bring(take(len(queue) - n_wide + 1), mine)
    total, send = merge(mine, residual, last, back)
    back = [hop_group(send, k) for k in masks[1:]]
    last = bring(take(n_wide - 3), send)
    gained, stream = norm(total, gain, last, back, req_grp)

    carry = ()
    for k in range(n_wide):
        x = hop(gained, "wide", k) if k else gained
        items = take(1) if k == 0 else []
        weights = [held[item] for item in (("gate", k), ("up", k), ("rest", k)) if item in held]
        carry, got = gate(x, weights, carry, items, plan, gate_up, down_weight)
        held.update(got)
    away = far[:-1]
    weights = [held["down", k] for k in away]
    (hidden, *sends), got = down(weights, carry, away, take(1), plan, gate_up, down_weight)
    held.update(got)
    back = [hop(send, "wide", k) for k, send in zip(away, sends)]
    weights = [held["down", 0]]
    (mine,), _ = down(weights, (hidden, sends[-1]), [0], [], plan, gate_up, down_weight)
    out, *sends = split(mine, stream, back)
    for k, send in zip(masks[1:], sends):
        out = out + hop_group(send, k).astype(F32)
    return out.astype(BF16)


def solution(mesh):
    in_specs = (
        P(("groups", "sub", "pair"), "wide", None),
        P(("groups", "sub", "pair"), "wide", None),
        P(("groups", "sub", "pair"), None),
        P(("groups", "sub", "pair")),
        P(("groups", "sub", "pair"), None),
        P("groups"),
        P(("wide", "sub"), None, "pair"),
        P(("wide", "sub"), "pair", None),
        P(("groups", "sub", "pair"), "wide"),
        P("wide"),
        P(None, None, ("wide", "sub", "pair")),
        P(("wide", "sub", "pair"), None),
    )
    out_specs = P(("groups", "sub", "pair"), "wide")
    return jax.shard_map(body, mesh=mesh, in_specs=in_specs, out_specs=out_specs, check_vma=False)
```

```python
import collections
import functools
import math

import jax
import jax.numpy as jnp
from jax import lax
from jax.experimental import pallas as pl
from jax.experimental.pallas import tpu as pltpu
from jax.sharding import PartitionSpec as P

D = 7168
KV_RANK = 512
ROPE = 64
NOPE = 128
F32 = jnp.float32
BF16 = jnp.bfloat16
TAIL = 8
VMEM = pl.BlockSpec(memory_space=pltpu.VMEM)
SMEM = pl.BlockSpec(memory_space=pltpu.SMEM)
ANY = pl.BlockSpec(memory_space=pl.ANY)
HBM = pl.BlockSpec(memory_space=pltpu.HBM)
SMALL = pltpu.CompilerParams(vmem_limit_bytes=4 * 2**20)


def hop(x, axis, k):
    n = lax.axis_size(axis)
    return lax.ppermute(x, axis, [(i, i ^ k) for i in range(n)])


def hop_group(x, k):
    n = lax.axis_size("sub") * lax.axis_size("pair")
    return lax.ppermute(x, ("sub", "pair"), [(i, i ^ k) for i in range(n)])


def in_hbm(x):
    return pltpu.with_memory_space_constraint(x, pltpu.HBM)


Plan = collections.namedtuple("Plan", ["width", "units", "full", "depth", "wide"])


def aligned(plan):
    return plan.width % 128 == 0


def item_shape(item, plan):
    kind, k = item
    cols = plan.width if aligned(plan) else plan.wide
    if kind == "out":
        return (plan.depth, cols)
    if kind == "down":
        return (plan.units, cols)
    if kind == "rest":
        return (plan.width, 2 * (plan.units - plan.full))
    return (plan.width, plan.full)


def item_copies(item, plan, source, out):
    kind, k = item
    start = (lax.axis_index("wide") ^ k) * plan.width
    if kind in ("out", "down"):
        if not aligned(plan):
            return [(source, out)]
        return [(source.at[:, pl.ds(pl.multiple_of(start, 128), plan.width)], out)]
    rows = pl.ds(pl.multiple_of(start, 64), plan.width)
    if kind == "rest":
        half = plan.units - plan.full
        return [
            (source.at[g, rows, plan.full :], out.at[:, g * half : (g + 1) * half])
            for g in range(2)
        ]
    return [(source.at[int(kind == "up"), rows, : plan.full], out)]


def start_items(items, plan, both, down, outs, sems):
    pairs = []
    for item, out in zip(items, outs):
        pairs += item_copies(item, plan, down if item[0] == "down" else both, out)
    copies = [
        pltpu.make_async_copy(source, out, sems.at[i]) for i, (source, out) in enumerate(pairs)
    ]

    @pl.when(lax.axis_index("wide") >= 0)
    def _():
        for copy in copies:
            copy.start()

    return copies


def item_shapes(items, plan):
    return [pltpu.VMEM(item_shape(item, plan), BF16) for item in items]


def item_sems(items):
    return pltpu.SemaphoreType.DMA((max(1, sum(2 if i[0] == "rest" else 1 for i in items)),))


def column_block(ref, k, plan, at):
    if aligned(plan):
        return ref[:, at]
    me = lax.axis_index("wide")
    block = ref[:, : plan.width]
    for w in range(1, plan.wide // plan.width):
        block = jnp.where((me ^ k) == w, ref[:, w * plan.width : (w + 1) * plan.width], block)
    return block


def in_tiles(loop, cols, work):
    if not loop or cols % 256:
        work(pl.ds(0, cols))
        return

    @pl.loop(0, cols // 256)
    def _(i):
        work(pl.ds(pl.multiple_of(i * 256, 256), 256))


def eye(rows, cols):
    row = lax.broadcasted_iota(jnp.int32, (rows, cols), 0)
    col = lax.broadcasted_iota(jnp.int32, (rows, cols), 1)
    return (row == col).astype(BF16)


def partial_scores(q_ref, cache_ref, bias):
    req, heads, latent = q_ref.shape
    scores = [
        lax.dot_general(
            q_ref[r], cache_ref[r], (((1,), (1,)), ((), ())), preferred_element_type=F32
        )
        * (NOPE + ROPE) ** (-0.5)
        + bias[r : r + 1, :]
        for r in range(req)
    ]
    return jnp.concatenate(scores, axis=0)


def partial_sums(expo, cache_ref, heads):
    expo = expo.astype(BF16)
    sums = [
        jnp.dot(
            expo[r * heads : (r + 1) * heads],
            cache_ref[r, :, :KV_RANK],
            preferred_element_type=F32,
        )
        for r in range(cache_ref.shape[0])
    ]
    return jnp.concatenate(sums, axis=0)


def payload_tail(lse):
    rows = lse.shape[0]
    hi = lse.astype(BF16).astype(F32)
    mid = (lse - hi).astype(BF16).astype(F32)
    lo = (lse - hi - mid).astype(BF16).astype(F32)
    lane = lax.broadcasted_iota(jnp.int32, (rows, 128), 1)
    spread = jnp.where(lane == 0, hi, jnp.where(lane == 1, mid, jnp.where(lane == 2, lo, 0.0)))
    turned = lax.dot_general(
        spread.astype(BF16), eye(rows, 128), (((0,), (0,)), ((), ())), preferred_element_type=F32
    )
    return jnp.pad(turned[:TAIL], ((0, 0), (0, KV_RANK - 128)))


def prepare_kernel(
    n_wide,
    plan,
    length_hbm,
    start_hbm,
    owner_hbm,
    gain_hbm,
    q_hbm,
    cache_hbm,
    fresh_hbm,
    residual_hbm,
    weight_hbm,
    out_ref,
    bias_ref,
    gain_out_ref,
    residual_out_ref,
    order_ref,
    cache_ref,
    *refs,
):
    weight_refs = refs[:n_wide]
    length_ref, start_ref, owner_ref, gain_ref, q_ref, fresh_ref, residual_ref, sems = refs[n_wide:]
    copies = [
        pltpu.make_async_copy(source, target, sems.at[i])
        for i, (source, target) in enumerate(
            [
                (length_hbm, length_ref),
                (start_hbm, start_ref),
                (owner_hbm, owner_ref),
                (gain_hbm, gain_ref),
                (q_hbm, q_ref),
                (cache_hbm, cache_ref),
                (fresh_hbm, fresh_ref),
                (residual_hbm, residual_ref),
            ]
            + sum(
                [
                    item_copies(("out", k), plan, weight_hbm, weight_refs[k])
                    for k in range(n_wide)
                ],
                [],
            )
        )
    ]
    for copy in copies:
        copy.start()
    for copy in copies[:4]:
        copy.wait()
    req, heads, latent = q_ref.shape
    block = cache_ref.shape[1]
    width = gain_ref.shape[0]
    me, me_sub = lax.axis_index("wide"), lax.axis_index("sub")
    group = me_sub * lax.axis_size("pair") + lax.axis_index("pair")

    owners = [owner_ref[group * req + r] for r in range(req)]
    placed = []
    for r in range(req):
        at = jnp.int32(0)
        for j in range(req):
            if j != r:
                ahead = owners[j] <= owners[r] if j < r else owners[j] < owners[r]
                at = at + jnp.where(ahead, 1, 0)
        placed.append(at)
        order_ref[r] = at

    gain_out_ref[...] = gain_ref[...].reshape(1, width).astype(F32)

    biases = []
    for r in range(req):
        following = jnp.where(
            me == n_wide - 1, length_ref[r], start_ref[r, jnp.minimum(me + 1, n_wide - 1)]
        )
        position = lax.broadcasted_iota(jnp.int32, (1, block), 1)
        biases.append(jnp.where(position < following - start_ref[r, me], 0.0, F32(-1e30)))
    bias = jnp.concatenate(biases, axis=0)
    bias_ref[...] = bias

    for copy in copies[4:8]:
        copy.wait()
    rows = []
    for i in range(req):
        row = jnp.zeros((1, width), F32)
        for r in range(req):
            row = jnp.where(placed[r] == i, residual_ref[r : r + 1, :].astype(F32), row)
        rows.append(row)
    residual_out_ref[...] = jnp.concatenate(rows, axis=0)

    scores = partial_scores(q_ref, cache_ref, bias)
    fresh = [fresh_ref[r : r + 1, :].astype(F32) for r in range(req)]
    own = jnp.concatenate(
        [
            jnp.sum(q_ref[r].astype(F32) * fresh[r], axis=1, keepdims=True)
            * (NOPE + ROPE) ** (-0.5)
            for r in range(req)
        ],
        axis=0,
    )
    top = jnp.maximum(jnp.max(scores, axis=1, keepdims=True), own)
    expo = jnp.exp(scores - top)
    expo_own = jnp.exp(own - top)
    den = jnp.sum(expo, axis=1, keepdims=True) + expo_own
    weight_own = expo_own.astype(BF16).astype(F32)
    num = partial_sums(expo, cache_ref, heads) + jnp.concatenate(
        [weight_own[r * heads : (r + 1) * heads] * fresh[r][:, :KV_RANK] for r in range(req)],
        axis=0,
    )
    count = req * heads
    out_ref[:count, :] = (num / den).astype(BF16)
    out_ref[count:, :] = payload_tail(top + jnp.log(den)).astype(BF16)
    for copy in copies[8:]:
        copy.wait()


def attend_cost(req, heads, block, latent):
    return pl.CostEstimate(
        flops=2 * req * heads * block * (latent + KV_RANK),
        bytes_accessed=2 * req * (block * latent + heads * (latent + KV_RANK)),
        transcendentals=req * heads * block,
    )


def prepare(length, start, owner, gain, q, cache, fresh, residual, weight, plan):
    req, heads, latent = q.shape
    block, width = cache.shape[1], residual.shape[1]
    n_wide = start.shape[1]
    operands = (length, start, owner, gain, q, cache, fresh, residual, weight)
    return pl.pallas_call(
        functools.partial(prepare_kernel, n_wide, plan),
        out_shape=[
            jax.ShapeDtypeStruct((req * heads + TAIL, KV_RANK), BF16),
            jax.ShapeDtypeStruct((req, block), F32),
            jax.ShapeDtypeStruct((1, width), F32),
            jax.ShapeDtypeStruct((req, width), F32),
            jax.ShapeDtypeStruct((req,), jnp.int32),
            pltpu.VMEM(cache.shape, BF16),
        ]
        + item_shapes([("out", k) for k in range(n_wide)], plan),
        in_specs=[HBM] * len(operands),
        out_specs=[VMEM] * 4 + [SMEM, VMEM] + [VMEM] * n_wide,
        scratch_shapes=[
            pltpu.SMEM(length.shape, jnp.int32),
            pltpu.SMEM(start.shape, jnp.int32),
            pltpu.SMEM(owner.shape, jnp.int32),
            pltpu.VMEM(gain.shape, BF16),
            pltpu.VMEM(q.shape, BF16),
            pltpu.VMEM(fresh.shape, BF16),
            pltpu.VMEM(residual.shape, BF16),
            pltpu.SemaphoreType.DMA((len(operands) - 1 + n_wide,)),
        ],
        compiler_params=SMALL,
        cost_estimate=pl.CostEstimate(
            flops=2 * req * heads * block * (latent + KV_RANK),
            bytes_accessed=2 * (weight.size + cache.size + q.size),
            transcendentals=req * heads * block,
        ),
        name="prepare",
    )(*[in_hbm(x) for x in operands])


def attend_kernel(q_ref, cache_ref, bias_ref, after_ref, out_ref):
    req, heads, latent = q_ref.shape
    scores = partial_scores(q_ref, cache_ref, bias_ref[...])
    top = jnp.max(scores, axis=1, keepdims=True)
    expo = jnp.exp(scores - top)
    den = jnp.sum(expo, axis=1, keepdims=True)
    num = partial_sums(expo, cache_ref, heads)
    count = req * heads
    out_ref[:count, :] = (num / den).astype(BF16)
    out_ref[count:, :] = payload_tail(top + jnp.log(den)).astype(BF16)


def attend(q, cache, bias, after):
    req, heads, latent = q.shape
    return pl.pallas_call(
        attend_kernel,
        out_shape=jax.ShapeDtypeStruct((req * heads + TAIL, KV_RANK), BF16),
        in_specs=[VMEM] * 3 + [ANY],
        out_specs=VMEM,
        compiler_params=SMALL,
        cost_estimate=attend_cost(req, heads, cache.shape[1], latent),
        name="attend",
    )(q, cache, bias, after)


def fetch_kernel(items, plan, both_hbm, down_hbm, after_ref, *refs):
    for copy in start_items(items, plan, both_hbm, down_hbm, refs[:-1], refs[-1]):
        copy.wait()


def fetch(items, plan, both, down, after):
    shapes = item_shapes(items, plan)
    out = pl.pallas_call(
        functools.partial(fetch_kernel, items, plan),
        out_shape=shapes,
        in_specs=[HBM, HBM, ANY],
        out_specs=[VMEM] * len(items),
        scratch_shapes=[item_sems(items)],
        compiler_params=SMALL,
        cost_estimate=pl.CostEstimate(
            flops=0,
            bytes_accessed=2 * sum(math.prod(shape.shape) for shape in shapes),
            transcendentals=0,
        ),
        name="fetch",
    )(in_hbm(both), in_hbm(down), after)
    return dict(zip(items, out))


def combine_kernel(n_wide, n_sub, req, order_any, after_ref, *refs):
    payloads, outs = refs[:n_wide], refs[n_wide : n_wide + n_sub]
    hold, order_ref, sem = refs[n_wide + n_sub :]
    copy = pltpu.make_async_copy(order_any, order_ref, sem)
    copy.start()
    rows = payloads[0].shape[0] - TAIL
    heads = rows // req
    heads_dev = heads // n_sub
    me_sub = lax.axis_index("sub")
    tails = [p[rows:, :].astype(F32) for p in payloads]
    lses = []
    for tail in tails:
        turned = lax.dot_general(
            eye(rows, 128),
            tail[:, :128].astype(BF16),
            (((1,), (1,)), ((), ())),
            preferred_element_type=F32,
        )
        lses.append(turned[:, 0:1] + turned[:, 1:2] + turned[:, 2:3])
    top = functools.reduce(jnp.maximum, lses)
    weights = [jnp.exp(lse - top) for lse in lses]
    inv = 1.0 / functools.reduce(jnp.add, weights)
    weights = [weight * inv for weight in weights]
    copy.wait()
    for r in range(req):
        at = slice(r * heads, (r + 1) * heads)
        attn = functools.reduce(
            jnp.add, [w[at] * p[at, :].astype(F32) for w, p in zip(weights, payloads)]
        ).astype(BF16)
        for s in range(n_sub):
            hold[s, order_ref[r]] = attn[s * heads_dev : (s + 1) * heads_dev]
    for k in range(n_sub):
        outs[k][...] = hold[me_sub ^ k]


def combine(order, after, payloads, req, n_sub):
    n_wide = len(payloads)
    heads_dev = (payloads[0].shape[0] - TAIL) // req // n_sub
    piece = jax.ShapeDtypeStruct((req, heads_dev, KV_RANK), BF16)
    return pl.pallas_call(
        functools.partial(combine_kernel, n_wide, n_sub, req),
        out_shape=[piece] * n_sub,
        in_specs=[ANY, ANY] + [VMEM] * n_wide,
        out_specs=[VMEM] * n_sub,
        scratch_shapes=[
            pltpu.VMEM((n_sub, req, heads_dev, KV_RANK), BF16),
            pltpu.SMEM(order.shape, jnp.int32),
            pltpu.SemaphoreType.DMA(()),
        ],
        compiler_params=SMALL,
        name="combine",
    )(order, after, *payloads)


def project_kernel(count, items, plan, up_ref, both_hbm, down_hbm, after_ref, *refs):
    n_wide = plan.wide // plan.width
    pieces, weights, refs = refs[:count], refs[count : count + n_wide], refs[count + n_wide :]
    outs, fetched, (vals, sems) = refs[:n_wide], refs[n_wide:-2], refs[-2:]
    copies = start_items(items, plan, both_hbm, down_hbm, fetched, sems)
    req, heads, rank = pieces[0].shape
    rows = count * req
    cols = up_ref.shape[1]
    stacked = jnp.concatenate([p[...].reshape(req * heads, rank) for p in pieces], axis=0)
    total = rows * heads
    to = lax.broadcasted_iota(jnp.int32, (total, total), 0)
    source = lax.broadcasted_iota(jnp.int32, (total, total), 1)
    turn = (to // rows == source % heads) & (to % rows == source // heads)
    turned = jnp.dot(turn.astype(BF16), stacked, preferred_element_type=F32).astype(BF16)
    for h in range(heads):
        val = lax.dot_general(
            turned[h * rows : (h + 1) * rows],
            up_ref[h],
            (((1,), (1,)), ((), ())),
            preferred_element_type=F32,
        )
        vals[:, h * cols : (h + 1) * cols] = val.astype(BF16)

    def work(at):
        for k in range(n_wide):
            block = column_block(weights[k], k, plan, at)
            out = jnp.dot(vals[...], block, preferred_element_type=F32)
            outs[k][:, at] = out.astype(outs[k].dtype)

    in_tiles(items, plan.width, work)
    for copy in copies:
        copy.wait()


def project(pieces, value_up, weights, items, plan, both, down, after):
    count = len(pieces)
    req, heads, rank = pieces[0].shape
    rows = count * req
    n_wide = len(weights)
    out = pl.pallas_call(
        functools.partial(project_kernel, count, items, plan),
        out_shape=[jax.ShapeDtypeStruct((rows, plan.width), F32)]
        + [jax.ShapeDtypeStruct((rows, plan.width), BF16)] * (n_wide - 1)
        + item_shapes(items, plan),
        in_specs=[VMEM, HBM, HBM, ANY] + [VMEM] * (count + n_wide),
        out_specs=[VMEM] * (n_wide + len(items)),
        scratch_shapes=[pltpu.VMEM((rows, plan.depth), BF16), item_sems(items)],
        compiler_params=SMALL,
        cost_estimate=pl.CostEstimate(
            flops=2 * rows * plan.depth * plan.wide,
            bytes_accessed=2 * plan.depth * plan.wide,
            transcendentals=0,
        ),
        name="project",
    )(value_up, in_hbm(both), in_hbm(down), after, *pieces, *weights)
    return out[0], out[1:n_wide], dict(zip(items, out[n_wide:]))


def merge_kernel(mine_ref, residual_ref, after_ref, *refs):
    arrived, (total_ref, send_ref) = refs[:-2], refs[-2:]
    req = residual_ref.shape[0]
    total = mine_ref[...]
    for a in arrived:
        total = total + a[...].astype(F32)
    total_ref[...] = total
    total_ref[:req, :] = total[:req] + residual_ref[...]
    send_ref[...] = total_ref[...].astype(BF16)


def merge(mine, residual, after, arrived):
    return pl.pallas_call(
        merge_kernel,
        out_shape=[jax.ShapeDtypeStruct(mine.shape, F32), jax.ShapeDtypeStruct(mine.shape, BF16)],
        in_specs=[VMEM, VMEM, ANY] + [VMEM] * len(arrived),
        out_specs=[VMEM] * 2,
        compiler_params=SMALL,
        name="merge",
    )(mine, residual, after, *arrived)


def norm_kernel(req, mine_ref, gain_ref, after_ref, *refs):
    arrived, (gained_ref, stream_ref) = refs[:-2], refs[-2:]
    width = mine_ref.shape[1]
    blocks = [mine_ref[i * req : (i + 1) * req, :] for i in range(len(arrived) + 1)]
    for j, a in enumerate(arrived):
        others = a[...].astype(F32)
        for i in range(len(blocks)):
            at = (i ^ (j + 1)) * req
            blocks[i] = blocks[i] + others[at : at + req]
    stream_ref[...] = blocks[0]
    total = jnp.concatenate(blocks, axis=0)
    gained_ref[:, :width] = (total * gain_ref[...]).astype(BF16)
    square = jnp.sum(total * total, axis=1, keepdims=True)
    hi = square.astype(BF16).astype(F32)
    mid = (square - hi).astype(BF16).astype(F32)
    lo = (square - hi - mid).astype(BF16).astype(F32)
    lane = lax.broadcasted_iota(jnp.int32, (total.shape[0], 128), 1)
    spread = jnp.where(lane == 0, hi, jnp.where(lane == 1, mid, jnp.where(lane == 2, lo, 0.0)))
    gained_ref[:, width:] = spread.astype(BF16)


def norm(mine, gain, after, arrived, req):
    rows, width = mine.shape
    return pl.pallas_call(
        functools.partial(norm_kernel, req),
        out_shape=[
            jax.ShapeDtypeStruct((rows, width + 128), BF16),
            jax.ShapeDtypeStruct((req, width), F32),
        ],
        in_specs=[VMEM, VMEM, ANY] + [VMEM] * len(arrived),
        out_specs=[VMEM] * 2,
        compiler_params=SMALL,
        name="norm",
    )(mine, gain, after, *arrived)


def gate_kernel(count, first, items, plan, x_ref, both_hbm, down_hbm, *refs):
    weights, refs = refs[:count], refs[count:]
    carry, refs = (None, refs) if first else (refs[: count + 1], refs[count + 1 :])
    outs, fetched, sems = refs[: count + 1], refs[count + 1 : -1], refs[-1]
    copies = start_items(items, plan, both_hbm, down_hbm, fetched, sems)
    square = x_ref[:, plan.width :].astype(F32)
    outs[count][...] = square if first else square + carry[count][...]
    x = x_ref[:, : plan.width]

    def multiply(i, at):
        product = jnp.dot(x, weights[i][:, at], preferred_element_type=F32)
        outs[i][:, at] = product if first else product + carry[i][:, at]

    def work(at):
        multiply(0, at)
        multiply(1, at)

    in_tiles(items, plan.full, work)
    for i in range(2, count):
        multiply(i, pl.ds(0, weights[i].shape[1]))
    for copy in copies:
        copy.wait()


def gate(x, weights, carry, items, plan, both, down):
    rows = x.shape[0]
    count = len(weights)
    shapes = [jax.ShapeDtypeStruct((rows, w.shape[1]), F32) for w in weights]
    shapes += [jax.ShapeDtypeStruct((rows, 128), F32)]
    out = pl.pallas_call(
        functools.partial(gate_kernel, count, not carry, items, plan),
        out_shape=shapes + item_shapes(items, plan),
        in_specs=[VMEM, HBM, HBM] + [VMEM] * (count + len(carry)),
        out_specs=[VMEM] * (count + 1 + len(items)),
        scratch_shapes=[item_sems(items)],
        compiler_params=SMALL,
        cost_estimate=pl.CostEstimate(
            flops=4 * rows * plan.width * plan.units,
            bytes_accessed=4 * plan.width * plan.units,
            transcendentals=0,
        ),
        name="gate",
    )(x, in_hbm(both), in_hbm(down), *weights, *carry)
    return out[: count + 1], dict(zip(items, out[count + 1 :]))


def down_kernel(ks, items, plan, count, both_hbm, down_hbm, *refs):
    weights, operands, refs = refs[: len(ks)], refs[len(ks) : count], refs[count:]
    sems = refs[-1]
    outs, fetched = refs[: -1 - len(items)], refs[-1 - len(items) : -1]
    copies = start_items(items, plan, both_hbm, down_hbm, fetched, sems)
    if len(operands) > 2:
        *sums, square_ref = operands
        hidden_ref, *outs = outs
        square = square_ref[:, 0:1] + square_ref[:, 1:2] + square_ref[:, 2:3]
        inv = lax.rsqrt(square / D + 1e-06)
        both = [sums[0][...], sums[1][...]]
        if len(sums) > 2:
            half = plan.units - plan.full
            both = [
                jnp.concatenate([part, sums[2][:, g * half : (g + 1) * half]], axis=1)
                for g, part in enumerate(both)
            ]
        g = both[0] * inv
        hidden = (g / (1.0 + jnp.exp(-g)) * (both[1] * inv)).astype(BF16)
        hidden_ref[...] = hidden
    else:
        hidden = operands[0][...]

    def work(at):
        for k, weight_ref, out in zip(ks, weights, outs):
            block = column_block(weight_ref, k, plan, at)
            out[:, at] = jnp.dot(hidden, block, preferred_element_type=F32).astype(out.dtype)

    in_tiles(items, plan.width, work)
    for copy in copies:
        copy.wait()


def down(weights, operands, ks, items, plan, both, down_weight):
    rows = operands[0].shape[0]
    first = len(operands) > 2
    shapes = [jax.ShapeDtypeStruct((rows, plan.width), BF16 if k else F32) for k in ks]
    if first:
        shapes = [jax.ShapeDtypeStruct((rows, plan.units), BF16)] + shapes
    count = len(ks) + len(operands)
    out = pl.pallas_call(
        functools.partial(down_kernel, ks, items, plan, count),
        out_shape=shapes + item_shapes(items, plan),
        in_specs=[HBM, HBM] + [VMEM] * len(ks) + ([VMEM] * len(operands) if first else [VMEM, ANY]),
        out_specs=[VMEM] * (len(shapes) + len(items)),
        scratch_shapes=[item_sems(items)],
        compiler_params=SMALL,
        cost_estimate=pl.CostEstimate(
            flops=2 * rows * plan.units * plan.width * len(ks),
            bytes_accessed=2 * plan.units * plan.width * len(ks),
            transcendentals=0,
        ),
        name="down",
    )(in_hbm(both), in_hbm(down_weight), *weights, *operands)
    return out[: len(shapes)], dict(zip(items, out[len(shapes) :]))


def split_kernel(mine_ref, stream_ref, *refs):
    req = stream_ref.shape[0]
    count = mine_ref.shape[0] // req
    arrived, outs = refs[:-count], refs[-count:]
    total = mine_ref[...]
    for a in arrived:
        total = total + a[...].astype(F32)
    outs[0][...] = total[:req] + stream_ref[...]
    for j in range(1, count):
        outs[j][...] = total[j * req : (j + 1) * req].astype(BF16)


def split(mine, stream, arrived):
    req, width = stream.shape
    count = mine.shape[0] // req
    return pl.pallas_call(
        split_kernel,
        out_shape=[jax.ShapeDtypeStruct((req, width), F32)]
        + [jax.ShapeDtypeStruct((req, width), BF16)] * (count - 1),
        in_specs=[VMEM] * (2 + len(arrived)),
        out_specs=[VMEM] * count,
        compiler_params=SMALL,
        name="split",
    )(mine, stream, *arrived)


def body(
    latent_cache,
    queries,
    new_latent,
    context_len,
    block_start,
    owner,
    value_up,
    out_proj,
    residual_in,
    norm_gain,
    gate_up,
    down_weight,
):
    n_wide = lax.axis_size("wide")
    n_sub = lax.axis_size("sub")
    n_pair = lax.axis_size("pair")
    req_grp = latent_cache.shape[0]
    width_dev = residual_in.shape[1]

    powers = [k for k in range(1, n_wide) if k & (k - 1) == 0]
    arrived = {k: hop(queries, "wide", k) for k in reversed(powers)}
    units = down_weight.shape[0]
    plan = Plan(
        width=width_dev,
        units=units,
        full=units - 128 if units % 256 == 128 else units,
        depth=out_proj.shape[0] * out_proj.shape[1],
        wide=D,
    )
    payload, bias, gain, residual, order, cache, *out_blocks = prepare(
        context_len,
        block_start,
        owner,
        norm_gain,
        queries,
        latent_cache,
        new_latent,
        residual_in,
        out_proj.reshape(plan.depth, D),
        plan,
    )

    kinds = ("gate", "rest", "up") if plan.full < units else ("gate", "up")
    held = {}

    def bring(items, after):
        got = fetch(items, plan, gate_up, down_weight, after)
        held.update(got)
        return got[items[-1]]

    far = list(range(n_wide - 1, -1, -1))
    queue = [(kind, k) for k in range(n_wide) for kind in kinds] + [("down", k) for k in far]

    def take(count):
        items = queue[:count]
        del queue[:count]
        return items

    payloads = [payload]
    waited = False
    for k in range(1, n_wide):
        if k not in arrived:
            low = k & -k
            arrived[k] = hop(arrived[k - low], "wide", low)
            if not waited:
                payload = bring(take(3), payload)
                waited = True
        elif k > 1:
            arrived[k], payload = lax.optimization_barrier((arrived[k], payload))
        payload = attend(arrived[k], cache, bias, payload)
        payloads.append(payload)
    last = bring(take(1), payload)
    payloads[1], last = lax.optimization_barrier((payloads[1], last))
    last = bring(take(3), last)
    payloads = [payloads[0]] + [hop(payloads[k], "wide", k) for k in range(1, n_wide)]
    chunks = combine(order, last, payloads, req_grp, n_sub)

    peers = [(ks, kp) for kp in range(n_pair) for ks in range(n_sub)]
    masks = [ks * n_pair + kp for ks, kp in peers]
    pieces = [chunks[0]] + [hop_group(chunks[ks], ks * n_pair + kp) for ks, kp in peers[1:]]
    last = bring(take(2), chunks[0])
    mine, sends, got = project(
        pieces,
        jnp.swapaxes(value_up, 1, 2),
        out_blocks,
        take(2),
        plan,
        gate_up,
        down_weight,
        last,
    )
    held.update(got)

    back = [hop(send, "wide", k + 1) for k, send in enumerate(sends)]
    last = bring(take(len(queue) - n_wide + 1), mine)
    total, send = merge(mine, residual, last, back)
    back = [hop_group(send, k) for k in masks[1:]]
    last = bring(take(n_wide - 3), send)
    gained, stream = norm(total, gain, last, back, req_grp)

    carry = ()
    for k in range(n_wide):
        x = hop(gained, "wide", k) if k else gained
        items = take(1) if k == 0 else []
        weights = [held[item] for item in (("gate", k), ("up", k), ("rest", k)) if item in held]
        carry, got = gate(x, weights, carry, items, plan, gate_up, down_weight)
        held.update(got)
    away = far[:-1]
    weights = [held["down", k] for k in away]
    (hidden, *sends), got = down(weights, carry, away, take(1), plan, gate_up, down_weight)
    held.update(got)
    back = [hop(send, "wide", k) for k, send in zip(away, sends)]
    weights = [held["down", 0]]
    (mine,), _ = down(weights, (hidden, sends[-1]), [0], [], plan, gate_up, down_weight)
    out, *sends = split(mine, stream, back)
    for k, send in zip(masks[1:], sends):
        out = out + hop_group(send, k).astype(F32)
    return out.astype(BF16)


def solution(mesh):
    in_specs = (
        P(("groups", "sub", "pair"), "wide", None),
        P(("groups", "sub", "pair"), "wide", None),
        P(("groups", "sub", "pair"), None),
        P(("groups", "sub", "pair")),
        P(("groups", "sub", "pair"), None),
        P("groups"),
        P(("wide", "sub"), None, "pair"),
        P(("wide", "sub"), "pair", None),
        P(("groups", "sub", "pair"), "wide"),
        P("wide"),
        P(None, None, ("wide", "sub", "pair")),
        P(("wide", "sub", "pair"), None),
    )
    out_specs = P(("groups", "sub", "pair"), "wide")
    return jax.shard_map(body, mesh=mesh, in_specs=in_specs, out_specs=out_specs, check_vma=False)
```

```python
import collections
import functools
import math

import jax
import jax.numpy as jnp
from jax import lax
from jax.experimental import pallas as pl
from jax.experimental.pallas import tpu as pltpu
from jax.sharding import PartitionSpec as P

D = 7168
KV_RANK = 512
ROPE = 64
NOPE = 128
F32 = jnp.float32
BF16 = jnp.bfloat16
TAIL = 8
VMEM = pl.BlockSpec(memory_space=pltpu.VMEM)
SMEM = pl.BlockSpec(memory_space=pltpu.SMEM)
ANY = pl.BlockSpec(memory_space=pl.ANY)
HBM = pl.BlockSpec(memory_space=pltpu.HBM)
SMALL = pltpu.CompilerParams(vmem_limit_bytes=4 * 2**20)


def hop(x, axis, k):
    n = lax.axis_size(axis)
    return lax.ppermute(x, axis, [(i, i ^ k) for i in range(n)])


def in_hbm(x):
    return pltpu.with_memory_space_constraint(x, pltpu.HBM)


Plan = collections.namedtuple("Plan", ["width", "units", "full", "depth", "wide"])


def aligned(plan):
    return plan.width % 128 == 0


def item_shape(item, plan):
    kind, k = item
    cols = plan.width if aligned(plan) else plan.wide
    if kind == "out":
        return (plan.depth, cols)
    if kind == "down":
        return (plan.units, cols)
    if kind == "rest":
        return (plan.width, 2 * (plan.units - plan.full))
    return (plan.width, plan.full)


def item_copies(item, plan, source, out):
    kind, k = item
    start = (lax.axis_index("wide") ^ k) * plan.width
    if kind in ("out", "down"):
        if not aligned(plan):
            return [(source, out)]
        return [(source.at[:, pl.ds(pl.multiple_of(start, 128), plan.width)], out)]
    rows = pl.ds(pl.multiple_of(start, 64), plan.width)
    if kind == "rest":
        half = plan.units - plan.full
        return [
            (source.at[g, rows, plan.full :], out.at[:, g * half : (g + 1) * half])
            for g in range(2)
        ]
    return [(source.at[int(kind == "up"), rows, : plan.full], out)]


def start_items(items, plan, both, down, outs, sems):
    pairs = []
    for item, out in zip(items, outs):
        pairs += item_copies(item, plan, down if item[0] == "down" else both, out)
    copies = [
        pltpu.make_async_copy(source, out, sems.at[i]) for i, (source, out) in enumerate(pairs)
    ]

    @pl.when(lax.axis_index("wide") >= 0)
    def _():
        for copy in copies:
            copy.start()

    return copies


def item_shapes(items, plan):
    return [pltpu.VMEM(item_shape(item, plan), BF16) for item in items]


def item_sems(items):
    return pltpu.SemaphoreType.DMA((max(1, sum(2 if i[0] == "rest" else 1 for i in items)),))


def column_block(ref, k, plan, at):
    if aligned(plan):
        return ref[:, at]
    me = lax.axis_index("wide")
    block = ref[:, : plan.width]
    for w in range(1, plan.wide // plan.width):
        block = jnp.where((me ^ k) == w, ref[:, w * plan.width : (w + 1) * plan.width], block)
    return block


def in_tiles(loop, cols, work):
    if not loop or cols % 256:
        work(pl.ds(0, cols))
        return

    @pl.loop(0, cols // 256)
    def _(i):
        work(pl.ds(pl.multiple_of(i * 256, 256), 256))


def eye(rows, cols):
    row = lax.broadcasted_iota(jnp.int32, (rows, cols), 0)
    col = lax.broadcasted_iota(jnp.int32, (rows, cols), 1)
    return (row == col).astype(BF16)


def partial_scores(q_ref, cache_ref, bias):
    req, heads, latent = q_ref.shape
    scores = [
        lax.dot_general(
            q_ref[r], cache_ref[r], (((1,), (1,)), ((), ())), preferred_element_type=F32
        )
        * (NOPE + ROPE) ** (-0.5)
        + bias[r : r + 1, :]
        for r in range(req)
    ]
    return jnp.concatenate(scores, axis=0)


def partial_sums(expo, cache_ref, heads):
    expo = expo.astype(BF16)
    sums = [
        jnp.dot(
            expo[r * heads : (r + 1) * heads],
            cache_ref[r, :, :KV_RANK],
            preferred_element_type=F32,
        )
        for r in range(cache_ref.shape[0])
    ]
    return jnp.concatenate(sums, axis=0)


def payload_tail(lse):
    rows = lse.shape[0]
    hi = lse.astype(BF16).astype(F32)
    mid = (lse - hi).astype(BF16).astype(F32)
    lo = (lse - hi - mid).astype(BF16).astype(F32)
    lane = lax.broadcasted_iota(jnp.int32, (rows, 128), 1)
    spread = jnp.where(lane == 0, hi, jnp.where(lane == 1, mid, jnp.where(lane == 2, lo, 0.0)))
    turned = lax.dot_general(
        spread.astype(BF16), eye(rows, 128), (((0,), (0,)), ((), ())), preferred_element_type=F32
    )
    return jnp.pad(turned[:TAIL], ((0, 0), (0, KV_RANK - 128)))


def prepare_kernel(
    n_wide,
    plan,
    length_hbm,
    start_hbm,
    owner_hbm,
    gain_hbm,
    q_hbm,
    cache_hbm,
    fresh_hbm,
    residual_hbm,
    weight_hbm,
    out_ref,
    bias_ref,
    gain_out_ref,
    residual_out_ref,
    order_ref,
    cache_ref,
    *refs,
):
    weight_refs = refs[:n_wide]
    length_ref, start_ref, owner_ref, gain_ref, q_ref, fresh_ref, residual_ref, sems = refs[n_wide:]
    copies = [
        pltpu.make_async_copy(source, target, sems.at[i])
        for i, (source, target) in enumerate(
            [
                (length_hbm, length_ref),
                (start_hbm, start_ref),
                (owner_hbm, owner_ref),
                (gain_hbm, gain_ref),
                (q_hbm, q_ref),
                (cache_hbm, cache_ref),
                (fresh_hbm, fresh_ref),
                (residual_hbm, residual_ref),
            ]
            + sum(
                [
                    item_copies(("out", k), plan, weight_hbm, weight_refs[k])
                    for k in range(n_wide)
                ],
                [],
            )
        )
    ]
    for copy in copies:
        copy.start()
    for copy in copies[:4]:
        copy.wait()
    req, heads, latent = q_ref.shape
    block = cache_ref.shape[1]
    width = gain_ref.shape[0]
    me, me_sub = lax.axis_index("wide"), lax.axis_index("sub")
    group = me_sub * lax.axis_size("pair") + lax.axis_index("pair")

    owners = [owner_ref[group * req + r] for r in range(req)]
    placed = []
    for r in range(req):
        at = jnp.int32(0)
        for j in range(req):
            if j != r:
                ahead = owners[j] <= owners[r] if j < r else owners[j] < owners[r]
                at = at + jnp.where(ahead, 1, 0)
        placed.append(at)
        order_ref[r] = at

    gain_out_ref[...] = gain_ref[...].reshape(1, width).astype(F32)

    biases = []
    for r in range(req):
        following = jnp.where(
            me == n_wide - 1, length_ref[r], start_ref[r, jnp.minimum(me + 1, n_wide - 1)]
        )
        position = lax.broadcasted_iota(jnp.int32, (1, block), 1)
        biases.append(jnp.where(position < following - start_ref[r, me], 0.0, F32(-1e30)))
    bias = jnp.concatenate(biases, axis=0)
    bias_ref[...] = bias

    for copy in copies[4:8]:
        copy.wait()
    rows = []
    for i in range(req):
        row = jnp.zeros((1, width), F32)
        for r in range(req):
            row = jnp.where(placed[r] == i, residual_ref[r : r + 1, :].astype(F32), row)
        rows.append(row)
    residual_out_ref[...] = jnp.concatenate(rows, axis=0)

    scores = partial_scores(q_ref, cache_ref, bias)
    fresh = [fresh_ref[r : r + 1, :].astype(F32) for r in range(req)]
    own = jnp.concatenate(
        [
            jnp.sum(q_ref[r].astype(F32) * fresh[r], axis=1, keepdims=True)
            * (NOPE + ROPE) ** (-0.5)
            for r in range(req)
        ],
        axis=0,
    )
    top = jnp.maximum(jnp.max(scores, axis=1, keepdims=True), own)
    expo = jnp.exp(scores - top)
    expo_own = jnp.exp(own - top)
    den = jnp.sum(expo, axis=1, keepdims=True) + expo_own
    weight_own = expo_own.astype(BF16).astype(F32)
    num = partial_sums(expo, cache_ref, heads) + jnp.concatenate(
        [weight_own[r * heads : (r + 1) * heads] * fresh[r][:, :KV_RANK] for r in range(req)],
        axis=0,
    )
    count = req * heads
    out_ref[:count, :] = (num / den).astype(BF16)
    out_ref[count:, :] = payload_tail(top + jnp.log(den)).astype(BF16)
    for copy in copies[8:]:
        copy.wait()


def attend_cost(req, heads, block, latent):
    return pl.CostEstimate(
        flops=2 * req * heads * block * (latent + KV_RANK),
        bytes_accessed=2 * req * (block * latent + heads * (latent + KV_RANK)),
        transcendentals=req * heads * block,
    )


def prepare(length, start, owner, gain, q, cache, fresh, residual, weight, plan):
    req, heads, latent = q.shape
    block, width = cache.shape[1], residual.shape[1]
    n_wide = start.shape[1]
    operands = (length, start, owner, gain, q, cache, fresh, residual, weight)
    return pl.pallas_call(
        functools.partial(prepare_kernel, n_wide, plan),
        out_shape=[
            jax.ShapeDtypeStruct((req * heads + TAIL, KV_RANK), BF16),
            jax.ShapeDtypeStruct((req, block), F32),
            jax.ShapeDtypeStruct((1, width), F32),
            jax.ShapeDtypeStruct((req, width), F32),
            jax.ShapeDtypeStruct((req,), jnp.int32),
            pltpu.VMEM(cache.shape, BF16),
        ]
        + item_shapes([("out", k) for k in range(n_wide)], plan),
        in_specs=[HBM] * len(operands),
        out_specs=[VMEM] * 4 + [SMEM, VMEM] + [VMEM] * n_wide,
        scratch_shapes=[
            pltpu.SMEM(length.shape, jnp.int32),
            pltpu.SMEM(start.shape, jnp.int32),
            pltpu.SMEM(owner.shape, jnp.int32),
            pltpu.VMEM(gain.shape, BF16),
            pltpu.VMEM(q.shape, BF16),
            pltpu.VMEM(fresh.shape, BF16),
            pltpu.VMEM(residual.shape, BF16),
            pltpu.SemaphoreType.DMA((len(operands) - 1 + n_wide,)),
        ],
        compiler_params=SMALL,
        cost_estimate=pl.CostEstimate(
            flops=2 * req * heads * block * (latent + KV_RANK),
            bytes_accessed=2 * (weight.size + cache.size + q.size),
            transcendentals=req * heads * block,
        ),
        name="prepare",
    )(*[in_hbm(x) for x in operands])


def attend_kernel(q_ref, cache_ref, bias_ref, after_ref, out_ref):
    req, heads, latent = q_ref.shape
    scores = partial_scores(q_ref, cache_ref, bias_ref[...])
    top = jnp.max(scores, axis=1, keepdims=True)
    expo = jnp.exp(scores - top)
    den = jnp.sum(expo, axis=1, keepdims=True)
    num = partial_sums(expo, cache_ref, heads)
    count = req * heads
    out_ref[:count, :] = (num / den).astype(BF16)
    out_ref[count:, :] = payload_tail(top + jnp.log(den)).astype(BF16)


def attend(q, cache, bias, after):
    req, heads, latent = q.shape
    return pl.pallas_call(
        attend_kernel,
        out_shape=jax.ShapeDtypeStruct((req * heads + TAIL, KV_RANK), BF16),
        in_specs=[VMEM] * 3 + [ANY],
        out_specs=VMEM,
        compiler_params=SMALL,
        cost_estimate=attend_cost(req, heads, cache.shape[1], latent),
        name="attend",
    )(q, cache, bias, after)


def fetch_kernel(items, plan, both_hbm, down_hbm, after_ref, *refs):
    for copy in start_items(items, plan, both_hbm, down_hbm, refs[:-1], refs[-1]):
        copy.wait()


def fetch(items, plan, both, down, after):
    shapes = item_shapes(items, plan)
    out = pl.pallas_call(
        functools.partial(fetch_kernel, items, plan),
        out_shape=shapes,
        in_specs=[HBM, HBM, ANY],
        out_specs=[VMEM] * len(items),
        scratch_shapes=[item_sems(items)],
        compiler_params=SMALL,
        cost_estimate=pl.CostEstimate(
            flops=0,
            bytes_accessed=2 * sum(math.prod(shape.shape) for shape in shapes),
            transcendentals=0,
        ),
        name="fetch",
    )(in_hbm(both), in_hbm(down), after)
    return dict(zip(items, out))


def combine_kernel(n_wide, n_sub, req, order_any, after_ref, *refs):
    payloads, outs = refs[:n_wide], refs[n_wide : n_wide + n_sub]
    hold, order_ref, sem = refs[n_wide + n_sub :]
    copy = pltpu.make_async_copy(order_any, order_ref, sem)
    copy.start()
    rows = payloads[0].shape[0] - TAIL
    heads = rows // req
    heads_dev = heads // n_sub
    me_sub = lax.axis_index("sub")
    tails = [p[rows:, :].astype(F32) for p in payloads]
    lses = []
    for tail in tails:
        turned = lax.dot_general(
            eye(rows, 128),
            tail[:, :128].astype(BF16),
            (((1,), (1,)), ((), ())),
            preferred_element_type=F32,
        )
        lses.append(turned[:, 0:1] + turned[:, 1:2] + turned[:, 2:3])
    top = functools.reduce(jnp.maximum, lses)
    weights = [jnp.exp(lse - top) for lse in lses]
    inv = 1.0 / functools.reduce(jnp.add, weights)
    weights = [weight * inv for weight in weights]
    copy.wait()
    for r in range(req):
        at = slice(r * heads, (r + 1) * heads)
        attn = functools.reduce(
            jnp.add, [w[at] * p[at, :].astype(F32) for w, p in zip(weights, payloads)]
        ).astype(BF16)
        for s in range(n_sub):
            hold[s, order_ref[r]] = attn[s * heads_dev : (s + 1) * heads_dev]
    for k in range(n_sub):
        outs[k][...] = hold[me_sub ^ k]


def combine(order, after, payloads, req, n_sub):
    n_wide = len(payloads)
    heads_dev = (payloads[0].shape[0] - TAIL) // req // n_sub
    piece = jax.ShapeDtypeStruct((req, heads_dev, KV_RANK), BF16)
    return pl.pallas_call(
        functools.partial(combine_kernel, n_wide, n_sub, req),
        out_shape=[piece] * n_sub,
        in_specs=[ANY, ANY] + [VMEM] * n_wide,
        out_specs=[VMEM] * n_sub,
        scratch_shapes=[
            pltpu.VMEM((n_sub, req, heads_dev, KV_RANK), BF16),
            pltpu.SMEM(order.shape, jnp.int32),
            pltpu.SemaphoreType.DMA(()),
        ],
        compiler_params=SMALL,
        name="combine",
    )(order, after, *payloads)


def project_kernel(count, items, plan, up_ref, both_hbm, down_hbm, after_ref, *refs):
    n_wide = plan.wide // plan.width
    pieces, weights, refs = refs[:count], refs[count : count + n_wide], refs[count + n_wide :]
    outs, fetched, (vals, sems) = refs[:n_wide], refs[n_wide:-2], refs[-2:]
    copies = start_items(items, plan, both_hbm, down_hbm, fetched, sems)
    req, heads, rank = pieces[0].shape
    rows = count * req
    cols = up_ref.shape[1]
    stacked = jnp.concatenate([p[...].reshape(req * heads, rank) for p in pieces], axis=0)
    total = rows * heads
    to = lax.broadcasted_iota(jnp.int32, (total, total), 0)
    source = lax.broadcasted_iota(jnp.int32, (total, total), 1)
    turn = (to // rows == source % heads) & (to % rows == source // heads)
    turned = jnp.dot(turn.astype(BF16), stacked, preferred_element_type=F32).astype(BF16)
    for h in range(heads):
        val = lax.dot_general(
            turned[h * rows : (h + 1) * rows],
            up_ref[h],
            (((1,), (1,)), ((), ())),
            preferred_element_type=F32,
        )
        vals[:, h * cols : (h + 1) * cols] = val.astype(BF16)

    def work(at):
        for k in range(n_wide):
            block = column_block(weights[k], k, plan, at)
            out = jnp.dot(vals[...], block, preferred_element_type=F32)
            outs[k][:, at] = out.astype(outs[k].dtype)

    in_tiles(items, plan.width, work)
    for copy in copies:
        copy.wait()


def project(pieces, value_up, weights, items, plan, both, down, after):
    count = len(pieces)
    req, heads, rank = pieces[0].shape
    rows = count * req
    n_wide = len(weights)
    out = pl.pallas_call(
        functools.partial(project_kernel, count, items, plan),
        out_shape=[jax.ShapeDtypeStruct((rows, plan.width), F32)]
        + [jax.ShapeDtypeStruct((rows, plan.width), BF16)] * (n_wide - 1)
        + item_shapes(items, plan),
        in_specs=[VMEM, HBM, HBM, ANY] + [VMEM] * (count + n_wide),
        out_specs=[VMEM] * (n_wide + len(items)),
        scratch_shapes=[pltpu.VMEM((rows, plan.depth), BF16), item_sems(items)],
        compiler_params=SMALL,
        cost_estimate=pl.CostEstimate(
            flops=2 * rows * plan.depth * plan.wide,
            bytes_accessed=2 * plan.depth * plan.wide,
            transcendentals=0,
        ),
        name="project",
    )(value_up, in_hbm(both), in_hbm(down), after, *pieces, *weights)
    return out[0], out[1:n_wide], dict(zip(items, out[n_wide:]))


def add_in_order(blocks, arrived):
    for j, a in arrived:
        others = a[...].astype(F32)
        req = blocks[0].shape[0]
        blocks = [
            block + others[(i ^ j) * req : ((i ^ j) + 1) * req] for i, block in enumerate(blocks)
        ]
    return blocks


def merge_kernel(js, mine_ref, residual_ref, after_ref, *refs):
    arrived, (total_ref, send_ref) = refs[:-2], refs[-2:]
    req = residual_ref.shape[0]
    if js is None:
        total = mine_ref[...]
        for a in arrived:
            total = total + a[...].astype(F32)
        total_ref[...] = total
        total_ref[:req, :] = total[:req] + residual_ref[...]
        total = total_ref[...]
    else:
        blocks = [mine_ref[i : i + req, :] for i in range(0, mine_ref.shape[0], req)]
        total = jnp.concatenate(add_in_order(blocks, zip(js, arrived)), axis=0)
        total_ref[...] = total
    send_ref[...] = total.astype(BF16)


def merge(mine, residual, after, arrived, js=None):
    return pl.pallas_call(
        functools.partial(merge_kernel, js),
        out_shape=[jax.ShapeDtypeStruct(mine.shape, F32), jax.ShapeDtypeStruct(mine.shape, BF16)],
        in_specs=[VMEM, VMEM, ANY] + [VMEM] * len(arrived),
        out_specs=[VMEM] * 2,
        compiler_params=SMALL,
        name="merge",
    )(mine, residual, after, *arrived)


def norm_kernel(js, req, mine_ref, gain_ref, after_ref, *refs):
    arrived, (gained_ref, stream_ref) = refs[:-2], refs[-2:]
    width = mine_ref.shape[1]
    blocks = [mine_ref[i : i + req, :] for i in range(0, mine_ref.shape[0], req)]
    blocks = add_in_order(blocks, zip(js, arrived))
    stream_ref[...] = blocks[0]
    total = jnp.concatenate(blocks, axis=0)
    gained_ref[:, :width] = (total * gain_ref[...]).astype(BF16)
    square = jnp.sum(total * total, axis=1, keepdims=True)
    hi = square.astype(BF16).astype(F32)
    mid = (square - hi).astype(BF16).astype(F32)
    lo = (square - hi - mid).astype(BF16).astype(F32)
    lane = lax.broadcasted_iota(jnp.int32, (total.shape[0], 128), 1)
    spread = jnp.where(lane == 0, hi, jnp.where(lane == 1, mid, jnp.where(lane == 2, lo, 0.0)))
    gained_ref[:, width:] = spread.astype(BF16)


def norm(mine, gain, after, arrived, js, req):
    rows, width = mine.shape
    return pl.pallas_call(
        functools.partial(norm_kernel, js, req),
        out_shape=[
            jax.ShapeDtypeStruct((rows, width + 128), BF16),
            jax.ShapeDtypeStruct((req, width), F32),
        ],
        in_specs=[VMEM, VMEM, ANY] + [VMEM] * len(arrived),
        out_specs=[VMEM] * 2,
        compiler_params=SMALL,
        name="norm",
    )(mine, gain, after, *arrived)


def gate_kernel(count, first, items, plan, x_ref, both_hbm, down_hbm, *refs):
    weights, refs = refs[:count], refs[count:]
    carry, refs = (None, refs) if first else (refs[: count + 1], refs[count + 1 :])
    outs, fetched, sems = refs[: count + 1], refs[count + 1 : -1], refs[-1]
    copies = start_items(items, plan, both_hbm, down_hbm, fetched, sems)
    square = x_ref[:, plan.width :].astype(F32)
    outs[count][...] = square if first else square + carry[count][...]
    x = x_ref[:, : plan.width]

    def multiply(i, at):
        product = jnp.dot(x, weights[i][:, at], preferred_element_type=F32)
        outs[i][:, at] = product if first else product + carry[i][:, at]

    def work(at):
        multiply(0, at)
        multiply(1, at)

    in_tiles(items, plan.full, work)
    for i in range(2, count):
        multiply(i, pl.ds(0, weights[i].shape[1]))
    for copy in copies:
        copy.wait()


def gate(x, weights, carry, items, plan, both, down):
    rows = x.shape[0]
    count = len(weights)
    shapes = [jax.ShapeDtypeStruct((rows, w.shape[1]), F32) for w in weights]
    shapes += [jax.ShapeDtypeStruct((rows, 128), F32)]
    out = pl.pallas_call(
        functools.partial(gate_kernel, count, not carry, items, plan),
        out_shape=shapes + item_shapes(items, plan),
        in_specs=[VMEM, HBM, HBM] + [VMEM] * (count + len(carry)),
        out_specs=[VMEM] * (count + 1 + len(items)),
        scratch_shapes=[item_sems(items)],
        compiler_params=SMALL,
        cost_estimate=pl.CostEstimate(
            flops=4 * rows * plan.width * plan.units,
            bytes_accessed=4 * plan.width * plan.units,
            transcendentals=0,
        ),
        name="gate",
    )(x, in_hbm(both), in_hbm(down), *weights, *carry)
    return out[: count + 1], dict(zip(items, out[count + 1 :]))


def down_kernel(ks, items, plan, count, both_hbm, down_hbm, *refs):
    weights, operands, refs = refs[: len(ks)], refs[len(ks) : count], refs[count:]
    sems = refs[-1]
    outs, fetched = refs[: -1 - len(items)], refs[-1 - len(items) : -1]
    copies = start_items(items, plan, both_hbm, down_hbm, fetched, sems)
    if len(operands) > 2:
        *sums, square_ref = operands
        hidden_ref, *outs = outs
        square = square_ref[:, 0:1] + square_ref[:, 1:2] + square_ref[:, 2:3]
        inv = lax.rsqrt(square / D + 1e-06)
        both = [sums[0][...], sums[1][...]]
        if len(sums) > 2:
            half = plan.units - plan.full
            both = [
                jnp.concatenate([part, sums[2][:, g * half : (g + 1) * half]], axis=1)
                for g, part in enumerate(both)
            ]
        g = both[0] * inv
        hidden = (g / (1.0 + jnp.exp(-g)) * (both[1] * inv)).astype(BF16)
        hidden_ref[...] = hidden
    else:
        hidden = operands[0][...]

    def work(at):
        for k, weight_ref, out in zip(ks, weights, outs):
            block = column_block(weight_ref, k, plan, at)
            out[:, at] = jnp.dot(hidden, block, preferred_element_type=F32).astype(out.dtype)

    in_tiles(items, plan.width, work)
    for copy in copies:
        copy.wait()


def down(weights, operands, ks, items, plan, both, down_weight):
    rows = operands[0].shape[0]
    first = len(operands) > 2
    shapes = [jax.ShapeDtypeStruct((rows, plan.width), BF16 if k else F32) for k in ks]
    if first:
        shapes = [jax.ShapeDtypeStruct((rows, plan.units), BF16)] + shapes
    count = len(ks) + len(operands)
    out = pl.pallas_call(
        functools.partial(down_kernel, ks, items, plan, count),
        out_shape=shapes + item_shapes(items, plan),
        in_specs=[HBM, HBM] + [VMEM] * len(ks) + ([VMEM] * len(operands) if first else [VMEM, ANY]),
        out_specs=[VMEM] * (len(shapes) + len(items)),
        scratch_shapes=[item_sems(items)],
        compiler_params=SMALL,
        cost_estimate=pl.CostEstimate(
            flops=2 * rows * plan.units * plan.width * len(ks),
            bytes_accessed=2 * plan.units * plan.width * len(ks),
            transcendentals=0,
        ),
        name="down",
    )(in_hbm(both), in_hbm(down_weight), *weights, *operands)
    return out[: len(shapes)], dict(zip(items, out[len(shapes) :]))


def split_kernel(kept, mine_ref, *refs):
    rows = mine_ref.shape[0]
    count = rows // kept
    arrived, outs = refs[:-count], refs[-count:]
    total = mine_ref[...]
    for a in arrived:
        total = total + a[...].astype(F32)
    outs[0][...] = total[:kept]
    for j in range(1, count):
        outs[j][...] = total[j * kept : (j + 1) * kept].astype(BF16)


def split(mine, arrived, kept):
    rows, width = mine.shape
    count = rows // kept
    return pl.pallas_call(
        functools.partial(split_kernel, kept),
        out_shape=[jax.ShapeDtypeStruct((kept, width), F32)]
        + [jax.ShapeDtypeStruct((kept, width), BF16)] * (count - 1),
        in_specs=[VMEM] * (1 + len(arrived)),
        out_specs=[VMEM] * count,
        compiler_params=SMALL,
        name="split",
    )(mine, *arrived)


def body(
    latent_cache,
    queries,
    new_latent,
    context_len,
    block_start,
    owner,
    value_up,
    out_proj,
    residual_in,
    norm_gain,
    gate_up,
    down_weight,
):
    n_wide = lax.axis_size("wide")
    n_sub = lax.axis_size("sub")
    n_pair = lax.axis_size("pair")
    req_grp = latent_cache.shape[0]
    width_dev = residual_in.shape[1]

    powers = [k for k in range(1, n_wide) if k & (k - 1) == 0]
    arrived = {k: hop(queries, "wide", k) for k in reversed(powers)}
    units = down_weight.shape[0]
    plan = Plan(
        width=width_dev,
        units=units,
        full=units - 128 if units % 256 == 128 else units,
        depth=out_proj.shape[0] * out_proj.shape[1],
        wide=D,
    )
    payload, bias, gain, residual, order, cache, *out_blocks = prepare(
        context_len,
        block_start,
        owner,
        norm_gain,
        queries,
        latent_cache,
        new_latent,
        residual_in,
        out_proj.reshape(plan.depth, D),
        plan,
    )

    kinds = ("gate", "rest", "up") if plan.full < units else ("gate", "up")
    held = {}

    def bring(items, after):
        got = fetch(items, plan, gate_up, down_weight, after)
        held.update(got)
        return got[items[-1]]

    far = list(range(n_wide - 1, -1, -1))
    queue = [(kind, k) for k in range(n_wide) for kind in kinds] + [("down", k) for k in far]

    def take(count):
        items = queue[:count]
        del queue[:count]
        return items

    payloads = [payload]
    waited = False
    for k in range(1, n_wide):
        if k not in arrived:
            low = k & -k
            arrived[k] = hop(arrived[k - low], "wide", low)
            if not waited:
                payload = bring(take(3), payload)
                waited = True
        elif k > 1:
            arrived[k], payload = lax.optimization_barrier((arrived[k], payload))
        payload = attend(arrived[k], cache, bias, payload)
        payloads.append(payload)
    last = bring(take(1), payload)
    payloads[1], last = lax.optimization_barrier((payloads[1], last))
    last = bring(take(3), last)
    payloads = [payloads[0]] + [hop(payloads[k], "wide", k) for k in range(1, n_wide)]
    chunks = combine(order, last, payloads, req_grp, n_sub)

    landed = [chunks[0]] + [hop(chunks[ks], "sub", ks) for ks in range(1, n_sub)]
    last = bring(take(1), chunks[0])
    landed[1:], last = lax.optimization_barrier((landed[1:], last))
    pieces = landed + [hop(p, "pair", kp) for kp in range(1, n_pair) for p in landed]
    mine, sends, got = project(
        pieces,
        jnp.swapaxes(value_up, 1, 2),
        out_blocks,
        take(3),
        plan,
        gate_up,
        down_weight,
        last,
    )
    held.update(got)

    back = [hop(sends[k - 1], "wide", k) for k in range(n_wide - 1, 0, -1)]
    last = bring(take(len(queue) - n_wide + 1), mine)
    total, send = merge(mine, residual, last, back)
    back = [hop(send, "pair", k) for k in range(1, n_pair)]
    total, send = merge(total, residual, send, back, [k * n_sub for k in range(1, n_pair)])
    back = [hop(send, "sub", k) for k in range(1, n_sub)]
    last = bring(take(n_wide - 3), send)
    gained, stream = norm(total, gain, last, back, list(range(1, n_sub)), req_grp)

    blocks = {k: hop(gained, "wide", k) for k in reversed(powers)}
    blocks[0] = gained
    carry = ()
    for k in range(n_wide):
        if k not in blocks:
            low = k & -k
            blocks[k] = hop(blocks[k - low], "wide", low)
        items = take(1) if k == 0 else []
        weights = [held[item] for item in (("gate", k), ("up", k), ("rest", k)) if item in held]
        (*carry,), got = gate(blocks[k], weights, carry, items, plan, gate_up, down_weight)
        held.update(got)
        if k == 0:
            for far_k in powers[1:]:
                blocks[far_k], carry[0] = lax.optimization_barrier((blocks[far_k], carry[0]))
    away = far[:-1]
    weights = [held["down", k] for k in away]
    (hidden, *sends), got = down(weights, carry, away, take(1), plan, gate_up, down_weight)
    held.update(got)
    back = [hop(send, "wide", k) for k, send in zip(away, sends)]
    weights = [held["down", 0]]
    (mine,), _ = down(weights, (hidden, sends[-1]), [0], [], plan, gate_up, down_weight)
    mine, *sends = split(mine, back, n_sub * req_grp)
    back = [hop(send, "pair", k + 1) for k, send in enumerate(sends)]
    out, *sends = split(mine, back, req_grp)
    out = out + stream
    for k, send in enumerate(sends):
        out = out + hop(send, "sub", k + 1).astype(F32)
    return out.astype(BF16)


def solution(mesh):
    in_specs = (
        P(("groups", "sub", "pair"), "wide", None),
        P(("groups", "sub", "pair"), "wide", None),
        P(("groups", "sub", "pair"), None),
        P(("groups", "sub", "pair")),
        P(("groups", "sub", "pair"), None),
        P("groups"),
        P(("wide", "sub"), None, "pair"),
        P(("wide", "sub"), "pair", None),
        P(("groups", "sub", "pair"), "wide"),
        P("wide"),
        P(None, None, ("wide", "sub", "pair")),
        P(("wide", "sub", "pair"), None),
    )
    out_specs = P(("groups", "sub", "pair"), "wide")
    return jax.shard_map(body, mesh=mesh, in_specs=in_specs, out_specs=out_specs, check_vma=False)
```

```python
import collections
import functools
import math

import jax
import jax.numpy as jnp
from jax import lax
from jax.experimental import pallas as pl
from jax.experimental.pallas import tpu as pltpu
from jax.sharding import PartitionSpec as P

D = 7168
KV_RANK = 512
ROPE = 64
NOPE = 128
F32 = jnp.float32
BF16 = jnp.bfloat16
TAIL = 8
VMEM = pl.BlockSpec(memory_space=pltpu.VMEM)
SMEM = pl.BlockSpec(memory_space=pltpu.SMEM)
ANY = pl.BlockSpec(memory_space=pl.ANY)
HBM = pl.BlockSpec(memory_space=pltpu.HBM)
SMALL = pltpu.CompilerParams(vmem_limit_bytes=4 * 2**20)


def hop(x, axis, k):
    n = lax.axis_size(axis)
    return lax.ppermute(x, axis, [(i, i ^ k) for i in range(n)])


def hop_group(x, k):
    n = lax.axis_size("sub") * lax.axis_size("pair")
    return lax.ppermute(x, ("sub", "pair"), [(i, i ^ k) for i in range(n)])


def in_hbm(x):
    return pltpu.with_memory_space_constraint(x, pltpu.HBM)


Plan = collections.namedtuple("Plan", ["width", "units", "full", "depth", "wide"])


def aligned(plan):
    return plan.width % 128 == 0


def item_shape(item, plan):
    kind, k = item
    cols = plan.width if aligned(plan) else plan.wide
    if kind == "out":
        return (plan.depth, cols)
    if kind == "rest":
        return (plan.width, 2 * (plan.units - plan.full))
    return (plan.width, plan.full)


def item_copies(item, plan, source, out):
    kind, k = item
    start = (lax.axis_index("wide") ^ k) * plan.width
    if kind == "out":
        if not aligned(plan):
            return [(source, out)]
        return [(source.at[:, pl.ds(pl.multiple_of(start, 128), plan.width)], out)]
    rows = pl.ds(pl.multiple_of(start, 64), plan.width)
    if kind == "rest":
        half = plan.units - plan.full
        return [
            (source.at[g, rows, plan.full :], out.at[:, g * half : (g + 1) * half])
            for g in range(2)
        ]
    return [(source.at[int(kind == "up"), rows, : plan.full], out)]


def start_items(items, plan, both, proj, outs, sems):
    pairs = []
    for item, out in zip(items, outs):
        pairs += item_copies(item, plan, proj if item[0] == "out" else both, out)
    copies = [
        pltpu.make_async_copy(source, out, sems.at[i]) for i, (source, out) in enumerate(pairs)
    ]

    @pl.when(lax.axis_index("wide") >= 0)
    def _():
        for copy in copies:
            copy.start()

    return copies


def item_shapes(items, plan):
    return [pltpu.VMEM(item_shape(item, plan), BF16) for item in items]


def item_sems(items):
    return pltpu.SemaphoreType.DMA((max(1, sum(2 if i[0] == "rest" else 1 for i in items)),))


def column_block(ref, k, plan, at):
    me = lax.axis_index("wide")
    if ref.shape[1] == plan.width:
        return ref[:, at]
    if aligned(plan):
        return ref[:, pl.ds(pl.multiple_of((me ^ k) * plan.width, 128), plan.width)]
    block = ref[:, : plan.width]
    for w in range(1, plan.wide // plan.width):
        block = jnp.where((me ^ k) == w, ref[:, w * plan.width : (w + 1) * plan.width], block)
    return block


def in_tiles(loop, cols, work):
    if not loop or cols % 256:
        work(pl.ds(0, cols))
        return

    @pl.loop(0, cols // 256)
    def _(i):
        work(pl.ds(pl.multiple_of(i * 256, 256), 256))


def eye(rows, cols):
    row = lax.broadcasted_iota(jnp.int32, (rows, cols), 0)
    col = lax.broadcasted_iota(jnp.int32, (rows, cols), 1)
    return (row == col).astype(BF16)


def partial_scores(q_ref, cache_ref, bias):
    req, heads, latent = q_ref.shape
    scores = [
        lax.dot_general(
            q_ref[r], cache_ref[r], (((1,), (1,)), ((), ())), preferred_element_type=F32
        )
        * (NOPE + ROPE) ** (-0.5)
        + bias[r : r + 1, :]
        for r in range(req)
    ]
    return jnp.concatenate(scores, axis=0)


def partial_sums(expo, cache_ref, heads):
    expo = expo.astype(BF16)
    sums = [
        jnp.dot(
            expo[r * heads : (r + 1) * heads],
            cache_ref[r, :, :KV_RANK],
            preferred_element_type=F32,
        )
        for r in range(cache_ref.shape[0])
    ]
    return jnp.concatenate(sums, axis=0)


def payload_tail(lse):
    rows = lse.shape[0]
    hi = lse.astype(BF16).astype(F32)
    mid = (lse - hi).astype(BF16).astype(F32)
    lo = (lse - hi - mid).astype(BF16).astype(F32)
    lane = lax.broadcasted_iota(jnp.int32, (rows, 128), 1)
    spread = jnp.where(lane == 0, hi, jnp.where(lane == 1, mid, jnp.where(lane == 2, lo, 0.0)))
    turned = lax.dot_general(
        spread.astype(BF16), eye(rows, 128), (((0,), (0,)), ((), ())), preferred_element_type=F32
    )
    return jnp.pad(turned[:TAIL], ((0, 0), (0, KV_RANK - 128)))


def prepare_kernel(
    n_wide,
    length_hbm,
    start_hbm,
    owner_hbm,
    gain_hbm,
    q_hbm,
    cache_hbm,
    fresh_hbm,
    residual_hbm,
    out_ref,
    bias_ref,
    gain_out_ref,
    residual_out_ref,
    order_ref,
    cache_ref,
    *refs,
):
    length_ref, start_ref, owner_ref, gain_ref, q_ref, fresh_ref, residual_ref, sems = refs
    copies = [
        pltpu.make_async_copy(source, target, sems.at[i])
        for i, (source, target) in enumerate(
            [
                (length_hbm, length_ref),
                (start_hbm, start_ref),
                (owner_hbm, owner_ref),
                (gain_hbm, gain_ref),
                (q_hbm, q_ref),
                (cache_hbm, cache_ref),
                (fresh_hbm, fresh_ref),
                (residual_hbm, residual_ref),
            ]
        )
    ]
    for copy in copies:
        copy.start()
    for copy in copies[:4]:
        copy.wait()
    req, heads, latent = q_ref.shape
    block = cache_ref.shape[1]
    width = gain_ref.shape[0]
    me, me_sub = lax.axis_index("wide"), lax.axis_index("sub")
    group = me_sub * lax.axis_size("pair") + lax.axis_index("pair")

    owners = [owner_ref[group * req + r] for r in range(req)]
    placed = []
    for r in range(req):
        at = jnp.int32(0)
        for j in range(req):
            if j != r:
                ahead = owners[j] <= owners[r] if j < r else owners[j] < owners[r]
                at = at + jnp.where(ahead, 1, 0)
        placed.append(at)
        order_ref[r] = at

    gain_out_ref[...] = gain_ref[...].reshape(1, width).astype(F32)

    biases = []
    for r in range(req):
        following = jnp.where(
            me == n_wide - 1, length_ref[r], start_ref[r, jnp.minimum(me + 1, n_wide - 1)]
        )
        position = lax.broadcasted_iota(jnp.int32, (1, block), 1)
        biases.append(jnp.where(position < following - start_ref[r, me], 0.0, F32(-1e30)))
    bias = jnp.concatenate(biases, axis=0)
    bias_ref[...] = bias

    for copy in copies[4:]:
        copy.wait()
    rows = []
    for i in range(req):
        row = jnp.zeros((1, width), F32)
        for r in range(req):
            row = jnp.where(placed[r] == i, residual_ref[r : r + 1, :].astype(F32), row)
        rows.append(row)
    residual_out_ref[...] = jnp.concatenate(rows, axis=0)

    scores = partial_scores(q_ref, cache_ref, bias)
    fresh = [fresh_ref[r : r + 1, :].astype(F32) for r in range(req)]
    own = jnp.concatenate(
        [
            jnp.sum(q_ref[r].astype(F32) * fresh[r], axis=1, keepdims=True)
            * (NOPE + ROPE) ** (-0.5)
            for r in range(req)
        ],
        axis=0,
    )
    top = jnp.maximum(jnp.max(scores, axis=1, keepdims=True), own)
    expo = jnp.exp(scores - top)
    expo_own = jnp.exp(own - top)
    den = jnp.sum(expo, axis=1, keepdims=True) + expo_own
    weight_own = expo_own.astype(BF16).astype(F32)
    num = partial_sums(expo, cache_ref, heads) + jnp.concatenate(
        [weight_own[r * heads : (r + 1) * heads] * fresh[r][:, :KV_RANK] for r in range(req)],
        axis=0,
    )
    count = req * heads
    out_ref[:count, :] = (num / den).astype(BF16)
    out_ref[count:, :] = payload_tail(top + jnp.log(den)).astype(BF16)


def attend_cost(req, heads, block, latent):
    return pl.CostEstimate(
        flops=2 * req * heads * block * (latent + KV_RANK),
        bytes_accessed=2 * req * (block * latent + heads * (latent + KV_RANK)),
        transcendentals=req * heads * block,
    )


def prepare(length, start, owner, gain, q, cache, fresh, residual):
    req, heads, latent = q.shape
    block, width = cache.shape[1], residual.shape[1]
    n_wide = start.shape[1]
    operands = (length, start, owner, gain, q, cache, fresh, residual)
    return pl.pallas_call(
        functools.partial(prepare_kernel, n_wide),
        out_shape=[
            jax.ShapeDtypeStruct((req * heads + TAIL, KV_RANK), BF16),
            jax.ShapeDtypeStruct((req, block), F32),
            jax.ShapeDtypeStruct((1, width), F32),
            jax.ShapeDtypeStruct((req, width), F32),
            jax.ShapeDtypeStruct((req,), jnp.int32),
            pltpu.VMEM(cache.shape, BF16),
        ],
        in_specs=[HBM] * len(operands),
        out_specs=[VMEM] * 4 + [SMEM, VMEM],
        scratch_shapes=[
            pltpu.SMEM(length.shape, jnp.int32),
            pltpu.SMEM(start.shape, jnp.int32),
            pltpu.SMEM(owner.shape, jnp.int32),
            pltpu.VMEM(gain.shape, BF16),
            pltpu.VMEM(q.shape, BF16),
            pltpu.VMEM(fresh.shape, BF16),
            pltpu.VMEM(residual.shape, BF16),
            pltpu.SemaphoreType.DMA((len(operands),)),
        ],
        compiler_params=SMALL,
        cost_estimate=pl.CostEstimate(
            flops=2 * req * heads * block * (latent + KV_RANK),
            bytes_accessed=2 * (cache.size + q.size),
            transcendentals=req * heads * block,
        ),
        name="prepare",
    )(*[in_hbm(x) for x in operands])


def attend_kernel(q_ref, cache_ref, bias_ref, after_ref, out_ref):
    req, heads, latent = q_ref.shape
    scores = partial_scores(q_ref, cache_ref, bias_ref[...])
    top = jnp.max(scores, axis=1, keepdims=True)
    expo = jnp.exp(scores - top)
    den = jnp.sum(expo, axis=1, keepdims=True)
    num = partial_sums(expo, cache_ref, heads)
    count = req * heads
    out_ref[:count, :] = (num / den).astype(BF16)
    out_ref[count:, :] = payload_tail(top + jnp.log(den)).astype(BF16)


def attend(q, cache, bias, after):
    req, heads, latent = q.shape
    return pl.pallas_call(
        attend_kernel,
        out_shape=jax.ShapeDtypeStruct((req * heads + TAIL, KV_RANK), BF16),
        in_specs=[VMEM] * 3 + [ANY],
        out_specs=VMEM,
        compiler_params=SMALL,
        cost_estimate=attend_cost(req, heads, cache.shape[1], latent),
        name="attend",
    )(q, cache, bias, after)


def fetch_kernel(items, plan, both_hbm, proj_hbm, after_ref, *refs):
    for copy in start_items(items, plan, both_hbm, proj_hbm, refs[:-1], refs[-1]):
        copy.wait()


def fetch(items, plan, both, proj, after):
    shapes = item_shapes(items, plan)
    out = pl.pallas_call(
        functools.partial(fetch_kernel, items, plan),
        out_shape=shapes,
        in_specs=[HBM, HBM, ANY],
        out_specs=[VMEM] * len(items),
        scratch_shapes=[item_sems(items)],
        compiler_params=SMALL,
        cost_estimate=pl.CostEstimate(
            flops=0,
            bytes_accessed=2 * sum(math.prod(shape.shape) for shape in shapes),
            transcendentals=0,
        ),
        name="fetch",
    )(in_hbm(both), in_hbm(proj), after)
    return dict(zip(items, out))


def combine_kernel(n_wide, n_sub, req, order_any, after_ref, *refs):
    payloads, outs = refs[:n_wide], refs[n_wide : n_wide + n_sub]
    hold, order_ref, sem = refs[n_wide + n_sub :]
    copy = pltpu.make_async_copy(order_any, order_ref, sem)
    copy.start()
    rows = payloads[0].shape[0] - TAIL
    heads = rows // req
    heads_dev = heads // n_sub
    me_sub = lax.axis_index("sub")
    tails = [p[rows:, :].astype(F32) for p in payloads]
    lses = []
    for tail in tails:
        turned = lax.dot_general(
            eye(rows, 128),
            tail[:, :128].astype(BF16),
            (((1,), (1,)), ((), ())),
            preferred_element_type=F32,
        )
        lses.append(turned[:, 0:1] + turned[:, 1:2] + turned[:, 2:3])
    top = functools.reduce(jnp.maximum, lses)
    weights = [jnp.exp(lse - top) for lse in lses]
    inv = 1.0 / functools.reduce(jnp.add, weights)
    weights = [weight * inv for weight in weights]
    copy.wait()
    for r in range(req):
        at = slice(r * heads, (r + 1) * heads)
        attn = functools.reduce(
            jnp.add, [w[at] * p[at, :].astype(F32) for w, p in zip(weights, payloads)]
        ).astype(BF16)
        for s in range(n_sub):
            hold[s, order_ref[r]] = attn[s * heads_dev : (s + 1) * heads_dev]
    for k in range(n_sub):
        outs[k][...] = hold[me_sub ^ k]


def combine(order, after, payloads, req, n_sub):
    n_wide = len(payloads)
    heads_dev = (payloads[0].shape[0] - TAIL) // req // n_sub
    piece = jax.ShapeDtypeStruct((req, heads_dev, KV_RANK), BF16)
    return pl.pallas_call(
        functools.partial(combine_kernel, n_wide, n_sub, req),
        out_shape=[piece] * n_sub,
        in_specs=[ANY, ANY] + [VMEM] * n_wide,
        out_specs=[VMEM] * n_sub,
        scratch_shapes=[
            pltpu.VMEM((n_sub, req, heads_dev, KV_RANK), BF16),
            pltpu.SMEM(order.shape, jnp.int32),
            pltpu.SemaphoreType.DMA(()),
        ],
        compiler_params=SMALL,
        name="combine",
    )(order, after, *payloads)


def project_kernel(count, items, plan, up_ref, both_hbm, proj_hbm, after_ref, *refs):
    n_wide = plan.wide // plan.width - 1
    pieces, weights, refs = refs[:count], refs[count : count + n_wide], refs[count + n_wide :]
    vals, outs, fetched, sems = refs[0], refs[1 : n_wide + 1], refs[n_wide + 1 : -1], refs[-1]
    copies = start_items(items, plan, both_hbm, proj_hbm, fetched, sems)
    req, heads, rank = pieces[0].shape
    rows = count * req
    cols = up_ref.shape[1]
    stacked = jnp.concatenate([p[...].reshape(req * heads, rank) for p in pieces], axis=0)
    total = rows * heads
    to = lax.broadcasted_iota(jnp.int32, (total, total), 0)
    source = lax.broadcasted_iota(jnp.int32, (total, total), 1)
    turn = (to // rows == source % heads) & (to % rows == source // heads)
    turned = jnp.dot(turn.astype(BF16), stacked, preferred_element_type=F32).astype(BF16)
    some = math.gcd(heads, max(1, 256 // cols))
    for first in range(0, heads, some):
        val = lax.dot_general(
            turned[first * rows : (first + some) * rows],
            up_ref[first : first + some].reshape(some * cols, rank),
            (((1,), (1,)), ((), ())),
            preferred_element_type=F32,
        ).astype(BF16)
        for i in range(some):
            at = slice((first + i) * cols, (first + i + 1) * cols)
            vals[:, at] = val[i * rows : (i + 1) * rows, i * cols : (i + 1) * cols]

    def work(at):
        for k in range(n_wide):
            block = column_block(weights[k], k + 1, plan, at)
            out = jnp.dot(vals[...], block, preferred_element_type=F32)
            outs[k][:, at] = out.astype(outs[k].dtype)

    in_tiles(items, plan.width, work)
    for copy in copies:
        copy.wait()


def project(pieces, value_up, weights, items, plan, both, proj, after):
    count = len(pieces)
    req, heads, rank = pieces[0].shape
    rows = count * req
    n_wide = len(weights)
    out = pl.pallas_call(
        functools.partial(project_kernel, count, items, plan),
        out_shape=[jax.ShapeDtypeStruct((rows, plan.depth), BF16)]
        + [jax.ShapeDtypeStruct((rows, plan.width), BF16)] * n_wide
        + item_shapes(items, plan),
        in_specs=[VMEM, HBM, HBM, ANY] + [VMEM] * (count + n_wide),
        out_specs=[VMEM] * (n_wide + 1 + len(items)),
        scratch_shapes=[item_sems(items)],
        compiler_params=SMALL,
        cost_estimate=pl.CostEstimate(
            flops=2 * rows * plan.depth * plan.wide,
            bytes_accessed=2 * plan.depth * plan.wide,
            transcendentals=0,
        ),
        name="project",
    )(value_up, in_hbm(both), in_hbm(proj), after, *pieces, *weights)
    return out[0], out[1 : n_wide + 1], dict(zip(items, out[n_wide + 1 :]))


def merge_kernel(mine_ref, residual_ref, after_ref, *refs):
    arrived, (total_ref, send_ref) = refs[:-2], refs[-2:]
    req = residual_ref.shape[0]
    total = mine_ref[...]
    for a in arrived:
        total = total + a[...].astype(F32)
    total_ref[...] = total
    total_ref[:req, :] = total[:req] + residual_ref[...]
    send_ref[...] = total_ref[...].astype(BF16)


def merge(mine, residual, after, arrived):
    return pl.pallas_call(
        merge_kernel,
        out_shape=[jax.ShapeDtypeStruct(mine.shape, F32), jax.ShapeDtypeStruct(mine.shape, BF16)],
        in_specs=[VMEM, VMEM, ANY] + [VMEM] * len(arrived),
        out_specs=[VMEM] * 2,
        compiler_params=SMALL,
        name="merge",
    )(mine, residual, after, *arrived)


def norm_kernel(req, mine_ref, gain_ref, after_ref, *refs):
    arrived, (gained_ref, stream_ref) = refs[:-2], refs[-2:]
    width = mine_ref.shape[1]
    blocks = [mine_ref[i * req : (i + 1) * req, :] for i in range(len(arrived) + 1)]
    for j, a in enumerate(arrived):
        others = a[...].astype(F32)
        for i in range(len(blocks)):
            at = (i ^ (j + 1)) * req
            blocks[i] = blocks[i] + others[at : at + req]
    stream_ref[...] = blocks[0]
    total = jnp.concatenate(blocks, axis=0)
    gained_ref[:, :width] = (total * gain_ref[...]).astype(BF16)
    square = jnp.sum(total * total, axis=1, keepdims=True)
    hi = square.astype(BF16).astype(F32)
    mid = (square - hi).astype(BF16).astype(F32)
    lo = (square - hi - mid).astype(BF16).astype(F32)
    lane = lax.broadcasted_iota(jnp.int32, (total.shape[0], 128), 1)
    spread = jnp.where(lane == 0, hi, jnp.where(lane == 1, mid, jnp.where(lane == 2, lo, 0.0)))
    gained_ref[:, width:] = spread.astype(BF16)


def norm(mine, gain, after, arrived, req):
    rows, width = mine.shape
    return pl.pallas_call(
        functools.partial(norm_kernel, req),
        out_shape=[
            jax.ShapeDtypeStruct((rows, width + 128), BF16),
            jax.ShapeDtypeStruct((req, width), F32),
        ],
        in_specs=[VMEM, VMEM, ANY] + [VMEM] * len(arrived),
        out_specs=[VMEM] * 2,
        compiler_params=SMALL,
        name="norm",
    )(mine, gain, after, *arrived)


def gate_kernel(count, first, plan, x_ref, *refs):
    weights, carry, outs = refs[:count], refs[count : -count - 1], refs[-count - 1 :]
    square = x_ref[:, plan.width :].astype(F32)
    outs[count][...] = square if first else square + carry[count][...]
    x = x_ref[:, : plan.width]

    def multiply(i, at):
        product = jnp.dot(x, weights[i][:, at], preferred_element_type=F32)
        outs[i][:, at] = product if first else product + carry[i][:, at]

    def work(at):
        multiply(0, at)
        multiply(1, at)

    in_tiles(True, plan.full, work)
    for i in range(2, count):
        multiply(i, pl.ds(0, weights[i].shape[1]))


def gate(x, weights, carry, plan):
    rows = x.shape[0]
    count = len(weights)
    return pl.pallas_call(
        functools.partial(gate_kernel, count, not carry, plan),
        out_shape=[jax.ShapeDtypeStruct((rows, w.shape[1]), F32) for w in weights]
        + [jax.ShapeDtypeStruct((rows, 128), F32)],
        in_specs=[VMEM] * (1 + count + len(carry)),
        out_specs=[VMEM] * (count + 1),
        compiler_params=SMALL,
        cost_estimate=pl.CostEstimate(
            flops=4 * rows * plan.width * plan.units,
            bytes_accessed=4 * plan.width * plan.units,
            transcendentals=0,
        ),
        name="gate",
    )(x, *weights, *carry)


def hidden_units(plan, operands):
    *sums, square_ref = operands
    square = square_ref[:, 0:1] + square_ref[:, 1:2] + square_ref[:, 2:3]
    inv = lax.rsqrt(square / D + 1e-06)
    both = [sums[0][...], sums[1][...]]
    if len(sums) > 2:
        half = plan.units - plan.full
        both = [
            jnp.concatenate([part, sums[2][:, g * half : (g + 1) * half]], axis=1)
            for g, part in enumerate(both)
        ]
    g = both[0] * inv
    return (g / (1.0 + jnp.exp(-g)) * (both[1] * inv)).astype(BF16)


def down_kernel(ks, plan, weight_ref, *refs):
    operands, hidden_ref, outs = refs[: -1 - len(ks)], refs[-1 - len(ks)], refs[-len(ks) :]
    hidden = hidden_units(plan, operands)
    hidden_ref[...] = hidden
    for k, out in zip(ks, outs):
        block = column_block(weight_ref, k, plan, pl.ds(0, plan.width))
        out[...] = jnp.dot(hidden, block, preferred_element_type=F32).astype(BF16)


def down(weight, operands, ks, plan):
    rows = operands[0].shape[0]
    return pl.pallas_call(
        functools.partial(down_kernel, ks, plan),
        out_shape=[jax.ShapeDtypeStruct((rows, plan.units), BF16)]
        + [jax.ShapeDtypeStruct((rows, plan.width), BF16)] * len(ks),
        in_specs=[VMEM] * (1 + len(operands)),
        out_specs=[VMEM] * (1 + len(ks)),
        compiler_params=SMALL,
        cost_estimate=pl.CostEstimate(
            flops=2 * rows * plan.units * plan.width * len(ks),
            bytes_accessed=2 * plan.units * plan.width * len(ks),
            transcendentals=0,
        ),
        name="down",
    )(weight, *operands)


def own_kernel(plan, weight_ref, rows_ref, after_ref, out_ref):
    block = column_block(weight_ref, 0, plan, pl.ds(0, plan.width))
    out_ref[...] = jnp.dot(rows_ref[...], block, preferred_element_type=F32)


def own(weight, rows, after, plan):
    return pl.pallas_call(
        functools.partial(own_kernel, plan),
        out_shape=jax.ShapeDtypeStruct((rows.shape[0], plan.width), F32),
        in_specs=[VMEM, VMEM, ANY],
        out_specs=VMEM,
        compiler_params=SMALL,
        cost_estimate=pl.CostEstimate(
            flops=2 * rows.size * plan.width,
            bytes_accessed=2 * rows.shape[1] * plan.width,
            transcendentals=0,
        ),
        name="own",
    )(weight, rows, after)


def split_kernel(mine_ref, stream_ref, *refs):
    req = stream_ref.shape[0]
    count = mine_ref.shape[0] // req
    arrived, outs = refs[:-count], refs[-count:]
    total = mine_ref[...]
    for a in arrived:
        total = total + a[...].astype(F32)
    outs[0][...] = total[:req] + stream_ref[...]
    for j in range(1, count):
        outs[j][...] = total[j * req : (j + 1) * req].astype(BF16)


def split(mine, stream, arrived):
    req, width = stream.shape
    count = mine.shape[0] // req
    return pl.pallas_call(
        split_kernel,
        out_shape=[jax.ShapeDtypeStruct((req, width), F32)]
        + [jax.ShapeDtypeStruct((req, width), BF16)] * (count - 1),
        in_specs=[VMEM] * (2 + len(arrived)),
        out_specs=[VMEM] * count,
        compiler_params=SMALL,
        name="split",
    )(mine, stream, *arrived)


def body(
    latent_cache,
    queries,
    new_latent,
    context_len,
    block_start,
    owner,
    value_up,
    out_proj,
    residual_in,
    norm_gain,
    gate_up,
    down_weight,
):
    n_wide = lax.axis_size("wide")
    n_sub = lax.axis_size("sub")
    n_pair = lax.axis_size("pair")
    req_grp = latent_cache.shape[0]
    width_dev = residual_in.shape[1]

    powers = [k for k in range(1, n_wide) if k & (k - 1) == 0]
    arrived = {k: hop(queries, "wide", k) for k in reversed(powers)}
    units = down_weight.shape[0]
    plan = Plan(
        width=width_dev,
        units=units,
        full=units - 128 if units % 256 == 128 else units,
        depth=out_proj.shape[0] * out_proj.shape[1],
        wide=D,
    )
    payload, bias, gain, residual, order, cache = prepare(
        context_len,
        block_start,
        owner,
        norm_gain,
        queries,
        latent_cache,
        new_latent,
        residual_in,
    )
    proj = out_proj.reshape(plan.depth, D)

    kinds = ("gate", "rest", "up") if plan.full < units else ("gate", "up")
    held = {}

    def bring(items, after):
        got = fetch(items, plan, gate_up, proj, after)
        held.update(got)
        return got[items[-1]]

    far = list(range(n_wide - 1, -1, -1))
    queue = [("out", k) for k in far] + [(kind, k) for k in range(n_wide) for kind in kinds]

    def take(count):
        items = queue[:count]
        del queue[:count]
        return items

    payloads = [payload]
    payload = bring(take(n_wide // 2), payload)
    waited = False
    for k in range(1, n_wide):
        if k not in arrived:
            low = k & -k
            arrived[k] = hop(arrived[k - low], "wide", low)
            if not waited:
                payload = bring(take(n_wide // 2), payload)
                waited = True
        elif k > 1:
            arrived[k], payload = lax.optimization_barrier((arrived[k], payload))
        payload = attend(arrived[k], cache, bias, payload)
        payloads.append(payload)
    last = bring(take(1), payload)
    payloads[1], last = lax.optimization_barrier((payloads[1], last))
    last = bring(take(3), last)
    payloads = [payloads[0]] + [hop(payloads[k], "wide", k) for k in range(1, n_wide)]
    chunks = combine(order, last, payloads, req_grp, n_sub)

    peers = [(ks, kp) for kp in range(n_pair) for ks in range(n_sub)]
    masks = [ks * n_pair + kp for ks, kp in peers]
    pieces = [chunks[0]] + [hop_group(chunks[ks], ks * n_pair + kp) for ks, kp in peers[1:]]
    last = bring(take(2), chunks[0])
    vals, sends, got = project(
        pieces,
        jnp.swapaxes(value_up, 1, 2),
        [held["out", k] for k in range(1, n_wide)],
        take(2),
        plan,
        gate_up,
        proj,
        last,
    )
    held.update(got)

    back = [hop(send, "wide", k + 1) for k, send in enumerate(sends)]
    last = bring(take(2), vals)
    mine = own(held["out", 0], vals, last, plan)
    total, send = merge(mine, residual, last, back)
    back = [hop_group(send, k) for k in masks[1:]]
    last = bring(take(len(queue)), send)
    gained, stream = norm(total, gain, last, back, req_grp)

    carry = ()
    for k in range(n_wide):
        x = hop(gained, "wide", k) if k else gained
        weights = [held[item] for item in (("gate", k), ("up", k), ("rest", k)) if item in held]
        carry = gate(x, weights, carry, plan)
    away = far[:-1]
    hidden, *sends = down(down_weight, carry, away, plan)
    back = [hop(send, "wide", k) for k, send in zip(away, sends)]
    mine = own(down_weight, hidden, sends[-1], plan)
    out, *sends = split(mine, stream, back)
    for k, send in zip(masks[1:], sends):
        out = out + hop_group(send, k).astype(F32)
    return out.astype(BF16)


def solution(mesh):
    in_specs = (
        P(("groups", "sub", "pair"), "wide", None),
        P(("groups", "sub", "pair"), "wide", None),
        P(("groups", "sub", "pair"), None),
        P(("groups", "sub", "pair")),
        P(("groups", "sub", "pair"), None),
        P("groups"),
        P(("wide", "sub"), None, "pair"),
        P(("wide", "sub"), "pair", None),
        P(("groups", "sub", "pair"), "wide"),
        P("wide"),
        P(None, None, ("wide", "sub", "pair")),
        P(("wide", "sub", "pair"), None),
    )
    out_specs = P(("groups", "sub", "pair"), "wide")
    return jax.shard_map(body, mesh=mesh, in_specs=in_specs, out_specs=out_specs, check_vma=False)
```

```python
import collections
import functools
import math

import jax
import jax.numpy as jnp
from jax import lax
from jax.experimental import pallas as pl
from jax.experimental.pallas import tpu as pltpu
from jax.sharding import PartitionSpec as P

D = 7168
KV_RANK = 512
ROPE = 64
NOPE = 128
F32 = jnp.float32
BF16 = jnp.bfloat16
TAIL = 8
VMEM = pl.BlockSpec(memory_space=pltpu.VMEM)
SMEM = pl.BlockSpec(memory_space=pltpu.SMEM)
ANY = pl.BlockSpec(memory_space=pl.ANY)
HBM = pl.BlockSpec(memory_space=pltpu.HBM)
SMALL = pltpu.CompilerParams(vmem_limit_bytes=4 * 2**20)


def hop(x, axis, k):
    n = lax.axis_size(axis)
    return lax.ppermute(x, axis, [(i, i ^ k) for i in range(n)])


def hop_group(x, k):
    n = lax.axis_size("sub") * lax.axis_size("pair")
    return lax.ppermute(x, ("sub", "pair"), [(i, i ^ k) for i in range(n)])


def in_hbm(x):
    return pltpu.with_memory_space_constraint(x, pltpu.HBM)


Plan = collections.namedtuple("Plan", ["width", "units", "full", "depth", "wide"])


def aligned(plan):
    return plan.width % 128 == 0


def item_shape(item, plan):
    kind, k = item
    cols = plan.width if aligned(plan) else plan.wide
    if kind == "out":
        return (plan.depth, cols)
    if kind == "rest":
        return (plan.width, 2 * (plan.units - plan.full))
    return (plan.width, plan.full)


def item_copies(item, plan, source, out):
    kind, k = item
    start = (lax.axis_index("wide") ^ k) * plan.width
    if kind == "out":
        if not aligned(plan):
            return [(source, out)]
        return [(source.at[:, pl.ds(pl.multiple_of(start, 128), plan.width)], out)]
    rows = pl.ds(pl.multiple_of(start, 64), plan.width)
    if kind == "rest":
        half = plan.units - plan.full
        return [
            (source.at[g, rows, plan.full :], out.at[:, g * half : (g + 1) * half])
            for g in range(2)
        ]
    return [(source.at[int(kind == "up"), rows, : plan.full], out)]


def start_items(items, plan, both, proj, outs, sems):
    pairs = []
    for item, out in zip(items, outs):
        pairs += item_copies(item, plan, proj if item[0] == "out" else both, out)
    copies = [
        pltpu.make_async_copy(source, out, sems.at[i]) for i, (source, out) in enumerate(pairs)
    ]

    @pl.when(lax.axis_index("wide") >= 0)
    def _():
        for copy in copies:
            copy.start()

    return copies


def item_shapes(items, plan):
    return [pltpu.VMEM(item_shape(item, plan), BF16) for item in items]


def item_sems(items):
    return pltpu.SemaphoreType.DMA((max(1, sum(2 if i[0] == "rest" else 1 for i in items)),))


def column_block(ref, k, plan, at):
    me = lax.axis_index("wide")
    if ref.shape[1] == plan.width:
        return ref[:, at]
    if aligned(plan):
        return ref[:, pl.ds(pl.multiple_of((me ^ k) * plan.width, 128), plan.width)]
    block = ref[:, : plan.width]
    for w in range(1, plan.wide // plan.width):
        block = jnp.where((me ^ k) == w, ref[:, w * plan.width : (w + 1) * plan.width], block)
    return block


def in_tiles(loop, cols, work):
    if not loop or cols % 256:
        work(pl.ds(0, cols))
        return

    @pl.loop(0, cols // 256)
    def _(i):
        work(pl.ds(pl.multiple_of(i * 256, 256), 256))


def eye(rows, cols):
    row = lax.broadcasted_iota(jnp.int32, (rows, cols), 0)
    col = lax.broadcasted_iota(jnp.int32, (rows, cols), 1)
    return (row == col).astype(BF16)


def partial_scores(q_ref, cache_ref, bias):
    req, heads, latent = q_ref.shape
    scores = [
        lax.dot_general(
            q_ref[r], cache_ref[r], (((1,), (1,)), ((), ())), preferred_element_type=F32
        )
        * (NOPE + ROPE) ** (-0.5)
        + bias[r : r + 1, :]
        for r in range(req)
    ]
    return jnp.concatenate(scores, axis=0)


def partial_sums(expo, cache_ref, heads):
    expo = expo.astype(BF16)
    sums = [
        jnp.dot(
            expo[r * heads : (r + 1) * heads],
            cache_ref[r, :, :KV_RANK],
            preferred_element_type=F32,
        )
        for r in range(cache_ref.shape[0])
    ]
    return jnp.concatenate(sums, axis=0)


def payload_tail(lse):
    rows = lse.shape[0]
    hi = lse.astype(BF16).astype(F32)
    mid = (lse - hi).astype(BF16).astype(F32)
    lo = (lse - hi - mid).astype(BF16).astype(F32)
    lane = lax.broadcasted_iota(jnp.int32, (rows, 128), 1)
    spread = jnp.where(lane == 0, hi, jnp.where(lane == 1, mid, jnp.where(lane == 2, lo, 0.0)))
    turned = lax.dot_general(
        spread.astype(BF16), eye(rows, 128), (((0,), (0,)), ((), ())), preferred_element_type=F32
    )
    return jnp.pad(turned[:TAIL], ((0, 0), (0, KV_RANK - 128)))


def prepare_kernel(
    n_wide,
    length_hbm,
    start_hbm,
    owner_hbm,
    gain_hbm,
    q_hbm,
    cache_hbm,
    fresh_hbm,
    residual_hbm,
    out_ref,
    bias_ref,
    gain_out_ref,
    residual_out_ref,
    order_ref,
    cache_ref,
    *refs,
):
    length_ref, start_ref, owner_ref, gain_ref, q_ref, fresh_ref, residual_ref, sems = refs
    copies = [
        pltpu.make_async_copy(source, target, sems.at[i])
        for i, (source, target) in enumerate(
            [
                (length_hbm, length_ref),
                (start_hbm, start_ref),
                (owner_hbm, owner_ref),
                (gain_hbm, gain_ref),
                (q_hbm, q_ref),
                (cache_hbm, cache_ref),
                (fresh_hbm, fresh_ref),
                (residual_hbm, residual_ref),
            ]
        )
    ]
    for copy in copies:
        copy.start()
    for copy in copies[:4]:
        copy.wait()
    req, heads, latent = q_ref.shape
    block = cache_ref.shape[1]
    width = gain_ref.shape[0]
    me, me_sub = lax.axis_index("wide"), lax.axis_index("sub")
    group = me_sub * lax.axis_size("pair") + lax.axis_index("pair")

    owners = [owner_ref[group * req + r] for r in range(req)]
    placed = []
    for r in range(req):
        at = jnp.int32(0)
        for j in range(req):
            if j != r:
                ahead = owners[j] <= owners[r] if j < r else owners[j] < owners[r]
                at = at + jnp.where(ahead, 1, 0)
        placed.append(at)
        order_ref[r] = at

    gain_out_ref[...] = gain_ref[...].reshape(1, width).astype(F32)

    biases = []
    for r in range(req):
        following = jnp.where(
            me == n_wide - 1, length_ref[r], start_ref[r, jnp.minimum(me + 1, n_wide - 1)]
        )
        position = lax.broadcasted_iota(jnp.int32, (1, block), 1)
        biases.append(jnp.where(position < following - start_ref[r, me], 0.0, F32(-1e30)))
    bias = jnp.concatenate(biases, axis=0)
    bias_ref[...] = bias

    for copy in copies[4:]:
        copy.wait()
    rows = []
    for i in range(req):
        row = jnp.zeros((1, width), F32)
        for r in range(req):
            row = jnp.where(placed[r] == i, residual_ref[r : r + 1, :].astype(F32), row)
        rows.append(row)
    residual_out_ref[...] = jnp.concatenate(rows, axis=0)

    scores = partial_scores(q_ref, cache_ref, bias)
    fresh = [fresh_ref[r : r + 1, :].astype(F32) for r in range(req)]
    own = jnp.concatenate(
        [
            jnp.sum(q_ref[r].astype(F32) * fresh[r], axis=1, keepdims=True)
            * (NOPE + ROPE) ** (-0.5)
            for r in range(req)
        ],
        axis=0,
    )
    top = jnp.maximum(jnp.max(scores, axis=1, keepdims=True), own)
    expo = jnp.exp(scores - top)
    expo_own = jnp.exp(own - top)
    den = jnp.sum(expo, axis=1, keepdims=True) + expo_own
    weight_own = expo_own.astype(BF16).astype(F32)
    num = partial_sums(expo, cache_ref, heads) + jnp.concatenate(
        [weight_own[r * heads : (r + 1) * heads] * fresh[r][:, :KV_RANK] for r in range(req)],
        axis=0,
    )
    count = req * heads
    out_ref[:count, :] = (num / den).astype(BF16)
    out_ref[count:, :] = payload_tail(top + jnp.log(den)).astype(BF16)


def attend_cost(req, heads, block, latent):
    return pl.CostEstimate(
        flops=2 * req * heads * block * (latent + KV_RANK),
        bytes_accessed=2 * req * (block * latent + heads * (latent + KV_RANK)),
        transcendentals=req * heads * block,
    )


def prepare(length, start, owner, gain, q, cache, fresh, residual):
    req, heads, latent = q.shape
    block, width = cache.shape[1], residual.shape[1]
    n_wide = start.shape[1]
    operands = (length, start, owner, gain, q, cache, fresh, residual)
    return pl.pallas_call(
        functools.partial(prepare_kernel, n_wide),
        out_shape=[
            jax.ShapeDtypeStruct((req * heads + TAIL, KV_RANK), BF16),
            jax.ShapeDtypeStruct((req, block), F32),
            jax.ShapeDtypeStruct((1, width), F32),
            jax.ShapeDtypeStruct((req, width), F32),
            jax.ShapeDtypeStruct((req,), jnp.int32),
            pltpu.VMEM(cache.shape, BF16),
        ],
        in_specs=[HBM] * len(operands),
        out_specs=[VMEM] * 4 + [SMEM, VMEM],
        scratch_shapes=[
            pltpu.SMEM(length.shape, jnp.int32),
            pltpu.SMEM(start.shape, jnp.int32),
            pltpu.SMEM(owner.shape, jnp.int32),
            pltpu.VMEM(gain.shape, BF16),
            pltpu.VMEM(q.shape, BF16),
            pltpu.VMEM(fresh.shape, BF16),
            pltpu.VMEM(residual.shape, BF16),
            pltpu.SemaphoreType.DMA((len(operands),)),
        ],
        compiler_params=SMALL,
        cost_estimate=pl.CostEstimate(
            flops=2 * req * heads * block * (latent + KV_RANK),
            bytes_accessed=2 * (cache.size + q.size),
            transcendentals=req * heads * block,
        ),
        name="prepare",
    )(*[in_hbm(x) for x in operands])


def attend_kernel(q_ref, cache_ref, bias_ref, after_ref, out_ref):
    req, heads, latent = q_ref.shape
    scores = partial_scores(q_ref, cache_ref, bias_ref[...])
    top = jnp.max(scores, axis=1, keepdims=True)
    expo = jnp.exp(scores - top)
    den = jnp.sum(expo, axis=1, keepdims=True)
    num = partial_sums(expo, cache_ref, heads)
    count = req * heads
    out_ref[:count, :] = (num / den).astype(BF16)
    out_ref[count:, :] = payload_tail(top + jnp.log(den)).astype(BF16)


def attend(q, cache, bias, after):
    req, heads, latent = q.shape
    return pl.pallas_call(
        attend_kernel,
        out_shape=jax.ShapeDtypeStruct((req * heads + TAIL, KV_RANK), BF16),
        in_specs=[VMEM] * 3 + [ANY],
        out_specs=VMEM,
        compiler_params=SMALL,
        cost_estimate=attend_cost(req, heads, cache.shape[1], latent),
        name="attend",
    )(q, cache, bias, after)


def fetch_kernel(items, plan, both_hbm, proj_hbm, after_ref, *refs):
    for copy in start_items(items, plan, both_hbm, proj_hbm, refs[:-1], refs[-1]):
        copy.wait()


def fetch(items, plan, both, proj, after):
    shapes = item_shapes(items, plan)
    out = pl.pallas_call(
        functools.partial(fetch_kernel, items, plan),
        out_shape=shapes,
        in_specs=[HBM, HBM, ANY],
        out_specs=[VMEM] * len(items),
        scratch_shapes=[item_sems(items)],
        compiler_params=SMALL,
        cost_estimate=pl.CostEstimate(
            flops=0,
            bytes_accessed=2 * sum(math.prod(shape.shape) for shape in shapes),
            transcendentals=0,
        ),
        name="fetch",
    )(in_hbm(both), in_hbm(proj), after)
    return dict(zip(items, out))


def combine_kernel(n_wide, n_sub, req, order_any, after_ref, *refs):
    payloads, outs = refs[:n_wide], refs[n_wide : n_wide + n_sub]
    hold, order_ref, sem = refs[n_wide + n_sub :]
    copy = pltpu.make_async_copy(order_any, order_ref, sem)
    copy.start()
    rows = payloads[0].shape[0] - TAIL
    heads = rows // req
    heads_dev = heads // n_sub
    me_sub = lax.axis_index("sub")
    tails = [p[rows:, :].astype(F32) for p in payloads]
    lses = []
    for tail in tails:
        turned = lax.dot_general(
            eye(rows, 128),
            tail[:, :128].astype(BF16),
            (((1,), (1,)), ((), ())),
            preferred_element_type=F32,
        )
        lses.append(turned[:, 0:1] + turned[:, 1:2] + turned[:, 2:3])
    top = functools.reduce(jnp.maximum, lses)
    weights = [jnp.exp(lse - top) for lse in lses]
    inv = 1.0 / functools.reduce(jnp.add, weights)
    weights = [weight * inv for weight in weights]
    copy.wait()
    for r in range(req):
        at = slice(r * heads, (r + 1) * heads)
        attn = functools.reduce(
            jnp.add, [w[at] * p[at, :].astype(F32) for w, p in zip(weights, payloads)]
        ).astype(BF16)
        for s in range(n_sub):
            hold[s, order_ref[r]] = attn[s * heads_dev : (s + 1) * heads_dev]
    for k in range(n_sub):
        outs[k][...] = hold[me_sub ^ k]


def combine(order, after, payloads, req, n_sub):
    n_wide = len(payloads)
    heads_dev = (payloads[0].shape[0] - TAIL) // req // n_sub
    piece = jax.ShapeDtypeStruct((req, heads_dev, KV_RANK), BF16)
    return pl.pallas_call(
        functools.partial(combine_kernel, n_wide, n_sub, req),
        out_shape=[piece] * n_sub,
        in_specs=[ANY, ANY] + [VMEM] * n_wide,
        out_specs=[VMEM] * n_sub,
        scratch_shapes=[
            pltpu.VMEM((n_sub, req, heads_dev, KV_RANK), BF16),
            pltpu.SMEM(order.shape, jnp.int32),
            pltpu.SemaphoreType.DMA(()),
        ],
        compiler_params=SMALL,
        name="combine",
    )(order, after, *payloads)


def project_kernel(count, items, plan, up_ref, both_hbm, proj_hbm, after_ref, *refs):
    n_wide = plan.wide // plan.width - 1
    pieces, weights, refs = refs[:count], refs[count : count + n_wide], refs[count + n_wide :]
    vals, outs, fetched, sems = refs[0], refs[1 : n_wide + 1], refs[n_wide + 1 : -1], refs[-1]
    copies = start_items(items, plan, both_hbm, proj_hbm, fetched, sems)
    req, heads, rank = pieces[0].shape
    rows = count * req
    cols = up_ref.shape[1]
    stacked = jnp.concatenate([p[...].reshape(req * heads, rank) for p in pieces], axis=0)
    total = rows * heads
    to = lax.broadcasted_iota(jnp.int32, (total, total), 0)
    source = lax.broadcasted_iota(jnp.int32, (total, total), 1)
    turn = (to // rows == source % heads) & (to % rows == source // heads)
    turned = jnp.dot(turn.astype(BF16), stacked, preferred_element_type=F32).astype(BF16)
    some = math.gcd(heads, max(1, 256 // cols))
    for first in range(0, heads, some):
        val = lax.dot_general(
            turned[first * rows : (first + some) * rows],
            up_ref[first : first + some].reshape(some * cols, rank),
            (((1,), (1,)), ((), ())),
            preferred_element_type=F32,
        ).astype(BF16)
        for i in range(some):
            at = slice((first + i) * cols, (first + i + 1) * cols)
            vals[:, at] = val[i * rows : (i + 1) * rows, i * cols : (i + 1) * cols]

    def work(at):
        for k in range(n_wide):
            block = column_block(weights[k], k + 1, plan, at)
            out = jnp.dot(vals[...], block, preferred_element_type=F32)
            outs[k][:, at] = out.astype(outs[k].dtype)

    in_tiles(items, plan.width, work)
    for copy in copies:
        copy.wait()


def project(pieces, value_up, weights, items, plan, both, proj, after):
    count = len(pieces)
    req, heads, rank = pieces[0].shape
    rows = count * req
    n_wide = len(weights)
    out = pl.pallas_call(
        functools.partial(project_kernel, count, items, plan),
        out_shape=[jax.ShapeDtypeStruct((rows, plan.depth), BF16)]
        + [jax.ShapeDtypeStruct((rows, plan.width), BF16)] * n_wide
        + item_shapes(items, plan),
        in_specs=[VMEM, HBM, HBM, ANY] + [VMEM] * (count + n_wide),
        out_specs=[VMEM] * (n_wide + 1 + len(items)),
        scratch_shapes=[item_sems(items)],
        compiler_params=SMALL,
        cost_estimate=pl.CostEstimate(
            flops=2 * rows * plan.depth * plan.wide,
            bytes_accessed=2 * plan.depth * plan.wide,
            transcendentals=0,
        ),
        name="project",
    )(value_up, in_hbm(both), in_hbm(proj), after, *pieces, *weights)
    return out[0], out[1 : n_wide + 1], dict(zip(items, out[n_wide + 1 :]))


def merge_kernel(mine_ref, residual_ref, after_ref, *refs):
    arrived, (total_ref, send_ref) = refs[:-2], refs[-2:]
    req = residual_ref.shape[0]
    total = mine_ref[...]
    for a in arrived:
        total = total + a[...].astype(F32)
    total_ref[...] = total
    total_ref[:req, :] = total[:req] + residual_ref[...]
    send_ref[...] = total_ref[...].astype(BF16)


def merge(mine, residual, after, arrived):
    return pl.pallas_call(
        merge_kernel,
        out_shape=[jax.ShapeDtypeStruct(mine.shape, F32), jax.ShapeDtypeStruct(mine.shape, BF16)],
        in_specs=[VMEM, VMEM, ANY] + [VMEM] * len(arrived),
        out_specs=[VMEM] * 2,
        compiler_params=SMALL,
        name="merge",
    )(mine, residual, after, *arrived)


def norm_kernel(req, mine_ref, gain_ref, after_ref, *refs):
    arrived, (gained_ref, stream_ref) = refs[:-2], refs[-2:]
    width = mine_ref.shape[1]
    blocks = [mine_ref[i * req : (i + 1) * req, :] for i in range(len(arrived) + 1)]
    for j, a in enumerate(arrived):
        others = a[...].astype(F32)
        for i in range(len(blocks)):
            at = (i ^ (j + 1)) * req
            blocks[i] = blocks[i] + others[at : at + req]
    stream_ref[...] = blocks[0]
    total = jnp.concatenate(blocks, axis=0)
    gained_ref[:, :width] = (total * gain_ref[...]).astype(BF16)
    square = jnp.sum(total * total, axis=1, keepdims=True)
    hi = square.astype(BF16).astype(F32)
    mid = (square - hi).astype(BF16).astype(F32)
    lo = (square - hi - mid).astype(BF16).astype(F32)
    lane = lax.broadcasted_iota(jnp.int32, (total.shape[0], 128), 1)
    spread = jnp.where(lane == 0, hi, jnp.where(lane == 1, mid, jnp.where(lane == 2, lo, 0.0)))
    gained_ref[:, width:] = spread.astype(BF16)


def norm(mine, gain, after, arrived, req):
    rows, width = mine.shape
    return pl.pallas_call(
        functools.partial(norm_kernel, req),
        out_shape=[
            jax.ShapeDtypeStruct((rows, width + 128), BF16),
            jax.ShapeDtypeStruct((req, width), F32),
        ],
        in_specs=[VMEM, VMEM, ANY] + [VMEM] * len(arrived),
        out_specs=[VMEM] * 2,
        compiler_params=SMALL,
        name="norm",
    )(mine, gain, after, *arrived)


def gate_kernel(count, first, plan, x_ref, later_ref, *refs):
    weights, carry, outs = refs[:count], refs[count : -count - 1], refs[-count - 1 :]
    square = x_ref[:, plan.width :].astype(F32)
    outs[count][...] = square if first else square + carry[count][...]
    x = x_ref[:, : plan.width]

    def multiply(i, at):
        product = jnp.dot(x, weights[i][:, at], preferred_element_type=F32)
        outs[i][:, at] = product if first else product + carry[i][:, at]

    def work(at):
        multiply(0, at)
        multiply(1, at)

    in_tiles(False, plan.full, work)
    for i in range(2, count):
        multiply(i, pl.ds(0, weights[i].shape[1]))


def gate(x, weights, carry, later, plan):
    rows = x.shape[0]
    count = len(weights)
    return pl.pallas_call(
        functools.partial(gate_kernel, count, not carry, plan),
        out_shape=[jax.ShapeDtypeStruct((rows, w.shape[1]), F32) for w in weights]
        + [jax.ShapeDtypeStruct((rows, 128), F32)],
        in_specs=[VMEM] * (2 + count + len(carry)),
        out_specs=[VMEM] * (count + 1),
        compiler_params=SMALL,
        cost_estimate=pl.CostEstimate(
            flops=4 * rows * plan.width * plan.units,
            bytes_accessed=4 * plan.width * plan.units,
            transcendentals=0,
        ),
        name="gate",
    )(x, later, *weights, *carry)


def hidden_units(plan, operands):
    *sums, square_ref = operands
    square = square_ref[:, 0:1] + square_ref[:, 1:2] + square_ref[:, 2:3]
    inv = lax.rsqrt(square / D + 1e-06)
    both = [sums[0][...], sums[1][...]]
    if len(sums) > 2:
        half = plan.units - plan.full
        both = [
            jnp.concatenate([part, sums[2][:, g * half : (g + 1) * half]], axis=1)
            for g, part in enumerate(both)
        ]
    g = both[0] * inv
    return (g / (1.0 + jnp.exp(-g)) * (both[1] * inv)).astype(BF16)


def down_kernel(ks, plan, weight_ref, *refs):
    operands, hidden_ref, outs = refs[: -1 - len(ks)], refs[-1 - len(ks)], refs[-len(ks) :]
    hidden = hidden_units(plan, operands)
    hidden_ref[...] = hidden
    for k, out in zip(ks, outs):
        block = column_block(weight_ref, k, plan, pl.ds(0, plan.width))
        out[...] = jnp.dot(hidden, block, preferred_element_type=F32).astype(BF16)


def down(weight, operands, ks, plan):
    rows = operands[0].shape[0]
    return pl.pallas_call(
        functools.partial(down_kernel, ks, plan),
        out_shape=[jax.ShapeDtypeStruct((rows, plan.units), BF16)]
        + [jax.ShapeDtypeStruct((rows, plan.width), BF16)] * len(ks),
        in_specs=[VMEM] * (1 + len(operands)),
        out_specs=[VMEM] * (1 + len(ks)),
        compiler_params=SMALL,
        cost_estimate=pl.CostEstimate(
            flops=2 * rows * plan.units * plan.width * len(ks),
            bytes_accessed=2 * plan.units * plan.width * len(ks),
            transcendentals=0,
        ),
        name="down",
    )(weight, *operands)


def own_kernel(plan, weight_ref, rows_ref, after_ref, out_ref):
    block = column_block(weight_ref, 0, plan, pl.ds(0, plan.width))
    out_ref[...] = jnp.dot(rows_ref[...], block, preferred_element_type=F32)


def own(weight, rows, after, plan):
    return pl.pallas_call(
        functools.partial(own_kernel, plan),
        out_shape=jax.ShapeDtypeStruct((rows.shape[0], plan.width), F32),
        in_specs=[VMEM, VMEM, ANY],
        out_specs=VMEM,
        compiler_params=SMALL,
        cost_estimate=pl.CostEstimate(
            flops=2 * rows.size * plan.width,
            bytes_accessed=2 * rows.shape[1] * plan.width,
            transcendentals=0,
        ),
        name="own",
    )(weight, rows, after)


def split_kernel(mine_ref, stream_ref, *refs):
    req = stream_ref.shape[0]
    count = mine_ref.shape[0] // req
    arrived, outs = refs[:-count], refs[-count:]
    total = mine_ref[...]
    for a in arrived:
        total = total + a[...].astype(F32)
    outs[0][...] = total[:req] + stream_ref[...]
    for j in range(1, count):
        outs[j][...] = total[j * req : (j + 1) * req].astype(BF16)


def split(mine, stream, arrived):
    req, width = stream.shape
    count = mine.shape[0] // req
    return pl.pallas_call(
        split_kernel,
        out_shape=[jax.ShapeDtypeStruct((req, width), F32)]
        + [jax.ShapeDtypeStruct((req, width), BF16)] * (count - 1),
        in_specs=[VMEM] * (2 + len(arrived)),
        out_specs=[VMEM] * count,
        compiler_params=SMALL,
        name="split",
    )(mine, stream, *arrived)


def body(
    latent_cache,
    queries,
    new_latent,
    context_len,
    block_start,
    owner,
    value_up,
    out_proj,
    residual_in,
    norm_gain,
    gate_up,
    down_weight,
):
    n_wide = lax.axis_size("wide")
    n_sub = lax.axis_size("sub")
    n_pair = lax.axis_size("pair")
    req_grp = latent_cache.shape[0]
    width_dev = residual_in.shape[1]

    powers = [k for k in range(1, n_wide) if k & (k - 1) == 0]
    arrived = {k: hop(queries, "wide", k) for k in reversed(powers)}
    units = down_weight.shape[0]
    plan = Plan(
        width=width_dev,
        units=units,
        full=units - 128 if units % 256 == 128 else units,
        depth=out_proj.shape[0] * out_proj.shape[1],
        wide=D,
    )
    payload, bias, gain, residual, order, cache = prepare(
        context_len,
        block_start,
        owner,
        norm_gain,
        queries,
        latent_cache,
        new_latent,
        residual_in,
    )
    proj = out_proj.reshape(plan.depth, D)

    kinds = ("gate", "rest", "up") if plan.full < units else ("gate", "up")
    held = {}

    def bring(items, after):
        got = fetch(items, plan, gate_up, proj, after)
        held.update(got)
        return got[items[-1]]

    far = list(range(n_wide - 1, -1, -1))
    queue = [("out", k) for k in far] + [(kind, k) for k in range(n_wide - 1) for kind in kinds]
    queue += [(kind, n_wide - 1) for kind in sorted(kinds, key=("rest", "gate", "up").index)]

    def take(count):
        items = queue[:count]
        del queue[:count]
        return items

    payloads = [payload]
    payload = bring(take(n_wide - 1), payload)
    waited = False
    for k in range(1, n_wide):
        if k not in arrived:
            low = k & -k
            arrived[k] = hop(arrived[k - low], "wide", low)
            if not waited:
                payload = bring(take(2), payload)
                waited = True
        elif k > 1:
            arrived[k], payload = lax.optimization_barrier((arrived[k], payload))
        payload = attend(arrived[k], cache, bias, payload)
        payloads.append(payload)
    last = bring(take(2), payload)
    payloads[1], last = lax.optimization_barrier((payloads[1], last))
    last = bring(take(3), last)
    payloads = [payloads[0]] + [hop(payloads[k], "wide", k) for k in range(1, n_wide)]
    chunks = combine(order, last, payloads, req_grp, n_sub)

    peers = [(ks, kp) for kp in range(n_pair) for ks in range(n_sub)]
    masks = [ks * n_pair + kp for ks, kp in peers]
    pieces = [chunks[0]] + [hop_group(chunks[ks], ks * n_pair + kp) for ks, kp in peers[1:]]
    last = bring(take(2), chunks[0])
    vals, sends, got = project(
        pieces,
        jnp.swapaxes(value_up, 1, 2),
        [held["out", k] for k in range(1, n_wide)],
        take(2),
        plan,
        gate_up,
        proj,
        last,
    )
    held.update(got)

    back = [hop(sends[k - 1], "wide", k) for k in range(n_wide - 1, 0, -1)]
    last = bring(take(len(queue)), vals)
    mine = own(held["out", 0], vals, last, plan)
    total, send = merge(mine, residual, last, back)
    back = [hop_group(send, k) for k in masks[1:]]
    gained, stream = norm(total, gain, last, back, req_grp)

    carry = ()
    for k in range(n_wide):
        x = hop(gained, "wide", k) if k else gained
        weights = [held[item] for item in (("gate", k), ("up", k), ("rest", k)) if item in held]
        carry = gate(x, weights, carry, down_weight, plan)
    away = far[:-1]
    hidden, *sends = down(down_weight, carry, away, plan)
    back = [hop(send, "wide", k) for k, send in zip(away, sends)]
    mine = own(down_weight, hidden, sends[-1], plan)
    out, *sends = split(mine, stream, back)
    for k, send in zip(masks[1:], sends):
        out = out + hop_group(send, k).astype(F32)
    return out.astype(BF16)


def solution(mesh):
    in_specs = (
        P(("groups", "sub", "pair"), "wide", None),
        P(("groups", "sub", "pair"), "wide", None),
        P(("groups", "sub", "pair"), None),
        P(("groups", "sub", "pair")),
        P(("groups", "sub", "pair"), None),
        P("groups"),
        P(("wide", "sub"), None, "pair"),
        P(("wide", "sub"), "pair", None),
        P(("groups", "sub", "pair"), "wide"),
        P("wide"),
        P(None, None, ("wide", "sub", "pair")),
        P(("wide", "sub", "pair"), None),
    )
    out_specs = P(("groups", "sub", "pair"), "wide")
    return jax.shard_map(body, mesh=mesh, in_specs=in_specs, out_specs=out_specs, check_vma=False)
```

```python
import collections
import functools
import math

import jax
import jax.numpy as jnp
from jax import lax
from jax.experimental import pallas as pl
from jax.experimental.pallas import tpu as pltpu
from jax.sharding import PartitionSpec as P

D = 7168
KV_RANK = 512
ROPE = 64
NOPE = 128
F32 = jnp.float32
BF16 = jnp.bfloat16
TAIL = 8
VMEM = pl.BlockSpec(memory_space=pltpu.VMEM)
SMEM = pl.BlockSpec(memory_space=pltpu.SMEM)
ANY = pl.BlockSpec(memory_space=pl.ANY)
HBM = pl.BlockSpec(memory_space=pltpu.HBM)
SMALL = pltpu.CompilerParams(vmem_limit_bytes=4 * 2**20)


def hop(x, axis, k):
    n = lax.axis_size(axis)
    return lax.ppermute(x, axis, [(i, i ^ k) for i in range(n)])


def hop_group(x, k):
    n = lax.axis_size("sub") * lax.axis_size("pair")
    return lax.ppermute(x, ("sub", "pair"), [(i, i ^ k) for i in range(n)])


def in_hbm(x):
    return pltpu.with_memory_space_constraint(x, pltpu.HBM)


Plan = collections.namedtuple("Plan", ["width", "units", "full", "depth", "wide"])


def aligned(plan):
    return plan.width % 128 == 0


def item_shape(item, plan):
    kind, k = item
    cols = plan.width if aligned(plan) else plan.wide
    if kind == "out":
        return (plan.depth, cols)
    if kind == "rest":
        return (plan.width, 2 * (plan.units - plan.full))
    return (plan.width, plan.full)


def item_copies(item, plan, source, out):
    kind, k = item
    start = (lax.axis_index("wide") ^ k) * plan.width
    if kind == "out":
        if not aligned(plan):
            return [(source, out)]
        return [(source.at[:, pl.ds(pl.multiple_of(start, 128), plan.width)], out)]
    rows = pl.ds(pl.multiple_of(start, 64), plan.width)
    if kind == "rest":
        half = plan.units - plan.full
        return [
            (source.at[g, rows, plan.full :], out.at[:, g * half : (g + 1) * half])
            for g in range(2)
        ]
    return [(source.at[int(kind == "up"), rows, : plan.full], out)]


def start_items(items, plan, both, proj, outs, sems):
    pairs = []
    for item, out in zip(items, outs):
        pairs += item_copies(item, plan, proj if item[0] == "out" else both, out)
    copies = [
        pltpu.make_async_copy(source, out, sems.at[i]) for i, (source, out) in enumerate(pairs)
    ]

    @pl.when(lax.axis_index("wide") >= 0)
    def _():
        for copy in copies:
            copy.start()

    return copies


def item_shapes(items, plan):
    return [pltpu.VMEM(item_shape(item, plan), BF16) for item in items]


def item_sems(items):
    return pltpu.SemaphoreType.DMA((max(1, sum(2 if i[0] == "rest" else 1 for i in items)),))


def column_block(ref, k, plan, at):
    me = lax.axis_index("wide")
    if ref.shape[1] == plan.width:
        return ref[:, at]
    if aligned(plan):
        return ref[:, pl.ds(pl.multiple_of((me ^ k) * plan.width, 128), plan.width)]
    block = ref[:, : plan.width]
    for w in range(1, plan.wide // plan.width):
        block = jnp.where((me ^ k) == w, ref[:, w * plan.width : (w + 1) * plan.width], block)
    return block


def in_tiles(loop, cols, work):
    if not loop or cols % 256:
        work(pl.ds(0, cols))
        return

    @pl.loop(0, cols // 256)
    def _(i):
        work(pl.ds(pl.multiple_of(i * 256, 256), 256))


def eye(rows, cols):
    row = lax.broadcasted_iota(jnp.int32, (rows, cols), 0)
    col = lax.broadcasted_iota(jnp.int32, (rows, cols), 1)
    return (row == col).astype(BF16)


def partial_scores(q_ref, cache_ref, bias):
    req, heads, latent = q_ref.shape
    scores = [
        lax.dot_general(
            q_ref[r], cache_ref[r], (((1,), (1,)), ((), ())), preferred_element_type=F32
        )
        * (NOPE + ROPE) ** (-0.5)
        + bias[r : r + 1, :]
        for r in range(req)
    ]
    return jnp.concatenate(scores, axis=0)


def partial_sums(expo, cache_ref, heads):
    expo = expo.astype(BF16)
    sums = [
        jnp.dot(
            expo[r * heads : (r + 1) * heads],
            cache_ref[r, :, :KV_RANK],
            preferred_element_type=F32,
        )
        for r in range(cache_ref.shape[0])
    ]
    return jnp.concatenate(sums, axis=0)


def payload_tail(lse):
    rows = lse.shape[0]
    hi = lse.astype(BF16).astype(F32)
    mid = (lse - hi).astype(BF16).astype(F32)
    lo = (lse - hi - mid).astype(BF16).astype(F32)
    lane = lax.broadcasted_iota(jnp.int32, (rows, 128), 1)
    spread = jnp.where(lane == 0, hi, jnp.where(lane == 1, mid, jnp.where(lane == 2, lo, 0.0)))
    turned = lax.dot_general(
        spread.astype(BF16), eye(rows, 128), (((0,), (0,)), ((), ())), preferred_element_type=F32
    )
    return jnp.pad(turned[:TAIL], ((0, 0), (0, KV_RANK - 128)))


def prepare_kernel(
    n_wide,
    length_hbm,
    start_hbm,
    owner_hbm,
    gain_hbm,
    q_hbm,
    cache_hbm,
    fresh_hbm,
    residual_hbm,
    out_ref,
    bias_ref,
    gain_out_ref,
    residual_out_ref,
    order_ref,
    cache_ref,
    *refs,
):
    length_ref, start_ref, owner_ref, gain_ref, q_ref, fresh_ref, residual_ref, sems = refs
    copies = [
        pltpu.make_async_copy(source, target, sems.at[i])
        for i, (source, target) in enumerate(
            [
                (length_hbm, length_ref),
                (start_hbm, start_ref),
                (owner_hbm, owner_ref),
                (gain_hbm, gain_ref),
                (q_hbm, q_ref),
                (cache_hbm, cache_ref),
                (fresh_hbm, fresh_ref),
                (residual_hbm, residual_ref),
            ]
        )
    ]
    for copy in copies:
        copy.start()
    for copy in copies[:4]:
        copy.wait()
    req, heads, latent = q_ref.shape
    block = cache_ref.shape[1]
    width = gain_ref.shape[0]
    me, me_sub = lax.axis_index("wide"), lax.axis_index("sub")
    group = me_sub * lax.axis_size("pair") + lax.axis_index("pair")

    owners = [owner_ref[group * req + r] for r in range(req)]
    placed = []
    for r in range(req):
        at = jnp.int32(0)
        for j in range(req):
            if j != r:
                ahead = owners[j] <= owners[r] if j < r else owners[j] < owners[r]
                at = at + jnp.where(ahead, 1, 0)
        placed.append(at)
        order_ref[r] = at

    gain_out_ref[...] = gain_ref[...].reshape(1, width).astype(F32)

    biases = []
    for r in range(req):
        following = jnp.where(
            me == n_wide - 1, length_ref[r], start_ref[r, jnp.minimum(me + 1, n_wide - 1)]
        )
        position = lax.broadcasted_iota(jnp.int32, (1, block), 1)
        biases.append(jnp.where(position < following - start_ref[r, me], 0.0, F32(-1e30)))
    bias = jnp.concatenate(biases, axis=0)
    bias_ref[...] = bias

    for copy in copies[4:]:
        copy.wait()
    rows = []
    for i in range(req):
        row = jnp.zeros((1, width), F32)
        for r in range(req):
            row = jnp.where(placed[r] == i, residual_ref[r : r + 1, :].astype(F32), row)
        rows.append(row)
    residual_out_ref[...] = jnp.concatenate(rows, axis=0)

    scores = partial_scores(q_ref, cache_ref, bias)
    fresh = [fresh_ref[r : r + 1, :].astype(F32) for r in range(req)]
    own = jnp.concatenate(
        [
            jnp.sum(q_ref[r].astype(F32) * fresh[r], axis=1, keepdims=True)
            * (NOPE + ROPE) ** (-0.5)
            for r in range(req)
        ],
        axis=0,
    )
    top = jnp.maximum(jnp.max(scores, axis=1, keepdims=True), own)
    expo = jnp.exp(scores - top)
    expo_own = jnp.exp(own - top)
    den = jnp.sum(expo, axis=1, keepdims=True) + expo_own
    weight_own = expo_own.astype(BF16).astype(F32)
    num = partial_sums(expo, cache_ref, heads) + jnp.concatenate(
        [weight_own[r * heads : (r + 1) * heads] * fresh[r][:, :KV_RANK] for r in range(req)],
        axis=0,
    )
    count = req * heads
    out_ref[:count, :] = (num / den).astype(BF16)
    out_ref[count:, :] = payload_tail(top + jnp.log(den)).astype(BF16)


def attend_cost(req, heads, block, latent):
    return pl.CostEstimate(
        flops=2 * req * heads * block * (latent + KV_RANK),
        bytes_accessed=2 * req * (block * latent + heads * (latent + KV_RANK)),
        transcendentals=req * heads * block,
    )


def prepare(length, start, owner, gain, q, cache, fresh, residual):
    req, heads, latent = q.shape
    block, width = cache.shape[1], residual.shape[1]
    n_wide = start.shape[1]
    operands = (length, start, owner, gain, q, cache, fresh, residual)
    return pl.pallas_call(
        functools.partial(prepare_kernel, n_wide),
        out_shape=[
            jax.ShapeDtypeStruct((req * heads + TAIL, KV_RANK), BF16),
            jax.ShapeDtypeStruct((req, block), F32),
            jax.ShapeDtypeStruct((1, width), F32),
            jax.ShapeDtypeStruct((req, width), F32),
            jax.ShapeDtypeStruct((req,), jnp.int32),
            pltpu.VMEM(cache.shape, BF16),
        ],
        in_specs=[HBM] * len(operands),
        out_specs=[VMEM] * 4 + [SMEM, VMEM],
        scratch_shapes=[
            pltpu.SMEM(length.shape, jnp.int32),
            pltpu.SMEM(start.shape, jnp.int32),
            pltpu.SMEM(owner.shape, jnp.int32),
            pltpu.VMEM(gain.shape, BF16),
            pltpu.VMEM(q.shape, BF16),
            pltpu.VMEM(fresh.shape, BF16),
            pltpu.VMEM(residual.shape, BF16),
            pltpu.SemaphoreType.DMA((len(operands),)),
        ],
        compiler_params=SMALL,
        cost_estimate=pl.CostEstimate(
            flops=2 * req * heads * block * (latent + KV_RANK),
            bytes_accessed=2 * (cache.size + q.size),
            transcendentals=req * heads * block,
        ),
        name="prepare",
    )(*[in_hbm(x) for x in operands])


def attend_kernel(q_ref, cache_ref, bias_ref, after_ref, out_ref):
    req, heads, latent = q_ref.shape
    scores = partial_scores(q_ref, cache_ref, bias_ref[...])
    top = jnp.max(scores, axis=1, keepdims=True)
    expo = jnp.exp(scores - top)
    den = jnp.sum(expo, axis=1, keepdims=True)
    num = partial_sums(expo, cache_ref, heads)
    count = req * heads
    out_ref[:count, :] = (num / den).astype(BF16)
    out_ref[count:, :] = payload_tail(top + jnp.log(den)).astype(BF16)


def attend(q, cache, bias, after):
    req, heads, latent = q.shape
    return pl.pallas_call(
        attend_kernel,
        out_shape=jax.ShapeDtypeStruct((req * heads + TAIL, KV_RANK), BF16),
        in_specs=[VMEM] * 3 + [ANY],
        out_specs=VMEM,
        compiler_params=SMALL,
        cost_estimate=attend_cost(req, heads, cache.shape[1], latent),
        name="attend",
    )(q, cache, bias, after)


def fetch_kernel(items, plan, both_hbm, proj_hbm, after_ref, *refs):
    for copy in start_items(items, plan, both_hbm, proj_hbm, refs[:-1], refs[-1]):
        copy.wait()


def fetch(items, plan, both, proj, after):
    shapes = item_shapes(items, plan)
    out = pl.pallas_call(
        functools.partial(fetch_kernel, items, plan),
        out_shape=shapes,
        in_specs=[HBM, HBM, ANY],
        out_specs=[VMEM] * len(items),
        scratch_shapes=[item_sems(items)],
        compiler_params=SMALL,
        cost_estimate=pl.CostEstimate(
            flops=0,
            bytes_accessed=2 * sum(math.prod(shape.shape) for shape in shapes),
            transcendentals=0,
        ),
        name="fetch",
    )(in_hbm(both), in_hbm(proj), after)
    return dict(zip(items, out))


def combine_kernel(n_wide, n_sub, req, order_any, after_ref, *refs):
    payloads, outs = refs[:n_wide], refs[n_wide : n_wide + n_sub]
    hold, order_ref, sem = refs[n_wide + n_sub :]
    copy = pltpu.make_async_copy(order_any, order_ref, sem)
    copy.start()
    rows = payloads[0].shape[0] - TAIL
    heads = rows // req
    heads_dev = heads // n_sub
    me_sub = lax.axis_index("sub")
    tails = [p[rows:, :].astype(F32) for p in payloads]
    lses = []
    for tail in tails:
        turned = lax.dot_general(
            eye(rows, 128),
            tail[:, :128].astype(BF16),
            (((1,), (1,)), ((), ())),
            preferred_element_type=F32,
        )
        lses.append(turned[:, 0:1] + turned[:, 1:2] + turned[:, 2:3])
    top = functools.reduce(jnp.maximum, lses)
    weights = [jnp.exp(lse - top) for lse in lses]
    inv = 1.0 / functools.reduce(jnp.add, weights)
    weights = [weight * inv for weight in weights]
    copy.wait()
    for r in range(req):
        at = slice(r * heads, (r + 1) * heads)
        attn = functools.reduce(
            jnp.add, [w[at] * p[at, :].astype(F32) for w, p in zip(weights, payloads)]
        ).astype(BF16)
        for s in range(n_sub):
            hold[s, order_ref[r]] = attn[s * heads_dev : (s + 1) * heads_dev]
    for k in range(n_sub):
        outs[k][...] = hold[me_sub ^ k]


def combine(order, after, payloads, req, n_sub):
    n_wide = len(payloads)
    heads_dev = (payloads[0].shape[0] - TAIL) // req // n_sub
    piece = jax.ShapeDtypeStruct((req, heads_dev, KV_RANK), BF16)
    return pl.pallas_call(
        functools.partial(combine_kernel, n_wide, n_sub, req),
        out_shape=[piece] * n_sub,
        in_specs=[ANY, ANY] + [VMEM] * n_wide,
        out_specs=[VMEM] * n_sub,
        scratch_shapes=[
            pltpu.VMEM((n_sub, req, heads_dev, KV_RANK), BF16),
            pltpu.SMEM(order.shape, jnp.int32),
            pltpu.SemaphoreType.DMA(()),
        ],
        compiler_params=SMALL,
        name="combine",
    )(order, after, *payloads)


def project_kernel(count, items, plan, up_ref, both_hbm, proj_hbm, after_ref, *refs):
    n_wide = plan.wide // plan.width - 1
    pieces, weights, refs = refs[:count], refs[count : count + n_wide], refs[count + n_wide :]
    vals, outs, fetched, sems = refs[0], refs[1 : n_wide + 1], refs[n_wide + 1 : -1], refs[-1]
    copies = start_items(items, plan, both_hbm, proj_hbm, fetched, sems)
    req, heads, rank = pieces[0].shape
    rows = count * req
    cols = up_ref.shape[1]
    stacked = jnp.concatenate([p[...].reshape(req * heads, rank) for p in pieces], axis=0)
    total = rows * heads
    to = lax.broadcasted_iota(jnp.int32, (total, total), 0)
    source = lax.broadcasted_iota(jnp.int32, (total, total), 1)
    turn = (to // rows == source % heads) & (to % rows == source // heads)
    turned = jnp.dot(turn.astype(BF16), stacked, preferred_element_type=F32).astype(BF16)
    some = math.gcd(heads, max(1, 256 // cols))
    for first in range(0, heads, some):
        val = lax.dot_general(
            turned[first * rows : (first + some) * rows],
            up_ref[first : first + some].reshape(some * cols, rank),
            (((1,), (1,)), ((), ())),
            preferred_element_type=F32,
        ).astype(BF16)
        for i in range(some):
            at = slice((first + i) * cols, (first + i + 1) * cols)
            vals[:, at] = val[i * rows : (i + 1) * rows, i * cols : (i + 1) * cols]

    def work(at):
        for k in range(n_wide):
            block = column_block(weights[k], k + 1, plan, at)
            out = jnp.dot(vals[...], block, preferred_element_type=F32)
            outs[k][:, at] = out.astype(outs[k].dtype)

    in_tiles(items, plan.width, work)
    for copy in copies:
        copy.wait()


def project(pieces, value_up, weights, items, plan, both, proj, after):
    count = len(pieces)
    req, heads, rank = pieces[0].shape
    rows = count * req
    n_wide = len(weights)
    out = pl.pallas_call(
        functools.partial(project_kernel, count, items, plan),
        out_shape=[jax.ShapeDtypeStruct((rows, plan.depth), BF16)]
        + [jax.ShapeDtypeStruct((rows, plan.width), BF16)] * n_wide
        + item_shapes(items, plan),
        in_specs=[VMEM, HBM, HBM, ANY] + [VMEM] * (count + n_wide),
        out_specs=[VMEM] * (n_wide + 1 + len(items)),
        scratch_shapes=[item_sems(items)],
        compiler_params=SMALL,
        cost_estimate=pl.CostEstimate(
            flops=2 * rows * plan.depth * plan.wide,
            bytes_accessed=2 * plan.depth * plan.wide,
            transcendentals=0,
        ),
        name="project",
    )(value_up, in_hbm(both), in_hbm(proj), after, *pieces, *weights)
    return out[0], out[1 : n_wide + 1], dict(zip(items, out[n_wide + 1 :]))


def merge_kernel(mine_ref, residual_ref, after_ref, *refs):
    arrived, (total_ref, send_ref) = refs[:-2], refs[-2:]
    req = residual_ref.shape[0]
    total = mine_ref[...]
    for a in arrived:
        total = total + a[...].astype(F32)
    total_ref[...] = total
    total_ref[:req, :] = total[:req] + residual_ref[...]
    send_ref[...] = total_ref[...].astype(BF16)


def merge(mine, residual, after, arrived):
    return pl.pallas_call(
        merge_kernel,
        out_shape=[jax.ShapeDtypeStruct(mine.shape, F32), jax.ShapeDtypeStruct(mine.shape, BF16)],
        in_specs=[VMEM, VMEM, ANY] + [VMEM] * len(arrived),
        out_specs=[VMEM] * 2,
        compiler_params=SMALL,
        name="merge",
    )(mine, residual, after, *arrived)


def norm_kernel(req, mine_ref, gain_ref, after_ref, *refs):
    arrived, (gained_ref, stream_ref) = refs[:-2], refs[-2:]
    width = mine_ref.shape[1]
    blocks = [mine_ref[i * req : (i + 1) * req, :] for i in range(len(arrived) + 1)]
    for j, a in enumerate(arrived):
        others = a[...].astype(F32)
        for i in range(len(blocks)):
            at = (i ^ (j + 1)) * req
            blocks[i] = blocks[i] + others[at : at + req]
    stream_ref[...] = blocks[0]
    total = jnp.concatenate(blocks, axis=0)
    gained_ref[:, :width] = (total * gain_ref[...]).astype(BF16)
    square = jnp.sum(total * total, axis=1, keepdims=True)
    hi = square.astype(BF16).astype(F32)
    mid = (square - hi).astype(BF16).astype(F32)
    lo = (square - hi - mid).astype(BF16).astype(F32)
    lane = lax.broadcasted_iota(jnp.int32, (total.shape[0], 128), 1)
    spread = jnp.where(lane == 0, hi, jnp.where(lane == 1, mid, jnp.where(lane == 2, lo, 0.0)))
    gained_ref[:, width:] = spread.astype(BF16)


def norm(mine, gain, after, arrived, req):
    rows, width = mine.shape
    return pl.pallas_call(
        functools.partial(norm_kernel, req),
        out_shape=[
            jax.ShapeDtypeStruct((rows, width + 128), BF16),
            jax.ShapeDtypeStruct((req, width), F32),
        ],
        in_specs=[VMEM, VMEM, ANY] + [VMEM] * len(arrived),
        out_specs=[VMEM] * 2,
        compiler_params=SMALL,
        name="norm",
    )(mine, gain, after, *arrived)


def gate_kernel(count, first, plan, x_ref, later_ref, *refs):
    weights, carry, outs = refs[:count], refs[count : -count - 1], refs[-count - 1 :]
    square = x_ref[:, plan.width :].astype(F32)
    outs[count][...] = square if first else square + carry[count][...]
    x = x_ref[:, : plan.width]

    def multiply(i, at):
        product = jnp.dot(x, weights[i][:, at], preferred_element_type=F32)
        outs[i][:, at] = product if first else product + carry[i][:, at]

    def work(at):
        multiply(0, at)
        multiply(1, at)

    in_tiles(False, plan.full, work)
    for i in range(2, count):
        multiply(i, pl.ds(0, weights[i].shape[1]))


def gate(x, weights, carry, later, plan):
    rows = x.shape[0]
    count = len(weights)
    return pl.pallas_call(
        functools.partial(gate_kernel, count, not carry, plan),
        out_shape=[jax.ShapeDtypeStruct((rows, w.shape[1]), F32) for w in weights]
        + [jax.ShapeDtypeStruct((rows, 128), F32)],
        in_specs=[VMEM] * (2 + count + len(carry)),
        out_specs=[VMEM] * (count + 1),
        compiler_params=SMALL,
        cost_estimate=pl.CostEstimate(
            flops=4 * rows * plan.width * plan.units,
            bytes_accessed=4 * plan.width * plan.units,
            transcendentals=0,
        ),
        name="gate",
    )(x, later, *weights, *carry)


def hidden_units(plan, operands):
    *sums, square_ref = operands
    square = square_ref[:, 0:1] + square_ref[:, 1:2] + square_ref[:, 2:3]
    inv = lax.rsqrt(square / D + 1e-06)
    both = [sums[0][...], sums[1][...]]
    if len(sums) > 2:
        half = plan.units - plan.full
        both = [
            jnp.concatenate([part, sums[2][:, g * half : (g + 1) * half]], axis=1)
            for g, part in enumerate(both)
        ]
    g = both[0] * inv
    return (g / (1.0 + jnp.exp(-g)) * (both[1] * inv)).astype(BF16)


def down_kernel(ks, plan, weight_ref, *refs):
    operands, hidden_ref, outs = refs[: -1 - len(ks)], refs[-1 - len(ks)], refs[-len(ks) :]
    hidden = hidden_units(plan, operands)
    hidden_ref[...] = hidden
    for k, out in zip(ks, outs):
        block = column_block(weight_ref, k, plan, pl.ds(0, plan.width))
        out[...] = jnp.dot(hidden, block, preferred_element_type=F32).astype(BF16)


def down(weight, operands, ks, plan):
    rows = operands[0].shape[0]
    return pl.pallas_call(
        functools.partial(down_kernel, ks, plan),
        out_shape=[jax.ShapeDtypeStruct((rows, plan.units), BF16)]
        + [jax.ShapeDtypeStruct((rows, plan.width), BF16)] * len(ks),
        in_specs=[VMEM] * (1 + len(operands)),
        out_specs=[VMEM] * (1 + len(ks)),
        compiler_params=SMALL,
        cost_estimate=pl.CostEstimate(
            flops=2 * rows * plan.units * plan.width * len(ks),
            bytes_accessed=2 * plan.units * plan.width * len(ks),
            transcendentals=0,
        ),
        name="down",
    )(weight, *operands)


def own_kernel(plan, weight_ref, rows_ref, after_ref, out_ref):
    block = column_block(weight_ref, 0, plan, pl.ds(0, plan.width))
    out_ref[...] = jnp.dot(rows_ref[...], block, preferred_element_type=F32)


def own(weight, rows, after, plan):
    return pl.pallas_call(
        functools.partial(own_kernel, plan),
        out_shape=jax.ShapeDtypeStruct((rows.shape[0], plan.width), F32),
        in_specs=[VMEM, VMEM, ANY],
        out_specs=VMEM,
        compiler_params=SMALL,
        cost_estimate=pl.CostEstimate(
            flops=2 * rows.size * plan.width,
            bytes_accessed=2 * rows.shape[1] * plan.width,
            transcendentals=0,
        ),
        name="own",
    )(weight, rows, after)


def split_kernel(mine_ref, stream_ref, *refs):
    req = stream_ref.shape[0]
    count = mine_ref.shape[0] // req
    arrived, outs = refs[:-count], refs[-count:]
    total = mine_ref[...]
    for a in arrived:
        total = total + a[...].astype(F32)
    outs[0][...] = total[:req] + stream_ref[...]
    for j in range(1, count):
        outs[j][...] = total[j * req : (j + 1) * req].astype(BF16)


def split(mine, stream, arrived):
    req, width = stream.shape
    count = mine.shape[0] // req
    return pl.pallas_call(
        split_kernel,
        out_shape=[jax.ShapeDtypeStruct((req, width), F32)]
        + [jax.ShapeDtypeStruct((req, width), BF16)] * (count - 1),
        in_specs=[VMEM] * (2 + len(arrived)),
        out_specs=[VMEM] * count,
        compiler_params=SMALL,
        name="split",
    )(mine, stream, *arrived)


def body(
    latent_cache,
    queries,
    new_latent,
    context_len,
    block_start,
    owner,
    value_up,
    out_proj,
    residual_in,
    norm_gain,
    gate_up,
    down_weight,
):
    n_wide = lax.axis_size("wide")
    n_sub = lax.axis_size("sub")
    n_pair = lax.axis_size("pair")
    req_grp = latent_cache.shape[0]
    width_dev = residual_in.shape[1]

    powers = [k for k in range(1, n_wide) if k & (k - 1) == 0]
    arrived = {k: hop(queries, "wide", k) for k in reversed(powers)}
    units = down_weight.shape[0]
    plan = Plan(
        width=width_dev,
        units=units,
        full=units - 128 if units % 256 == 128 else units,
        depth=out_proj.shape[0] * out_proj.shape[1],
        wide=D,
    )
    payload, bias, gain, residual, order, cache = prepare(
        context_len,
        block_start,
        owner,
        norm_gain,
        queries,
        latent_cache,
        new_latent,
        residual_in,
    )
    proj = out_proj.reshape(plan.depth, D)

    kinds = ("gate", "rest", "up") if plan.full < units else ("gate", "up")
    held = {}

    def bring(items, after):
        got = fetch(items, plan, gate_up, proj, after)
        held.update(got)
        return got[items[-1]]

    far = list(range(n_wide - 1, -1, -1))
    queue = [("out", k) for k in far] + [(kind, k) for k in range(n_wide - 1) for kind in kinds]
    queue += [(kind, n_wide - 1) for kind in sorted(kinds, key=("rest", "gate", "up").index)]

    def take(count):
        items = queue[:count]
        del queue[:count]
        return items

    payloads = [payload]
    payload = bring(take(n_wide - 1), payload)
    waited = False
    for k in range(1, n_wide):
        if k not in arrived:
            low = k & -k
            arrived[k] = hop(arrived[k - low], "wide", low)
            if not waited:
                payload = bring(take(2), payload)
                waited = True
        elif k > 1:
            arrived[k], payload = lax.optimization_barrier((arrived[k], payload))
        payload = attend(arrived[k], cache, bias, payload)
        payloads.append(payload)
    last = bring(take(2), payload)
    payloads[1], last = lax.optimization_barrier((payloads[1], last))
    last = bring(take(3), last)
    payloads = [payloads[0]] + [hop(payloads[k], "wide", k) for k in range(1, n_wide)]
    chunks = combine(order, last, payloads, req_grp, n_sub)

    peers = [(ks, kp) for kp in range(n_pair) for ks in range(n_sub)]
    masks = [ks * n_pair + kp for ks, kp in peers]
    pieces = [chunks[0]] + [hop_group(chunks[ks], ks * n_pair + kp) for ks, kp in peers[1:]]
    last = bring(take(2), chunks[0])
    vals, sends, got = project(
        pieces,
        jnp.swapaxes(value_up, 1, 2),
        [held["out", k] for k in range(1, n_wide)],
        take(2),
        plan,
        gate_up,
        proj,
        last,
    )
    held.update(got)

    back = [hop(sends[k - 1], "wide", k) for k in range(n_wide - 1, 0, -1)]
    mine = own(held["out", 0], vals, vals, plan)
    last = bring(take(1), mine)
    total, send = merge(mine, residual, last, back)
    back = [hop_group(send, k) for k in masks[1:]]
    last = bring(take(len(queue)), send)
    gained, stream = norm(total, gain, last, back, req_grp)

    carry = ()
    for k in range(n_wide):
        x = hop(gained, "wide", k) if k else gained
        weights = [held[item] for item in (("gate", k), ("up", k), ("rest", k)) if item in held]
        carry = gate(x, weights, carry, down_weight, plan)
    away = far[:-1]
    hidden, *sends = down(down_weight, carry, away, plan)
    back = [hop(send, "wide", k) for k, send in zip(away, sends)]
    mine = own(down_weight, hidden, sends[-1], plan)
    out, *sends = split(mine, stream, back)
    for k, send in zip(masks[1:], sends):
        out = out + hop_group(send, k).astype(F32)
    return out.astype(BF16)


def solution(mesh):
    in_specs = (
        P(("groups", "sub", "pair"), "wide", None),
        P(("groups", "sub", "pair"), "wide", None),
        P(("groups", "sub", "pair"), None),
        P(("groups", "sub", "pair")),
        P(("groups", "sub", "pair"), None),
        P("groups"),
        P(("wide", "sub"), None, "pair"),
        P(("wide", "sub"), "pair", None),
        P(("groups", "sub", "pair"), "wide"),
        P("wide"),
        P(None, None, ("wide", "sub", "pair")),
        P(("wide", "sub", "pair"), None),
    )
    out_specs = P(("groups", "sub", "pair"), "wide")
    return jax.shard_map(body, mesh=mesh, in_specs=in_specs, out_specs=out_specs, check_vma=False)
```

```python
import collections
import functools
import math

import jax
import jax.numpy as jnp
from jax import lax
from jax.experimental import pallas as pl
from jax.experimental.pallas import tpu as pltpu
from jax.sharding import PartitionSpec as P

D = 7168
KV_RANK = 512
ROPE = 64
NOPE = 128
F32 = jnp.float32
BF16 = jnp.bfloat16
TAIL = 8
VMEM = pl.BlockSpec(memory_space=pltpu.VMEM)
SMEM = pl.BlockSpec(memory_space=pltpu.SMEM)
ANY = pl.BlockSpec(memory_space=pl.ANY)
HBM = pl.BlockSpec(memory_space=pltpu.HBM)
SMALL = pltpu.CompilerParams(vmem_limit_bytes=4 * 2**20)


def hop(x, axis, k):
    n = lax.axis_size(axis)
    return lax.ppermute(x, axis, [(i, i ^ k) for i in range(n)])


def hop_group(x, k):
    n = lax.axis_size("sub") * lax.axis_size("pair")
    return lax.ppermute(x, ("sub", "pair"), [(i, i ^ k) for i in range(n)])


def in_hbm(x):
    return pltpu.with_memory_space_constraint(x, pltpu.HBM)


Plan = collections.namedtuple("Plan", ["width", "units", "full", "depth", "wide"])


def aligned(plan):
    return plan.width % 128 == 0


def item_shape(item, plan):
    kind, k = item
    cols = plan.width if aligned(plan) else plan.wide
    if kind == "out":
        return (plan.depth, cols)
    if kind == "rest":
        return (plan.width, 2 * (plan.units - plan.full))
    return (plan.width, plan.full)


def item_copies(item, plan, source, out):
    kind, k = item
    start = (lax.axis_index("wide") ^ k) * plan.width
    if kind == "out":
        if not aligned(plan):
            return [(source, out)]
        return [(source.at[:, pl.ds(pl.multiple_of(start, 128), plan.width)], out)]
    rows = pl.ds(pl.multiple_of(start, 64), plan.width)
    if kind == "rest":
        half = plan.units - plan.full
        return [
            (source.at[g, rows, plan.full :], out.at[:, g * half : (g + 1) * half])
            for g in range(2)
        ]
    return [(source.at[int(kind == "up"), rows, : plan.full], out)]


def start_items(items, plan, both, proj, outs, sems):
    pairs = []
    for item, out in zip(items, outs):
        pairs += item_copies(item, plan, proj if item[0] == "out" else both, out)
    copies = [
        pltpu.make_async_copy(source, out, sems.at[i]) for i, (source, out) in enumerate(pairs)
    ]

    @pl.when(lax.axis_index("wide") >= 0)
    def _():
        for copy in copies:
            copy.start()

    return copies


def item_shapes(items, plan):
    return [pltpu.VMEM(item_shape(item, plan), BF16) for item in items]


def item_sems(items):
    return pltpu.SemaphoreType.DMA((max(1, sum(2 if i[0] == "rest" else 1 for i in items)),))


def column_block(ref, k, plan, at):
    me = lax.axis_index("wide")
    if ref.shape[1] == plan.width:
        return ref[:, at]
    if aligned(plan):
        return ref[:, pl.ds(pl.multiple_of((me ^ k) * plan.width, 128), plan.width)]
    block = ref[:, : plan.width]
    for w in range(1, plan.wide // plan.width):
        block = jnp.where((me ^ k) == w, ref[:, w * plan.width : (w + 1) * plan.width], block)
    return block


def in_tiles(loop, cols, work):
    if not loop or cols % 256:
        work(pl.ds(0, cols))
        return

    @pl.loop(0, cols // 256)
    def _(i):
        work(pl.ds(pl.multiple_of(i * 256, 256), 256))


def eye(rows, cols):
    row = lax.broadcasted_iota(jnp.int32, (rows, cols), 0)
    col = lax.broadcasted_iota(jnp.int32, (rows, cols), 1)
    return (row == col).astype(BF16)


def partial_scores(q_ref, cache_ref, bias):
    req, heads, latent = q_ref.shape
    scores = [
        lax.dot_general(
            q_ref[r], cache_ref[r], (((1,), (1,)), ((), ())), preferred_element_type=F32
        )
        * (NOPE + ROPE) ** (-0.5)
        + bias[r : r + 1, :]
        for r in range(req)
    ]
    return jnp.concatenate(scores, axis=0)


def partial_sums(expo, cache_ref, heads):
    expo = expo.astype(BF16)
    sums = [
        jnp.dot(
            expo[r * heads : (r + 1) * heads],
            cache_ref[r, :, :KV_RANK],
            preferred_element_type=F32,
        )
        for r in range(cache_ref.shape[0])
    ]
    return jnp.concatenate(sums, axis=0)


def payload_tail(lse):
    rows = lse.shape[0]
    hi = lse.astype(BF16).astype(F32)
    mid = (lse - hi).astype(BF16).astype(F32)
    lo = (lse - hi - mid).astype(BF16).astype(F32)
    lane = lax.broadcasted_iota(jnp.int32, (rows, 128), 1)
    spread = jnp.where(lane == 0, hi, jnp.where(lane == 1, mid, jnp.where(lane == 2, lo, 0.0)))
    turned = lax.dot_general(
        spread.astype(BF16), eye(rows, 128), (((0,), (0,)), ((), ())), preferred_element_type=F32
    )
    return jnp.pad(turned[:TAIL], ((0, 0), (0, KV_RANK - 128)))


def prepare_kernel(
    n_wide,
    length_hbm,
    start_hbm,
    owner_hbm,
    gain_hbm,
    q_hbm,
    cache_hbm,
    fresh_hbm,
    residual_hbm,
    out_ref,
    bias_ref,
    gain_out_ref,
    residual_out_ref,
    order_ref,
    cache_ref,
    *refs,
):
    length_ref, start_ref, owner_ref, gain_ref, q_ref, fresh_ref, residual_ref, sems = refs
    copies = [
        pltpu.make_async_copy(source, target, sems.at[i])
        for i, (source, target) in enumerate(
            [
                (length_hbm, length_ref),
                (start_hbm, start_ref),
                (owner_hbm, owner_ref),
                (gain_hbm, gain_ref),
                (q_hbm, q_ref),
                (cache_hbm, cache_ref),
                (fresh_hbm, fresh_ref),
                (residual_hbm, residual_ref),
            ]
        )
    ]
    for copy in copies:
        copy.start()
    for copy in copies[:4]:
        copy.wait()
    req, heads, latent = q_ref.shape
    block = cache_ref.shape[1]
    width = gain_ref.shape[0]
    me, me_sub = lax.axis_index("wide"), lax.axis_index("sub")
    group = me_sub * lax.axis_size("pair") + lax.axis_index("pair")

    owners = [owner_ref[group * req + r] for r in range(req)]
    placed = []
    for r in range(req):
        at = jnp.int32(0)
        for j in range(req):
            if j != r:
                ahead = owners[j] <= owners[r] if j < r else owners[j] < owners[r]
                at = at + jnp.where(ahead, 1, 0)
        placed.append(at)
        order_ref[r] = at

    gain_out_ref[...] = gain_ref[...].reshape(1, width).astype(F32)

    biases = []
    for r in range(req):
        following = jnp.where(
            me == n_wide - 1, length_ref[r], start_ref[r, jnp.minimum(me + 1, n_wide - 1)]
        )
        position = lax.broadcasted_iota(jnp.int32, (1, block), 1)
        biases.append(jnp.where(position < following - start_ref[r, me], 0.0, F32(-1e30)))
    bias = jnp.concatenate(biases, axis=0)
    bias_ref[...] = bias

    for copy in copies[4:]:
        copy.wait()
    rows = []
    for i in range(req):
        row = jnp.zeros((1, width), F32)
        for r in range(req):
            row = jnp.where(placed[r] == i, residual_ref[r : r + 1, :].astype(F32), row)
        rows.append(row)
    residual_out_ref[...] = jnp.concatenate(rows, axis=0)

    scores = partial_scores(q_ref, cache_ref, bias)
    fresh = [fresh_ref[r : r + 1, :].astype(F32) for r in range(req)]
    own = jnp.concatenate(
        [
            jnp.sum(q_ref[r].astype(F32) * fresh[r], axis=1, keepdims=True)
            * (NOPE + ROPE) ** (-0.5)
            for r in range(req)
        ],
        axis=0,
    )
    top = jnp.maximum(jnp.max(scores, axis=1, keepdims=True), own)
    expo = jnp.exp(scores - top)
    expo_own = jnp.exp(own - top)
    den = jnp.sum(expo, axis=1, keepdims=True) + expo_own
    weight_own = expo_own.astype(BF16).astype(F32)
    num = partial_sums(expo, cache_ref, heads) + jnp.concatenate(
        [weight_own[r * heads : (r + 1) * heads] * fresh[r][:, :KV_RANK] for r in range(req)],
        axis=0,
    )
    count = req * heads
    out_ref[:count, :] = (num / den).astype(BF16)
    out_ref[count:, :] = payload_tail(top + jnp.log(den)).astype(BF16)


def attend_cost(req, heads, block, latent):
    return pl.CostEstimate(
        flops=2 * req * heads * block * (latent + KV_RANK),
        bytes_accessed=2 * req * (block * latent + heads * (latent + KV_RANK)),
        transcendentals=req * heads * block,
    )


def prepare(length, start, owner, gain, q, cache, fresh, residual):
    req, heads, latent = q.shape
    block, width = cache.shape[1], residual.shape[1]
    n_wide = start.shape[1]
    operands = (length, start, owner, gain, q, cache, fresh, residual)
    return pl.pallas_call(
        functools.partial(prepare_kernel, n_wide),
        out_shape=[
            jax.ShapeDtypeStruct((req * heads + TAIL, KV_RANK), BF16),
            jax.ShapeDtypeStruct((req, block), F32),
            jax.ShapeDtypeStruct((1, width), F32),
            jax.ShapeDtypeStruct((req, width), F32),
            jax.ShapeDtypeStruct((req,), jnp.int32),
            pltpu.VMEM(cache.shape, BF16),
        ],
        in_specs=[HBM] * len(operands),
        out_specs=[VMEM] * 4 + [SMEM, VMEM],
        scratch_shapes=[
            pltpu.SMEM(length.shape, jnp.int32),
            pltpu.SMEM(start.shape, jnp.int32),
            pltpu.SMEM(owner.shape, jnp.int32),
            pltpu.VMEM(gain.shape, BF16),
            pltpu.VMEM(q.shape, BF16),
            pltpu.VMEM(fresh.shape, BF16),
            pltpu.VMEM(residual.shape, BF16),
            pltpu.SemaphoreType.DMA((len(operands),)),
        ],
        compiler_params=SMALL,
        cost_estimate=pl.CostEstimate(
            flops=2 * req * heads * block * (latent + KV_RANK),
            bytes_accessed=2 * (cache.size + q.size),
            transcendentals=req * heads * block,
        ),
        name="prepare",
    )(*[in_hbm(x) for x in operands])


def attend_kernel(q_ref, cache_ref, bias_ref, after_ref, out_ref):
    req, heads, latent = q_ref.shape
    scores = partial_scores(q_ref, cache_ref, bias_ref[...])
    top = jnp.max(scores, axis=1, keepdims=True)
    expo = jnp.exp(scores - top)
    den = jnp.sum(expo, axis=1, keepdims=True)
    num = partial_sums(expo, cache_ref, heads)
    count = req * heads
    out_ref[:count, :] = (num / den).astype(BF16)
    out_ref[count:, :] = payload_tail(top + jnp.log(den)).astype(BF16)


def attend(q, cache, bias, after):
    req, heads, latent = q.shape
    return pl.pallas_call(
        attend_kernel,
        out_shape=jax.ShapeDtypeStruct((req * heads + TAIL, KV_RANK), BF16),
        in_specs=[VMEM] * 3 + [ANY],
        out_specs=VMEM,
        compiler_params=SMALL,
        cost_estimate=attend_cost(req, heads, cache.shape[1], latent),
        name="attend",
    )(q, cache, bias, after)


def fetch_kernel(items, plan, both_hbm, proj_hbm, after_ref, *refs):
    for copy in start_items(items, plan, both_hbm, proj_hbm, refs[:-1], refs[-1]):
        copy.wait()


def fetch(items, plan, both, proj, after):
    shapes = item_shapes(items, plan)
    out = pl.pallas_call(
        functools.partial(fetch_kernel, items, plan),
        out_shape=shapes,
        in_specs=[HBM, HBM, ANY],
        out_specs=[VMEM] * len(items),
        scratch_shapes=[item_sems(items)],
        compiler_params=SMALL,
        cost_estimate=pl.CostEstimate(
            flops=0,
            bytes_accessed=2 * sum(math.prod(shape.shape) for shape in shapes),
            transcendentals=0,
        ),
        name="fetch",
    )(in_hbm(both), in_hbm(proj), after)
    return dict(zip(items, out))


def combine_kernel(n_wide, n_sub, req, order_any, after_ref, *refs):
    payloads, outs = refs[:n_wide], refs[n_wide : n_wide + n_sub]
    hold, order_ref, sem = refs[n_wide + n_sub :]
    copy = pltpu.make_async_copy(order_any, order_ref, sem)
    copy.start()
    rows = payloads[0].shape[0] - TAIL
    heads = rows // req
    heads_dev = heads // n_sub
    me_sub = lax.axis_index("sub")
    tails = [p[rows:, :].astype(F32) for p in payloads]
    lses = []
    for tail in tails:
        turned = lax.dot_general(
            eye(rows, 128),
            tail[:, :128].astype(BF16),
            (((1,), (1,)), ((), ())),
            preferred_element_type=F32,
        )
        lses.append(turned[:, 0:1] + turned[:, 1:2] + turned[:, 2:3])
    top = functools.reduce(jnp.maximum, lses)
    weights = [jnp.exp(lse - top) for lse in lses]
    inv = 1.0 / functools.reduce(jnp.add, weights)
    weights = [weight * inv for weight in weights]
    copy.wait()
    for r in range(req):
        at = slice(r * heads, (r + 1) * heads)
        attn = functools.reduce(
            jnp.add, [w[at] * p[at, :].astype(F32) for w, p in zip(weights, payloads)]
        ).astype(BF16)
        for s in range(n_sub):
            hold[s, order_ref[r]] = attn[s * heads_dev : (s + 1) * heads_dev]
    for k in range(n_sub):
        outs[k][...] = hold[me_sub ^ k]


def combine(order, after, payloads, req, n_sub):
    n_wide = len(payloads)
    heads_dev = (payloads[0].shape[0] - TAIL) // req // n_sub
    piece = jax.ShapeDtypeStruct((req, heads_dev, KV_RANK), BF16)
    return pl.pallas_call(
        functools.partial(combine_kernel, n_wide, n_sub, req),
        out_shape=[piece] * n_sub,
        in_specs=[ANY, ANY] + [VMEM] * n_wide,
        out_specs=[VMEM] * n_sub,
        scratch_shapes=[
            pltpu.VMEM((n_sub, req, heads_dev, KV_RANK), BF16),
            pltpu.SMEM(order.shape, jnp.int32),
            pltpu.SemaphoreType.DMA(()),
        ],
        compiler_params=SMALL,
        name="combine",
    )(order, after, *payloads)


def project_kernel(count, items, plan, up_ref, both_hbm, proj_hbm, after_ref, *refs):
    n_wide = plan.wide // plan.width - 1
    pieces, weights, refs = refs[:count], refs[count : count + n_wide], refs[count + n_wide :]
    vals, outs, fetched, sems = refs[0], refs[1 : n_wide + 1], refs[n_wide + 1 : -1], refs[-1]
    copies = start_items(items, plan, both_hbm, proj_hbm, fetched, sems)
    req, heads, rank = pieces[0].shape
    rows = count * req
    cols = up_ref.shape[1]
    stacked = jnp.concatenate([p[...].reshape(req * heads, rank) for p in pieces], axis=0)
    total = rows * heads
    to = lax.broadcasted_iota(jnp.int32, (total, total), 0)
    source = lax.broadcasted_iota(jnp.int32, (total, total), 1)
    turn = (to // rows == source % heads) & (to % rows == source // heads)
    turned = jnp.dot(turn.astype(BF16), stacked, preferred_element_type=F32).astype(BF16)
    some = math.gcd(heads, max(1, 256 // cols))
    for first in range(0, heads, some):
        val = lax.dot_general(
            turned[first * rows : (first + some) * rows],
            up_ref[first : first + some].reshape(some * cols, rank),
            (((1,), (1,)), ((), ())),
            preferred_element_type=F32,
        ).astype(BF16)
        for i in range(some):
            at = slice((first + i) * cols, (first + i + 1) * cols)
            vals[:, at] = val[i * rows : (i + 1) * rows, i * cols : (i + 1) * cols]

    def work(at):
        for k in range(n_wide):
            block = column_block(weights[k], k + 1, plan, at)
            out = jnp.dot(vals[...], block, preferred_element_type=F32)
            outs[k][:, at] = out.astype(outs[k].dtype)

    in_tiles(items, plan.width, work)
    for copy in copies:
        copy.wait()


def project(pieces, value_up, weights, items, plan, both, proj, after):
    count = len(pieces)
    req, heads, rank = pieces[0].shape
    rows = count * req
    n_wide = len(weights)
    out = pl.pallas_call(
        functools.partial(project_kernel, count, items, plan),
        out_shape=[jax.ShapeDtypeStruct((rows, plan.depth), BF16)]
        + [jax.ShapeDtypeStruct((rows, plan.width), BF16)] * n_wide
        + item_shapes(items, plan),
        in_specs=[VMEM, HBM, HBM, ANY] + [VMEM] * (count + n_wide),
        out_specs=[VMEM] * (n_wide + 1 + len(items)),
        scratch_shapes=[item_sems(items)],
        compiler_params=SMALL,
        cost_estimate=pl.CostEstimate(
            flops=2 * rows * plan.depth * plan.wide,
            bytes_accessed=2 * plan.depth * plan.wide,
            transcendentals=0,
        ),
        name="project",
    )(value_up, in_hbm(both), in_hbm(proj), after, *pieces, *weights)
    return out[0], out[1 : n_wide + 1], dict(zip(items, out[n_wide + 1 :]))


def merge_kernel(mine_ref, residual_ref, after_ref, *refs):
    arrived, (total_ref, send_ref) = refs[:-2], refs[-2:]
    req = residual_ref.shape[0]
    total = mine_ref[...]
    for a in arrived:
        total = total + a[...].astype(F32)
    total_ref[...] = total
    total_ref[:req, :] = total[:req] + residual_ref[...]
    send_ref[...] = total_ref[...].astype(BF16)


def merge(mine, residual, after, arrived):
    return pl.pallas_call(
        merge_kernel,
        out_shape=[jax.ShapeDtypeStruct(mine.shape, F32), jax.ShapeDtypeStruct(mine.shape, BF16)],
        in_specs=[VMEM, VMEM, ANY] + [VMEM] * len(arrived),
        out_specs=[VMEM] * 2,
        compiler_params=SMALL,
        name="merge",
    )(mine, residual, after, *arrived)


def norm_kernel(req, mine_ref, gain_ref, after_ref, *refs):
    arrived, (gained_ref, stream_ref) = refs[:-2], refs[-2:]
    width = mine_ref.shape[1]
    blocks = [mine_ref[i * req : (i + 1) * req, :] for i in range(len(arrived) + 1)]
    for j, a in enumerate(arrived):
        others = a[...].astype(F32)
        for i in range(len(blocks)):
            at = (i ^ (j + 1)) * req
            blocks[i] = blocks[i] + others[at : at + req]
    stream_ref[...] = blocks[0]
    total = jnp.concatenate(blocks, axis=0)
    gained_ref[:, :width] = (total * gain_ref[...]).astype(BF16)
    square = jnp.sum(total * total, axis=1, keepdims=True)
    hi = square.astype(BF16).astype(F32)
    mid = (square - hi).astype(BF16).astype(F32)
    lo = (square - hi - mid).astype(BF16).astype(F32)
    lane = lax.broadcasted_iota(jnp.int32, (total.shape[0], 128), 1)
    spread = jnp.where(lane == 0, hi, jnp.where(lane == 1, mid, jnp.where(lane == 2, lo, 0.0)))
    gained_ref[:, width:] = spread.astype(BF16)


def norm(mine, gain, after, arrived, req):
    rows, width = mine.shape
    return pl.pallas_call(
        functools.partial(norm_kernel, req),
        out_shape=[
            jax.ShapeDtypeStruct((rows, width + 128), BF16),
            jax.ShapeDtypeStruct((req, width), F32),
        ],
        in_specs=[VMEM, VMEM, ANY] + [VMEM] * len(arrived),
        out_specs=[VMEM] * 2,
        compiler_params=SMALL,
        name="norm",
    )(mine, gain, after, *arrived)


def gate_kernel(count, first, plan, x_ref, later_ref, *refs):
    weights, carry, outs = refs[:count], refs[count : -count - 1], refs[-count - 1 :]
    square = x_ref[:, plan.width :].astype(F32)
    outs[count][...] = square if first else square + carry[count][...]
    x = x_ref[:, : plan.width]

    def multiply(i, at):
        product = jnp.dot(x, weights[i][:, at], preferred_element_type=F32)
        outs[i][:, at] = product if first else product + carry[i][:, at]

    def work(at):
        multiply(0, at)
        multiply(1, at)

    in_tiles(False, plan.full, work)
    for i in range(2, count):
        multiply(i, pl.ds(0, weights[i].shape[1]))


def gate(x, weights, carry, later, plan):
    rows = x.shape[0]
    count = len(weights)
    return pl.pallas_call(
        functools.partial(gate_kernel, count, not carry, plan),
        out_shape=[jax.ShapeDtypeStruct((rows, w.shape[1]), F32) for w in weights]
        + [jax.ShapeDtypeStruct((rows, 128), F32)],
        in_specs=[VMEM] * (2 + count + len(carry)),
        out_specs=[VMEM] * (count + 1),
        compiler_params=SMALL,
        cost_estimate=pl.CostEstimate(
            flops=4 * rows * plan.width * plan.units,
            bytes_accessed=4 * plan.width * plan.units,
            transcendentals=0,
        ),
        name="gate",
    )(x, later, *weights, *carry)


def hidden_units(plan, operands):
    *sums, square_ref = operands
    square = square_ref[:, 0:1] + square_ref[:, 1:2] + square_ref[:, 2:3]
    inv = lax.rsqrt(square / D + 1e-06)
    both = [sums[0][...], sums[1][...]]
    if len(sums) > 2:
        half = plan.units - plan.full
        both = [
            jnp.concatenate([part, sums[2][:, g * half : (g + 1) * half]], axis=1)
            for g, part in enumerate(both)
        ]
    g = both[0] * inv
    return (g / (1.0 + jnp.exp(-g)) * (both[1] * inv)).astype(BF16)


def down_kernel(ks, plan, weight_ref, *refs):
    operands, hidden_ref, outs = refs[: -1 - len(ks)], refs[-1 - len(ks)], refs[-len(ks) :]
    hidden = hidden_units(plan, operands)
    hidden_ref[...] = hidden
    for k, out in zip(ks, outs):
        block = column_block(weight_ref, k, plan, pl.ds(0, plan.width))
        out[...] = jnp.dot(hidden, block, preferred_element_type=F32).astype(BF16)


def down(weight, operands, ks, plan):
    rows = operands[0].shape[0]
    return pl.pallas_call(
        functools.partial(down_kernel, ks, plan),
        out_shape=[jax.ShapeDtypeStruct((rows, plan.units), BF16)]
        + [jax.ShapeDtypeStruct((rows, plan.width), BF16)] * len(ks),
        in_specs=[VMEM] * (1 + len(operands)),
        out_specs=[VMEM] * (1 + len(ks)),
        compiler_params=SMALL,
        cost_estimate=pl.CostEstimate(
            flops=2 * rows * plan.units * plan.width * len(ks),
            bytes_accessed=2 * plan.units * plan.width * len(ks),
            transcendentals=0,
        ),
        name="down",
    )(weight, *operands)


def own_kernel(plan, weight_ref, rows_ref, after_ref, out_ref):
    block = column_block(weight_ref, 0, plan, pl.ds(0, plan.width))
    out_ref[...] = jnp.dot(rows_ref[...], block, preferred_element_type=F32)


def own(weight, rows, after, plan):
    return pl.pallas_call(
        functools.partial(own_kernel, plan),
        out_shape=jax.ShapeDtypeStruct((rows.shape[0], plan.width), F32),
        in_specs=[VMEM, VMEM, ANY],
        out_specs=VMEM,
        compiler_params=SMALL,
        cost_estimate=pl.CostEstimate(
            flops=2 * rows.size * plan.width,
            bytes_accessed=2 * rows.shape[1] * plan.width,
            transcendentals=0,
        ),
        name="own",
    )(weight, rows, after)


def split_kernel(mine_ref, stream_ref, *refs):
    req = stream_ref.shape[0]
    count = mine_ref.shape[0] // req
    arrived, outs = refs[:-count], refs[-count:]
    total = mine_ref[...]
    for a in arrived:
        total = total + a[...].astype(F32)
    outs[0][...] = total[:req] + stream_ref[...]
    for j in range(1, count):
        outs[j][...] = total[j * req : (j + 1) * req].astype(BF16)


def split(mine, stream, arrived):
    req, width = stream.shape
    count = mine.shape[0] // req
    return pl.pallas_call(
        split_kernel,
        out_shape=[jax.ShapeDtypeStruct((req, width), F32)]
        + [jax.ShapeDtypeStruct((req, width), BF16)] * (count - 1),
        in_specs=[VMEM] * (2 + len(arrived)),
        out_specs=[VMEM] * count,
        compiler_params=SMALL,
        name="split",
    )(mine, stream, *arrived)


def body(
    latent_cache,
    queries,
    new_latent,
    context_len,
    block_start,
    owner,
    value_up,
    out_proj,
    residual_in,
    norm_gain,
    gate_up,
    down_weight,
):
    n_wide = lax.axis_size("wide")
    n_sub = lax.axis_size("sub")
    n_pair = lax.axis_size("pair")
    req_grp = latent_cache.shape[0]
    width_dev = residual_in.shape[1]

    powers = [k for k in range(1, n_wide) if k & (k - 1) == 0]
    arrived = {k: hop(queries, "wide", k) for k in reversed(powers)}
    units = down_weight.shape[0]
    plan = Plan(
        width=width_dev,
        units=units,
        full=units - 128 if units % 256 == 128 else units,
        depth=out_proj.shape[0] * out_proj.shape[1],
        wide=D,
    )
    payload, bias, gain, residual, order, cache = prepare(
        context_len,
        block_start,
        owner,
        norm_gain,
        queries,
        latent_cache,
        new_latent,
        residual_in,
    )
    proj = out_proj.reshape(plan.depth, D)

    kinds = ("gate", "rest", "up") if plan.full < units else ("gate", "up")
    held = {}

    def bring(items, after):
        got = fetch(items, plan, gate_up, proj, after)
        held.update(got)
        return got[items[-1]]

    far = list(range(n_wide - 1, -1, -1))
    queue = [("out", k) for k in far] + [(kind, k) for k in range(n_wide - 1) for kind in kinds]
    queue += [(kind, n_wide - 1) for kind in sorted(kinds, key=("rest", "gate", "up").index)]

    def take(count):
        items = queue[:count]
        del queue[:count]
        return items

    payloads = [payload]
    payload = bring(take(n_wide - 1), payload)
    waited = False
    for k in range(1, n_wide):
        if k not in arrived:
            low = k & -k
            arrived[k] = hop(arrived[k - low], "wide", low)
            if not waited:
                payload = bring(take(2), payload)
                waited = True
        elif k > 1:
            arrived[k], payload = lax.optimization_barrier((arrived[k], payload))
        payload = attend(arrived[k], cache, bias, payload)
        payloads.append(payload)
    payloads[1], payloads[-1] = lax.optimization_barrier((payloads[1], payloads[-1]))
    last = bring(take(5), payload)
    payloads = [payloads[0]] + [hop(payloads[k], "wide", k) for k in range(1, n_wide)]
    chunks = combine(order, last, payloads, req_grp, n_sub)

    peers = [(ks, kp) for kp in range(n_pair) for ks in range(n_sub)]
    masks = [ks * n_pair + kp for ks, kp in peers]
    pieces = [chunks[0]] + [hop_group(chunks[ks], ks * n_pair + kp) for ks, kp in peers[1:]]
    last = bring(take(2), chunks[0])
    vals, sends, got = project(
        pieces,
        jnp.swapaxes(value_up, 1, 2),
        [held["out", k] for k in range(1, n_wide)],
        take(2),
        plan,
        gate_up,
        proj,
        last,
    )
    held.update(got)

    back = [hop(sends[k - 1], "wide", k) for k in range(n_wide - 1, 0, -1)]
    mine = own(held["out", 0], vals, vals, plan)
    last = bring(take(len(queue)), mine)
    total, send = merge(mine, residual, last, back)
    back = [hop_group(send, k) for k in masks[1:]]
    gained, stream = norm(total, gain, last, back, req_grp)

    carry = ()
    for k in range(n_wide):
        x = hop(gained, "wide", k) if k else gained
        weights = [held[item] for item in (("gate", k), ("up", k), ("rest", k)) if item in held]
        carry = gate(x, weights, carry, down_weight, plan)
    away = far[:-1]
    hidden, *sends = down(down_weight, carry, away, plan)
    back = [hop(send, "wide", k) for k, send in zip(away, sends)]
    mine = own(down_weight, hidden, sends[-1], plan)
    out, *sends = split(mine, stream, back)
    for k, send in zip(masks[1:], sends):
        out = out + hop_group(send, k).astype(F32)
    return out.astype(BF16)


def solution(mesh):
    in_specs = (
        P(("groups", "sub", "pair"), "wide", None),
        P(("groups", "sub", "pair"), "wide", None),
        P(("groups", "sub", "pair"), None),
        P(("groups", "sub", "pair")),
        P(("groups", "sub", "pair"), None),
        P("groups"),
        P(("wide", "sub"), None, "pair"),
        P(("wide", "sub"), "pair", None),
        P(("groups", "sub", "pair"), "wide"),
        P("wide"),
        P(None, None, ("wide", "sub", "pair")),
        P(("wide", "sub", "pair"), None),
    )
    out_specs = P(("groups", "sub", "pair"), "wide")
    return jax.shard_map(body, mesh=mesh, in_specs=in_specs, out_specs=out_specs, check_vma=False)
```

```python
import collections
import functools
import math

import jax
import jax.numpy as jnp
from jax import lax
from jax.experimental import pallas as pl
from jax.experimental.pallas import tpu as pltpu
from jax.sharding import PartitionSpec as P

D = 7168
KV_RANK = 512
ROPE = 64
NOPE = 128
F32 = jnp.float32
BF16 = jnp.bfloat16
TAIL = 8
VMEM = pl.BlockSpec(memory_space=pltpu.VMEM)
SMEM = pl.BlockSpec(memory_space=pltpu.SMEM)
ANY = pl.BlockSpec(memory_space=pl.ANY)
HBM = pl.BlockSpec(memory_space=pltpu.HBM)
SMALL = pltpu.CompilerParams(vmem_limit_bytes=4 * 2**20)


def hop(x, axis, k):
    n = lax.axis_size(axis)
    return lax.ppermute(x, axis, [(i, i ^ k) for i in range(n)])


def hop_group(x, k):
    n = lax.axis_size("sub") * lax.axis_size("pair")
    return lax.ppermute(x, ("sub", "pair"), [(i, i ^ k) for i in range(n)])


def in_hbm(x):
    return pltpu.with_memory_space_constraint(x, pltpu.HBM)


Plan = collections.namedtuple("Plan", ["width", "units", "full", "depth", "wide"])


def aligned(plan):
    return plan.width % 128 == 0


def item_shape(item, plan):
    kind, k = item
    cols = plan.width if aligned(plan) else plan.wide
    if kind == "out":
        return (plan.depth, cols)
    if kind == "rest":
        return (plan.width, 2 * (plan.units - plan.full))
    return (plan.width, plan.full)


def item_copies(item, plan, source, out):
    kind, k = item
    start = (lax.axis_index("wide") ^ k) * plan.width
    if kind == "out":
        if not aligned(plan):
            return [(source, out)]
        return [(source.at[:, pl.ds(pl.multiple_of(start, 128), plan.width)], out)]
    rows = pl.ds(pl.multiple_of(start, 64), plan.width)
    if kind == "rest":
        half = plan.units - plan.full
        return [
            (source.at[g, rows, plan.full :], out.at[:, g * half : (g + 1) * half])
            for g in range(2)
        ]
    return [(source.at[int(kind == "up"), rows, : plan.full], out)]


def start_items(items, plan, both, proj, outs, sems):
    pairs = []
    for item, out in zip(items, outs):
        pairs += item_copies(item, plan, proj if item[0] == "out" else both, out)
    copies = [
        pltpu.make_async_copy(source, out, sems.at[i]) for i, (source, out) in enumerate(pairs)
    ]

    @pl.when(lax.axis_index("wide") >= 0)
    def _():
        for copy in copies:
            copy.start()

    return copies


def item_shapes(items, plan):
    return [pltpu.VMEM(item_shape(item, plan), BF16) for item in items]


def item_sems(items):
    return pltpu.SemaphoreType.DMA((max(1, sum(2 if i[0] == "rest" else 1 for i in items)),))


def column_block(ref, k, plan, at):
    me = lax.axis_index("wide")
    if ref.shape[1] == plan.width:
        return ref[:, at]
    if aligned(plan):
        return ref[:, pl.ds(pl.multiple_of((me ^ k) * plan.width, 128), plan.width)]
    block = ref[:, : plan.width]
    for w in range(1, plan.wide // plan.width):
        block = jnp.where((me ^ k) == w, ref[:, w * plan.width : (w + 1) * plan.width], block)
    return block


def in_tiles(loop, cols, work):
    if not loop or cols % 256:
        work(pl.ds(0, cols))
        return

    @pl.loop(0, cols // 256)
    def _(i):
        work(pl.ds(pl.multiple_of(i * 256, 256), 256))


def eye(rows, cols):
    row = lax.broadcasted_iota(jnp.int32, (rows, cols), 0)
    col = lax.broadcasted_iota(jnp.int32, (rows, cols), 1)
    return (row == col).astype(BF16)


def partial_scores(q_ref, cache_ref, bias):
    req, heads, latent = q_ref.shape
    scores = [
        lax.dot_general(
            q_ref[r], cache_ref[r], (((1,), (1,)), ((), ())), preferred_element_type=F32
        )
        * (NOPE + ROPE) ** (-0.5)
        + bias[r : r + 1, :]
        for r in range(req)
    ]
    return jnp.concatenate(scores, axis=0)


def partial_sums(expo, cache_ref, heads):
    expo = expo.astype(BF16)
    sums = [
        jnp.dot(
            expo[r * heads : (r + 1) * heads],
            cache_ref[r, :, :KV_RANK],
            preferred_element_type=F32,
        )
        for r in range(cache_ref.shape[0])
    ]
    return jnp.concatenate(sums, axis=0)


def payload_tail(lse):
    rows = lse.shape[0]
    hi = lse.astype(BF16).astype(F32)
    mid = (lse - hi).astype(BF16).astype(F32)
    lo = (lse - hi - mid).astype(BF16).astype(F32)
    lane = lax.broadcasted_iota(jnp.int32, (rows, 128), 1)
    spread = jnp.where(lane == 0, hi, jnp.where(lane == 1, mid, jnp.where(lane == 2, lo, 0.0)))
    turned = lax.dot_general(
        spread.astype(BF16), eye(rows, 128), (((0,), (0,)), ((), ())), preferred_element_type=F32
    )
    return jnp.pad(turned[:TAIL], ((0, 0), (0, KV_RANK - 128)))


def prepare_kernel(
    n_wide,
    length_hbm,
    start_hbm,
    owner_hbm,
    gain_hbm,
    q_hbm,
    cache_hbm,
    fresh_hbm,
    residual_hbm,
    out_ref,
    bias_ref,
    gain_out_ref,
    residual_out_ref,
    order_ref,
    cache_ref,
    *refs,
):
    length_ref, start_ref, owner_ref, gain_ref, q_ref, fresh_ref, residual_ref, sems = refs
    copies = [
        pltpu.make_async_copy(source, target, sems.at[i])
        for i, (source, target) in enumerate(
            [
                (length_hbm, length_ref),
                (start_hbm, start_ref),
                (owner_hbm, owner_ref),
                (gain_hbm, gain_ref),
                (q_hbm, q_ref),
                (cache_hbm, cache_ref),
                (fresh_hbm, fresh_ref),
                (residual_hbm, residual_ref),
            ]
        )
    ]
    for copy in copies:
        copy.start()
    for copy in copies[:4]:
        copy.wait()
    req, heads, latent = q_ref.shape
    block = cache_ref.shape[1]
    width = gain_ref.shape[0]
    me, me_sub = lax.axis_index("wide"), lax.axis_index("sub")
    group = me_sub * lax.axis_size("pair") + lax.axis_index("pair")

    owners = [owner_ref[group * req + r] for r in range(req)]
    placed = []
    for r in range(req):
        at = jnp.int32(0)
        for j in range(req):
            if j != r:
                ahead = owners[j] <= owners[r] if j < r else owners[j] < owners[r]
                at = at + jnp.where(ahead, 1, 0)
        placed.append(at)
        order_ref[r] = at

    gain_out_ref[...] = gain_ref[...].reshape(1, width).astype(F32)

    biases = []
    for r in range(req):
        following = jnp.where(
            me == n_wide - 1, length_ref[r], start_ref[r, jnp.minimum(me + 1, n_wide - 1)]
        )
        position = lax.broadcasted_iota(jnp.int32, (1, block), 1)
        biases.append(jnp.where(position < following - start_ref[r, me], 0.0, F32(-1e30)))
    bias = jnp.concatenate(biases, axis=0)
    bias_ref[...] = bias

    for copy in copies[4:]:
        copy.wait()
    rows = []
    for i in range(req):
        row = jnp.zeros((1, width), F32)
        for r in range(req):
            row = jnp.where(placed[r] == i, residual_ref[r : r + 1, :].astype(F32), row)
        rows.append(row)
    residual_out_ref[...] = jnp.concatenate(rows, axis=0)

    scores = partial_scores(q_ref, cache_ref, bias)
    fresh = [fresh_ref[r : r + 1, :].astype(F32) for r in range(req)]
    own = jnp.concatenate(
        [
            jnp.sum(q_ref[r].astype(F32) * fresh[r], axis=1, keepdims=True)
            * (NOPE + ROPE) ** (-0.5)
            for r in range(req)
        ],
        axis=0,
    )
    top = jnp.maximum(jnp.max(scores, axis=1, keepdims=True), own)
    expo = jnp.exp(scores - top)
    expo_own = jnp.exp(own - top)
    den = jnp.sum(expo, axis=1, keepdims=True) + expo_own
    weight_own = expo_own.astype(BF16).astype(F32)
    num = partial_sums(expo, cache_ref, heads) + jnp.concatenate(
        [weight_own[r * heads : (r + 1) * heads] * fresh[r][:, :KV_RANK] for r in range(req)],
        axis=0,
    )
    count = req * heads
    out_ref[:count, :] = (num / den).astype(BF16)
    out_ref[count:, :] = payload_tail(top + jnp.log(den)).astype(BF16)


def attend_cost(req, heads, block, latent):
    return pl.CostEstimate(
        flops=2 * req * heads * block * (latent + KV_RANK),
        bytes_accessed=2 * req * (block * latent + heads * (latent + KV_RANK)),
        transcendentals=req * heads * block,
    )


def prepare(length, start, owner, gain, q, cache, fresh, residual):
    req, heads, latent = q.shape
    block, width = cache.shape[1], residual.shape[1]
    n_wide = start.shape[1]
    operands = (length, start, owner, gain, q, cache, fresh, residual)
    return pl.pallas_call(
        functools.partial(prepare_kernel, n_wide),
        out_shape=[
            jax.ShapeDtypeStruct((req * heads + TAIL, KV_RANK), BF16),
            jax.ShapeDtypeStruct((req, block), F32),
            jax.ShapeDtypeStruct((1, width), F32),
            jax.ShapeDtypeStruct((req, width), F32),
            jax.ShapeDtypeStruct((req,), jnp.int32),
            pltpu.VMEM(cache.shape, BF16),
        ],
        in_specs=[HBM] * len(operands),
        out_specs=[VMEM] * 4 + [SMEM, VMEM],
        scratch_shapes=[
            pltpu.SMEM(length.shape, jnp.int32),
            pltpu.SMEM(start.shape, jnp.int32),
            pltpu.SMEM(owner.shape, jnp.int32),
            pltpu.VMEM(gain.shape, BF16),
            pltpu.VMEM(q.shape, BF16),
            pltpu.VMEM(fresh.shape, BF16),
            pltpu.VMEM(residual.shape, BF16),
            pltpu.SemaphoreType.DMA((len(operands),)),
        ],
        compiler_params=SMALL,
        cost_estimate=pl.CostEstimate(
            flops=2 * req * heads * block * (latent + KV_RANK),
            bytes_accessed=2 * (cache.size + q.size),
            transcendentals=req * heads * block,
        ),
        name="prepare",
    )(*[in_hbm(x) for x in operands])


def attend_kernel(q_ref, cache_ref, bias_ref, after_ref, out_ref):
    req, heads, latent = q_ref.shape
    scores = partial_scores(q_ref, cache_ref, bias_ref[...])
    top = jnp.max(scores, axis=1, keepdims=True)
    expo = jnp.exp(scores - top)
    den = jnp.sum(expo, axis=1, keepdims=True)
    num = partial_sums(expo, cache_ref, heads)
    count = req * heads
    out_ref[:count, :] = (num / den).astype(BF16)
    out_ref[count:, :] = payload_tail(top + jnp.log(den)).astype(BF16)


def attend(q, cache, bias, after):
    req, heads, latent = q.shape
    return pl.pallas_call(
        attend_kernel,
        out_shape=jax.ShapeDtypeStruct((req * heads + TAIL, KV_RANK), BF16),
        in_specs=[VMEM] * 3 + [ANY],
        out_specs=VMEM,
        compiler_params=SMALL,
        cost_estimate=attend_cost(req, heads, cache.shape[1], latent),
        name="attend",
    )(q, cache, bias, after)


def fetch_kernel(items, plan, both_hbm, proj_hbm, after_ref, *refs):
    for copy in start_items(items, plan, both_hbm, proj_hbm, refs[:-1], refs[-1]):
        copy.wait()


def fetch(items, plan, both, proj, after):
    shapes = item_shapes(items, plan)
    out = pl.pallas_call(
        functools.partial(fetch_kernel, items, plan),
        out_shape=shapes,
        in_specs=[HBM, HBM, ANY],
        out_specs=[VMEM] * len(items),
        scratch_shapes=[item_sems(items)],
        compiler_params=SMALL,
        cost_estimate=pl.CostEstimate(
            flops=0,
            bytes_accessed=2 * sum(math.prod(shape.shape) for shape in shapes),
            transcendentals=0,
        ),
        name="fetch",
    )(in_hbm(both), in_hbm(proj), after)
    return dict(zip(items, out))


def combine_kernel(n_wide, n_sub, req, order_any, after_ref, *refs):
    payloads, outs = refs[:n_wide], refs[n_wide : n_wide + n_sub]
    hold, order_ref, sem = refs[n_wide + n_sub :]
    copy = pltpu.make_async_copy(order_any, order_ref, sem)
    copy.start()
    rows = payloads[0].shape[0] - TAIL
    heads = rows // req
    heads_dev = heads // n_sub
    me_sub = lax.axis_index("sub")
    tails = [p[rows:, :].astype(F32) for p in payloads]
    lses = []
    for tail in tails:
        turned = lax.dot_general(
            eye(rows, 128),
            tail[:, :128].astype(BF16),
            (((1,), (1,)), ((), ())),
            preferred_element_type=F32,
        )
        lses.append(turned[:, 0:1] + turned[:, 1:2] + turned[:, 2:3])
    top = functools.reduce(jnp.maximum, lses)
    weights = [jnp.exp(lse - top) for lse in lses]
    inv = 1.0 / functools.reduce(jnp.add, weights)
    weights = [weight * inv for weight in weights]
    copy.wait()
    for r in range(req):
        at = slice(r * heads, (r + 1) * heads)
        attn = functools.reduce(
            jnp.add, [w[at] * p[at, :].astype(F32) for w, p in zip(weights, payloads)]
        ).astype(BF16)
        for s in range(n_sub):
            hold[s, order_ref[r]] = attn[s * heads_dev : (s + 1) * heads_dev]
    for k in range(n_sub):
        outs[k][...] = hold[me_sub ^ k]


def combine(order, after, payloads, req, n_sub):
    n_wide = len(payloads)
    heads_dev = (payloads[0].shape[0] - TAIL) // req // n_sub
    piece = jax.ShapeDtypeStruct((req, heads_dev, KV_RANK), BF16)
    return pl.pallas_call(
        functools.partial(combine_kernel, n_wide, n_sub, req),
        out_shape=[piece] * n_sub,
        in_specs=[ANY, ANY] + [VMEM] * n_wide,
        out_specs=[VMEM] * n_sub,
        scratch_shapes=[
            pltpu.VMEM((n_sub, req, heads_dev, KV_RANK), BF16),
            pltpu.SMEM(order.shape, jnp.int32),
            pltpu.SemaphoreType.DMA(()),
        ],
        compiler_params=SMALL,
        name="combine",
    )(order, after, *payloads)


def project_kernel(count, items, plan, up_ref, both_hbm, proj_hbm, after_ref, *refs):
    n_wide = plan.wide // plan.width - 1
    pieces, weights, refs = refs[:count], refs[count : count + n_wide], refs[count + n_wide :]
    vals, outs, fetched, sems = refs[0], refs[1 : n_wide + 1], refs[n_wide + 1 : -1], refs[-1]
    copies = start_items(items, plan, both_hbm, proj_hbm, fetched, sems)
    req, heads, rank = pieces[0].shape
    rows = count * req
    cols = up_ref.shape[1]
    stacked = jnp.concatenate([p[...].reshape(req * heads, rank) for p in pieces], axis=0)
    total = rows * heads
    to = lax.broadcasted_iota(jnp.int32, (total, total), 0)
    source = lax.broadcasted_iota(jnp.int32, (total, total), 1)
    turn = (to // rows == source % heads) & (to % rows == source // heads)
    turned = jnp.dot(turn.astype(BF16), stacked, preferred_element_type=F32).astype(BF16)
    some = math.gcd(heads, max(1, 256 // cols))
    for first in range(0, heads, some):
        val = lax.dot_general(
            turned[first * rows : (first + some) * rows],
            up_ref[first : first + some].reshape(some * cols, rank),
            (((1,), (1,)), ((), ())),
            preferred_element_type=F32,
        ).astype(BF16)
        for i in range(some):
            at = slice((first + i) * cols, (first + i + 1) * cols)
            vals[:, at] = val[i * rows : (i + 1) * rows, i * cols : (i + 1) * cols]

    def work(at):
        for k in range(n_wide):
            block = column_block(weights[k], k + 1, plan, at)
            out = jnp.dot(vals[...], block, preferred_element_type=F32)
            outs[k][:, at] = out.astype(outs[k].dtype)

    in_tiles(items, plan.width, work)
    for copy in copies:
        copy.wait()


def project(pieces, value_up, weights, items, plan, both, proj, after):
    count = len(pieces)
    req, heads, rank = pieces[0].shape
    rows = count * req
    n_wide = len(weights)
    out = pl.pallas_call(
        functools.partial(project_kernel, count, items, plan),
        out_shape=[jax.ShapeDtypeStruct((rows, plan.depth), BF16)]
        + [jax.ShapeDtypeStruct((rows, plan.width), BF16)] * n_wide
        + item_shapes(items, plan),
        in_specs=[VMEM, HBM, HBM, ANY] + [VMEM] * (count + n_wide),
        out_specs=[VMEM] * (n_wide + 1 + len(items)),
        scratch_shapes=[item_sems(items)],
        compiler_params=SMALL,
        cost_estimate=pl.CostEstimate(
            flops=2 * rows * plan.depth * plan.wide,
            bytes_accessed=2 * plan.depth * plan.wide,
            transcendentals=0,
        ),
        name="project",
    )(value_up, in_hbm(both), in_hbm(proj), after, *pieces, *weights)
    return out[0], out[1 : n_wide + 1], dict(zip(items, out[n_wide + 1 :]))


def merge_kernel(mine_ref, residual_ref, after_ref, *refs):
    arrived, (total_ref, send_ref) = refs[:-2], refs[-2:]
    req = residual_ref.shape[0]
    total = mine_ref[...]
    for a in arrived:
        total = total + a[...].astype(F32)
    total_ref[...] = total
    total_ref[:req, :] = total[:req] + residual_ref[...]
    send_ref[...] = total_ref[...].astype(BF16)


def merge(mine, residual, after, arrived):
    return pl.pallas_call(
        merge_kernel,
        out_shape=[jax.ShapeDtypeStruct(mine.shape, F32), jax.ShapeDtypeStruct(mine.shape, BF16)],
        in_specs=[VMEM, VMEM, ANY] + [VMEM] * len(arrived),
        out_specs=[VMEM] * 2,
        compiler_params=SMALL,
        name="merge",
    )(mine, residual, after, *arrived)


def norm_kernel(req, mine_ref, gain_ref, after_ref, *refs):
    arrived, (gained_ref, stream_ref) = refs[:-2], refs[-2:]
    width = mine_ref.shape[1]
    blocks = [mine_ref[i * req : (i + 1) * req, :] for i in range(len(arrived) + 1)]
    for j, a in enumerate(arrived):
        others = a[...].astype(F32)
        for i in range(len(blocks)):
            at = (i ^ (j + 1)) * req
            blocks[i] = blocks[i] + others[at : at + req]
    stream_ref[...] = blocks[0]
    total = jnp.concatenate(blocks, axis=0)
    gained_ref[:, :width] = (total * gain_ref[...]).astype(BF16)
    square = jnp.sum(total * total, axis=1, keepdims=True)
    hi = square.astype(BF16).astype(F32)
    mid = (square - hi).astype(BF16).astype(F32)
    lo = (square - hi - mid).astype(BF16).astype(F32)
    lane = lax.broadcasted_iota(jnp.int32, (total.shape[0], 128), 1)
    spread = jnp.where(lane == 0, hi, jnp.where(lane == 1, mid, jnp.where(lane == 2, lo, 0.0)))
    gained_ref[:, width:] = spread.astype(BF16)


def norm(mine, gain, after, arrived, req):
    rows, width = mine.shape
    return pl.pallas_call(
        functools.partial(norm_kernel, req),
        out_shape=[
            jax.ShapeDtypeStruct((rows, width + 128), BF16),
            jax.ShapeDtypeStruct((req, width), F32),
        ],
        in_specs=[VMEM, VMEM, ANY] + [VMEM] * len(arrived),
        out_specs=[VMEM] * 2,
        compiler_params=SMALL,
        name="norm",
    )(mine, gain, after, *arrived)


def gate_kernel(count, first, plan, x_ref, later_ref, *refs):
    weights, carry, outs = refs[:count], refs[count : -count - 1], refs[-count - 1 :]
    square = x_ref[:, plan.width :].astype(F32)
    outs[count][...] = square if first else square + carry[count][...]
    x = x_ref[:, : plan.width]

    def multiply(i, at):
        product = jnp.dot(x, weights[i][:, at], preferred_element_type=F32)
        outs[i][:, at] = product if first else product + carry[i][:, at]

    def work(at):
        multiply(0, at)
        multiply(1, at)

    in_tiles(False, plan.full, work)
    for i in range(2, count):
        multiply(i, pl.ds(0, weights[i].shape[1]))


def gate(x, weights, carry, later, plan):
    rows = x.shape[0]
    count = len(weights)
    return pl.pallas_call(
        functools.partial(gate_kernel, count, not carry, plan),
        out_shape=[jax.ShapeDtypeStruct((rows, w.shape[1]), F32) for w in weights]
        + [jax.ShapeDtypeStruct((rows, 128), F32)],
        in_specs=[VMEM] * (2 + count + len(carry)),
        out_specs=[VMEM] * (count + 1),
        compiler_params=SMALL,
        cost_estimate=pl.CostEstimate(
            flops=4 * rows * plan.width * plan.units,
            bytes_accessed=4 * plan.width * plan.units,
            transcendentals=0,
        ),
        name="gate",
    )(x, later, *weights, *carry)


def hidden_units(plan, operands):
    *sums, square_ref = operands
    square = square_ref[:, 0:1] + square_ref[:, 1:2] + square_ref[:, 2:3]
    inv = lax.rsqrt(square / D + 1e-06)
    both = [sums[0][...], sums[1][...]]
    if len(sums) > 2:
        half = plan.units - plan.full
        both = [
            jnp.concatenate([part, sums[2][:, g * half : (g + 1) * half]], axis=1)
            for g, part in enumerate(both)
        ]
    g = both[0] * inv
    return (g / (1.0 + jnp.exp(-g)) * (both[1] * inv)).astype(BF16)


def down_kernel(ks, plan, weight_ref, *refs):
    operands, (hidden_ref, keep_ref, send_ref) = refs[:-3], refs[-3:]
    hidden = hidden_units(plan, operands)
    hidden_ref[...] = hidden
    kept = keep_ref.shape[0]
    for i, k in enumerate(ks):
        block = column_block(weight_ref, k, plan, pl.ds(0, plan.width))
        out = jnp.dot(hidden, block, preferred_element_type=F32)
        at = slice(i * plan.width, (i + 1) * plan.width)
        keep_ref[:, at] = out[:kept]
        send_ref[:, at] = out[kept:].astype(BF16)


def down(weight, operands, ks, kept, plan):
    rows = operands[0].shape[0]
    cols = len(ks) * plan.width
    return pl.pallas_call(
        functools.partial(down_kernel, ks, plan),
        out_shape=[
            jax.ShapeDtypeStruct((rows, plan.units), BF16),
            jax.ShapeDtypeStruct((kept, cols), F32),
            jax.ShapeDtypeStruct((rows - kept, cols), BF16),
        ],
        in_specs=[VMEM] * (1 + len(operands)),
        out_specs=[VMEM] * 3,
        compiler_params=SMALL,
        cost_estimate=pl.CostEstimate(
            flops=2 * rows * plan.units * plan.width * len(ks),
            bytes_accessed=2 * plan.units * plan.width * len(ks),
            transcendentals=0,
        ),
        name="down",
    )(weight, *operands)


def join_kernel(keep_ref, *refs):
    width = refs[-1].shape[1]
    count = keep_ref.shape[1] // width
    total = keep_ref[...]
    for a in refs[:-count]:
        total = total + a[...].astype(F32)
    for i, out in enumerate(refs[-count:]):
        out[...] = total[:, i * width : (i + 1) * width].astype(BF16)


def join(keep, arrived, width):
    rows, cols = keep.shape
    count = cols // width
    return pl.pallas_call(
        join_kernel,
        out_shape=[jax.ShapeDtypeStruct((rows, width), BF16)] * count,
        in_specs=[VMEM] * (1 + len(arrived)),
        out_specs=[VMEM] * count,
        compiler_params=SMALL,
        name="join",
    )(keep, *arrived)


def own_kernel(plan, weight_ref, rows_ref, after_ref, keep_ref, *sends):
    block = column_block(weight_ref, 0, plan, pl.ds(0, plan.width))
    out = jnp.dot(rows_ref[...], block, preferred_element_type=F32)
    kept = keep_ref.shape[0]
    keep_ref[...] = out[:kept]
    for send in sends:
        send[...] = out[kept:].astype(BF16)


def own(weight, rows, after, kept, plan):
    count = rows.shape[0]
    shapes = [jax.ShapeDtypeStruct((kept, plan.width), F32)]
    if kept < count:
        shapes.append(jax.ShapeDtypeStruct((count - kept, plan.width), BF16))
    return pl.pallas_call(
        functools.partial(own_kernel, plan),
        out_shape=shapes,
        in_specs=[VMEM, VMEM, ANY],
        out_specs=[VMEM] * len(shapes),
        compiler_params=SMALL,
        cost_estimate=pl.CostEstimate(
            flops=2 * rows.size * plan.width,
            bytes_accessed=2 * rows.shape[1] * plan.width,
            transcendentals=0,
        ),
        name="own",
    )(weight, rows, after)


def split_kernel(mine_ref, stream_ref, *refs):
    req = stream_ref.shape[0]
    count = mine_ref.shape[0] // req
    arrived, outs = refs[:-count], refs[-count:]
    total = mine_ref[...]
    for a in arrived:
        total = total + a[...].astype(F32)
    outs[0][...] = total[:req] + stream_ref[...]
    for j in range(1, count):
        outs[j][...] = total[j * req : (j + 1) * req].astype(BF16)


def split(mine, stream, arrived):
    req, width = stream.shape
    count = mine.shape[0] // req
    return pl.pallas_call(
        split_kernel,
        out_shape=[jax.ShapeDtypeStruct((req, width), F32)]
        + [jax.ShapeDtypeStruct((req, width), BF16)] * (count - 1),
        in_specs=[VMEM] * (2 + len(arrived)),
        out_specs=[VMEM] * count,
        compiler_params=SMALL,
        name="split",
    )(mine, stream, *arrived)


def body(
    latent_cache,
    queries,
    new_latent,
    context_len,
    block_start,
    owner,
    value_up,
    out_proj,
    residual_in,
    norm_gain,
    gate_up,
    down_weight,
):
    n_wide = lax.axis_size("wide")
    n_sub = lax.axis_size("sub")
    n_pair = lax.axis_size("pair")
    req_grp = latent_cache.shape[0]
    width_dev = residual_in.shape[1]

    powers = [k for k in range(1, n_wide) if k & (k - 1) == 0]
    arrived = {k: hop(queries, "wide", k) for k in reversed(powers)}
    units = down_weight.shape[0]
    plan = Plan(
        width=width_dev,
        units=units,
        full=units - 128 if units % 256 == 128 else units,
        depth=out_proj.shape[0] * out_proj.shape[1],
        wide=D,
    )
    payload, bias, gain, residual, order, cache = prepare(
        context_len,
        block_start,
        owner,
        norm_gain,
        queries,
        latent_cache,
        new_latent,
        residual_in,
    )
    proj = out_proj.reshape(plan.depth, D)

    kinds = ("gate", "rest", "up") if plan.full < units else ("gate", "up")
    held = {}

    def bring(items, after):
        got = fetch(items, plan, gate_up, proj, after)
        held.update(got)
        return got[items[-1]]

    far = list(range(n_wide - 1, -1, -1))
    queue = [("out", k) for k in far] + [(kind, k) for k in range(n_wide - 1) for kind in kinds]
    queue += [(kind, n_wide - 1) for kind in sorted(kinds, key=("rest", "gate", "up").index)]

    def take(count):
        items = queue[:count]
        del queue[:count]
        return items

    payloads = [payload]
    payload = bring(take(n_wide - 1), payload)
    waited = False
    for k in range(1, n_wide):
        if k not in arrived:
            low = k & -k
            arrived[k] = hop(arrived[k - low], "wide", low)
            if not waited:
                payload = bring(take(2), payload)
                waited = True
        elif k > 1:
            arrived[k], payload = lax.optimization_barrier((arrived[k], payload))
        payload = attend(arrived[k], cache, bias, payload)
        payloads.append(payload)
    payloads[1], payloads[-1] = lax.optimization_barrier((payloads[1], payloads[-1]))
    last = bring(take(5), payload)
    payloads = [payloads[0]] + [hop(payloads[k], "wide", k) for k in range(1, n_wide)]
    chunks = combine(order, last, payloads, req_grp, n_sub)

    peers = [(ks, kp) for kp in range(n_pair) for ks in range(n_sub)]
    masks = [ks * n_pair + kp for ks, kp in peers]
    pieces = [chunks[0]] + [hop_group(chunks[ks], ks * n_pair + kp) for ks, kp in peers[1:]]
    last = bring(take(2), chunks[0])
    vals, sends, got = project(
        pieces,
        jnp.swapaxes(value_up, 1, 2),
        [held["out", k] for k in range(1, n_wide)],
        take(2),
        plan,
        gate_up,
        proj,
        last,
    )
    held.update(got)

    back = [hop(sends[k - 1], "wide", k) for k in range(n_wide - 1, 0, -1)]
    (mine,) = own(held["out", 0], vals, vals, vals.shape[0], plan)
    last = bring(take(len(queue)), mine)
    total, send = merge(mine, residual, last, back)
    back = [hop_group(send, k) for k in masks[1:]]
    gained, stream = norm(total, gain, last, back, req_grp)

    blocks = {k: hop(gained, "wide", k) for k in range(n_wide - 1, 0, -1)}
    blocks[0] = gained
    carry = ()
    for k in [0, n_wide - 1, *range(1, n_wide - 1)]:
        weights = [held[item] for item in (("gate", k), ("up", k), ("rest", k)) if item in held]
        carry = gate(blocks[k], weights, carry, down_weight, plan)

    kept = n_sub * req_grp

    def to_pair(send):
        return [hop(send[(k - 1) * kept : k * kept], "pair", k) for k in range(1, n_pair)]

    hidden, keep, send = down(down_weight, carry, far[:-1], kept, plan)
    back = to_pair(send)
    mine, send = own(down_weight, hidden, send, kept, plan)
    mine_back = to_pair(send)
    sends = join(keep, back, width_dev)
    mine_back += [hop(send, "wide", k) for k, send in zip(far, sends)]
    out, *sends = split(mine, stream, mine_back)
    for k, send in enumerate(sends):
        out = out + hop(send, "sub", k + 1).astype(F32)
    return out.astype(BF16)


def solution(mesh):
    in_specs = (
        P(("groups", "sub", "pair"), "wide", None),
        P(("groups", "sub", "pair"), "wide", None),
        P(("groups", "sub", "pair"), None),
        P(("groups", "sub", "pair")),
        P(("groups", "sub", "pair"), None),
        P("groups"),
        P(("wide", "sub"), None, "pair"),
        P(("wide", "sub"), "pair", None),
        P(("groups", "sub", "pair"), "wide"),
        P("wide"),
        P(None, None, ("wide", "sub", "pair")),
        P(("wide", "sub", "pair"), None),
    )
    out_specs = P(("groups", "sub", "pair"), "wide")
    return jax.shard_map(body, mesh=mesh, in_specs=in_specs, out_specs=out_specs, check_vma=False)
```

```python
import collections
import functools
import math

import jax
import jax.numpy as jnp
from jax import lax
from jax.experimental import pallas as pl
from jax.experimental.pallas import tpu as pltpu
from jax.sharding import PartitionSpec as P

D = 7168
KV_RANK = 512
ROPE = 64
NOPE = 128
F32 = jnp.float32
BF16 = jnp.bfloat16
TAIL = 8
VMEM = pl.BlockSpec(memory_space=pltpu.VMEM)
SMEM = pl.BlockSpec(memory_space=pltpu.SMEM)
ANY = pl.BlockSpec(memory_space=pl.ANY)
HBM = pl.BlockSpec(memory_space=pltpu.HBM)
SMALL = pltpu.CompilerParams(vmem_limit_bytes=4 * 2**20)


def hop(x, axis, k):
    n = lax.axis_size(axis)
    return lax.ppermute(x, axis, [(i, i ^ k) for i in range(n)])


def hop_group(x, k):
    n = lax.axis_size("sub") * lax.axis_size("pair")
    return lax.ppermute(x, ("sub", "pair"), [(i, i ^ k) for i in range(n)])


def in_hbm(x):
    return pltpu.with_memory_space_constraint(x, pltpu.HBM)


Plan = collections.namedtuple("Plan", ["width", "units", "full", "depth", "wide"])


def aligned(plan):
    return plan.width % 128 == 0


def item_shape(item, plan):
    kind, k = item
    cols = plan.width if aligned(plan) else plan.wide
    if kind == "out":
        return (plan.depth, cols)
    if kind == "rest":
        return (plan.width, 2 * (plan.units - plan.full))
    return (plan.width, plan.full)


def item_copies(item, plan, source, out):
    kind, k = item
    start = (lax.axis_index("wide") ^ k) * plan.width
    if kind == "out":
        if not aligned(plan):
            return [(source, out)]
        return [(source.at[:, pl.ds(pl.multiple_of(start, 128), plan.width)], out)]
    rows = pl.ds(pl.multiple_of(start, 64), plan.width)
    if kind == "rest":
        half = plan.units - plan.full
        return [
            (source.at[g, rows, plan.full :], out.at[:, g * half : (g + 1) * half])
            for g in range(2)
        ]
    return [(source.at[int(kind == "up"), rows, : plan.full], out)]


def start_items(items, plan, both, proj, outs, sems):
    pairs = []
    for item, out in zip(items, outs):
        pairs += item_copies(item, plan, proj if item[0] == "out" else both, out)
    copies = [
        pltpu.make_async_copy(source, out, sems.at[i]) for i, (source, out) in enumerate(pairs)
    ]

    @pl.when(lax.axis_index("wide") >= 0)
    def _():
        for copy in copies:
            copy.start()

    return copies


def item_shapes(items, plan):
    return [pltpu.VMEM(item_shape(item, plan), BF16) for item in items]


def item_sems(items):
    return pltpu.SemaphoreType.DMA((max(1, sum(2 if i[0] == "rest" else 1 for i in items)),))


def column_block(ref, k, plan, at):
    me = lax.axis_index("wide")
    if ref.shape[1] == plan.width:
        return ref[:, at]
    if aligned(plan):
        return ref[:, pl.ds(pl.multiple_of((me ^ k) * plan.width, 128), plan.width)]
    block = ref[:, : plan.width]
    for w in range(1, plan.wide // plan.width):
        block = jnp.where((me ^ k) == w, ref[:, w * plan.width : (w + 1) * plan.width], block)
    return block


def in_tiles(loop, cols, work):
    if not loop or cols % 256:
        work(pl.ds(0, cols))
        return

    @pl.loop(0, cols // 256)
    def _(i):
        work(pl.ds(pl.multiple_of(i * 256, 256), 256))


def eye(rows, cols):
    row = lax.broadcasted_iota(jnp.int32, (rows, cols), 0)
    col = lax.broadcasted_iota(jnp.int32, (rows, cols), 1)
    return (row == col).astype(BF16)


def partial_scores(q_ref, cache_ref, bias):
    req, heads, latent = q_ref.shape
    scores = [
        lax.dot_general(
            q_ref[r], cache_ref[r], (((1,), (1,)), ((), ())), preferred_element_type=F32
        )
        * (NOPE + ROPE) ** (-0.5)
        + bias[r : r + 1, :]
        for r in range(req)
    ]
    return jnp.concatenate(scores, axis=0)


def partial_sums(expo, cache_ref, heads):
    expo = expo.astype(BF16)
    sums = [
        jnp.dot(
            expo[r * heads : (r + 1) * heads],
            cache_ref[r, :, :KV_RANK],
            preferred_element_type=F32,
        )
        for r in range(cache_ref.shape[0])
    ]
    return jnp.concatenate(sums, axis=0)


def payload_tail(lse):
    rows = lse.shape[0]
    hi = lse.astype(BF16).astype(F32)
    mid = (lse - hi).astype(BF16).astype(F32)
    lo = (lse - hi - mid).astype(BF16).astype(F32)
    lane = lax.broadcasted_iota(jnp.int32, (rows, 128), 1)
    spread = jnp.where(lane == 0, hi, jnp.where(lane == 1, mid, jnp.where(lane == 2, lo, 0.0)))
    turned = lax.dot_general(
        spread.astype(BF16), eye(rows, 128), (((0,), (0,)), ((), ())), preferred_element_type=F32
    )
    return jnp.pad(turned[:TAIL], ((0, 0), (0, KV_RANK - 128)))


def prepare_kernel(
    n_wide,
    length_hbm,
    start_hbm,
    owner_hbm,
    gain_hbm,
    q_hbm,
    cache_hbm,
    fresh_hbm,
    residual_hbm,
    out_ref,
    bias_ref,
    gain_out_ref,
    residual_out_ref,
    order_ref,
    cache_ref,
    q_ref,
    *refs,
):
    length_ref, start_ref, owner_ref, gain_ref, fresh_ref, residual_ref, sems = refs
    copies = [
        pltpu.make_async_copy(source, target, sems.at[i])
        for i, (source, target) in enumerate(
            [
                (length_hbm, length_ref),
                (start_hbm, start_ref),
                (owner_hbm, owner_ref),
                (gain_hbm, gain_ref),
                (q_hbm, q_ref),
                (cache_hbm, cache_ref),
                (fresh_hbm, fresh_ref),
                (residual_hbm, residual_ref),
            ]
        )
    ]
    for copy in copies:
        copy.start()
    for copy in copies[:4]:
        copy.wait()
    req, heads, latent = q_ref.shape
    block = cache_ref.shape[1]
    width = gain_ref.shape[0]
    me, me_sub = lax.axis_index("wide"), lax.axis_index("sub")
    group = me_sub * lax.axis_size("pair") + lax.axis_index("pair")

    owners = [owner_ref[group * req + r] for r in range(req)]
    placed = []
    for r in range(req):
        at = jnp.int32(0)
        for j in range(req):
            if j != r:
                ahead = owners[j] <= owners[r] if j < r else owners[j] < owners[r]
                at = at + jnp.where(ahead, 1, 0)
        placed.append(at)
        order_ref[r] = at

    gain_out_ref[...] = gain_ref[...].reshape(1, width).astype(F32)

    biases = []
    for r in range(req):
        following = jnp.where(
            me == n_wide - 1, length_ref[r], start_ref[r, jnp.minimum(me + 1, n_wide - 1)]
        )
        position = lax.broadcasted_iota(jnp.int32, (1, block), 1)
        biases.append(jnp.where(position < following - start_ref[r, me], 0.0, F32(-1e30)))
    bias = jnp.concatenate(biases, axis=0)
    bias_ref[...] = bias

    for copy in copies[4:]:
        copy.wait()
    rows = []
    for i in range(req):
        row = jnp.zeros((1, width), F32)
        for r in range(req):
            row = jnp.where(placed[r] == i, residual_ref[r : r + 1, :].astype(F32), row)
        rows.append(row)
    residual_out_ref[...] = jnp.concatenate(rows, axis=0)

    scores = partial_scores(q_ref, cache_ref, bias)
    fresh = [fresh_ref[r : r + 1, :].astype(F32) for r in range(req)]
    own = jnp.concatenate(
        [
            jnp.sum(q_ref[r].astype(F32) * fresh[r], axis=1, keepdims=True)
            * (NOPE + ROPE) ** (-0.5)
            for r in range(req)
        ],
        axis=0,
    )
    top = jnp.maximum(jnp.max(scores, axis=1, keepdims=True), own)
    expo = jnp.exp(scores - top)
    expo_own = jnp.exp(own - top)
    den = jnp.sum(expo, axis=1, keepdims=True) + expo_own
    weight_own = expo_own.astype(BF16).astype(F32)
    num = partial_sums(expo, cache_ref, heads) + jnp.concatenate(
        [weight_own[r * heads : (r + 1) * heads] * fresh[r][:, :KV_RANK] for r in range(req)],
        axis=0,
    )
    count = req * heads
    out_ref[:count, :] = (num / den).astype(BF16)
    out_ref[count:, :] = payload_tail(top + jnp.log(den)).astype(BF16)


def attend_cost(req, heads, block, latent):
    return pl.CostEstimate(
        flops=2 * req * heads * block * (latent + KV_RANK),
        bytes_accessed=2 * req * (block * latent + heads * (latent + KV_RANK)),
        transcendentals=req * heads * block,
    )


def prepare(length, start, owner, gain, q, cache, fresh, residual):
    req, heads, latent = q.shape
    block, width = cache.shape[1], residual.shape[1]
    n_wide = start.shape[1]
    operands = (length, start, owner, gain, q, cache, fresh, residual)
    return pl.pallas_call(
        functools.partial(prepare_kernel, n_wide),
        out_shape=[
            jax.ShapeDtypeStruct((req * heads + TAIL, KV_RANK), BF16),
            jax.ShapeDtypeStruct((req, block), F32),
            jax.ShapeDtypeStruct((1, width), F32),
            jax.ShapeDtypeStruct((req, width), F32),
            jax.ShapeDtypeStruct((req,), jnp.int32),
            pltpu.VMEM(cache.shape, BF16),
            pltpu.VMEM(q.shape, BF16),
        ],
        in_specs=[HBM] * len(operands),
        out_specs=[VMEM] * 4 + [SMEM, VMEM, VMEM],
        scratch_shapes=[
            pltpu.SMEM(length.shape, jnp.int32),
            pltpu.SMEM(start.shape, jnp.int32),
            pltpu.SMEM(owner.shape, jnp.int32),
            pltpu.VMEM(gain.shape, BF16),
            pltpu.VMEM(fresh.shape, BF16),
            pltpu.VMEM(residual.shape, BF16),
            pltpu.SemaphoreType.DMA((len(operands),)),
        ],
        compiler_params=SMALL,
        cost_estimate=pl.CostEstimate(
            flops=2 * req * heads * block * (latent + KV_RANK),
            bytes_accessed=2 * (cache.size + q.size),
            transcendentals=req * heads * block,
        ),
        name="prepare",
    )(*[in_hbm(x) for x in operands])


def attend_kernel(q_ref, cache_ref, bias_ref, after_ref, out_ref):
    req, heads, latent = q_ref.shape
    scores = partial_scores(q_ref, cache_ref, bias_ref[...])
    top = jnp.max(scores, axis=1, keepdims=True)
    expo = jnp.exp(scores - top)
    den = jnp.sum(expo, axis=1, keepdims=True)
    num = partial_sums(expo, cache_ref, heads)
    count = req * heads
    out_ref[:count, :] = (num / den).astype(BF16)
    out_ref[count:, :] = payload_tail(top + jnp.log(den)).astype(BF16)


def attend(q, cache, bias, after):
    req, heads, latent = q.shape
    return pl.pallas_call(
        attend_kernel,
        out_shape=jax.ShapeDtypeStruct((req * heads + TAIL, KV_RANK), BF16),
        in_specs=[VMEM] * 3 + [ANY],
        out_specs=VMEM,
        compiler_params=SMALL,
        cost_estimate=attend_cost(req, heads, cache.shape[1], latent),
        name="attend",
    )(q, cache, bias, after)


def fetch_kernel(items, plan, both_hbm, proj_hbm, after_ref, *refs):
    for copy in start_items(items, plan, both_hbm, proj_hbm, refs[:-1], refs[-1]):
        copy.wait()


def fetch(items, plan, both, proj, after):
    shapes = item_shapes(items, plan)
    out = pl.pallas_call(
        functools.partial(fetch_kernel, items, plan),
        out_shape=shapes,
        in_specs=[HBM, HBM, ANY],
        out_specs=[VMEM] * len(items),
        scratch_shapes=[item_sems(items)],
        compiler_params=SMALL,
        cost_estimate=pl.CostEstimate(
            flops=0,
            bytes_accessed=2 * sum(math.prod(shape.shape) for shape in shapes),
            transcendentals=0,
        ),
        name="fetch",
    )(in_hbm(both), in_hbm(proj), after)
    return dict(zip(items, out))


def combine_kernel(n_wide, n_sub, req, order_any, after_ref, *refs):
    payloads, outs = refs[:n_wide], refs[n_wide : n_wide + n_sub]
    hold, order_ref, sem = refs[n_wide + n_sub :]
    copy = pltpu.make_async_copy(order_any, order_ref, sem)
    copy.start()
    rows = payloads[0].shape[0] - TAIL
    heads = rows // req
    heads_dev = heads // n_sub
    me_sub = lax.axis_index("sub")
    tails = [p[rows:, :].astype(F32) for p in payloads]
    lses = []
    for tail in tails:
        turned = lax.dot_general(
            eye(rows, 128),
            tail[:, :128].astype(BF16),
            (((1,), (1,)), ((), ())),
            preferred_element_type=F32,
        )
        lses.append(turned[:, 0:1] + turned[:, 1:2] + turned[:, 2:3])
    top = functools.reduce(jnp.maximum, lses)
    weights = [jnp.exp(lse - top) for lse in lses]
    inv = 1.0 / functools.reduce(jnp.add, weights)
    weights = [weight * inv for weight in weights]
    copy.wait()
    for r in range(req):
        at = slice(r * heads, (r + 1) * heads)
        attn = functools.reduce(
            jnp.add, [w[at] * p[at, :].astype(F32) for w, p in zip(weights, payloads)]
        ).astype(BF16)
        for s in range(n_sub):
            hold[s, order_ref[r]] = attn[s * heads_dev : (s + 1) * heads_dev]
    for k in range(n_sub):
        outs[k][...] = hold[me_sub ^ k]


def combine(order, after, payloads, req, n_sub):
    n_wide = len(payloads)
    heads_dev = (payloads[0].shape[0] - TAIL) // req // n_sub
    piece = jax.ShapeDtypeStruct((req, heads_dev, KV_RANK), BF16)
    return pl.pallas_call(
        functools.partial(combine_kernel, n_wide, n_sub, req),
        out_shape=[piece] * n_sub,
        in_specs=[ANY, ANY] + [VMEM] * n_wide,
        out_specs=[VMEM] * n_sub,
        scratch_shapes=[
            pltpu.VMEM((n_sub, req, heads_dev, KV_RANK), BF16),
            pltpu.SMEM(order.shape, jnp.int32),
            pltpu.SemaphoreType.DMA(()),
        ],
        compiler_params=SMALL,
        name="combine",
    )(order, after, *payloads)


def project_kernel(count, items, plan, up_ref, both_hbm, proj_hbm, after_ref, *refs):
    n_wide = plan.wide // plan.width - 1
    pieces, weights, refs = refs[:count], refs[count : count + n_wide], refs[count + n_wide :]
    vals, outs, fetched, sems = refs[0], refs[1 : n_wide + 1], refs[n_wide + 1 : -1], refs[-1]
    copies = start_items(items, plan, both_hbm, proj_hbm, fetched, sems)
    req, heads, rank = pieces[0].shape
    rows = count * req
    cols = up_ref.shape[1]
    stacked = jnp.concatenate([p[...].reshape(req * heads, rank) for p in pieces], axis=0)
    total = rows * heads
    to = lax.broadcasted_iota(jnp.int32, (total, total), 0)
    source = lax.broadcasted_iota(jnp.int32, (total, total), 1)
    turn = (to // rows == source % heads) & (to % rows == source // heads)
    turned = jnp.dot(turn.astype(BF16), stacked, preferred_element_type=F32).astype(BF16)
    some = math.gcd(heads, max(1, 256 // cols))
    for first in range(0, heads, some):
        val = lax.dot_general(
            turned[first * rows : (first + some) * rows],
            up_ref[first : first + some].reshape(some * cols, rank),
            (((1,), (1,)), ((), ())),
            preferred_element_type=F32,
        ).astype(BF16)
        for i in range(some):
            at = slice((first + i) * cols, (first + i + 1) * cols)
            vals[:, at] = val[i * rows : (i + 1) * rows, i * cols : (i + 1) * cols]

    def work(at):
        for k in range(n_wide):
            block = column_block(weights[k], k + 1, plan, at)
            out = jnp.dot(vals[...], block, preferred_element_type=F32)
            outs[k][:, at] = out.astype(outs[k].dtype)

    in_tiles(items, plan.width, work)
    for copy in copies:
        copy.wait()


def project(pieces, value_up, weights, items, plan, both, proj, after):
    count = len(pieces)
    req, heads, rank = pieces[0].shape
    rows = count * req
    n_wide = len(weights)
    out = pl.pallas_call(
        functools.partial(project_kernel, count, items, plan),
        out_shape=[jax.ShapeDtypeStruct((rows, plan.depth), BF16)]
        + [jax.ShapeDtypeStruct((rows, plan.width), BF16)] * n_wide
        + item_shapes(items, plan),
        in_specs=[VMEM, HBM, HBM, ANY] + [VMEM] * (count + n_wide),
        out_specs=[VMEM] * (n_wide + 1 + len(items)),
        scratch_shapes=[item_sems(items)],
        compiler_params=SMALL,
        cost_estimate=pl.CostEstimate(
            flops=2 * rows * plan.depth * plan.wide,
            bytes_accessed=2 * plan.depth * plan.wide,
            transcendentals=0,
        ),
        name="project",
    )(value_up, in_hbm(both), in_hbm(proj), after, *pieces, *weights)
    return out[0], out[1 : n_wide + 1], dict(zip(items, out[n_wide + 1 :]))


def merge_kernel(mine_ref, residual_ref, after_ref, *refs):
    arrived, (total_ref, send_ref) = refs[:-2], refs[-2:]
    req = residual_ref.shape[0]
    total = mine_ref[...]
    for a in arrived:
        total = total + a[...].astype(F32)
    total_ref[...] = total
    total_ref[:req, :] = total[:req] + residual_ref[...]
    send_ref[...] = total_ref[...].astype(BF16)


def merge(mine, residual, after, arrived):
    return pl.pallas_call(
        merge_kernel,
        out_shape=[jax.ShapeDtypeStruct(mine.shape, F32), jax.ShapeDtypeStruct(mine.shape, BF16)],
        in_specs=[VMEM, VMEM, ANY] + [VMEM] * len(arrived),
        out_specs=[VMEM] * 2,
        compiler_params=SMALL,
        name="merge",
    )(mine, residual, after, *arrived)


def norm_kernel(req, mine_ref, gain_ref, after_ref, *refs):
    arrived, (gained_ref, stream_ref) = refs[:-2], refs[-2:]
    width = mine_ref.shape[1]
    blocks = [mine_ref[i * req : (i + 1) * req, :] for i in range(len(arrived) + 1)]
    for j, a in enumerate(arrived):
        others = a[...].astype(F32)
        for i in range(len(blocks)):
            at = (i ^ (j + 1)) * req
            blocks[i] = blocks[i] + others[at : at + req]
    stream_ref[...] = blocks[0]
    total = jnp.concatenate(blocks, axis=0)
    gained_ref[:, :width] = (total * gain_ref[...]).astype(BF16)
    square = jnp.sum(total * total, axis=1, keepdims=True)
    hi = square.astype(BF16).astype(F32)
    mid = (square - hi).astype(BF16).astype(F32)
    lo = (square - hi - mid).astype(BF16).astype(F32)
    lane = lax.broadcasted_iota(jnp.int32, (total.shape[0], 128), 1)
    spread = jnp.where(lane == 0, hi, jnp.where(lane == 1, mid, jnp.where(lane == 2, lo, 0.0)))
    gained_ref[:, width:] = spread.astype(BF16)


def norm(mine, gain, after, arrived, req):
    rows, width = mine.shape
    return pl.pallas_call(
        functools.partial(norm_kernel, req),
        out_shape=[
            jax.ShapeDtypeStruct((rows, width + 128), BF16),
            jax.ShapeDtypeStruct((req, width), F32),
        ],
        in_specs=[VMEM, VMEM, ANY] + [VMEM] * len(arrived),
        out_specs=[VMEM] * 2,
        compiler_params=SMALL,
        name="norm",
    )(mine, gain, after, *arrived)


def gate_kernel(count, first, plan, x_ref, later_ref, *refs):
    weights, carry, outs = refs[:count], refs[count : -count - 1], refs[-count - 1 :]
    square = x_ref[:, plan.width :].astype(F32)
    outs[count][...] = square if first else square + carry[count][...]
    x = x_ref[:, : plan.width]

    def multiply(i, at):
        product = jnp.dot(x, weights[i][:, at], preferred_element_type=F32)
        outs[i][:, at] = product if first else product + carry[i][:, at]

    def work(at):
        multiply(0, at)
        multiply(1, at)

    in_tiles(False, plan.full, work)
    for i in range(2, count):
        multiply(i, pl.ds(0, weights[i].shape[1]))


def gate(x, weights, carry, later, plan):
    rows = x.shape[0]
    count = len(weights)
    return pl.pallas_call(
        functools.partial(gate_kernel, count, not carry, plan),
        out_shape=[jax.ShapeDtypeStruct((rows, w.shape[1]), F32) for w in weights]
        + [jax.ShapeDtypeStruct((rows, 128), F32)],
        in_specs=[VMEM] * (2 + count + len(carry)),
        out_specs=[VMEM] * (count + 1),
        compiler_params=SMALL,
        cost_estimate=pl.CostEstimate(
            flops=4 * rows * plan.width * plan.units,
            bytes_accessed=4 * plan.width * plan.units,
            transcendentals=0,
        ),
        name="gate",
    )(x, later, *weights, *carry)


def hidden_units(plan, operands):
    *sums, square_ref = operands
    square = square_ref[:, 0:1] + square_ref[:, 1:2] + square_ref[:, 2:3]
    inv = lax.rsqrt(square / D + 1e-06)
    both = [sums[0][...], sums[1][...]]
    if len(sums) > 2:
        half = plan.units - plan.full
        both = [
            jnp.concatenate([part, sums[2][:, g * half : (g + 1) * half]], axis=1)
            for g, part in enumerate(both)
        ]
    g = both[0] * inv
    return (g / (1.0 + jnp.exp(-g)) * (both[1] * inv)).astype(BF16)


def down_kernel(ks, plan, weight_ref, *refs):
    operands, hidden_ref, outs = refs[: -1 - len(ks)], refs[-1 - len(ks)], refs[-len(ks) :]
    hidden = hidden_units(plan, operands)
    hidden_ref[...] = hidden
    for k, out in zip(ks, outs):
        block = column_block(weight_ref, k, plan, pl.ds(0, plan.width))
        out[...] = jnp.dot(hidden, block, preferred_element_type=F32).astype(BF16)


def down(weight, operands, ks, plan):
    rows = operands[0].shape[0]
    return pl.pallas_call(
        functools.partial(down_kernel, ks, plan),
        out_shape=[jax.ShapeDtypeStruct((rows, plan.units), BF16)]
        + [jax.ShapeDtypeStruct((rows, plan.width), BF16)] * len(ks),
        in_specs=[VMEM] * (1 + len(operands)),
        out_specs=[VMEM] * (1 + len(ks)),
        compiler_params=SMALL,
        cost_estimate=pl.CostEstimate(
            flops=2 * rows * plan.units * plan.width * len(ks),
            bytes_accessed=2 * plan.units * plan.width * len(ks),
            transcendentals=0,
        ),
        name="down",
    )(weight, *operands)


def own_kernel(plan, weight_ref, rows_ref, after_ref, out_ref):
    block = column_block(weight_ref, 0, plan, pl.ds(0, plan.width))
    out_ref[...] = jnp.dot(rows_ref[...], block, preferred_element_type=F32)


def own(weight, rows, after, plan):
    return pl.pallas_call(
        functools.partial(own_kernel, plan),
        out_shape=jax.ShapeDtypeStruct((rows.shape[0], plan.width), F32),
        in_specs=[VMEM, VMEM, ANY],
        out_specs=VMEM,
        compiler_params=SMALL,
        cost_estimate=pl.CostEstimate(
            flops=2 * rows.size * plan.width,
            bytes_accessed=2 * rows.shape[1] * plan.width,
            transcendentals=0,
        ),
        name="own",
    )(weight, rows, after)


def split_kernel(mine_ref, stream_ref, *refs):
    req = stream_ref.shape[0]
    count = mine_ref.shape[0] // req
    arrived, outs = refs[:-count], refs[-count:]
    total = mine_ref[...]
    for a in arrived:
        total = total + a[...].astype(F32)
    outs[0][...] = total[:req] + stream_ref[...]
    for j in range(1, count):
        outs[j][...] = total[j * req : (j + 1) * req].astype(BF16)


def split(mine, stream, arrived):
    req, width = stream.shape
    count = mine.shape[0] // req
    return pl.pallas_call(
        split_kernel,
        out_shape=[jax.ShapeDtypeStruct((req, width), F32)]
        + [jax.ShapeDtypeStruct((req, width), BF16)] * (count - 1),
        in_specs=[VMEM] * (2 + len(arrived)),
        out_specs=[VMEM] * count,
        compiler_params=SMALL,
        name="split",
    )(mine, stream, *arrived)


def body(
    latent_cache,
    queries,
    new_latent,
    context_len,
    block_start,
    owner,
    value_up,
    out_proj,
    residual_in,
    norm_gain,
    gate_up,
    down_weight,
):
    n_wide = lax.axis_size("wide")
    n_sub = lax.axis_size("sub")
    n_pair = lax.axis_size("pair")
    req_grp = latent_cache.shape[0]
    width_dev = residual_in.shape[1]

    powers = [k for k in range(1, n_wide) if k & (k - 1) == 0]
    arrived = {k: hop(queries, "wide", k) for k in reversed(powers[1:])}
    units = down_weight.shape[0]
    plan = Plan(
        width=width_dev,
        units=units,
        full=units - 128 if units % 256 == 128 else units,
        depth=out_proj.shape[0] * out_proj.shape[1],
        wide=D,
    )
    payload, bias, gain, residual, order, cache, near_q = prepare(
        context_len,
        block_start,
        owner,
        norm_gain,
        queries,
        latent_cache,
        new_latent,
        residual_in,
    )
    proj = out_proj.reshape(plan.depth, D)

    kinds = ("gate", "rest", "up") if plan.full < units else ("gate", "up")
    held = {}

    def bring(items, after):
        got = fetch(items, plan, gate_up, proj, after)
        held.update(got)
        return got[items[-1]]

    far = list(range(n_wide - 1, -1, -1))
    queue = [("out", k) for k in far] + [(kind, k) for k in range(n_wide - 1) for kind in kinds]
    queue += [(kind, n_wide - 1) for kind in sorted(kinds, key=("rest", "gate", "up").index)]

    def take(count):
        items = queue[:count]
        del queue[:count]
        return items

    arrived[1] = hop(near_q, "wide", 1)
    payloads = {0: payload}
    payload = bring(take(n_wide - 1), payload)
    for k in powers[1:]:
        arrived[k], payload = lax.optimization_barrier((arrived[k], payload))
    waited = False
    for k in powers[1:] + powers[:1] + [k for k in range(n_wide) if k not in [0] + powers]:
        if k not in arrived:
            low = k & -k
            arrived[k] = hop(arrived[k - low], "wide", low)
            if not waited:
                payload = bring(take(2), payload)
                waited = True
        payload = attend(arrived[k], cache, bias, payload)
        payloads[k] = payload
    far_k = n_wide - 1
    payloads[1], payloads[far_k] = lax.optimization_barrier((payloads[1], payloads[far_k]))
    last = bring(take(5), payload)
    payloads = [payloads[0]] + [hop(payloads[k], "wide", k) for k in range(1, n_wide)]
    chunks = combine(order, last, payloads, req_grp, n_sub)

    peers = [(ks, kp) for kp in range(n_pair) for ks in range(n_sub)]
    masks = [ks * n_pair + kp for ks, kp in peers]
    pieces = [chunks[0]] + [hop_group(chunks[ks], ks * n_pair + kp) for ks, kp in peers[1:]]
    last = bring(take(2), chunks[0])
    vals, sends, got = project(
        pieces,
        jnp.swapaxes(value_up, 1, 2),
        [held["out", k] for k in range(1, n_wide)],
        take(2),
        plan,
        gate_up,
        proj,
        last,
    )
    held.update(got)

    back = [hop(sends[k - 1], "wide", k) for k in range(n_wide - 1, 0, -1)]
    mine = own(held["out", 0], vals, vals, plan)
    last = bring(take(len(queue)), mine)
    total, send = merge(mine, residual, last, back)
    back = [hop_group(send, k) for k in masks[1:]]
    gained, stream = norm(total, gain, last, back, req_grp)

    carry = ()
    for k in range(n_wide):
        x = hop(gained, "wide", k) if k else gained
        weights = [held[item] for item in (("gate", k), ("up", k), ("rest", k)) if item in held]
        carry = gate(x, weights, carry, down_weight, plan)
    away = far[:-1]
    hidden, *sends = down(down_weight, carry, away, plan)
    back = [hop(send, "wide", k) for k, send in zip(away, sends)]
    mine = own(down_weight, hidden, sends[-1], plan)
    out, *sends = split(mine, stream, back)
    for k, send in zip(masks[1:], sends):
        out = out + hop_group(send, k).astype(F32)
    return out.astype(BF16)


def solution(mesh):
    in_specs = (
        P(("groups", "sub", "pair"), "wide", None),
        P(("groups", "sub", "pair"), "wide", None),
        P(("groups", "sub", "pair"), None),
        P(("groups", "sub", "pair")),
        P(("groups", "sub", "pair"), None),
        P("groups"),
        P(("wide", "sub"), None, "pair"),
        P(("wide", "sub"), "pair", None),
        P(("groups", "sub", "pair"), "wide"),
        P("wide"),
        P(None, None, ("wide", "sub", "pair")),
        P(("wide", "sub", "pair"), None),
    )
    out_specs = P(("groups", "sub", "pair"), "wide")
    return jax.shard_map(body, mesh=mesh, in_specs=in_specs, out_specs=out_specs, check_vma=False)
```

```python
import collections
import functools
import math

import jax
import jax.numpy as jnp
from jax import lax
from jax.experimental import pallas as pl
from jax.experimental.pallas import tpu as pltpu
from jax.sharding import PartitionSpec as P

D = 7168
KV_RANK = 512
ROPE = 64
NOPE = 128
F32 = jnp.float32
BF16 = jnp.bfloat16
TAIL = 8
VMEM = pl.BlockSpec(memory_space=pltpu.VMEM)
SMEM = pl.BlockSpec(memory_space=pltpu.SMEM)
ANY = pl.BlockSpec(memory_space=pl.ANY)
HBM = pl.BlockSpec(memory_space=pltpu.HBM)
SMALL = pltpu.CompilerParams(vmem_limit_bytes=4 * 2**20)


def hop(x, axis, k):
    n = lax.axis_size(axis)
    return lax.ppermute(x, axis, [(i, i ^ k) for i in range(n)])


def hop_group(x, k):
    n = lax.axis_size("sub") * lax.axis_size("pair")
    return lax.ppermute(x, ("sub", "pair"), [(i, i ^ k) for i in range(n)])


def in_hbm(x):
    return pltpu.with_memory_space_constraint(x, pltpu.HBM)


Plan = collections.namedtuple("Plan", ["width", "units", "full", "depth", "wide"])


def aligned(plan):
    return plan.width % 128 == 0


def item_shape(item, plan):
    kind, k = item
    cols = plan.width if aligned(plan) else plan.wide
    if kind == "out":
        return (plan.depth, cols)
    if kind == "rest":
        return (plan.width, 2 * (plan.units - plan.full))
    return (plan.width, plan.full)


def item_copies(item, plan, source, out):
    kind, k = item
    start = (lax.axis_index("wide") ^ k) * plan.width
    if kind == "out":
        if not aligned(plan):
            return [(source, out)]
        return [(source.at[:, pl.ds(pl.multiple_of(start, 128), plan.width)], out)]
    rows = pl.ds(pl.multiple_of(start, 64), plan.width)
    if kind == "rest":
        half = plan.units - plan.full
        return [
            (source.at[g, rows, plan.full :], out.at[:, g * half : (g + 1) * half])
            for g in range(2)
        ]
    return [(source.at[int(kind == "up"), rows, : plan.full], out)]


def start_items(items, plan, both, proj, outs, sems):
    pairs = []
    for item, out in zip(items, outs):
        pairs += item_copies(item, plan, proj if item[0] == "out" else both, out)
    copies = [
        pltpu.make_async_copy(source, out, sems.at[i]) for i, (source, out) in enumerate(pairs)
    ]

    @pl.when(lax.axis_index("wide") >= 0)
    def _():
        for copy in copies:
            copy.start()

    return copies


def item_shapes(items, plan):
    return [pltpu.VMEM(item_shape(item, plan), BF16) for item in items]


def item_sems(items):
    return pltpu.SemaphoreType.DMA((max(1, sum(2 if i[0] == "rest" else 1 for i in items)),))


def column_block(ref, k, plan, at):
    me = lax.axis_index("wide")
    if ref.shape[1] == plan.width:
        return ref[:, at]
    if aligned(plan):
        return ref[:, pl.ds(pl.multiple_of((me ^ k) * plan.width, 128), plan.width)]
    block = ref[:, : plan.width]
    for w in range(1, plan.wide // plan.width):
        block = jnp.where((me ^ k) == w, ref[:, w * plan.width : (w + 1) * plan.width], block)
    return block


def in_tiles(loop, cols, work):
    if not loop or cols % 256:
        work(pl.ds(0, cols))
        return

    @pl.loop(0, cols // 256)
    def _(i):
        work(pl.ds(pl.multiple_of(i * 256, 256), 256))


def eye(rows, cols):
    row = lax.broadcasted_iota(jnp.int32, (rows, cols), 0)
    col = lax.broadcasted_iota(jnp.int32, (rows, cols), 1)
    return (row == col).astype(BF16)


def partial_scores(q_ref, cache_ref, bias):
    req, heads, latent = q_ref.shape
    scores = [
        lax.dot_general(
            q_ref[r], cache_ref[r], (((1,), (1,)), ((), ())), preferred_element_type=F32
        )
        * (NOPE + ROPE) ** (-0.5)
        + bias[r : r + 1, :]
        for r in range(req)
    ]
    return jnp.concatenate(scores, axis=0)


def partial_sums(expo, cache_ref, heads):
    expo = expo.astype(BF16)
    sums = [
        jnp.dot(
            expo[r * heads : (r + 1) * heads],
            cache_ref[r, :, :KV_RANK],
            preferred_element_type=F32,
        )
        for r in range(cache_ref.shape[0])
    ]
    return jnp.concatenate(sums, axis=0)


def payload_tail(lse):
    rows = lse.shape[0]
    hi = lse.astype(BF16).astype(F32)
    mid = (lse - hi).astype(BF16).astype(F32)
    lo = (lse - hi - mid).astype(BF16).astype(F32)
    lane = lax.broadcasted_iota(jnp.int32, (rows, 128), 1)
    spread = jnp.where(lane == 0, hi, jnp.where(lane == 1, mid, jnp.where(lane == 2, lo, 0.0)))
    turned = lax.dot_general(
        spread.astype(BF16), eye(rows, 128), (((0,), (0,)), ((), ())), preferred_element_type=F32
    )
    return jnp.pad(turned[:TAIL], ((0, 0), (0, KV_RANK - 128)))


def prepare_kernel(
    n_wide,
    length_hbm,
    start_hbm,
    owner_hbm,
    gain_hbm,
    q_hbm,
    cache_hbm,
    fresh_hbm,
    residual_hbm,
    out_ref,
    bias_ref,
    gain_out_ref,
    residual_out_ref,
    order_ref,
    cache_ref,
    *refs,
):
    length_ref, start_ref, owner_ref, gain_ref, q_ref, fresh_ref, residual_ref, sems = refs
    copies = [
        pltpu.make_async_copy(source, target, sems.at[i])
        for i, (source, target) in enumerate(
            [
                (length_hbm, length_ref),
                (start_hbm, start_ref),
                (owner_hbm, owner_ref),
                (gain_hbm, gain_ref),
                (q_hbm, q_ref),
                (cache_hbm, cache_ref),
                (fresh_hbm, fresh_ref),
                (residual_hbm, residual_ref),
            ]
        )
    ]
    for copy in copies:
        copy.start()
    for copy in copies[:4]:
        copy.wait()
    req, heads, latent = q_ref.shape
    block = cache_ref.shape[1]
    width = gain_ref.shape[0]
    me, me_sub = lax.axis_index("wide"), lax.axis_index("sub")
    group = me_sub * lax.axis_size("pair") + lax.axis_index("pair")

    owners = [owner_ref[group * req + r] for r in range(req)]
    placed = []
    for r in range(req):
        at = jnp.int32(0)
        for j in range(req):
            if j != r:
                ahead = owners[j] <= owners[r] if j < r else owners[j] < owners[r]
                at = at + jnp.where(ahead, 1, 0)
        placed.append(at)
        order_ref[r] = at

    gain_out_ref[...] = gain_ref[...].reshape(1, width).astype(F32)

    biases = []
    for r in range(req):
        following = jnp.where(
            me == n_wide - 1, length_ref[r], start_ref[r, jnp.minimum(me + 1, n_wide - 1)]
        )
        position = lax.broadcasted_iota(jnp.int32, (1, block), 1)
        biases.append(jnp.where(position < following - start_ref[r, me], 0.0, F32(-1e30)))
    bias = jnp.concatenate(biases, axis=0)
    bias_ref[...] = bias

    for copy in copies[4:]:
        copy.wait()
    rows = []
    for i in range(req):
        row = jnp.zeros((1, width), F32)
        for r in range(req):
            row = jnp.where(placed[r] == i, residual_ref[r : r + 1, :].astype(F32), row)
        rows.append(row)
    residual_out_ref[...] = jnp.concatenate(rows, axis=0)

    scores = partial_scores(q_ref, cache_ref, bias)
    fresh = [fresh_ref[r : r + 1, :].astype(F32) for r in range(req)]
    own = jnp.concatenate(
        [
            jnp.sum(q_ref[r].astype(F32) * fresh[r], axis=1, keepdims=True)
            * (NOPE + ROPE) ** (-0.5)
            for r in range(req)
        ],
        axis=0,
    )
    top = jnp.maximum(jnp.max(scores, axis=1, keepdims=True), own)
    expo = jnp.exp(scores - top)
    expo_own = jnp.exp(own - top)
    den = jnp.sum(expo, axis=1, keepdims=True) + expo_own
    weight_own = expo_own.astype(BF16).astype(F32)
    num = partial_sums(expo, cache_ref, heads) + jnp.concatenate(
        [weight_own[r * heads : (r + 1) * heads] * fresh[r][:, :KV_RANK] for r in range(req)],
        axis=0,
    )
    count = req * heads
    out_ref[:count, :] = (num / den).astype(BF16)
    out_ref[count:, :] = payload_tail(top + jnp.log(den)).astype(BF16)


def attend_cost(req, heads, block, latent):
    return pl.CostEstimate(
        flops=2 * req * heads * block * (latent + KV_RANK),
        bytes_accessed=2 * req * (block * latent + heads * (latent + KV_RANK)),
        transcendentals=req * heads * block,
    )


def prepare(length, start, owner, gain, q, cache, fresh, residual):
    req, heads, latent = q.shape
    block, width = cache.shape[1], residual.shape[1]
    n_wide = start.shape[1]
    operands = (length, start, owner, gain, q, cache, fresh, residual)
    return pl.pallas_call(
        functools.partial(prepare_kernel, n_wide),
        out_shape=[
            jax.ShapeDtypeStruct((req * heads + TAIL, KV_RANK), BF16),
            jax.ShapeDtypeStruct((req, block), F32),
            jax.ShapeDtypeStruct((1, width), F32),
            jax.ShapeDtypeStruct((req, width), F32),
            jax.ShapeDtypeStruct((req,), jnp.int32),
            pltpu.VMEM(cache.shape, BF16),
        ],
        in_specs=[HBM] * len(operands),
        out_specs=[VMEM] * 4 + [SMEM, VMEM],
        scratch_shapes=[
            pltpu.SMEM(length.shape, jnp.int32),
            pltpu.SMEM(start.shape, jnp.int32),
            pltpu.SMEM(owner.shape, jnp.int32),
            pltpu.VMEM(gain.shape, BF16),
            pltpu.VMEM(q.shape, BF16),
            pltpu.VMEM(fresh.shape, BF16),
            pltpu.VMEM(residual.shape, BF16),
            pltpu.SemaphoreType.DMA((len(operands),)),
        ],
        compiler_params=SMALL,
        cost_estimate=pl.CostEstimate(
            flops=2 * req * heads * block * (latent + KV_RANK),
            bytes_accessed=2 * (cache.size + q.size),
            transcendentals=req * heads * block,
        ),
        name="prepare",
    )(*[in_hbm(x) for x in operands])


def attend_kernel(q_ref, cache_ref, bias_ref, after_ref, out_ref):
    req, heads, latent = q_ref.shape
    scores = partial_scores(q_ref, cache_ref, bias_ref[...])
    top = jnp.max(scores, axis=1, keepdims=True)
    expo = jnp.exp(scores - top)
    den = jnp.sum(expo, axis=1, keepdims=True)
    num = partial_sums(expo, cache_ref, heads)
    count = req * heads
    out_ref[:count, :] = (num / den).astype(BF16)
    out_ref[count:, :] = payload_tail(top + jnp.log(den)).astype(BF16)


def attend(q, cache, bias, after):
    req, heads, latent = q.shape
    return pl.pallas_call(
        attend_kernel,
        out_shape=jax.ShapeDtypeStruct((req * heads + TAIL, KV_RANK), BF16),
        in_specs=[VMEM] * 3 + [ANY],
        out_specs=VMEM,
        compiler_params=SMALL,
        cost_estimate=attend_cost(req, heads, cache.shape[1], latent),
        name="attend",
    )(q, cache, bias, after)


def fetch_kernel(items, plan, both_hbm, proj_hbm, after_ref, *refs):
    for copy in start_items(items, plan, both_hbm, proj_hbm, refs[:-1], refs[-1]):
        copy.wait()


def fetch(items, plan, both, proj, after):
    shapes = item_shapes(items, plan)
    out = pl.pallas_call(
        functools.partial(fetch_kernel, items, plan),
        out_shape=shapes,
        in_specs=[HBM, HBM, ANY],
        out_specs=[VMEM] * len(items),
        scratch_shapes=[item_sems(items)],
        compiler_params=SMALL,
        cost_estimate=pl.CostEstimate(
            flops=0,
            bytes_accessed=2 * sum(math.prod(shape.shape) for shape in shapes),
            transcendentals=0,
        ),
        name="fetch",
    )(in_hbm(both), in_hbm(proj), after)
    return dict(zip(items, out))


def combine_kernel(n_wide, n_sub, req, order_any, after_ref, *refs):
    payloads, outs = refs[:n_wide], refs[n_wide : n_wide + n_sub]
    hold, order_ref, sem = refs[n_wide + n_sub :]
    copy = pltpu.make_async_copy(order_any, order_ref, sem)
    copy.start()
    rows = payloads[0].shape[0] - TAIL
    heads = rows // req
    heads_dev = heads // n_sub
    me_sub = lax.axis_index("sub")
    tails = [p[rows:, :].astype(F32) for p in payloads]
    lses = []
    for tail in tails:
        turned = lax.dot_general(
            eye(rows, 128),
            tail[:, :128].astype(BF16),
            (((1,), (1,)), ((), ())),
            preferred_element_type=F32,
        )
        lses.append(turned[:, 0:1] + turned[:, 1:2] + turned[:, 2:3])
    top = functools.reduce(jnp.maximum, lses)
    weights = [jnp.exp(lse - top) for lse in lses]
    inv = 1.0 / functools.reduce(jnp.add, weights)
    weights = [weight * inv for weight in weights]
    copy.wait()
    for r in range(req):
        at = slice(r * heads, (r + 1) * heads)
        attn = functools.reduce(
            jnp.add, [w[at] * p[at, :].astype(F32) for w, p in zip(weights, payloads)]
        ).astype(BF16)
        for s in range(n_sub):
            hold[s, order_ref[r]] = attn[s * heads_dev : (s + 1) * heads_dev]
    for k in range(n_sub):
        outs[k][...] = hold[me_sub ^ k]


def combine(order, after, payloads, req, n_sub):
    n_wide = len(payloads)
    heads_dev = (payloads[0].shape[0] - TAIL) // req // n_sub
    piece = jax.ShapeDtypeStruct((req, heads_dev, KV_RANK), BF16)
    return pl.pallas_call(
        functools.partial(combine_kernel, n_wide, n_sub, req),
        out_shape=[piece] * n_sub,
        in_specs=[ANY, ANY] + [VMEM] * n_wide,
        out_specs=[VMEM] * n_sub,
        scratch_shapes=[
            pltpu.VMEM((n_sub, req, heads_dev, KV_RANK), BF16),
            pltpu.SMEM(order.shape, jnp.int32),
            pltpu.SemaphoreType.DMA(()),
        ],
        compiler_params=SMALL,
        name="combine",
    )(order, after, *payloads)


def project_kernel(count, items, plan, up_ref, both_hbm, proj_hbm, after_ref, *refs):
    n_wide = plan.wide // plan.width - 1
    pieces, weights, refs = refs[:count], refs[count : count + n_wide], refs[count + n_wide :]
    vals, outs, fetched, sems = refs[0], refs[1 : n_wide + 1], refs[n_wide + 1 : -1], refs[-1]
    copies = start_items(items, plan, both_hbm, proj_hbm, fetched, sems)
    req, heads, rank = pieces[0].shape
    rows = count * req
    cols = up_ref.shape[1]
    stacked = jnp.concatenate([p[...].reshape(req * heads, rank) for p in pieces], axis=0)
    total = rows * heads
    to = lax.broadcasted_iota(jnp.int32, (total, total), 0)
    source = lax.broadcasted_iota(jnp.int32, (total, total), 1)
    turn = (to // rows == source % heads) & (to % rows == source // heads)
    turned = jnp.dot(turn.astype(BF16), stacked, preferred_element_type=F32).astype(BF16)
    some = math.gcd(heads, max(1, 256 // cols))
    for first in range(0, heads, some):
        val = lax.dot_general(
            turned[first * rows : (first + some) * rows],
            up_ref[first : first + some].reshape(some * cols, rank),
            (((1,), (1,)), ((), ())),
            preferred_element_type=F32,
        ).astype(BF16)
        for i in range(some):
            at = slice((first + i) * cols, (first + i + 1) * cols)
            vals[:, at] = val[i * rows : (i + 1) * rows, i * cols : (i + 1) * cols]

    def work(at):
        for k in range(n_wide):
            block = column_block(weights[k], k + 1, plan, at)
            out = jnp.dot(vals[...], block, preferred_element_type=F32)
            outs[k][:, at] = out.astype(outs[k].dtype)

    in_tiles(items, plan.width, work)
    for copy in copies:
        copy.wait()


def project(pieces, value_up, weights, items, plan, both, proj, after):
    count = len(pieces)
    req, heads, rank = pieces[0].shape
    rows = count * req
    n_wide = len(weights)
    out = pl.pallas_call(
        functools.partial(project_kernel, count, items, plan),
        out_shape=[jax.ShapeDtypeStruct((rows, plan.depth), BF16)]
        + [jax.ShapeDtypeStruct((rows, plan.width), BF16)] * n_wide
        + item_shapes(items, plan),
        in_specs=[VMEM, HBM, HBM, ANY] + [VMEM] * (count + n_wide),
        out_specs=[VMEM] * (n_wide + 1 + len(items)),
        scratch_shapes=[item_sems(items)],
        compiler_params=SMALL,
        cost_estimate=pl.CostEstimate(
            flops=2 * rows * plan.depth * plan.wide,
            bytes_accessed=2 * plan.depth * plan.wide,
            transcendentals=0,
        ),
        name="project",
    )(value_up, in_hbm(both), in_hbm(proj), after, *pieces, *weights)
    return out[0], out[1 : n_wide + 1], dict(zip(items, out[n_wide + 1 :]))


def merge_kernel(mine_ref, residual_ref, after_ref, *refs):
    arrived, (total_ref, send_ref) = refs[:-2], refs[-2:]
    req = residual_ref.shape[0]
    total = mine_ref[...]
    for a in arrived:
        total = total + a[...].astype(F32)
    total_ref[...] = total
    total_ref[:req, :] = total[:req] + residual_ref[...]
    send_ref[...] = total_ref[...].astype(BF16)


def merge(mine, residual, after, arrived):
    return pl.pallas_call(
        merge_kernel,
        out_shape=[jax.ShapeDtypeStruct(mine.shape, F32), jax.ShapeDtypeStruct(mine.shape, BF16)],
        in_specs=[VMEM, VMEM, ANY] + [VMEM] * len(arrived),
        out_specs=[VMEM] * 2,
        compiler_params=SMALL,
        name="merge",
    )(mine, residual, after, *arrived)


def norm_kernel(req, mine_ref, gain_ref, after_ref, *refs):
    arrived, (gained_ref, stream_ref) = refs[:-2], refs[-2:]
    width = mine_ref.shape[1]
    blocks = [mine_ref[i * req : (i + 1) * req, :] for i in range(len(arrived) + 1)]
    for j, a in enumerate(arrived):
        others = a[...].astype(F32)
        for i in range(len(blocks)):
            at = (i ^ (j + 1)) * req
            blocks[i] = blocks[i] + others[at : at + req]
    stream_ref[...] = blocks[0]
    total = jnp.concatenate(blocks, axis=0)
    gained_ref[:, :width] = (total * gain_ref[...]).astype(BF16)
    square = jnp.sum(total * total, axis=1, keepdims=True)
    hi = square.astype(BF16).astype(F32)
    mid = (square - hi).astype(BF16).astype(F32)
    lo = (square - hi - mid).astype(BF16).astype(F32)
    lane = lax.broadcasted_iota(jnp.int32, (total.shape[0], 128), 1)
    spread = jnp.where(lane == 0, hi, jnp.where(lane == 1, mid, jnp.where(lane == 2, lo, 0.0)))
    gained_ref[:, width:] = spread.astype(BF16)


def norm(mine, gain, after, arrived, req):
    rows, width = mine.shape
    return pl.pallas_call(
        functools.partial(norm_kernel, req),
        out_shape=[
            jax.ShapeDtypeStruct((rows, width + 128), BF16),
            jax.ShapeDtypeStruct((req, width), F32),
        ],
        in_specs=[VMEM, VMEM, ANY] + [VMEM] * len(arrived),
        out_specs=[VMEM] * 2,
        compiler_params=SMALL,
        name="norm",
    )(mine, gain, after, *arrived)


def gate_kernel(count, first, plan, x_ref, later_ref, *refs):
    weights, carry, outs = refs[:count], refs[count : -count - 1], refs[-count - 1 :]
    square = x_ref[:, plan.width :].astype(F32)
    outs[count][...] = square if first else square + carry[count][...]
    x = x_ref[:, : plan.width]

    def multiply(i, at):
        product = jnp.dot(x, weights[i][:, at], preferred_element_type=F32)
        outs[i][:, at] = product if first else product + carry[i][:, at]

    def work(at):
        multiply(0, at)
        multiply(1, at)

    in_tiles(False, plan.full, work)
    for i in range(2, count):
        multiply(i, pl.ds(0, weights[i].shape[1]))


def gate(x, weights, carry, later, plan):
    rows = x.shape[0]
    count = len(weights)
    return pl.pallas_call(
        functools.partial(gate_kernel, count, not carry, plan),
        out_shape=[jax.ShapeDtypeStruct((rows, w.shape[1]), F32) for w in weights]
        + [jax.ShapeDtypeStruct((rows, 128), F32)],
        in_specs=[VMEM] * (2 + count + len(carry)),
        out_specs=[VMEM] * (count + 1),
        compiler_params=SMALL,
        cost_estimate=pl.CostEstimate(
            flops=4 * rows * plan.width * plan.units,
            bytes_accessed=4 * plan.width * plan.units,
            transcendentals=0,
        ),
        name="gate",
    )(x, later, *weights, *carry)


def hidden_units(plan, operands):
    *sums, square_ref = operands
    square = square_ref[:, 0:1] + square_ref[:, 1:2] + square_ref[:, 2:3]
    inv = lax.rsqrt(square / D + 1e-06)
    both = [sums[0][...], sums[1][...]]
    if len(sums) > 2:
        half = plan.units - plan.full
        both = [
            jnp.concatenate([part, sums[2][:, g * half : (g + 1) * half]], axis=1)
            for g, part in enumerate(both)
        ]
    g = both[0] * inv
    return (g / (1.0 + jnp.exp(-g)) * (both[1] * inv)).astype(BF16)


def down_kernel(ks, plan, weight_ref, *refs):
    operands, hidden_ref, outs = refs[: -1 - len(ks)], refs[-1 - len(ks)], refs[-len(ks) :]
    hidden = hidden_units(plan, operands)
    hidden_ref[...] = hidden
    for k, out in zip(ks, outs):
        block = column_block(weight_ref, k, plan, pl.ds(0, plan.width))
        out[...] = jnp.dot(hidden, block, preferred_element_type=F32).astype(BF16)


def down(weight, operands, ks, plan):
    rows = operands[0].shape[0]
    return pl.pallas_call(
        functools.partial(down_kernel, ks, plan),
        out_shape=[jax.ShapeDtypeStruct((rows, plan.units), BF16)]
        + [jax.ShapeDtypeStruct((rows, plan.width), BF16)] * len(ks),
        in_specs=[VMEM] * (1 + len(operands)),
        out_specs=[VMEM] * (1 + len(ks)),
        compiler_params=SMALL,
        cost_estimate=pl.CostEstimate(
            flops=2 * rows * plan.units * plan.width * len(ks),
            bytes_accessed=2 * plan.units * plan.width * len(ks),
            transcendentals=0,
        ),
        name="down",
    )(weight, *operands)


def own_kernel(plan, weight_ref, rows_ref, after_ref, out_ref):
    block = column_block(weight_ref, 0, plan, pl.ds(0, plan.width))
    out_ref[...] = jnp.dot(rows_ref[...], block, preferred_element_type=F32)


def own(weight, rows, after, plan):
    return pl.pallas_call(
        functools.partial(own_kernel, plan),
        out_shape=jax.ShapeDtypeStruct((rows.shape[0], plan.width), F32),
        in_specs=[VMEM, VMEM, ANY],
        out_specs=VMEM,
        compiler_params=SMALL,
        cost_estimate=pl.CostEstimate(
            flops=2 * rows.size * plan.width,
            bytes_accessed=2 * rows.shape[1] * plan.width,
            transcendentals=0,
        ),
        name="own",
    )(weight, rows, after)


def split_kernel(mine_ref, stream_ref, *refs):
    req = stream_ref.shape[0]
    count = mine_ref.shape[0] // req
    arrived, outs = refs[:-count], refs[-count:]
    total = mine_ref[...]
    for a in arrived:
        total = total + a[...].astype(F32)
    outs[0][...] = total[:req] + stream_ref[...]
    for j in range(1, count):
        outs[j][...] = total[j * req : (j + 1) * req].astype(BF16)


def split(mine, stream, arrived):
    req, width = stream.shape
    count = mine.shape[0] // req
    return pl.pallas_call(
        split_kernel,
        out_shape=[jax.ShapeDtypeStruct((req, width), F32)]
        + [jax.ShapeDtypeStruct((req, width), BF16)] * (count - 1),
        in_specs=[VMEM] * (2 + len(arrived)),
        out_specs=[VMEM] * count,
        compiler_params=SMALL,
        name="split",
    )(mine, stream, *arrived)


def body(
    latent_cache,
    queries,
    new_latent,
    context_len,
    block_start,
    owner,
    value_up,
    out_proj,
    residual_in,
    norm_gain,
    gate_up,
    down_weight,
):
    n_wide = lax.axis_size("wide")
    n_sub = lax.axis_size("sub")
    n_pair = lax.axis_size("pair")
    req_grp = latent_cache.shape[0]
    width_dev = residual_in.shape[1]

    powers = [k for k in range(1, n_wide) if k & (k - 1) == 0]
    arrived = {k: hop(queries, "wide", k) for k in reversed(powers)}
    units = down_weight.shape[0]
    plan = Plan(
        width=width_dev,
        units=units,
        full=units - 128 if units % 256 == 128 else units,
        depth=out_proj.shape[0] * out_proj.shape[1],
        wide=D,
    )
    payload, bias, gain, residual, order, cache = prepare(
        context_len,
        block_start,
        owner,
        norm_gain,
        queries,
        latent_cache,
        new_latent,
        residual_in,
    )
    proj = out_proj.reshape(plan.depth, D)

    kinds = ("gate", "rest", "up") if plan.full < units else ("gate", "up")
    held = {}

    def bring(items, after):
        got = fetch(items, plan, gate_up, proj, after)
        held.update(got)
        return got[items[-1]]

    far = list(range(n_wide - 1, -1, -1))
    queue = [("out", k) for k in far] + [(kind, k) for k in range(n_wide - 1) for kind in kinds]
    queue += [(kind, n_wide - 1) for kind in sorted(kinds, key=("rest", "gate", "up").index)]

    def take(count):
        items = queue[:count]
        del queue[:count]
        return items

    payloads = [payload]
    payload = bring(take(n_wide - 1), payload)
    waited = False
    for k in range(1, n_wide):
        if k not in arrived:
            low = k & -k
            arrived[k] = hop(arrived[k - low], "wide", low)
            if not waited:
                payload = bring(take(2), payload)
                waited = True
        elif k > 1:
            arrived[k], payload = lax.optimization_barrier((arrived[k], payload))
        payload = attend(arrived[k], cache, bias, payload)
        payloads.append(payload)
    payloads[1], payloads[-1] = lax.optimization_barrier((payloads[1], payloads[-1]))
    last = bring(take(4), payload)
    payloads = [payloads[0]] + [hop(payloads[k], "wide", k) for k in range(1, n_wide)]
    chunks = combine(order, last, payloads, req_grp, n_sub)

    peers = [(ks, kp) for kp in range(n_pair) for ks in range(n_sub)]
    masks = [ks * n_pair + kp for ks, kp in peers]
    pieces = [chunks[0]] + [hop_group(chunks[ks], ks * n_pair + kp) for ks, kp in peers[1:]]
    last = bring(take(2), chunks[0])
    vals, sends, got = project(
        pieces,
        jnp.swapaxes(value_up, 1, 2),
        [held["out", k] for k in range(1, n_wide)],
        take(3),
        plan,
        gate_up,
        proj,
        last,
    )
    held.update(got)

    back = [hop(sends[k - 1], "wide", k) for k in range(n_wide - 1, 0, -1)]
    mine = own(held["out", 0], vals, vals, plan)
    last = bring(take(len(queue)), mine)
    total, send = merge(mine, residual, last, back)
    back = [hop_group(send, k) for k in masks[1:]]
    gained, stream = norm(total, gain, last, back, req_grp)

    carry = ()
    for k in range(n_wide):
        x = hop(gained, "wide", k) if k else gained
        weights = [held[item] for item in (("gate", k), ("up", k), ("rest", k)) if item in held]
        carry = gate(x, weights, carry, down_weight, plan)
    away = far[:-1]
    hidden, *sends = down(down_weight, carry, away, plan)
    back = [hop(send, "wide", k) for k, send in zip(away, sends)]
    mine = own(down_weight, hidden, sends[-1], plan)
    out, *sends = split(mine, stream, back)
    for k, send in zip(masks[1:], sends):
        out = out + hop_group(send, k).astype(F32)
    return out.astype(BF16)


def solution(mesh):
    in_specs = (
        P(("groups", "sub", "pair"), "wide", None),
        P(("groups", "sub", "pair"), "wide", None),
        P(("groups", "sub", "pair"), None),
        P(("groups", "sub", "pair")),
        P(("groups", "sub", "pair"), None),
        P("groups"),
        P(("wide", "sub"), None, "pair"),
        P(("wide", "sub"), "pair", None),
        P(("groups", "sub", "pair"), "wide"),
        P("wide"),
        P(None, None, ("wide", "sub", "pair")),
        P(("wide", "sub", "pair"), None),
    )
    out_specs = P(("groups", "sub", "pair"), "wide")
    return jax.shard_map(body, mesh=mesh, in_specs=in_specs, out_specs=out_specs, check_vma=False)
```

```python
import collections
import functools
import math

import jax
import jax.numpy as jnp
from jax import lax
from jax.experimental import pallas as pl
from jax.experimental.pallas import tpu as pltpu
from jax.sharding import PartitionSpec as P

D = 7168
KV_RANK = 512
ROPE = 64
NOPE = 128
F32 = jnp.float32
BF16 = jnp.bfloat16
TAIL = 8
VMEM = pl.BlockSpec(memory_space=pltpu.VMEM)
SMEM = pl.BlockSpec(memory_space=pltpu.SMEM)
ANY = pl.BlockSpec(memory_space=pl.ANY)
HBM = pl.BlockSpec(memory_space=pltpu.HBM)
SMALL = pltpu.CompilerParams(vmem_limit_bytes=4 * 2**20)


def hop(x, axis, k):
    n = lax.axis_size(axis)
    return lax.ppermute(x, axis, [(i, i ^ k) for i in range(n)])


def hop_group(x, k):
    n = lax.axis_size("sub") * lax.axis_size("pair")
    return lax.ppermute(x, ("sub", "pair"), [(i, i ^ k) for i in range(n)])


def in_hbm(x):
    return pltpu.with_memory_space_constraint(x, pltpu.HBM)


Plan = collections.namedtuple("Plan", ["width", "units", "full", "depth", "wide"])


def aligned(plan):
    return plan.width % 128 == 0


def item_shape(item, plan):
    kind, k = item
    cols = plan.width if aligned(plan) else plan.wide
    if kind == "out":
        return (plan.depth, cols)
    if kind == "rest":
        return (plan.width, 2 * (plan.units - plan.full))
    return (plan.width, plan.full)


def item_copies(item, plan, source, out):
    kind, k = item
    start = (lax.axis_index("wide") ^ k) * plan.width
    if kind == "out":
        if not aligned(plan):
            return [(source, out)]
        return [(source.at[:, pl.ds(pl.multiple_of(start, 128), plan.width)], out)]
    rows = pl.ds(pl.multiple_of(start, 64), plan.width)
    if kind == "rest":
        half = plan.units - plan.full
        return [
            (source.at[g, rows, plan.full :], out.at[:, g * half : (g + 1) * half])
            for g in range(2)
        ]
    return [(source.at[int(kind == "up"), rows, : plan.full], out)]


def start_items(items, plan, both, proj, outs, sems):
    pairs = []
    for item, out in zip(items, outs):
        pairs += item_copies(item, plan, proj if item[0] == "out" else both, out)
    copies = [
        pltpu.make_async_copy(source, out, sems.at[i]) for i, (source, out) in enumerate(pairs)
    ]

    @pl.when(lax.axis_index("wide") >= 0)
    def _():
        for copy in copies:
            copy.start()

    return copies


def item_shapes(items, plan):
    return [pltpu.VMEM(item_shape(item, plan), BF16) for item in items]


def item_sems(items):
    return pltpu.SemaphoreType.DMA((max(1, sum(2 if i[0] == "rest" else 1 for i in items)),))


def column_block(ref, k, plan, at):
    me = lax.axis_index("wide")
    if ref.shape[1] == plan.width:
        return ref[:, at]
    if aligned(plan):
        return ref[:, pl.ds(pl.multiple_of((me ^ k) * plan.width, 128), plan.width)]
    block = ref[:, : plan.width]
    for w in range(1, plan.wide // plan.width):
        block = jnp.where((me ^ k) == w, ref[:, w * plan.width : (w + 1) * plan.width], block)
    return block


def in_tiles(loop, cols, work):
    if not loop or cols % 256:
        work(pl.ds(0, cols))
        return

    @pl.loop(0, cols // 256)
    def _(i):
        work(pl.ds(pl.multiple_of(i * 256, 256), 256))


def eye(rows, cols):
    row = lax.broadcasted_iota(jnp.int32, (rows, cols), 0)
    col = lax.broadcasted_iota(jnp.int32, (rows, cols), 1)
    return (row == col).astype(BF16)


def partial_scores(q_ref, cache_ref, bias):
    req, heads, latent = q_ref.shape
    scores = [
        lax.dot_general(
            q_ref[r], cache_ref[r], (((1,), (1,)), ((), ())), preferred_element_type=F32
        )
        * (NOPE + ROPE) ** (-0.5)
        + bias[r : r + 1, :]
        for r in range(req)
    ]
    return jnp.concatenate(scores, axis=0)


def partial_sums(expo, cache_ref, heads):
    expo = expo.astype(BF16)
    sums = [
        jnp.dot(
            expo[r * heads : (r + 1) * heads],
            cache_ref[r, :, :KV_RANK],
            preferred_element_type=F32,
        )
        for r in range(cache_ref.shape[0])
    ]
    return jnp.concatenate(sums, axis=0)


def payload_tail(lse):
    rows = lse.shape[0]
    hi = lse.astype(BF16).astype(F32)
    mid = (lse - hi).astype(BF16).astype(F32)
    lo = (lse - hi - mid).astype(BF16).astype(F32)
    lane = lax.broadcasted_iota(jnp.int32, (rows, 128), 1)
    spread = jnp.where(lane == 0, hi, jnp.where(lane == 1, mid, jnp.where(lane == 2, lo, 0.0)))
    turned = lax.dot_general(
        spread.astype(BF16), eye(rows, 128), (((0,), (0,)), ((), ())), preferred_element_type=F32
    )
    return jnp.pad(turned[:TAIL], ((0, 0), (0, KV_RANK - 128)))


def prepare_kernel(
    n_wide,
    length_hbm,
    start_hbm,
    owner_hbm,
    gain_hbm,
    q_hbm,
    cache_hbm,
    fresh_hbm,
    residual_hbm,
    out_ref,
    bias_ref,
    gain_out_ref,
    residual_out_ref,
    order_ref,
    cache_ref,
    *refs,
):
    length_ref, start_ref, owner_ref, gain_ref, q_ref, fresh_ref, residual_ref, sems = refs
    copies = [
        pltpu.make_async_copy(source, target, sems.at[i])
        for i, (source, target) in enumerate(
            [
                (length_hbm, length_ref),
                (start_hbm, start_ref),
                (owner_hbm, owner_ref),
                (gain_hbm, gain_ref),
                (q_hbm, q_ref),
                (cache_hbm, cache_ref),
                (fresh_hbm, fresh_ref),
                (residual_hbm, residual_ref),
            ]
        )
    ]
    for copy in copies:
        copy.start()
    for copy in copies[:4]:
        copy.wait()
    req, heads, latent = q_ref.shape
    block = cache_ref.shape[1]
    width = gain_ref.shape[0]
    me, me_sub = lax.axis_index("wide"), lax.axis_index("sub")
    group = me_sub * lax.axis_size("pair") + lax.axis_index("pair")

    owners = [owner_ref[group * req + r] for r in range(req)]
    placed = []
    for r in range(req):
        at = jnp.int32(0)
        for j in range(req):
            if j != r:
                ahead = owners[j] <= owners[r] if j < r else owners[j] < owners[r]
                at = at + jnp.where(ahead, 1, 0)
        placed.append(at)
        order_ref[r] = at

    gain_out_ref[...] = gain_ref[...].reshape(1, width).astype(F32)

    biases = []
    for r in range(req):
        following = jnp.where(
            me == n_wide - 1, length_ref[r], start_ref[r, jnp.minimum(me + 1, n_wide - 1)]
        )
        position = lax.broadcasted_iota(jnp.int32, (1, block), 1)
        biases.append(jnp.where(position < following - start_ref[r, me], 0.0, F32(-1e30)))
    bias = jnp.concatenate(biases, axis=0)
    bias_ref[...] = bias

    for copy in copies[4:]:
        copy.wait()
    rows = []
    for i in range(req):
        row = jnp.zeros((1, width), F32)
        for r in range(req):
            row = jnp.where(placed[r] == i, residual_ref[r : r + 1, :].astype(F32), row)
        rows.append(row)
    residual_out_ref[...] = jnp.concatenate(rows, axis=0)

    scores = partial_scores(q_ref, cache_ref, bias)
    fresh = [fresh_ref[r : r + 1, :].astype(F32) for r in range(req)]
    own = jnp.concatenate(
        [
            jnp.sum(q_ref[r].astype(F32) * fresh[r], axis=1, keepdims=True)
            * (NOPE + ROPE) ** (-0.5)
            for r in range(req)
        ],
        axis=0,
    )
    top = jnp.maximum(jnp.max(scores, axis=1, keepdims=True), own)
    expo = jnp.exp(scores - top)
    expo_own = jnp.exp(own - top)
    den = jnp.sum(expo, axis=1, keepdims=True) + expo_own
    weight_own = expo_own.astype(BF16).astype(F32)
    num = partial_sums(expo, cache_ref, heads) + jnp.concatenate(
        [weight_own[r * heads : (r + 1) * heads] * fresh[r][:, :KV_RANK] for r in range(req)],
        axis=0,
    )
    count = req * heads
    out_ref[:count, :] = (num / den).astype(BF16)
    out_ref[count:, :] = payload_tail(top + jnp.log(den)).astype(BF16)


def attend_cost(req, heads, block, latent):
    return pl.CostEstimate(
        flops=2 * req * heads * block * (latent + KV_RANK),
        bytes_accessed=2 * req * (block * latent + heads * (latent + KV_RANK)),
        transcendentals=req * heads * block,
    )


def prepare(length, start, owner, gain, q, cache, fresh, residual):
    req, heads, latent = q.shape
    block, width = cache.shape[1], residual.shape[1]
    n_wide = start.shape[1]
    operands = (length, start, owner, gain, q, cache, fresh, residual)
    return pl.pallas_call(
        functools.partial(prepare_kernel, n_wide),
        out_shape=[
            jax.ShapeDtypeStruct((req * heads + TAIL, KV_RANK), BF16),
            jax.ShapeDtypeStruct((req, block), F32),
            jax.ShapeDtypeStruct((1, width), F32),
            jax.ShapeDtypeStruct((req, width), F32),
            jax.ShapeDtypeStruct((req,), jnp.int32),
            pltpu.VMEM(cache.shape, BF16),
        ],
        in_specs=[HBM] * len(operands),
        out_specs=[VMEM] * 4 + [SMEM, VMEM],
        scratch_shapes=[
            pltpu.SMEM(length.shape, jnp.int32),
            pltpu.SMEM(start.shape, jnp.int32),
            pltpu.SMEM(owner.shape, jnp.int32),
            pltpu.VMEM(gain.shape, BF16),
            pltpu.VMEM(q.shape, BF16),
            pltpu.VMEM(fresh.shape, BF16),
            pltpu.VMEM(residual.shape, BF16),
            pltpu.SemaphoreType.DMA((len(operands),)),
        ],
        compiler_params=SMALL,
        cost_estimate=pl.CostEstimate(
            flops=2 * req * heads * block * (latent + KV_RANK),
            bytes_accessed=2 * (cache.size + q.size),
            transcendentals=req * heads * block,
        ),
        name="prepare",
    )(*[in_hbm(x) for x in operands])


def attend_kernel(q_ref, cache_ref, bias_ref, after_ref, out_ref):
    req, heads, latent = q_ref.shape
    scores = partial_scores(q_ref, cache_ref, bias_ref[...])
    top = jnp.max(scores, axis=1, keepdims=True)
    expo = jnp.exp(scores - top)
    den = jnp.sum(expo, axis=1, keepdims=True)
    num = partial_sums(expo, cache_ref, heads)
    count = req * heads
    out_ref[:count, :] = (num / den).astype(BF16)
    out_ref[count:, :] = payload_tail(top + jnp.log(den)).astype(BF16)


def attend(q, cache, bias, after):
    req, heads, latent = q.shape
    return pl.pallas_call(
        attend_kernel,
        out_shape=jax.ShapeDtypeStruct((req * heads + TAIL, KV_RANK), BF16),
        in_specs=[VMEM] * 3 + [ANY],
        out_specs=VMEM,
        compiler_params=SMALL,
        cost_estimate=attend_cost(req, heads, cache.shape[1], latent),
        name="attend",
    )(q, cache, bias, after)


def fetch_kernel(items, plan, both_hbm, proj_hbm, after_ref, *refs):
    for copy in start_items(items, plan, both_hbm, proj_hbm, refs[:-1], refs[-1]):
        copy.wait()


def fetch(items, plan, both, proj, after):
    shapes = item_shapes(items, plan)
    out = pl.pallas_call(
        functools.partial(fetch_kernel, items, plan),
        out_shape=shapes,
        in_specs=[HBM, HBM, ANY],
        out_specs=[VMEM] * len(items),
        scratch_shapes=[item_sems(items)],
        compiler_params=SMALL,
        cost_estimate=pl.CostEstimate(
            flops=0,
            bytes_accessed=2 * sum(math.prod(shape.shape) for shape in shapes),
            transcendentals=0,
        ),
        name="fetch",
    )(in_hbm(both), in_hbm(proj), after)
    return dict(zip(items, out))


def combine_kernel(n_wide, n_sub, req, order_any, after_ref, *refs):
    payloads, outs = refs[:n_wide], refs[n_wide : n_wide + n_sub]
    hold, order_ref, sem = refs[n_wide + n_sub :]
    copy = pltpu.make_async_copy(order_any, order_ref, sem)
    copy.start()
    rows = payloads[0].shape[0] - TAIL
    heads = rows // req
    heads_dev = heads // n_sub
    me_sub = lax.axis_index("sub")
    tails = [p[rows:, :].astype(F32) for p in payloads]
    lses = []
    for tail in tails:
        turned = lax.dot_general(
            eye(rows, 128),
            tail[:, :128].astype(BF16),
            (((1,), (1,)), ((), ())),
            preferred_element_type=F32,
        )
        lses.append(turned[:, 0:1] + turned[:, 1:2] + turned[:, 2:3])
    top = functools.reduce(jnp.maximum, lses)
    weights = [jnp.exp(lse - top) for lse in lses]
    inv = 1.0 / functools.reduce(jnp.add, weights)
    weights = [weight * inv for weight in weights]
    copy.wait()
    for r in range(req):
        at = slice(r * heads, (r + 1) * heads)
        attn = functools.reduce(
            jnp.add, [w[at] * p[at, :].astype(F32) for w, p in zip(weights, payloads)]
        ).astype(BF16)
        for s in range(n_sub):
            hold[s, order_ref[r]] = attn[s * heads_dev : (s + 1) * heads_dev]
    for k in range(n_sub):
        outs[k][...] = hold[me_sub ^ k]


def combine(order, after, payloads, req, n_sub):
    n_wide = len(payloads)
    heads_dev = (payloads[0].shape[0] - TAIL) // req // n_sub
    piece = jax.ShapeDtypeStruct((req, heads_dev, KV_RANK), BF16)
    return pl.pallas_call(
        functools.partial(combine_kernel, n_wide, n_sub, req),
        out_shape=[piece] * n_sub,
        in_specs=[ANY, ANY] + [VMEM] * n_wide,
        out_specs=[VMEM] * n_sub,
        scratch_shapes=[
            pltpu.VMEM((n_sub, req, heads_dev, KV_RANK), BF16),
            pltpu.SMEM(order.shape, jnp.int32),
            pltpu.SemaphoreType.DMA(()),
        ],
        compiler_params=SMALL,
        name="combine",
    )(order, after, *payloads)


def project_kernel(count, items, plan, up_ref, both_hbm, proj_hbm, after_ref, *refs):
    n_wide = plan.wide // plan.width - 1
    pieces, weights, refs = refs[:count], refs[count : count + n_wide], refs[count + n_wide :]
    vals, outs, fetched, sems = refs[0], refs[1 : n_wide + 1], refs[n_wide + 1 : -1], refs[-1]
    copies = start_items(items, plan, both_hbm, proj_hbm, fetched, sems)
    req, heads, rank = pieces[0].shape
    rows = count * req
    cols = up_ref.shape[1]
    stacked = jnp.concatenate([p[...].reshape(req * heads, rank) for p in pieces], axis=0)
    total = rows * heads
    to = lax.broadcasted_iota(jnp.int32, (total, total), 0)
    source = lax.broadcasted_iota(jnp.int32, (total, total), 1)
    turn = (to // rows == source % heads) & (to % rows == source // heads)
    turned = jnp.dot(turn.astype(BF16), stacked, preferred_element_type=F32).astype(BF16)
    some = math.gcd(heads, max(1, 256 // cols))
    for first in range(0, heads, some):
        val = lax.dot_general(
            turned[first * rows : (first + some) * rows],
            up_ref[first : first + some].reshape(some * cols, rank),
            (((1,), (1,)), ((), ())),
            preferred_element_type=F32,
        ).astype(BF16)
        for i in range(some):
            at = slice((first + i) * cols, (first + i + 1) * cols)
            vals[:, at] = val[i * rows : (i + 1) * rows, i * cols : (i + 1) * cols]

    def work(at):
        for k in range(n_wide):
            block = column_block(weights[k], k + 1, plan, at)
            out = jnp.dot(vals[...], block, preferred_element_type=F32)
            outs[k][:, at] = out.astype(outs[k].dtype)

    in_tiles(items, plan.width, work)
    for copy in copies:
        copy.wait()


def project(pieces, value_up, weights, items, plan, both, proj, after):
    count = len(pieces)
    req, heads, rank = pieces[0].shape
    rows = count * req
    n_wide = len(weights)
    out = pl.pallas_call(
        functools.partial(project_kernel, count, items, plan),
        out_shape=[jax.ShapeDtypeStruct((rows, plan.depth), BF16)]
        + [jax.ShapeDtypeStruct((rows, plan.width), BF16)] * n_wide
        + item_shapes(items, plan),
        in_specs=[VMEM, HBM, HBM, ANY] + [VMEM] * (count + n_wide),
        out_specs=[VMEM] * (n_wide + 1 + len(items)),
        scratch_shapes=[item_sems(items)],
        compiler_params=SMALL,
        cost_estimate=pl.CostEstimate(
            flops=2 * rows * plan.depth * plan.wide,
            bytes_accessed=2 * plan.depth * plan.wide,
            transcendentals=0,
        ),
        name="project",
    )(value_up, in_hbm(both), in_hbm(proj), after, *pieces, *weights)
    return out[0], out[1 : n_wide + 1], dict(zip(items, out[n_wide + 1 :]))


def merge_kernel(mine_ref, residual_ref, after_ref, *refs):
    arrived, (total_ref, send_ref) = refs[:-2], refs[-2:]
    req = residual_ref.shape[0]
    total = mine_ref[...]
    for a in arrived:
        total = total + a[...].astype(F32)
    total_ref[...] = total
    total_ref[:req, :] = total[:req] + residual_ref[...]
    send_ref[...] = total_ref[...].astype(BF16)


def merge(mine, residual, after, arrived):
    return pl.pallas_call(
        merge_kernel,
        out_shape=[jax.ShapeDtypeStruct(mine.shape, F32), jax.ShapeDtypeStruct(mine.shape, BF16)],
        in_specs=[VMEM, VMEM, ANY] + [VMEM] * len(arrived),
        out_specs=[VMEM] * 2,
        compiler_params=SMALL,
        name="merge",
    )(mine, residual, after, *arrived)


def norm_kernel(req, mine_ref, gain_ref, after_ref, *refs):
    arrived, (gained_ref, stream_ref) = refs[:-2], refs[-2:]
    width = mine_ref.shape[1]
    blocks = [mine_ref[i * req : (i + 1) * req, :] for i in range(len(arrived) + 1)]
    for j, a in enumerate(arrived):
        others = a[...].astype(F32)
        for i in range(len(blocks)):
            at = (i ^ (j + 1)) * req
            blocks[i] = blocks[i] + others[at : at + req]
    stream_ref[...] = blocks[0]
    total = jnp.concatenate(blocks, axis=0)
    gained_ref[:, :width] = (total * gain_ref[...]).astype(BF16)
    square = jnp.sum(total * total, axis=1, keepdims=True)
    hi = square.astype(BF16).astype(F32)
    mid = (square - hi).astype(BF16).astype(F32)
    lo = (square - hi - mid).astype(BF16).astype(F32)
    lane = lax.broadcasted_iota(jnp.int32, (total.shape[0], 128), 1)
    spread = jnp.where(lane == 0, hi, jnp.where(lane == 1, mid, jnp.where(lane == 2, lo, 0.0)))
    gained_ref[:, width:] = spread.astype(BF16)


def norm(mine, gain, after, arrived, req):
    rows, width = mine.shape
    return pl.pallas_call(
        functools.partial(norm_kernel, req),
        out_shape=[
            jax.ShapeDtypeStruct((rows, width + 128), BF16),
            jax.ShapeDtypeStruct((req, width), F32),
        ],
        in_specs=[VMEM, VMEM, ANY] + [VMEM] * len(arrived),
        out_specs=[VMEM] * 2,
        compiler_params=SMALL,
        name="norm",
    )(mine, gain, after, *arrived)


def gate_kernel(count, first, plan, x_ref, later_ref, *refs):
    weights, carry, outs = refs[:count], refs[count : -count - 1], refs[-count - 1 :]
    square = x_ref[:, plan.width :].astype(F32)
    outs[count][...] = square if first else square + carry[count][...]
    x = x_ref[:, : plan.width]

    def multiply(i, at):
        product = jnp.dot(x, weights[i][:, at], preferred_element_type=F32)
        outs[i][:, at] = product if first else product + carry[i][:, at]

    def work(at):
        multiply(0, at)
        multiply(1, at)

    in_tiles(False, plan.full, work)
    for i in range(2, count):
        multiply(i, pl.ds(0, weights[i].shape[1]))


def gate(x, weights, carry, later, plan):
    rows = x.shape[0]
    count = len(weights)
    return pl.pallas_call(
        functools.partial(gate_kernel, count, not carry, plan),
        out_shape=[jax.ShapeDtypeStruct((rows, w.shape[1]), F32) for w in weights]
        + [jax.ShapeDtypeStruct((rows, 128), F32)],
        in_specs=[VMEM] * (2 + count + len(carry)),
        out_specs=[VMEM] * (count + 1),
        compiler_params=SMALL,
        cost_estimate=pl.CostEstimate(
            flops=4 * rows * plan.width * plan.units,
            bytes_accessed=4 * plan.width * plan.units,
            transcendentals=0,
        ),
        name="gate",
    )(x, later, *weights, *carry)


def hidden_units(plan, operands):
    *sums, square_ref = operands
    square = square_ref[:, 0:1] + square_ref[:, 1:2] + square_ref[:, 2:3]
    inv = lax.rsqrt(square / D + 1e-06)
    both = [sums[0][...], sums[1][...]]
    if len(sums) > 2:
        half = plan.units - plan.full
        both = [
            jnp.concatenate([part, sums[2][:, g * half : (g + 1) * half]], axis=1)
            for g, part in enumerate(both)
        ]
    g = both[0] * inv
    return (g / (1.0 + jnp.exp(-g)) * (both[1] * inv)).astype(BF16)


def down_kernel(ks, plan, weight_ref, *refs):
    operands, hidden_ref, outs = refs[: -1 - len(ks)], refs[-1 - len(ks)], refs[-len(ks) :]
    hidden = hidden_units(plan, operands)
    hidden_ref[...] = hidden
    for k, out in zip(ks, outs):
        block = column_block(weight_ref, k, plan, pl.ds(0, plan.width))
        out[...] = jnp.dot(hidden, block, preferred_element_type=F32).astype(BF16)


def down(weight, operands, ks, plan):
    rows = operands[0].shape[0]
    return pl.pallas_call(
        functools.partial(down_kernel, ks, plan),
        out_shape=[jax.ShapeDtypeStruct((rows, plan.units), BF16)]
        + [jax.ShapeDtypeStruct((rows, plan.width), BF16)] * len(ks),
        in_specs=[VMEM] * (1 + len(operands)),
        out_specs=[VMEM] * (1 + len(ks)),
        compiler_params=SMALL,
        cost_estimate=pl.CostEstimate(
            flops=2 * rows * plan.units * plan.width * len(ks),
            bytes_accessed=2 * plan.units * plan.width * len(ks),
            transcendentals=0,
        ),
        name="down",
    )(weight, *operands)


def own_kernel(plan, weight_ref, rows_ref, after_ref, out_ref):
    block = column_block(weight_ref, 0, plan, pl.ds(0, plan.width))
    out_ref[...] = jnp.dot(rows_ref[...], block, preferred_element_type=F32)


def own(weight, rows, after, plan):
    return pl.pallas_call(
        functools.partial(own_kernel, plan),
        out_shape=jax.ShapeDtypeStruct((rows.shape[0], plan.width), F32),
        in_specs=[VMEM, VMEM, ANY],
        out_specs=VMEM,
        compiler_params=SMALL,
        cost_estimate=pl.CostEstimate(
            flops=2 * rows.size * plan.width,
            bytes_accessed=2 * rows.shape[1] * plan.width,
            transcendentals=0,
        ),
        name="own",
    )(weight, rows, after)


def split_kernel(mine_ref, stream_ref, *refs):
    req = stream_ref.shape[0]
    count = mine_ref.shape[0] // req
    arrived, outs = refs[:-count], refs[-count:]
    total = mine_ref[...]
    for a in arrived:
        total = total + a[...].astype(F32)
    outs[0][...] = total[:req] + stream_ref[...]
    for j in range(1, count):
        outs[j][...] = total[j * req : (j + 1) * req].astype(BF16)


def split(mine, stream, arrived):
    req, width = stream.shape
    count = mine.shape[0] // req
    return pl.pallas_call(
        split_kernel,
        out_shape=[jax.ShapeDtypeStruct((req, width), F32)]
        + [jax.ShapeDtypeStruct((req, width), BF16)] * (count - 1),
        in_specs=[VMEM] * (2 + len(arrived)),
        out_specs=[VMEM] * count,
        compiler_params=SMALL,
        name="split",
    )(mine, stream, *arrived)


def body(
    latent_cache,
    queries,
    new_latent,
    context_len,
    block_start,
    owner,
    value_up,
    out_proj,
    residual_in,
    norm_gain,
    gate_up,
    down_weight,
):
    n_wide = lax.axis_size("wide")
    n_sub = lax.axis_size("sub")
    n_pair = lax.axis_size("pair")
    req_grp = latent_cache.shape[0]
    width_dev = residual_in.shape[1]

    powers = [k for k in range(1, n_wide) if k & (k - 1) == 0]
    arrived = {k: hop(queries, "wide", k) for k in reversed(powers)}
    units = down_weight.shape[0]
    plan = Plan(
        width=width_dev,
        units=units,
        full=units - 128 if units % 256 == 128 else units,
        depth=out_proj.shape[0] * out_proj.shape[1],
        wide=D,
    )
    payload, bias, gain, residual, order, cache = prepare(
        context_len,
        block_start,
        owner,
        norm_gain,
        queries,
        latent_cache,
        new_latent,
        residual_in,
    )
    proj = out_proj.reshape(plan.depth, D)

    kinds = ("gate", "rest", "up") if plan.full < units else ("gate", "up")
    held = {}

    def bring(items, after):
        got = fetch(items, plan, gate_up, proj, after)
        held.update(got)
        return got[items[-1]]

    far = list(range(n_wide - 1, -1, -1))
    queue = [("out", k) for k in far] + [(kind, k) for k in range(n_wide - 1) for kind in kinds]
    queue += [(kind, n_wide - 1) for kind in sorted(kinds, key=("rest", "gate", "up").index)]

    def take(count):
        items = queue[:count]
        del queue[:count]
        return items

    payloads = [payload]
    payload = bring(take(n_wide - 1), payload)
    waited = False
    for k in range(1, n_wide):
        if k not in arrived:
            low = k & -k
            arrived[k] = hop(arrived[k - low], "wide", low)
            if not waited:
                payload = bring(take(1), payload)
                waited = True
        elif k > 1:
            arrived[k], payload = lax.optimization_barrier((arrived[k], payload))
        payload = attend(arrived[k], cache, bias, payload)
        payloads.append(payload)
    payloads[1], payloads[-1] = lax.optimization_barrier((payloads[1], payloads[-1]))
    last = bring(take(5), payload)
    payloads = [payloads[0]] + [hop(payloads[k], "wide", k) for k in range(1, n_wide)]
    chunks = combine(order, last, payloads, req_grp, n_sub)

    peers = [(ks, kp) for kp in range(n_pair) for ks in range(n_sub)]
    masks = [ks * n_pair + kp for ks, kp in peers]
    pieces = [chunks[0]] + [hop_group(chunks[ks], ks * n_pair + kp) for ks, kp in peers[1:]]
    last = bring(take(2), chunks[0])
    vals, sends, got = project(
        pieces,
        jnp.swapaxes(value_up, 1, 2),
        [held["out", k] for k in range(1, n_wide)],
        take(3),
        plan,
        gate_up,
        proj,
        last,
    )
    held.update(got)

    back = [hop(sends[k - 1], "wide", k) for k in range(n_wide - 1, 0, -1)]
    mine = own(held["out", 0], vals, vals, plan)
    last = bring(take(len(queue)), mine)
    total, send = merge(mine, residual, last, back)
    back = [hop_group(send, k) for k in masks[1:]]
    gained, stream = norm(total, gain, last, back, req_grp)

    carry = ()
    for k in range(n_wide):
        x = hop(gained, "wide", k) if k else gained
        weights = [held[item] for item in (("gate", k), ("up", k), ("rest", k)) if item in held]
        carry = gate(x, weights, carry, down_weight, plan)
    away = far[:-1]
    hidden, *sends = down(down_weight, carry, away, plan)
    back = [hop(send, "wide", k) for k, send in zip(away, sends)]
    mine = own(down_weight, hidden, sends[-1], plan)
    out, *sends = split(mine, stream, back)
    for k, send in zip(masks[1:], sends):
        out = out + hop_group(send, k).astype(F32)
    return out.astype(BF16)


def solution(mesh):
    in_specs = (
        P(("groups", "sub", "pair"), "wide", None),
        P(("groups", "sub", "pair"), "wide", None),
        P(("groups", "sub", "pair"), None),
        P(("groups", "sub", "pair")),
        P(("groups", "sub", "pair"), None),
        P("groups"),
        P(("wide", "sub"), None, "pair"),
        P(("wide", "sub"), "pair", None),
        P(("groups", "sub", "pair"), "wide"),
        P("wide"),
        P(None, None, ("wide", "sub", "pair")),
        P(("wide", "sub", "pair"), None),
    )
    out_specs = P(("groups", "sub", "pair"), "wide")
    return jax.shard_map(body, mesh=mesh, in_specs=in_specs, out_specs=out_specs, check_vma=False)
```
